32 devices in a mesh: dp: 4 (over y, core), blk: 8 (over z, x).
Axes of the slice: x: 2, y: 2, z: 4, core: 2. Of those that a mesh axis runs over, the one named last changes fastest.
Arguments:
- dec_in: bfloat16 [4, 4096, 768], P('dp', 'blk'), may hold values from -6 to 6
- encodings: bfloat16 [4, 1024, 768], P('dp', 'blk'), may hold values from -6 to 6
- enc_question: int32 [4, 1024], P('dp', 'blk'), may hold values from 0 to 3, as said below
- enc_valid: int32 [4, 1024], P('dp', 'blk'), may hold values from 0 to 1, as said below
- tgt_question: int32 [4, 128], P('dp', 'blk'), may hold values from 0 to 3, as said below
- gain_self: float32 [768], replicated, may hold values from 0.5 to 1.5
- w_qkv: bfloat16 [768, 2304], replicated, may hold values from -0.109375 to 0.109375
- rel_bias: float32 [32, 12], replicated, may hold values from -4 to 4
- w_self_out: bfloat16 [768, 768], replicated, may hold values from -0.875 to 0.875
- gain_cross: float32 [768], replicated, may hold values from 0.5 to 1.5
- w_cross_q: bfloat16 [768, 768], replicated, may hold values from -0.0546875 to 0.0546875
- w_cross_kv: bfloat16 [768, 1536], replicated, may hold values from -0.21875 to 0.21875
- w_cross_out: bfloat16 [768, 768], replicated, may hold values from -0.875 to 0.875
- gain_ff: float32 [768], replicated, may hold values from 0.5 to 1.5
- w_ff_in: bfloat16 [768, 3072], replicated, may hold values from -0.21875 to 0.21875
- w_ff_out: bfloat16 [3072, 768], replicated, may hold values from -0.109375 to 0.109375
- grad_out: bfloat16 [4, 4096, 768], P('dp', 'blk'), may hold values from -6 to 6
Outputs:
- dec_out: bfloat16 [4, 4096, 768], P('dp', 'blk')
- grad_dec: float32 [4, 4096, 768], P('dp', 'blk')
- grad_enc: float32 [4, 1024, 768], P('dp', 'blk')
- grad_gain_self: float32 [768], P('blk')
- grad_qkv: float32 [768, 2304], P('blk')
- grad_rel_bias: float32 [32, 12], P('blk')
- grad_self_out: float32 [768, 768], P('blk')
- grad_gain_cross: float32 [768], P('blk')
- grad_cross_q: float32 [768, 768], P('blk')
- grad_cross_kv: float32 [768, 1536], P('blk')
- grad_cross_out: float32 [768, 768], P('blk')
- grad_gain_ff: float32 [768], P('blk')
- grad_ff_in: float32 [768, 3072], P('blk')
- grad_ff_out: float32 [3072, 768], P('blk')
The draws below stay inside these ranges and needn't reach their ends.
Inputs may be any that keep to these rules, and one draw needn't show every extreme that they name: `enc_question`: passages of 64 to 384 tokens lie end to end (the last one cut at the group's end); all tokens of a passage share its question; each passage has valid tokens from its start on, at least half of it; one question, drawn from the seed, holds the passages at the group's first, middle and last token, which are fully valid. `enc_valid`: padding lies at the end of each passage. `tgt_question`: each target names a question that has valid encoding tokens in its group; the first target of a group names the question that spans the group.
All inputs are finite; a program needn't handle non-finite values.
Results may differ from the reference program's by a relative error of at most 0.025.
Values may be sent and summed in bfloat16 or wider, within the bound.
No kernel may reach another device: no remote copies, remote signals or barrier semaphores. Data moves between devices by JAX's collectives and lax.ppermute only.
A program may use at most 192 MiB of HBM per device.

```python
import math
import jax
import jax.numpy as jnp
import numpy as np
from jax import lax

D = 768
H = 12
FF = 3072
NB = 32
TLEN = 32
QUEST = 4
PMIN = 64
PMAX = 384
GROUPS = 4
TGTS = 128
QTOK = 4096
ENC = 1024


def one_group(key):
    most_passages = ENC // PMIN + 1
    key_len, key_valid, key_question, key_target = jax.random.split(key, 4)
    lengths = jax.random.randint(key_len, (most_passages,), PMIN, PMAX + 1).at[0].set(PMAX)
    pass_ends = jnp.cumsum(lengths)
    starts = pass_ends - lengths
    positions = jnp.arange(ENC, dtype=jnp.int32)
    passage = jnp.sum((pass_ends[None, :] <= positions[:, None]).astype(jnp.int32), 1)
    one_hot = passage[:, None] == jnp.arange(most_passages)[None, :]
    middle = passage[ENC // 2]
    last_passage = passage[ENC - 1]
    indices = jnp.arange(most_passages)
    forced = (indices == 0) | (indices == middle) | (indices == last_passage)
    keep_len = jax.random.randint(key_valid, (most_passages,), (lengths + 1) // 2, lengths + 1)
    keep_len = jnp.where(forced, lengths, keep_len)
    inside = positions - jnp.sum(jnp.where(one_hot, starts[None, :], 0), 1)
    token_valid = (inside < jnp.sum(jnp.where(one_hot, keep_len[None, :], 0), 1)).astype(jnp.int32)
    questions = jax.random.randint(key_question, (most_passages,), 0, QUEST)
    chosen = questions[0]
    questions = jnp.where(forced, chosen, questions)
    token_question = jnp.sum(jnp.where(one_hot, questions[None, :], 0), 1).astype(jnp.int32)
    picked = jax.random.randint(key_target, (TGTS,), 0, last_passage + 1)
    target_question = questions[picked].at[0].set(chosen).astype(jnp.int32)
    return (token_question, token_valid, target_question)


def passage_layout(key):
    group_keys = jax.random.split(key, GROUPS)
    return jax.vmap(one_group)(group_keys)


def draw_enc_question(key, part):
    layout = passage_layout(key)
    return layout[0]


def draw_enc_valid(key, part):
    layout = passage_layout(key)
    return layout[1]


def draw_tgt_question(key, part):
    layout = passage_layout(key)
    return layout[2]


def shard_levels(own_key, shape, cuts, low, high):
    loudness = 1.0
    for position, blocks in cuts:
        draws = jax.random.uniform(jax.random.fold_in(jax.random.fold_in(own_key, 6), position), (blocks,), jnp.float32, low / len(cuts), high / len(cuts))
        loudness = loudness * jnp.repeat(jnp.exp(draws), shape[position] // blocks).reshape((-1,) + (1,) * (len(shape) - 1 - position))
    return loudness


def normal_values(own_key, extent, deviation, bound, pieces=(), kind=jnp.bfloat16):
    values = deviation * jax.random.normal(own_key, extent, jnp.float32)
    if pieces:
        values = values * shard_levels(own_key, extent, pieces, -0.22, 0.18)
    return jnp.clip(values, -bound, bound).astype(kind)


def setup_inputs(seed: int = 0) -> dict:
    keys = jax.random.split(jax.random.key(seed), 18)
    return {
        "dec_in": normal_values(keys[0], (GROUPS, QTOK, D), 1.0, 6.0, ((0, 4), (1, 8))),
        "encodings": normal_values(keys[1], (GROUPS, ENC, D), 1.0, 6.0, ((0, 4), (1, 8))),
        "enc_question": draw_enc_question(jax.random.fold_in(keys[17], 71), 0),
        "enc_valid": draw_enc_valid(jax.random.fold_in(keys[17], 71), 0),
        "tgt_question": draw_tgt_question(jax.random.fold_in(keys[17], 71), 0),
        "gain_self": jnp.clip(1.0 + 0.1 * jax.random.normal(keys[5], (D,), jnp.float32), 0.5, 1.5),
        "w_qkv": normal_values(keys[6], (D, 3 * D), (4 * D) ** -0.5, 0.109375),
        "rel_bias": normal_values(keys[7], (NB, H), 1.0, 4.0, (), jnp.float32),
        "w_self_out": normal_values(keys[8], (D, D), (D // 16) ** -0.5, 0.875),
        "gain_cross": jnp.clip(1.0 + 0.1 * jax.random.normal(keys[9], (D,), jnp.float32), 0.5, 1.5),
        "w_cross_q": normal_values(keys[10], (D, D), (16 * D) ** -0.5, 0.0546875),
        "w_cross_kv": normal_values(keys[11], (D, 2 * D), D ** -0.5, 0.21875),
        "w_cross_out": normal_values(keys[12], (D, D), (D // 16) ** -0.5, 0.875),
        "gain_ff": jnp.clip(1.0 + 0.1 * jax.random.normal(keys[13], (D,), jnp.float32), 0.5, 1.5),
        "w_ff_in": normal_values(keys[14], (D, FF), D ** -0.5, 0.21875),
        "w_ff_out": normal_values(keys[15], (FF, D), FF ** -0.5, 0.109375),
        "grad_out": normal_values(keys[16], (GROUPS, QTOK, D), 1.0, 6.0, ((0, 4), (1, 8))),
    }


EPSILON = 1e-06
NEG_LARGE = -1e+30
HIGHEST_PREC = lax.Precision.HIGHEST

@jax.custom_vjp
def low(v):
    return lax.optimization_barrier(v.astype(jnp.bfloat16)).astype(jnp.float32)

@jax.custom_vjp
def low_back(v):
    return v

def low_keep(v):
    return (low(v), None)

def low_pass(kept, grad):
    return (grad,)

def back_keep(v):
    return (v, None)

def back_low(kept, grad):
    return (low(grad),)
low.defvjp(low_keep, low_pass)
low_back.defvjp(back_keep, back_low)

def bucket_table(length, bucket_count):
    exact_count = bucket_count // 2
    bucket_ids = np.zeros((length, length), np.int32)
    for query_pos in range(length):
        for key_pos in range(length):
            distance = max(query_pos - key_pos, 0)
            if distance < exact_count:
                bucket_ids[query_pos, key_pos] = distance
            else:
                bucket_ids[query_pos, key_pos] = min(bucket_count - 1, exact_count + int(math.log(distance / exact_count) / math.log(128.0 / exact_count) * exact_count))
    return bucket_ids

def rms_gain(values, gain):
    return values * lax.rsqrt(lax.optimization_barrier(jnp.mean(values * values, axis=-1, keepdims=True)) + EPSILON) * gain

def group_layer(hidden_in, enc_rows, query_tags, key_tags, gain_self, w_qkv, rel_bias, w_self_out, gain_cross, w_cross_q, w_cross_kv, w_cross_out, gain_ff, w_ff_in, w_ff_out):
    num_rows, model_width = hidden_in.shape
    num_heads = rel_bias.shape[1]
    head_dim = model_width // num_heads
    bucket_ids = bucket_table(TLEN, rel_bias.shape[0])
    causal = jnp.asarray(np.tril(np.ones((TLEN, TLEN), bool)))
    self_bias = jnp.transpose(rel_bias[jnp.asarray(bucket_ids)], (2, 0, 1))
    norm_one = low(rms_gain(hidden_in, gain_self))
    qkv = low(low_back(jnp.dot(norm_one, w_qkv, precision=HIGHEST_PREC)))
    qkv = qkv.reshape(num_rows // TLEN, TLEN, 3, num_heads, head_dim)
    scores = low_back(jnp.einsum('tqhd,tkhd->thqk', qkv[:, :, 0], qkv[:, :, 1], precision=HIGHEST_PREC) + self_bias[None])
    masked = jnp.where(causal, scores, NEG_LARGE)
    exp_terms = jnp.where(causal, jnp.exp(masked - lax.optimization_barrier(jnp.max(masked, -1, keepdims=True))), 0.0)
    self_probs = exp_terms / lax.optimization_barrier(jnp.sum(exp_terms, -1, keepdims=True))
    self_att = jnp.einsum('thqk,tkhd->tqhd', low(self_probs), qkv[:, :, 2], precision=HIGHEST_PREC)
    self_att = low(low_back(self_att.reshape(num_rows, model_width)))
    after_self = hidden_in + low_back(jnp.dot(self_att, w_self_out, precision=HIGHEST_PREC))
    norm_two = low(rms_gain(after_self, gain_cross))
    cross_q = low(low_back(jnp.dot(norm_two, w_cross_q, precision=HIGHEST_PREC))).reshape(num_rows, num_heads, head_dim)
    key_vals = low(low_back(jnp.dot(enc_rows, w_cross_kv, precision=HIGHEST_PREC))).reshape(-1, 2, num_heads, head_dim)
    block_rows = math.gcd(num_rows, 1024)

    def cross_block(inputs):
        query_block, tag_block = inputs
        cross_scores = low_back(jnp.einsum('qhd,khd->hqk', query_block, key_vals[:, 0], precision=HIGHEST_PREC))
        key_match = (tag_block[:, None] == key_tags[None, :])[None]
        cross_masked = jnp.where(key_match, cross_scores, NEG_LARGE)
        cross_exp = jnp.where(key_match, jnp.exp(cross_masked - lax.optimization_barrier(jnp.max(cross_masked, -1, keepdims=True))), 0.0)
        cross_probs = cross_exp / lax.optimization_barrier(jnp.sum(cross_exp, -1, keepdims=True))
        return jnp.einsum('hqk,khd->qhd', low(cross_probs), key_vals[:, 1], precision=HIGHEST_PREC)
    cross_att = lax.map(jax.checkpoint(cross_block), (cross_q.reshape(num_rows // block_rows, block_rows, num_heads, head_dim), query_tags.reshape(num_rows // block_rows, block_rows)))
    cross_att = low(low_back(cross_att.reshape(num_rows, model_width)))
    after_cross = after_self + low_back(jnp.dot(cross_att, w_cross_out, precision=HIGHEST_PREC))
    norm_three = low(rms_gain(after_cross, gain_ff))
    pre_act = low_back(jnp.dot(norm_three, w_ff_in, precision=HIGHEST_PREC))
    ff_hidden = low(jax.nn.gelu(pre_act, approximate=True))
    return after_cross + low_back(jnp.dot(ff_hidden, w_ff_out, precision=HIGHEST_PREC))

def reference(dec_in, encodings, enc_question, enc_valid, tgt_question, gain_self, w_qkv, rel_bias, w_self_out, gain_cross, w_cross_q, w_cross_kv, w_cross_out, gain_ff, w_ff_in, w_ff_out, grad_out):
    key_tags = jnp.where(enc_valid == 1, enc_question, -1).astype(jnp.int32)
    query_tags = jnp.repeat(tgt_question, TLEN, axis=1).astype(jnp.int32)
    weights = (gain_self, w_qkv.astype(jnp.float32), rel_bias, w_self_out.astype(jnp.float32), gain_cross, w_cross_q.astype(jnp.float32), w_cross_kv.astype(jnp.float32), w_cross_out.astype(jnp.float32), gain_ff, w_ff_in.astype(jnp.float32), w_ff_out.astype(jnp.float32))

    def forward(hidden_all, enc_all, *params):
        results = [group_layer(hidden_all[group], enc_all[group], query_tags[group], key_tags[group], *params) for group in range(GROUPS)]
        return jnp.stack(results)
    output, backward = jax.vjp(forward, dec_in.astype(jnp.float32), encodings.astype(jnp.float32), *weights)
    grads = backward(grad_out.astype(jnp.float32))
    return (output.astype(jnp.bfloat16), grads[0], grads[1], grads[2], grads[3], grads[4], grads[5], grads[6], grads[7], grads[8], grads[9], grads[10], grads[11], grads[12])
```

```python
import functools
import math

import jax
import jax.numpy as jnp
import numpy as np
from jax import lax
from jax.experimental import pallas as pl
from jax.experimental.pallas import tpu as pltpu
from jax.sharding import PartitionSpec as P

TLEN = 32
EPSILON = 1e-06
NEG_LARGE = -1e30
GROUP = 128
LOG2E = 1.4426950408889634
BF = jnp.bfloat16
F32 = jnp.float32
VMEM = pl.BlockSpec(memory_space=pltpu.VMEM)
SMEM = pl.BlockSpec(memory_space=pltpu.SMEM)
ANY = pl.BlockSpec(memory_space=pl.ANY)
MIB = 2**20


def bucket_of(distance, bucket_count):
    exact_count = bucket_count // 2
    if distance < exact_count:
        return distance
    scaled = math.log(distance / exact_count) / math.log(128.0 / exact_count) * exact_count
    return min(bucket_count - 1, exact_count + int(scaled))


def bucket_ids(bucket_count):
    ids = np.full((GROUP, GROUP), -1, np.int32)
    for row in range(GROUP):
        first = row - row % TLEN
        for col in range(first, row + 1):
            ids[row, col] = bucket_of(row - col, bucket_count)
    return ids


def dot_nn(a, b):
    return jnp.dot(a, b, preferred_element_type=F32)


def dot_nt(a, b):
    return lax.dot_general(a, b, (((1,), (1,)), ((), ())), preferred_element_type=F32)


def dot_tn(a, b):
    return lax.dot_general(a, b, (((0,), (0,)), ((), ())), preferred_element_type=F32)


def inv_rms(v):
    return lax.rsqrt(jnp.mean(v * v, axis=-1, keepdims=True) + EPSILON)


def rms_back(dy, v, gain):
    r = inv_rms(v)
    vr = v * r
    dg = dy * gain
    dv = r * (dg - vr * jnp.mean(dg * vr, axis=-1, keepdims=True))
    return dv, jnp.sum(dy * vr, axis=0, keepdims=True)


def half_masks(rows):
    lane = lax.broadcasted_iota(jnp.int32, (rows, 128), 1)
    low = (lane < 64).astype(F32)
    return low.astype(BF), (1.0 - low).astype(BF)


def chunk_place(chunk, blk, bits):
    rel = jnp.bitwise_xor(chunk, blk)
    place = jnp.int32(0)
    for bit in bits:
        place = place * 2 + jnp.where(jnp.bitwise_and(rel, bit) != 0, 1, 0)
    return place


def query_block(rows, tokens):
    return max(GROUP, min(rows, rows * 1024 // tokens))


def store_chunks(ref, value, col, blk, bits, chunks):
    rows = value.shape[0] // chunks
    for c in range(chunks):
        ref[chunk_place(c, blk, bits), :, col : col + value.shape[1]] = value[
            c * rows : (c + 1) * rows, :
        ].astype(BF)


def call(body, out_shape, in_specs, out_specs, scratch=(), limit=56, flops=0, nbytes=0):
    return pl.pallas_call(
        body,
        out_shape=out_shape,
        in_specs=in_specs,
        out_specs=out_specs,
        scratch_shapes=list(scratch),
        compiler_params=pltpu.CompilerParams(vmem_limit_bytes=limit * MIB),
        cost_estimate=pl.CostEstimate(flops=flops, bytes_accessed=nbytes, transcendentals=0),
    )


def self_forward(x, gain_self, w_qkv, rel_bias, w_self_out, gain_cross, w_cross_q):
    rows, width = x.shape
    bucket_count, heads = rel_bias.shape
    pairs = heads // 2
    groups = rows // GROUP
    ids = bucket_ids(bucket_count)
    used = sorted(set(ids[ids >= 0].tolist()))

    def body(
        x_ref, gs_ref, wqkv_ref, ids_ref, rb_ref, wso_ref, gc_ref, wcq_ref,
        a1_ref, qkv_ref, p1_ref, o1_ref, h1_ref, a2_ref, cq_ref, bias,
    ):
        xf = x_ref[...].astype(F32)
        a1 = (xf * inv_rms(xf) * gs_ref[...]).astype(BF)
        a1_ref[...] = a1
        qkv_ref[...] = dot_nn(a1, wqkv_ref[...]).astype(BF)
        idv = ids_ref[...]

        def make_bias(h, carry):
            val = jnp.full((GROUP, GROUP), NEG_LARGE, F32)
            for b in used:
                val = jnp.where(idv == b, rb_ref[b, h], val)
            bias[h] = val
            return carry

        lax.fori_loop(0, heads, make_bias, 0)
        m0, m1 = half_masks(GROUP)

        def attend(g, carry):
            at = pl.ds(pl.multiple_of(g * GROUP, GROUP), GROUP)
            for pair in range(pairs):
                lo = pair * 128
                q = qkv_ref[at, lo : lo + 128]
                k = qkv_ref[at, width + lo : width + lo + 128]
                v = qkv_ref[at, 2 * width + lo : 2 * width + lo + 128]
                s = dot_nt(jnp.concatenate([q * m0, q * m1], 0), k)
                s = s + jnp.concatenate([bias[2 * pair], bias[2 * pair + 1]], 0)
                e = jnp.exp(s - jnp.max(s, -1, keepdims=True))
                p = (e / jnp.sum(e, -1, keepdims=True)).astype(BF)
                p1_ref[g, pair] = p
                o = dot_nn(
                    jnp.concatenate([p[:GROUP], p[GROUP:]], 1),
                    jnp.concatenate([v * m0, v * m1], 0),
                )
                o1_ref[at, lo : lo + 128] = o.astype(BF)
            return carry

        lax.fori_loop(0, groups, attend, 0)
        h1 = x_ref[...].astype(F32) + dot_nn(o1_ref[...], wso_ref[...])
        h1_ref[...] = h1
        a2 = (h1 * inv_rms(h1) * gc_ref[...]).astype(BF)
        a2_ref[...] = a2
        cq_ref[...] = dot_nn(a2, wcq_ref[...]).astype(BF)

    sds = jax.ShapeDtypeStruct
    return call(
        body,
        (
            sds((rows, width), BF),
            sds((rows, 3 * width), BF),
            sds((groups, pairs, 2 * GROUP, GROUP), BF),
            sds((rows, width), BF),
            sds((rows, width), F32),
            sds((rows, width), BF),
            sds((rows, width), BF),
        ),
        [VMEM, VMEM, VMEM, VMEM, SMEM, VMEM, VMEM, VMEM],
        (VMEM,) * 7,
        [pltpu.VMEM((heads, GROUP, GROUP), F32)],
        flops=12 * 10**9,
        nbytes=16 * 10**6,
    )(
        x, gain_self.reshape(1, width), w_qkv, jnp.asarray(ids), rel_bias, w_self_out,
        gain_cross.reshape(1, width), w_cross_q,
    )


def cross_forward(gathered, shard_rows, tgt_question, cq, h1, w_cross_kv, w_cross_out, gain_ff):
    rows, width = cq.shape
    pairs = width // 128
    pieces, piece_rows, _ = gathered.shape
    tokens = pieces * shard_rows
    targets = rows // TLEN
    block_rows = query_block(rows, tokens)
    blocks = rows // block_rows
    steps = pairs * blocks

    def body(
        enc_ref, tq_ref, cq_ref, h1_ref, wkv_ref, wco_ref, gf_ref,
        kv_ref, e_ref, inv_ref, o2_ref, h2_ref, a3_ref,
        enc, kfeat, qfeat, ebuf, sem,
    ):
        lane = lax.rem(lax.broadcasted_iota(jnp.int32, (shard_rows, 128), 1), 64).astype(F32)
        for piece in range(pieces):
            at = slice(piece * shard_rows, (piece + 1) * shard_rows)
            enc[at, :] = enc_ref[piece, :shard_rows, :]
            tag = enc_ref[piece, shard_rows : shard_rows + 1, :shard_rows].astype(F32)
            tag = jnp.transpose(jnp.broadcast_to(tag, (128, shard_rows)))
            kfeat[at, :] = jnp.where(tag == lane, 0.0, NEG_LARGE).astype(BF)
        lane_t = lax.rem(lax.broadcasted_iota(jnp.int32, (TLEN, 128), 1), 64)
        for t in range(targets):
            qfeat[t * TLEN : (t + 1) * TLEN, :] = jnp.where(lane_t == tq_ref[t], 1.0, 0.0).astype(BF)
        kv_ref[...] = dot_nn(enc[...], wkv_ref[...]).astype(BF)
        q0, q1 = half_masks(block_rows)
        k0, k1 = half_masks(tokens)
        qmask, kmask = (q0, q1), (k0, k1)
        low = lax.broadcasted_iota(jnp.int32, (block_rows, 128), 1) < 64

        def out_copy(slot, step):
            pair, block = step // blocks, lax.rem(step, blocks)
            return pltpu.make_async_copy(
                ebuf.at[slot],
                e_ref.at[pl.ds(2 * pair, 2), pl.ds(block * block_rows, block_rows)],
                sem.at[slot],
            )

        def attend(step, carry):
            slot = lax.rem(step, 2)
            pair, block = step // blocks, lax.rem(step, blocks)
            lo = pl.multiple_of(pair * 128, 128)
            at = pl.ds(pl.multiple_of(block * block_rows, block_rows), block_rows)

            @pl.when(step >= 2)
            def _():
                out_copy(slot, step - 2).wait()

            q = cq_ref[at, pl.ds(lo, 128)]
            k = kv_ref[:, pl.ds(lo, 128)]
            v = kv_ref[:, pl.ds(width + lo, 128)]
            outs = []
            for h in range(2):
                qa = q * qmask[h] + qfeat[at, :] * qmask[1 - h]
                ka = k * kmask[h] + kfeat[...] * kmask[1 - h]
                s = dot_nt(qa, ka)
                top = jnp.max(s, -1, keepdims=True)
                e = jnp.exp(s - top).astype(BF)
                ebuf[slot, h] = e
                outs.append(dot_nn(e, v * kmask[h] + kmask[1 - h]))
            out_copy(slot, step).start()
            total = jnp.where(low, pltpu.roll(outs[0], 64, 1), pltpu.roll(outs[1], 64, 1))
            inv = 1.0 / total
            inv_ref[at, pl.ds(lo, 128)] = inv
            o2_ref[at, pl.ds(lo, 128)] = (jnp.where(low, outs[0], outs[1]) * inv).astype(BF)
            return carry

        lax.fori_loop(0, steps, attend, 0)
        h2 = h1_ref[...] + dot_nn(o2_ref[...], wco_ref[...])
        h2_ref[...] = h2
        a3_ref[...] = (h2 * inv_rms(h2) * gf_ref[...]).astype(BF)
        for step in range(max(0, steps - 2), steps):
            out_copy(step % 2, jnp.int32(step)).wait()

    sds = jax.ShapeDtypeStruct
    return call(
        body,
        (
            sds((tokens, 2 * width), BF),
            sds((2 * pairs, rows, tokens), BF),
            sds((rows, width), F32),
            sds((rows, width), BF),
            sds((rows, width), F32),
            sds((rows, width), BF),
        ),
        [VMEM, SMEM, VMEM, VMEM, VMEM, VMEM, VMEM],
        (VMEM, ANY, VMEM, VMEM, VMEM, VMEM),
        [
            pltpu.VMEM((tokens, width), BF),
            pltpu.VMEM((tokens, 128), BF),
            pltpu.VMEM((rows, 128), BF),
            pltpu.VMEM((2, 2, block_rows, tokens), BF),
            pltpu.SemaphoreType.DMA((2,)),
        ],
        flops=16 * 10**9,
        nbytes=30 * 10**6,
    )(gathered, tgt_question, cq, h1, w_cross_kv, w_cross_out, gain_ff.reshape(1, width))


def feed_forward(place, a3, h2, gain_ff, gy, w_ff_in, w_ff_out, bits, chunks):
    rows, width = a3.shape
    hidden = w_ff_in.shape[1]
    tile = width
    steps = hidden // tile
    part = width // chunks
    half_steps = steps // 2
    half = width // 2
    cols = hidden
    sub = hidden // width
    per_tile = chunks * tile // hidden
    scale = math.sqrt(2.0 / math.pi)

    def body(
        place_ref, a3_ref, h2_ref, gf_ref, gy_ref, w1_ref, w2_ref,
        out_ref, dh2_ref, gain_ref, keep_ref, send_ref,
        acc_out, acc_back,
    ):
        core, blk = place_ref[0], place_ref[1]
        step = pl.program_id(0)

        @pl.when(step == 0)
        def _():
            acc_out[...] = jnp.zeros_like(acc_out)
            acc_back[...] = jnp.zeros_like(acc_back)

        a3v = a3_ref[...]
        gyv = gy_ref[...]
        pre = dot_nn(a3v, w1_ref[...])
        dhid = dot_nt(gyv, w2_ref[...])
        sq = pre * pre
        t = jnp.tanh(scale * pre * (1.0 + 0.044715 * sq))
        hid = (0.5 * pre * (1.0 + t)).astype(BF)
        slope = 0.5 * (1.0 + t) + 0.5 * pre * (1.0 - t * t) * (scale * (1.0 + 0.134145 * sq))
        dpre = (dhid * slope).astype(BF)
        acc_out[...] += dot_nn(hid, w2_ref[...])
        acc_back[...] += dot_nt(dpre, w1_ref[...])
        g_in = dot_tn(a3v, dpre)
        mine = step // half_steps == core
        col = pl.multiple_of(lax.rem(step, half_steps) * tile, tile)
        for wanted, ref in ((True, keep_ref), (False, send_ref)):

            @pl.when(mine == wanted)
            def _():
                for c in range(chunks):
                    ref[chunk_place(c, blk, bits), :, pl.ds(col, tile)] = g_in[
                        c * part : (c + 1) * part, :
                    ].astype(BF)

        g_out = dot_tn(hid, gyv)
        swap = core == 1
        low_half, high_half = g_out[:, :half], g_out[:, half:]
        g_keep = jnp.where(swap, high_half, low_half).astype(BF)
        g_send = jnp.where(swap, low_half, high_half).astype(BF)
        for value, ref in ((g_keep, keep_ref), (g_send, send_ref)):
            for i in range(per_tile):
                for j in range(sub):
                    first = (i * sub + j) * part
                    ref[
                        chunk_place(step * per_tile + i, blk, bits),
                        :,
                        hidden // 2 + j * half : hidden // 2 + (j + 1) * half,
                    ] = value[first : first + part, :]

        @pl.when(step == steps - 1)
        def _():
            h2v = h2_ref[...]
            out_ref[...] = (h2v + acc_out[...]).astype(BF)
            dv, dgain = rms_back(acc_back[...], h2v, gf_ref[...])
            dh2_ref[...] = gyv.astype(F32) + dv
            gain_ref[...] = dgain

    sds = jax.ShapeDtypeStruct
    whole = lambda *shape: pl.BlockSpec(shape, lambda s, *_: (0,) * len(shape))
    return pl.pallas_call(
        body,
        out_shape=(
            sds((rows, width), BF),
            sds((rows, width), F32),
            sds((1, width), F32),
            sds((chunks, part, cols), BF),
            sds((chunks, part, cols), BF),
        ),
        grid_spec=pltpu.PrefetchScalarGridSpec(
            num_scalar_prefetch=1,
            grid=(steps,),
            in_specs=[
                whole(rows, width),
                whole(rows, width),
                whole(1, width),
                whole(rows, width),
                pl.BlockSpec((width, tile), lambda s, *_: (0, s)),
                pl.BlockSpec((tile, width), lambda s, *_: (s, 0)),
            ],
            out_specs=(
                whole(rows, width),
                whole(rows, width),
                whole(1, width),
                whole(chunks, part, cols),
                whole(chunks, part, cols),
            ),
            scratch_shapes=[pltpu.VMEM((rows, width), F32), pltpu.VMEM((rows, width), F32)],
        ),
        compiler_params=pltpu.CompilerParams(vmem_limit_bytes=56 * MIB),
        cost_estimate=pl.CostEstimate(flops=15 * 10**9, bytes_accessed=25 * 10**6, transcendentals=0),
    )(place, a3, h2, gain_ff.reshape(1, width), gy, w_ff_in, w_ff_out)


def cross_backward(dh2, o2, inv, cq, kv, e, w_cross_out):
    rows, width = cq.shape
    pairs = width // 128
    tokens = kv.shape[0]
    block_rows = query_block(rows, tokens)
    blocks = rows // block_rows

    def body(
        dh2_ref, wco_ref, o2_ref, inv_ref, cq_ref, k_ref, v_ref, e_ref,
        dcq_ref, dkt_ref, dvt_ref,
        do2,
    ):
        pair = pl.program_id(0)

        @pl.when(pair == 0)
        def _():
            do2v = dot_nt(dh2_ref[...].astype(BF), wco_ref[...]).astype(BF)
            for i in range(pairs):
                do2[i] = do2v[:, i * 128 : (i + 1) * 128]

        q0, q1 = half_masks(block_rows)
        k0, k1 = half_masks(tokens)
        qmask, kmask = (q0, q1), (k0, k1)
        lane = lax.broadcasted_iota(jnp.int32, (block_rows, 128), 1)
        low = lane < 64
        first = lax.rem(lane, 64) == 0
        second = lax.rem(lane, 64) == 1
        k, v = k_ref[...], v_ref[...]
        sums = [0.0] * 4
        for block in range(blocks):
            at = slice(block * block_rows, (block + 1) * block_rows)
            q = cq_ref[at, :]
            dof = do2[pair, at, :].astype(F32) * inv_ref[at, :]
            dob = dof.astype(BF)
            prod = dof * o2_ref[at, :].astype(F32)
            qt = jnp.transpose(q)
            dot_t = jnp.transpose(dob)
            dqs = []
            for h in range(2):
                own = low if h == 0 else jnp.logical_not(low)
                delta = -jnp.sum(jnp.where(own, prod, 0.0), -1, keepdims=True)
                hi = delta.astype(BF).astype(F32)
                feat = jnp.where(first, hi, jnp.where(second, delta - hi, 0.0)).astype(BF)
                doa = dob * qmask[h] + feat * qmask[1 - h]
                dp = dot_nt(doa, v * kmask[h] + kmask[1 - h])
                ev = e_ref[h, at, :]
                ds = (ev.astype(F32) * dp).astype(BF)
                dqs.append(dot_nn(ds, k))
                sums[h] = sums[h] + dot_nn(qt[h * 64 : (h + 1) * 64, :], ds)
                sums[2 + h] = sums[2 + h] + dot_nn(dot_t[h * 64 : (h + 1) * 64, :], ev)
            dcq_ref[at, :] = jnp.where(low, dqs[0], dqs[1]).astype(BF)
        for h in range(2):
            dkt_ref[h * 64 : (h + 1) * 64, :] = sums[h].astype(BF)
            dvt_ref[h * 64 : (h + 1) * 64, :] = sums[2 + h].astype(BF)

    sds = jax.ShapeDtypeStruct
    column = lambda n: pl.BlockSpec((n, 128), lambda p: (0, p))
    return pl.pallas_call(
        body,
        out_shape=(sds((rows, width), BF), sds((width, tokens), BF), sds((width, tokens), BF)),
        grid=(pairs,),
        in_specs=[
            pl.BlockSpec((rows, width), lambda p: (0, 0)),
            pl.BlockSpec((width, width), lambda p: (0, 0)),
            column(rows),
            column(rows),
            column(rows),
            column(tokens),
            pl.BlockSpec((tokens, 128), lambda p: (0, p + pairs)),
            pl.BlockSpec((2, rows, tokens), lambda p: (p, 0, 0)),
        ],
        out_specs=(
            column(rows),
            pl.BlockSpec((128, tokens), lambda p: (p, 0)),
            pl.BlockSpec((128, tokens), lambda p: (p, 0)),
        ),
        scratch_shapes=[pltpu.VMEM((pairs, rows, 128), BF)],
        compiler_params=pltpu.CompilerParams(vmem_limit_bytes=56 * MIB),
        cost_estimate=pl.CostEstimate(flops=15 * 10**9, bytes_accessed=25 * 10**6, transcendentals=0),
    )(dh2, w_cross_out, o2, inv, cq, kv, kv, e)


def cross_weights(
    place, dh2, o2, dcq, dkt, dvt, gathered, shard_rows, a2, h1, gain_cross,
    w_cross_kv, w_cross_q, bits, chunks,
):
    rows, width = dcq.shape
    pieces, piece_rows, _ = gathered.shape
    part = width // chunks
    half = width // 2
    cols = 2 * width
    tokens = pieces * shard_rows
    tile_pieces = min(pieces, max(1, 1024 // shard_rows))
    tile = tile_pieces * shard_rows
    steps = tokens // tile

    def body(
        place_ref, dh2_ref, o2_ref, dcq_ref, dkt_ref, dvt_ref, enc_ref, a2_ref, h1_ref,
        gc_ref, wkv_ref, wcq_ref,
        dh1_ref, gain_ref, genc_ref, keep_ref, send_ref,
        *accs,
    ):
        core, blk = place_ref[0], place_ref[1]
        step = pl.program_id(0)

        @pl.when(step == 0)
        def _():
            dcqv = dcq_ref[...]
            da2 = dot_nt(dcqv, wcq_ref[...])
            dv, dgain = rms_back(da2, h1_ref[...], gc_ref[...])
            dh1_ref[...] = dh2_ref[...] + dv
            gain_ref[...] = dgain
            for which, ref in ((core, keep_ref), (1 - core, send_ref)):
                at = pl.ds(pl.multiple_of(which * half, 128), half)
                gco = dot_tn(o2_ref[...], dh2_ref[:, at].astype(BF))
                store_chunks(ref, gco, 0, blk, bits, chunks)
                gcq = dot_tn(a2_ref[...], dcq_ref[:, at])
                store_chunks(ref, gcq, half, blk, bits, chunks)

        wkv = wkv_ref[...]
        genc = dot_tn(dkt_ref[...], jnp.transpose(wkv[:, :width]))
        genc = genc + dot_tn(dvt_ref[...], jnp.transpose(wkv[:, width:]))
        genc_ref[...] = genc.astype(BF)
        enct = jnp.concatenate(
            [jnp.transpose(enc_ref[i, :shard_rows, :]) for i in range(tile_pieces)], 1
        )
        gk = dot_nt(enct, dkt_ref[...])
        gv = dot_nt(enct, dvt_ref[...])
        if accs:
            gk = gk + jnp.where(step == 0, 0.0, accs[0][...])
            gv = gv + jnp.where(step == 0, 0.0, accs[1][...])
            accs[0][...] = gk
            accs[1][...] = gv

        @pl.when(step == steps - 1)
        def _():
            for core_is in range(2):
                own, other = (gk, gv) if core_is == 0 else (gv, gk)

                @pl.when(core == core_is)
                def _():
                    store_chunks(keep_ref, own, width, blk, bits, chunks)
                    store_chunks(send_ref, other, width, blk, bits, chunks)

    sds = jax.ShapeDtypeStruct
    whole = lambda *shape: pl.BlockSpec(shape, lambda s, *_: (0,) * len(shape))
    return pl.pallas_call(
        body,
        out_shape=(
            sds((rows, width), F32),
            sds((1, width), F32),
            sds((tokens, width), BF),
            sds((chunks, part, cols), BF),
            sds((chunks, part, cols), BF),
        ),
        grid_spec=pltpu.PrefetchScalarGridSpec(
            num_scalar_prefetch=1,
            grid=(steps,),
            in_specs=[
                whole(rows, width),
                whole(rows, width),
                whole(rows, width),
                pl.BlockSpec((width, tile), lambda s, *_: (0, s)),
                pl.BlockSpec((width, tile), lambda s, *_: (0, s)),
                pl.BlockSpec((tile_pieces, piece_rows, width), lambda s, *_: (s, 0, 0)),
                whole(rows, width),
                whole(rows, width),
                whole(1, width),
                whole(width, 2 * width),
                whole(width, width),
            ],
            out_specs=(
                whole(rows, width),
                whole(1, width),
                pl.BlockSpec((tile, width), lambda s, *_: (s, 0)),
                whole(chunks, part, cols),
                whole(chunks, part, cols),
            ),
            scratch_shapes=[pltpu.VMEM((width, width), F32)] * (2 if steps > 1 else 0),
        ),
        compiler_params=pltpu.CompilerParams(vmem_limit_bytes=56 * MIB),
        cost_estimate=pl.CostEstimate(flops=10 * 10**9, bytes_accessed=25 * 10**6, transcendentals=0),
    )(
        place, dh2, o2, dcq, dkt, dvt, gathered, a2, h1, gain_cross.reshape(1, width),
        w_cross_kv, w_cross_q,
    )


def self_backward(
    place, dh1, o1, qkv, p1, a1, x, gain_self, w_self_out, w_qkv, gain_cross_grad, gain_ff_grad,
    bucket_count, heads, bits, chunks,
):
    rows, width = x.shape
    pairs = heads // 2
    groups = rows // GROUP
    ids = bucket_ids(bucket_count)
    used = sorted(set(ids[ids >= 0].tolist()))
    part = width // chunks
    half = width // 2
    cols = half + 3 * half
    ids_small = np.concatenate([ids[t * TLEN : (t + 1) * TLEN] for t in range(1)], 0)
    ids_small = np.tile(ids_small[:, :TLEN], (1, GROUP // TLEN))

    def body(
        place_ref, dh1_ref, o1_ref, qkv_ref, p1_ref, a1_ref, x_ref, gs_ref, wso_ref, wqkv_ref,
        ids_ref, ggc_ref, ggf_ref,
        out_ref, keep_ref, send_ref, misc_ref,
        do1, dqkv, acc,
    ):
        core, blk = place_ref[0], place_ref[1]
        gs = dh1_ref[...].astype(BF)
        do1[...] = dot_nt(gs, wso_ref[...]).astype(BF)
        m0, m1 = half_masks(GROUP)
        acc[...] = jnp.zeros_like(acc)

        def attend(g, carry):
            at = pl.ds(pl.multiple_of(g * GROUP, GROUP), GROUP)
            for pair in range(pairs):
                lo = pair * 128
                q = qkv_ref[at, lo : lo + 128]
                k = qkv_ref[at, width + lo : width + lo + 128]
                v = qkv_ref[at, 2 * width + lo : 2 * width + lo + 128]
                do = do1[at, lo : lo + 128]
                do_two = jnp.concatenate([do * m0, do * m1], 0)
                pb = p1_ref[g, pair]
                pf = pb.astype(F32)
                dp = dot_nt(do_two, v)
                ds = (pf * (dp - jnp.sum(pf * dp, -1, keepdims=True))).astype(BF)
                dsf = ds.astype(F32)
                for h in range(2):
                    total = dsf[h * GROUP : h * GROUP + TLEN]
                    for t in range(1, GROUP // TLEN):
                        total = total + dsf[h * GROUP + t * TLEN : h * GROUP + (t + 1) * TLEN]
                    acc[2 * pair + h] += total
                dq = dot_nn(
                    jnp.concatenate([ds[:GROUP], ds[GROUP:]], 1),
                    jnp.concatenate([k * m0, k * m1], 0),
                )
                dk = dot_tn(ds, jnp.concatenate([q * m0, q * m1], 0))
                dv = dot_tn(pb, do_two)
                dqkv[at, lo : lo + 128] = dq.astype(BF)
                dqkv[at, width + lo : width + lo + 128] = dk.astype(BF)
                dqkv[at, 2 * width + lo : 2 * width + lo + 128] = dv.astype(BF)
            return carry

        lax.fori_loop(0, groups, attend, 0)
        for which, ref in ((1 - core, send_ref), (core, keep_ref)):
            gso = dot_tn(o1_ref[...], dh1_ref[:, pl.ds(pl.multiple_of(which * half, 128), half)].astype(BF))
            store_chunks(ref, gso, 0, blk, bits, chunks)
            gqkv = dot_tn(a1_ref[...], dqkv[:, pl.ds(pl.multiple_of(which * 3 * half, 128), 3 * half)])
            store_chunks(ref, gqkv, half, blk, bits, chunks)
        da1 = dot_nt(dqkv[...], wqkv_ref[...])
        dvx, dgain = rms_back(da1, x_ref[...].astype(F32), gs_ref[...])
        out_ref[...] = dh1_ref[...] + dvx
        idv = ids_ref[...]
        lane = lax.broadcasted_iota(jnp.int32, (16, 128), 1)
        bias = jnp.zeros((16, 128), F32)
        accv = acc[...]
        pad = jnp.zeros((16 - heads, 1), F32)
        for b in used:
            part_sum = jnp.sum(jnp.where((idv == b)[None], accv, 0.0), axis=1)
            col = jnp.sum(part_sum, -1, keepdims=True)
            bias = jnp.where(lane == b, jnp.concatenate([col, pad], 0), bias)
        misc_ref[...] = jnp.zeros_like(misc_ref)
        misc_ref[0:16, 0:128] = bias
        misc_ref[12:13, 0:width] = dgain
        misc_ref[13:14, 0:width] = ggc_ref[...]
        misc_ref[14:15, 0:width] = ggf_ref[...]

    sds = jax.ShapeDtypeStruct
    return call(
        body,
        (
            sds((rows, width), F32),
            sds((chunks, part, cols), BF),
            sds((chunks, part, cols), BF),
            sds((16, cols), F32),
        ),
        [SMEM] + [VMEM] * 12,
        (VMEM,) * 4,
        [
            pltpu.VMEM((rows, width), BF),
            pltpu.VMEM((rows, 3 * width), BF),
            pltpu.VMEM((heads, TLEN, GROUP), F32),
        ],
        flops=14 * 10**9,
        nbytes=25 * 10**6,
    )(
        place, dh1, o1, qkv, p1, a1, x, gain_self.reshape(1, width), w_self_out, w_qkv,
        jnp.asarray(ids_small), gain_cross_grad, gain_ff_grad,
    )


def swap(value, axis, bit):
    size = lax.axis_size(axis)
    return lax.ppermute(value, axis, [(i, i ^ bit) for i in range(size)])


def add_up(terms):
    total = terms[0].astype(F32)
    for term in terms[1:]:
        total = total + term.astype(F32)
    return total


def reduce_chunks(keep, send, bits, dp_bits, extra=None):
    chunks, part, cols = keep.shape
    rows = chunks * part
    terms = [keep.reshape(rows, cols)]
    send = send.reshape(rows, cols)
    if extra is not None:
        extra_low = extra.astype(BF)
        got = swap(jnp.concatenate([send, extra_low], 0), "dp", 1)
        terms.append(got[:rows])
        extra = extra_low.astype(F32) + got[rows:].astype(F32)
    else:
        terms.append(swap(send, "dp", 1))
    for bit in bits:
        rows //= 2
        out = add_up([t[rows : 2 * rows] for t in terms]).astype(BF)
        terms = [t[:rows] for t in terms]
        if extra is not None:
            extra_low = extra.astype(BF)
            got = swap(jnp.concatenate([out, extra_low], 0), "blk", bit)
            extra = extra_low.astype(F32) + got[rows:].astype(F32)
            terms.append(got[:rows])
        else:
            terms.append(swap(out, "blk", bit))
    total = add_up(terms)
    for bit in dp_bits:
        if bit == 1:
            continue
        out = total.astype(BF)
        if extra is not None:
            extra_low = extra.astype(BF)
            got = swap(jnp.concatenate([out, extra_low], 0), "dp", bit)
            extra = extra_low.astype(F32) + got[rows:].astype(F32)
            total = out.astype(F32) + got[:rows].astype(F32)
        else:
            total = out.astype(F32) + swap(out, "dp", bit).astype(F32)
    own = total.astype(BF)
    return own, swap(own, "dp", 1), extra


def join_halves(place, own, other, widths, stacks):
    part = own.shape[0]

    def body(place_ref, own_ref, other_ref, *outs):
        core = place_ref[0]
        col = 0
        for out, width, stack in zip(outs, widths, stacks):
            half = width // 2
            for j in range(stack):
                for which, ref in ((core, own_ref), (1 - core, other_ref)):
                    at = pl.ds(pl.multiple_of(which * half, 128), half)
                    out[j * part : (j + 1) * part, at] = ref[:, col : col + half].astype(F32)
                col += half

    return call(
        body,
        tuple(jax.ShapeDtypeStruct((stack * part, width), F32) for width, stack in zip(widths, stacks)),
        [SMEM, VMEM, VMEM],
        (VMEM,) * len(widths),
        limit=24,
        nbytes=4 * 10**6,
    )(place, own, other)


def local(
    dec_in,
    encodings,
    enc_question,
    enc_valid,
    tgt_question,
    gain_self,
    w_qkv,
    rel_bias,
    w_self_out,
    gain_cross,
    w_cross_q,
    w_cross_kv,
    w_cross_out,
    gain_ff,
    w_ff_in,
    w_ff_out,
    grad_out,
):
    x = dec_in[0]
    gy = grad_out[0]
    rows, width = x.shape
    bucket_count, heads = rel_bias.shape
    hidden = w_ff_in.shape[1]
    chunks = lax.axis_size("blk")
    dp_size = lax.axis_size("dp")
    shard_rows = encodings.shape[1]
    bits = [1 << i for i in range(chunks.bit_length() - 1)]
    dp_bits = [1 << i for i in range(dp_size.bit_length() - 1)]
    blk = lax.axis_index("blk")
    core = lax.rem(lax.axis_index("dp"), 2)
    place = jnp.stack([core, blk]).astype(jnp.int32)

    tags = jnp.where(enc_valid[0] == 1, enc_question[0], -1).astype(BF)
    tag_rows = jnp.zeros((16, width), BF).at[0, :shard_rows].set(tags)
    gathered = jnp.concatenate([encodings[0], tag_rows], 0)[None]
    for bit in reversed(bits):
        gathered = jnp.concatenate([gathered, swap(gathered, "blk", bit)], 0)

    a1, qkv, p1, o1, h1, a2, cq = self_forward(
        x, gain_self, w_qkv, rel_bias, w_self_out, gain_cross, w_cross_q
    )
    kv, e, inv, o2, h2, a3 = cross_forward(
        gathered, shard_rows, tgt_question[0], cq, h1, w_cross_kv, w_cross_out, gain_ff
    )
    out, dh2, gain_ff_grad, keep_ff, send_ff = feed_forward(
        place, a3, h2, gain_ff, gy, w_ff_in, w_ff_out, bits, chunks
    )
    own_ff, other_ff, _ = reduce_chunks(keep_ff, send_ff, bits, dp_bits)
    dcq, dkt, dvt = cross_backward(dh2, o2, inv, cq, kv, e, w_cross_out)
    dh1, gain_cross_grad, genc, keep_x, send_x = cross_weights(
        place, dh2, o2, dcq, dkt, dvt, gathered, shard_rows, a2, h1, gain_cross,
        w_cross_kv, w_cross_q, bits, chunks,
    )
    own_x, other_x, _ = reduce_chunks(keep_x, send_x, bits, dp_bits)
    terms = [genc]
    left = chunks * shard_rows
    for bit in bits:
        left //= 2
        sent = add_up([t[left : 2 * left] for t in terms]).astype(BF)
        terms = [t[:left] for t in terms] + [swap(sent, "blk", bit)]
    grad_enc = add_up(terms)
    grad_dec, keep_s, send_s, misc = self_backward(
        place, dh1, o1, qkv, p1, a1, x, gain_self, w_self_out, w_qkv, gain_cross_grad, gain_ff_grad,
        bucket_count, heads, bits, chunks,
    )
    own_s, other_s, misc = reduce_chunks(keep_s, send_s, bits, dp_bits, misc)
    misc = misc.astype(BF).astype(F32)

    grad_ff_in, grad_ff_out = join_halves(
        place, own_ff, other_ff, (hidden, width), (1, hidden // width)
    )
    grad_cross_out, grad_cross_q, grad_cross_kv = join_halves(
        place, own_x, other_x, (width, width, 2 * width), (1, 1, 1)
    )
    grad_self_out, grad_qkv = join_halves(place, own_s, other_s, (width, 3 * width), (1, 1))
    part = width // chunks
    gains = lax.dynamic_slice(misc, (12, blk * part), (3, part))
    bias_part = bucket_count // chunks
    grad_bias = lax.dynamic_slice(misc, (0, blk * bias_part), (heads, bias_part)).T
    return (
        out[None],
        grad_dec[None],
        grad_enc[None],
        gains[0],
        grad_qkv,
        grad_bias,
        grad_self_out,
        gains[1],
        grad_cross_q,
        grad_cross_kv,
        grad_cross_out,
        gains[2],
        grad_ff_in,
        grad_ff_out,
    )


def solution(mesh):
    return jax.shard_map(
        local,
        mesh=mesh,
        in_specs=(
            P("dp", "blk", None),
            P("dp", "blk", None),
            P("dp", "blk"),
            P("dp", "blk"),
            P("dp", "blk"),
            P(),
            P(),
            P(),
            P(),
            P(),
            P(),
            P(),
            P(),
            P(),
            P(),
            P(),
            P("dp", "blk", None),
        ),
        out_specs=(
            P("dp", "blk", None),
            P("dp", "blk", None),
            P("dp", "blk", None),
            P("blk"),
            P("blk", None),
            P("blk", None),
            P("blk", None),
            P("blk"),
            P("blk", None),
            P("blk", None),
            P("blk", None),
            P("blk"),
            P("blk", None),
            P("blk", None),
        ),
        check_vma=False,
    )
```

```python
import functools
import math

import jax
import jax.numpy as jnp
import numpy as np
from jax import lax
from jax.experimental import pallas as pl
from jax.experimental.pallas import tpu as pltpu
from jax.sharding import PartitionSpec as P

TLEN = 32
EPSILON = 1e-06
NEG_LARGE = -1e30
GROUP = 128
LOG2E = 1.4426950408889634
BF = jnp.bfloat16
F32 = jnp.float32
VMEM = pl.BlockSpec(memory_space=pltpu.VMEM)
SMEM = pl.BlockSpec(memory_space=pltpu.SMEM)
ANY = pl.BlockSpec(memory_space=pl.ANY)
MIB = 2**20
LIMITS = dict(
    self_attention=24, self_project=14, cross_forward=34, hidden_gradient=10, feed_hidden=32, feed_weights=20,
    feed_back=16, feed_out=14, cross_backward=20, cross_query_back=14, cross_weights=34, self_backward=18,
    self_weights=28, sum_kernel=24, join_halves=20,
)


def bucket_of(distance, bucket_count):
    exact_count = bucket_count // 2
    if distance < exact_count:
        return distance
    scaled = math.log(distance / exact_count) / math.log(128.0 / exact_count) * exact_count
    return min(bucket_count - 1, exact_count + int(scaled))


def bucket_ids(bucket_count):
    ids = np.full((GROUP, GROUP), -1, np.int32)
    for row in range(GROUP):
        first = row - row % TLEN
        for col in range(first, row + 1):
            ids[row, col] = bucket_of(row - col, bucket_count)
    return ids


def dot_nn(a, b):
    return jnp.dot(a, b, preferred_element_type=F32)


def dot_nt(a, b):
    return lax.dot_general(a, b, (((1,), (1,)), ((), ())), preferred_element_type=F32)


def dot_tn(a, b):
    return lax.dot_general(a, b, (((0,), (0,)), ((), ())), preferred_element_type=F32)


def inv_rms(v):
    return lax.rsqrt(jnp.mean(v * v, axis=-1, keepdims=True) + EPSILON)


def rms_back(dy, v, gain):
    r = inv_rms(v)
    vr = v * r
    dg = dy * gain
    dv = r * (dg - vr * jnp.mean(dg * vr, axis=-1, keepdims=True))
    return dv, jnp.sum(dy * vr, axis=0, keepdims=True)


def half_masks(rows):
    lane = lax.broadcasted_iota(jnp.int32, (rows, 128), 1)
    low = (lane < 64).astype(F32)
    return low.astype(BF), (1.0 - low).astype(BF)


def chunk_place(chunk, blk, bits):
    rel = jnp.bitwise_xor(chunk, blk)
    place = jnp.int32(0)
    for bit in bits:
        place = place * 2 + jnp.where(jnp.bitwise_and(rel, bit) != 0, 1, 0)
    return place


def chunk_spot(rel, bits):
    spot = 0
    for bit in bits:
        spot = spot * 2 + (1 if rel & bit else 0)
    return spot


def query_block(rows, tokens):
    return max(GROUP, min(rows, rows * 1024 // tokens))


def big(tokens):
    return 56 if tokens > 1024 else None


def call(
    name, body, out_shape, in_specs, out_specs, operands, after=(), scratch=(), grid=(), prefetch=0,
    limit=None, flops=0, nbytes=0,
):
    real = prefetch + len(in_specs)

    def ordered(*refs):
        body(*refs[:real], *refs[real + len(after) :])

    return pl.pallas_call(
        ordered,
        out_shape=out_shape,
        grid_spec=pltpu.PrefetchScalarGridSpec(
            num_scalar_prefetch=prefetch,
            grid=grid,
            in_specs=list(in_specs) + [ANY] * len(after),
            out_specs=out_specs,
            scratch_shapes=list(scratch),
        ),
        compiler_params=pltpu.CompilerParams(vmem_limit_bytes=(limit or LIMITS[name]) * MIB),
        name=name,
        cost_estimate=pl.CostEstimate(flops=flops * 8, bytes_accessed=nbytes * 8, transcendentals=0),
    )(*operands, *after)


def whole(*shape):
    return pl.BlockSpec(shape, lambda *_: (0,) * len(shape))


def shape_of(dtype, *shape):
    return jax.ShapeDtypeStruct(shape, dtype)


class Columns:
    def __init__(self, names, cuts, chunks, part, bits, y_bits):
        self.names, self.cuts = names, cuts
        self.chunks, self.part, self.bits, self.y_bits = chunks, part, bits, y_bits

    def shapes(self):
        return [
            shape_of(BF, parts, self.chunks, self.part, (end - start) // parts)
            for start, end, parts in self.cuts
        ]

    def pieces(self, name):
        first = 0
        for other, width in self.names:
            if other == name:
                break
            first += width
        found = []
        for i, (start, end, parts) in enumerate(self.cuts):
            size = (end - start) // parts
            for y in range(parts):
                lo = max(first, start + y * size)
                hi = min(first + width, start + (y + 1) * size)
                if lo < hi:
                    found.append((i, y, lo - start - y * size, lo - first, hi - lo))
        return found

    def y_place(self, y, place_ref, parts):
        return chunk_place(y, place_ref[2], [b for b in self.y_bits]) if parts > 1 else 0

    def store(self, refs, name, value, place_ref, chunks=None, column=0):
        chunks = range(self.chunks) if chunks is None else chunks
        for i, y, at, first, width in self.pieces(name):
            lo, hi = max(first, column), min(first + width, column + value.shape[1])
            if lo >= hi:
                continue
            yp = self.y_place(y, place_ref, self.cuts[i][2])
            for n, c in enumerate(chunks):
                refs[i][
                    yp, chunk_place(c, place_ref[1], self.bits), :, at + lo - first : at + hi - first
                ] = value[n * self.part : (n + 1) * self.part, lo - column : hi - column].astype(BF)


def self_attention(x, gain_self, w_qkv, rel_bias, after):
    rows, width = x.shape
    bucket_count, heads = rel_bias.shape
    pairs = heads // 2
    groups = rows // GROUP
    ids = bucket_ids(bucket_count)
    used = sorted(set(ids[ids >= 0].tolist()))

    def body(x_ref, gs_ref, wqkv_ref, ids_ref, rb_ref, a1_ref, qkv_ref, p1_ref, o1_ref, bias):
        xf = x_ref[...].astype(F32)
        a1 = (xf * inv_rms(xf) * gs_ref[...]).astype(BF)
        a1_ref[...] = a1
        qkv_ref[...] = dot_nn(a1, wqkv_ref[...]).astype(BF)
        idv = ids_ref[...]

        def make_bias(h, carry):
            val = jnp.full((GROUP, GROUP), NEG_LARGE, F32)
            for b in used:
                val = jnp.where(idv == b, rb_ref[b, h], val)
            bias[h] = val
            return carry

        lax.fori_loop(0, heads, make_bias, 0)
        m0, m1 = half_masks(GROUP)

        def attend(g, carry):
            at = pl.ds(pl.multiple_of(g * GROUP, GROUP), GROUP)
            for pair in range(pairs):
                lo = pair * 128
                q = qkv_ref[at, lo : lo + 128]
                k = qkv_ref[at, width + lo : width + lo + 128]
                v = qkv_ref[at, 2 * width + lo : 2 * width + lo + 128]
                s = dot_nt(jnp.concatenate([q * m0, q * m1], 0), k)
                s = s + jnp.concatenate([bias[2 * pair], bias[2 * pair + 1]], 0)
                e = jnp.exp(s - jnp.max(s, -1, keepdims=True))
                p = (e / jnp.sum(e, -1, keepdims=True)).astype(BF)
                p1_ref[g, pair] = p
                o = dot_nn(
                    jnp.concatenate([p[:GROUP], p[GROUP:]], 1),
                    jnp.concatenate([v * m0, v * m1], 0),
                )
                o1_ref[at, lo : lo + 128] = o.astype(BF)
            return carry

        lax.fori_loop(0, groups, attend, 0)

    return call(
        "self_attention",
        body,
        (
            shape_of(BF, rows, width),
            shape_of(BF, rows, 3 * width),
            shape_of(BF, groups, pairs, 2 * GROUP, GROUP),
            shape_of(BF, rows, width),
        ),
        [VMEM, VMEM, VMEM, VMEM, SMEM],
        (VMEM,) * 4,
        (x, gain_self.reshape(1, width), w_qkv, jnp.asarray(ids), rel_bias),
        after,
        [pltpu.VMEM((heads, GROUP, GROUP), F32)],
        flops=9 * 10**9,
        nbytes=12 * 10**6,
    )


def self_project(x, o1, w_self_out, gain_cross, w_cross_q, after):
    rows, width = x.shape

    def body(x_ref, o1_ref, wso_ref, gc_ref, wcq_ref, h1_ref, a2_ref, cq_ref):
        h1 = x_ref[...].astype(F32) + dot_nn(o1_ref[...], wso_ref[...])
        h1_ref[...] = h1
        a2 = (h1 * inv_rms(h1) * gc_ref[...]).astype(BF)
        a2_ref[...] = a2
        cq_ref[...] = dot_nn(a2, wcq_ref[...]).astype(BF)

    return call(
        "self_project",
        body,
        (shape_of(F32, rows, width), shape_of(BF, rows, width), shape_of(BF, rows, width)),
        [VMEM] * 5,
        (VMEM,) * 3,
        (x, o1, w_self_out, gain_cross.reshape(1, width), w_cross_q),
        after,
        flops=3 * 10**9,
        nbytes=8 * 10**6,
    )


def cross_forward(
    pieces, order, shard_rows, tgt_question, cq, h1, w_cross_kv, w_cross_out, gain_ff, after
):
    rows, width = cq.shape
    pairs = width // 128
    tokens = sum(len(o) for o in order) * shard_rows
    targets = rows // TLEN
    block_rows = query_block(rows, tokens)
    blocks = rows // block_rows
    steps = pairs * blocks

    def body(*refs):
        piece_refs = refs[: len(pieces)]
        (
            tq_ref, cq_ref, h1_ref, wkv_ref, wco_ref, gf_ref,
            enc_ref, kv_ref, e_ref, inv_ref, o2_ref, h2_ref, a3_ref,
            kfeat, qfeat, ebuf, sem,
        ) = refs[len(pieces) :]
        lane = lax.rem(lax.broadcasted_iota(jnp.int32, (shard_rows, 128), 1), 64).astype(F32)
        for ref, places in zip(piece_refs, order):
            for j, spot in enumerate(places):
                at = slice(spot * shard_rows, (spot + 1) * shard_rows)
                enc_ref[at, :] = ref[j, :shard_rows, :]
                tag = ref[j, shard_rows : shard_rows + 1, :shard_rows].astype(F32)
                tag = jnp.transpose(jnp.broadcast_to(tag, (128, shard_rows)))
                kfeat[at, :] = jnp.where(tag == lane, 0.0, NEG_LARGE).astype(BF)
        lane_t = lax.rem(lax.broadcasted_iota(jnp.int32, (TLEN, 128), 1), 64)
        for t in range(targets):
            qfeat[t * TLEN : (t + 1) * TLEN, :] = jnp.where(lane_t == tq_ref[t], 1.0, 0.0).astype(BF)
        kv_ref[...] = dot_nn(enc_ref[...], wkv_ref[...]).astype(BF)
        q0, q1 = half_masks(block_rows)
        k0, k1 = half_masks(tokens)
        qmask, kmask = (q0, q1), (k0, k1)
        low = lax.broadcasted_iota(jnp.int32, (block_rows, 128), 1) < 64

        def out_copy(slot, step):
            pair, block = step // blocks, lax.rem(step, blocks)
            return pltpu.make_async_copy(
                ebuf.at[slot],
                e_ref.at[pl.ds(2 * pair, 2), pl.ds(block * block_rows, block_rows)],
                sem.at[slot],
            )

        def attend(step, carry):
            slot = lax.rem(step, 2)
            pair, block = step // blocks, lax.rem(step, blocks)
            lo = pl.multiple_of(pair * 128, 128)
            at = pl.ds(pl.multiple_of(block * block_rows, block_rows), block_rows)

            @pl.when(step >= 2)
            def _():
                out_copy(slot, step - 2).wait()

            q = cq_ref[at, pl.ds(lo, 128)]
            k = kv_ref[:, pl.ds(lo, 128)]
            v = kv_ref[:, pl.ds(width + lo, 128)]
            outs = []
            for h in range(2):
                qa = q * qmask[h] + qfeat[at, :] * qmask[1 - h]
                ka = k * kmask[h] + kfeat[...] * kmask[1 - h]
                s = dot_nt(qa, ka)
                top = jnp.max(s, -1, keepdims=True)
                e = jnp.exp(s - top).astype(BF)
                ebuf[slot, h] = e
                outs.append(dot_nn(e, v * kmask[h] + kmask[1 - h]))
            out_copy(slot, step).start()
            total = jnp.where(low, pltpu.roll(outs[0], 64, 1), pltpu.roll(outs[1], 64, 1))
            inv = 1.0 / total
            inv_ref[at, pl.ds(lo, 128)] = inv
            o2_ref[at, pl.ds(lo, 128)] = (jnp.where(low, outs[0], outs[1]) * inv).astype(BF)
            return carry

        lax.fori_loop(0, steps, attend, 0)
        h2 = h1_ref[...] + dot_nn(o2_ref[...], wco_ref[...])
        h2_ref[...] = h2
        a3_ref[...] = (h2 * inv_rms(h2) * gf_ref[...]).astype(BF)
        for step in range(max(0, steps - 2), steps):
            out_copy(step % 2, jnp.int32(step)).wait()

    return call(
        "cross_forward",
        body,
        (
            shape_of(BF, tokens, width),
            shape_of(BF, tokens, 2 * width),
            shape_of(BF, 2 * pairs, rows, tokens),
            shape_of(F32, rows, width),
            shape_of(BF, rows, width),
            shape_of(F32, rows, width),
            shape_of(BF, rows, width),
        ),
        [VMEM] * len(pieces) + [SMEM] + [VMEM] * 5,
        (VMEM, VMEM, ANY, VMEM, VMEM, VMEM, VMEM),
        (*pieces, tgt_question, cq, h1, w_cross_kv, w_cross_out, gain_ff.reshape(1, width)),
        after,
        [
            pltpu.VMEM((tokens, 128), BF),
            pltpu.VMEM((rows, 128), BF),
            pltpu.VMEM((2, 2, block_rows, tokens), BF),
            pltpu.SemaphoreType.DMA((2,)),
        ],
        limit=big(tokens),
        flops=16 * 10**9,
        nbytes=30 * 10**6,
    )


def hidden_gradient(gy, w_ff_out, after):
    rows, width = gy.shape
    hidden = w_ff_out.shape[0]

    def body(gy_ref, w2_ref, out_ref):
        out_ref[...] = dot_nt(gy_ref[...], w2_ref[...]).astype(BF)

    return call(
        "hidden_gradient",
        body,
        shape_of(BF, rows, hidden),
        [whole(rows, width), pl.BlockSpec((width, width), lambda s: (s, 0))],
        pl.BlockSpec((rows, width), lambda s: (0, s)),
        (gy, w_ff_out),
        after,
        grid=(hidden // width,),
        flops=24 * 10**8,
        nbytes=9 * 10**6,
    )


def feed_hidden(place, a3, gy, dhid, w_ff_in, columns, after):
    rows, width = a3.shape
    hidden = w_ff_in.shape[1]
    tile = width
    steps = hidden // tile
    half = width // 2
    sub = hidden // width
    chunks, part = columns.chunks, columns.part
    per_tile = chunks * tile // hidden
    scale = math.sqrt(2.0 / math.pi)
    shapes = columns.shapes()
    n = len(shapes)

    def body(place_ref, a3_ref, gy_ref, dhid_ref, w1_ref, hid_ref, dpre_ref, *refs):
        core = place_ref[0]
        step = pl.program_id(0)
        gyv = gy_ref[...]
        pre = dot_nn(a3_ref[...], w1_ref[...])
        sq = pre * pre
        t = jnp.tanh(scale * pre * (1.0 + 0.044715 * sq))
        hid = (0.5 * pre * (1.0 + t)).astype(BF)
        slope = 0.5 * (1.0 + t) + 0.5 * pre * (1.0 - t * t) * (scale * (1.0 + 0.134145 * sq))
        hid_ref[...] = hid
        dpre_ref[...] = (dhid_ref[...].astype(F32) * slope).astype(BF)
        g = dot_tn(hid, gyv)
        swapped = core == 1
        keep = jnp.where(swapped, g[:, half:], g[:, :half])
        send = jnp.where(swapped, g[:, :half], g[:, half:])
        for value, outs in ((keep, refs[:n]), (send, refs[n:])):
            for i in range(per_tile):
                for j in range(sub):
                    first = (i * sub + j) * part
                    columns.store(
                        outs, "out", value[first : first + part], place_ref,
                        [step * per_tile + i], j * half,
                    )

    tiles = pl.BlockSpec((rows, tile), lambda s, *_: (0, s))
    return call(
        "feed_hidden",
        body,
        (shape_of(BF, rows, hidden), shape_of(BF, rows, hidden), *shapes, *shapes),
        [
            whole(rows, width),
            whole(rows, width),
            tiles,
            pl.BlockSpec((width, tile), lambda s, *_: (0, s)),
        ],
        (tiles, tiles) + tuple(whole(*x.shape) for x in shapes) * 2,
        (place, a3, gy, dhid, w_ff_in),
        after,
        grid=(steps,),
        prefetch=1,
        flops=5 * 10**9,
        nbytes=20 * 10**6,
    )


def feed_weights(place, a3, dpre, columns, after):
    rows, width = a3.shape
    hidden = dpre.shape[1]
    tile = width
    steps = hidden // tile
    half_steps = steps // 2
    shapes = columns.shapes()
    n = len(shapes)

    def body(place_ref, a3_ref, dpre_ref, *refs):
        core = place_ref[0]
        step = pl.program_id(0)
        g = dot_tn(a3_ref[...], dpre_ref[...])
        for s in range(steps):
            for c in range(2):

                @pl.when(jnp.logical_and(step == s, core == c))
                def _():
                    outs = refs[:n] if s // half_steps == c else refs[n:]
                    columns.store(outs, "in", g, place_ref, None, (s % half_steps) * tile)

    return call(
        "feed_weights",
        body,
        (*shapes, *shapes),
        [whole(rows, width), pl.BlockSpec((rows, tile), lambda s, *_: (0, s))],
        tuple(whole(*x.shape) for x in shapes) * 2,
        (place, a3, dpre),
        after,
        grid=(steps,),
        prefetch=1,
        flops=24 * 10**8,
        nbytes=9 * 10**6,
    )


def feed_back(dpre, w_ff_in, h2, gain_ff, gy, after):
    rows, width = h2.shape
    hidden = dpre.shape[1]
    tile = width
    steps = hidden // tile

    def body(dpre_ref, w1_ref, h2_ref, gf_ref, gy_ref, dh2_ref, gain_ref, acc):
        step = pl.program_id(0)
        term = dot_nt(dpre_ref[...], w1_ref[...])

        @pl.when(step == 0)
        def _():
            acc[...] = term

        @pl.when(step > 0)
        def _():
            acc[...] += term

        @pl.when(step == steps - 1)
        def _():
            dv, dgain = rms_back(acc[...], h2_ref[...], gf_ref[...])
            dh2_ref[...] = gy_ref[...].astype(F32) + dv
            gain_ref[...] = dgain

    return call(
        "feed_back",
        body,
        (shape_of(F32, rows, width), shape_of(F32, 1, width)),
        [
            pl.BlockSpec((rows, tile), lambda s: (0, s)),
            pl.BlockSpec((width, tile), lambda s: (0, s)),
            whole(rows, width),
            whole(1, width),
            whole(rows, width),
        ],
        (whole(rows, width), whole(1, width)),
        (dpre, w_ff_in, h2, gain_ff.reshape(1, width), gy),
        after,
        [pltpu.VMEM((rows, width), F32)],
        grid=(steps,),
        flops=24 * 10**8,
        nbytes=12 * 10**6,
    )


def feed_out(hid, w_ff_out, h2, after):
    rows, width = h2.shape
    hidden = hid.shape[1]
    steps = hidden // width

    def body(hid_ref, w2_ref, h2_ref, out_ref, acc):
        step = pl.program_id(0)
        term = dot_nn(hid_ref[...], w2_ref[...])

        @pl.when(step == 0)
        def _():
            acc[...] = h2_ref[...] + term

        @pl.when(step > 0)
        def _():
            acc[...] += term

        @pl.when(step == steps - 1)
        def _():
            out_ref[...] = acc[...].astype(BF)

    return call(
        "feed_out",
        body,
        shape_of(BF, rows, width),
        [
            pl.BlockSpec((rows, width), lambda s: (0, s)),
            pl.BlockSpec((width, width), lambda s: (s, 0)),
            whole(rows, width),
        ],
        whole(rows, width),
        (hid, w_ff_out, h2),
        after,
        [pltpu.VMEM((rows, width), F32)],
        grid=(steps,),
        flops=24 * 10**8,
        nbytes=11 * 10**6,
    )


def cross_backward(first_pair, last_pair, dh2, o2, inv, cq, kv, e, w_cross_out, after):
    rows, width = cq.shape
    pairs = width // 128
    count = last_pair - first_pair
    tokens = kv.shape[0]
    block_rows = query_block(rows, tokens)
    blocks = rows // block_rows

    def body(
        dh2_ref, wco_ref, o2_ref, inv_ref, cq_ref, k_ref, v_ref, e_ref,
        dcq_ref, dkt_ref, dvt_ref,
        do2,
    ):
        pair = pl.program_id(0)

        @pl.when(pair == 0)
        def _():
            do2v = dot_nt(dh2_ref[...].astype(BF), wco_ref[...]).astype(BF)
            for i in range(count):
                do2[i] = do2v[:, i * 128 : (i + 1) * 128]

        q0, q1 = half_masks(block_rows)
        k0, k1 = half_masks(tokens)
        qmask, kmask = (q0, q1), (k0, k1)
        lane = lax.broadcasted_iota(jnp.int32, (block_rows, 128), 1)
        low = lane < 64
        first = lax.rem(lane, 64) == 0
        second = lax.rem(lane, 64) == 1
        k, v = k_ref[...], v_ref[...]
        sums = [0.0] * 4
        for block in range(blocks):
            at = slice(block * block_rows, (block + 1) * block_rows)
            q = cq_ref[at, :]
            dof = do2[pair, at, :].astype(F32) * inv_ref[at, :]
            dob = dof.astype(BF)
            prod = dof * o2_ref[at, :].astype(F32)
            qt = jnp.transpose(q)
            dot_t = jnp.transpose(dob)
            dqs = []
            for h in range(2):
                own = low if h == 0 else jnp.logical_not(low)
                delta = -jnp.sum(jnp.where(own, prod, 0.0), -1, keepdims=True)
                hi = delta.astype(BF).astype(F32)
                feat = jnp.where(first, hi, jnp.where(second, delta - hi, 0.0)).astype(BF)
                doa = dob * qmask[h] + feat * qmask[1 - h]
                dp = dot_nt(doa, v * kmask[h] + kmask[1 - h])
                ev = e_ref[h, at, :]
                ds = (ev.astype(F32) * dp).astype(BF)
                dqs.append(dot_nn(ds, k))
                sums[h] = sums[h] + dot_nn(qt[h * 64 : (h + 1) * 64, :], ds)
                sums[2 + h] = sums[2 + h] + dot_nn(dot_t[h * 64 : (h + 1) * 64, :], ev)
            dcq_ref[at, :] = jnp.where(low, dqs[0], dqs[1]).astype(BF)
        for h in range(2):
            dkt_ref[h * 64 : (h + 1) * 64, :] = sums[h].astype(BF)
            dvt_ref[h * 64 : (h + 1) * 64, :] = sums[2 + h].astype(BF)

    def column(n, first=first_pair):
        return pl.BlockSpec((n, 128), lambda p: (0, p + first))

    return call(
        "cross_backward",
        body,
        (
            shape_of(BF, rows, count * 128),
            shape_of(BF, count * 128, tokens),
            shape_of(BF, count * 128, tokens),
        ),
        [
            whole(rows, width),
            pl.BlockSpec((count * 128, width), lambda p: (first_pair // count, 0)),
            column(rows),
            column(rows),
            column(rows),
            column(tokens),
            column(tokens, first_pair + pairs),
            pl.BlockSpec((2, rows, tokens), lambda p: (p + first_pair, 0, 0)),
        ],
        (
            column(rows, 0),
            pl.BlockSpec((128, tokens), lambda p: (p, 0)),
            pl.BlockSpec((128, tokens), lambda p: (p, 0)),
        ),
        (dh2, w_cross_out, o2, inv, cq, kv, kv, e),
        after,
        [pltpu.VMEM((count, rows, 128), BF)],
        grid=(count,),
        limit=big(tokens),
        flops=8 * 10**9,
        nbytes=14 * 10**6,
    )


def cross_query_back(dcq, w_cross_q, h1, gain_cross, dh2, after):
    rows, width = h1.shape
    n = len(dcq)
    size = width // n

    def body(*refs):
        wcq_ref, h1_ref, gc_ref, dh2_ref, dh1_ref, gain_ref = refs[n:]
        da2 = 0.0
        for i in range(n):
            da2 = da2 + dot_nt(refs[i][...], wcq_ref[:, i * size : (i + 1) * size])
        dv, dgain = rms_back(da2, h1_ref[...], gc_ref[...])
        dh1_ref[...] = dh2_ref[...] + dv
        gain_ref[...] = dgain

    return call(
        "cross_query_back",
        body,
        (shape_of(F32, rows, width), shape_of(F32, 1, width)),
        [VMEM] * (n + 4),
        (VMEM,) * 2,
        (*dcq, w_cross_q, h1, gain_cross.reshape(1, width), dh2),
        after,
        flops=6 * 10**8,
        nbytes=8 * 10**6,
    )


def cross_weights(place, dh2, o2, dcq, dkt, dvt, enc, a2, w_cross_kv, columns, after):
    rows, width = dh2.shape
    tokens = enc.shape[0]
    half = width // 2
    tile = min(tokens, 1024)
    steps = tokens // tile
    n = len(dcq)
    size = width // n
    shapes = columns.shapes()
    ns = len(shapes)

    def body(place_ref, dh2_ref, o2_ref, enc_ref, a2_ref, wkv_ref, *refs):
        core = place_ref[0]
        dcq_refs, dkt_refs, dvt_refs = refs[:n], refs[n : 2 * n], refs[2 * n : 3 * n]
        genc_ref = refs[3 * n]
        keep, send = refs[3 * n + 1 : 3 * n + 1 + ns], refs[3 * n + 1 + ns : 3 * n + 1 + 2 * ns]
        accs = refs[3 * n + 1 + 2 * ns :]
        step = pl.program_id(0)

        @pl.when(step == 0)
        def _():
            dcqv = jnp.concatenate([r[...] for r in dcq_refs], 1)
            for name, lhs, rhs in (
                ("out", o2_ref[...], dh2_ref[...].astype(BF)),
                ("q", a2_ref[...], dcqv),
            ):
                g = dot_tn(lhs, rhs)
                swapped = core == 1
                columns.store(keep, name, jnp.where(swapped, g[:, half:], g[:, :half]), place_ref)
                columns.store(send, name, jnp.where(swapped, g[:, :half], g[:, half:]), place_ref)

        wkt = jnp.transpose(wkv_ref[...])
        dkvt = jnp.concatenate([r[...] for r in dkt_refs + dvt_refs], 0)
        genc_ref[...] = dot_tn(dkvt, wkt).astype(BF)
        g = dot_nt(jnp.transpose(enc_ref[...]), dkvt)
        if accs:
            g = g + jnp.where(step == 0, 0.0, accs[0][...])
            accs[0][...] = g

        @pl.when(step == steps - 1)
        def _():
            swapped = core == 1
            columns.store(keep, "kv", jnp.where(swapped, g[:, width:], g[:, :width]), place_ref)
            columns.store(send, "kv", jnp.where(swapped, g[:, :width], g[:, width:]), place_ref)

    sized = pl.BlockSpec((size, tile), lambda s, *_: (0, s))
    return call(
        "cross_weights",
        body,
        (shape_of(BF, tokens, width), *shapes, *shapes),
        [
            whole(rows, width),
            whole(rows, width),
            pl.BlockSpec((tile, width), lambda s, *_: (s, 0)),
            whole(rows, width),
            whole(width, 2 * width),
        ]
        + [whole(rows, size)] * n
        + [sized] * (2 * n),
        (pl.BlockSpec((tile, width), lambda s, *_: (s, 0)),)
        + tuple(whole(*x.shape) for x in shapes) * 2,
        (place, dh2, o2, enc, a2, w_cross_kv, *dcq, *dkt, *dvt),
        after,
        [pltpu.VMEM((width, 2 * width), F32)] * (1 if steps > 1 else 0),
        grid=(steps,),
        prefetch=1,
        limit=big(tokens),
        flops=64 * 10**8,
        nbytes=18 * 10**6,
    )


def self_backward(dh1, w_self_out, qkv, p1, bucket_count, heads, after):
    rows, width = dh1.shape
    pairs = heads // 2
    groups = rows // GROUP
    ids = bucket_ids(bucket_count)
    used = sorted(set(ids[ids >= 0].tolist()))
    small = np.tile(ids[:TLEN, :TLEN], (1, GROUP // TLEN))

    def body(dh1_ref, wso_ref, qkv_ref, p1_ref, ids_ref, dqkv_ref, gbias_ref, do1, acc):
        do1[...] = dot_nt(dh1_ref[...].astype(BF), wso_ref[...]).astype(BF)
        m0, m1 = half_masks(GROUP)
        acc[...] = jnp.zeros_like(acc)

        def attend(g, carry):
            at = pl.ds(pl.multiple_of(g * GROUP, GROUP), GROUP)
            for pair in range(pairs):
                lo = pair * 128
                q = qkv_ref[at, lo : lo + 128]
                k = qkv_ref[at, width + lo : width + lo + 128]
                v = qkv_ref[at, 2 * width + lo : 2 * width + lo + 128]
                do = do1[at, lo : lo + 128]
                do_two = jnp.concatenate([do * m0, do * m1], 0)
                pb = p1_ref[g, pair]
                pf = pb.astype(F32)
                dp = dot_nt(do_two, v)
                ds = (pf * (dp - jnp.sum(pf * dp, -1, keepdims=True))).astype(BF)
                dsf = ds.astype(F32)
                for h in range(2):
                    total = dsf[h * GROUP : h * GROUP + TLEN]
                    for t in range(1, GROUP // TLEN):
                        total = total + dsf[h * GROUP + t * TLEN : h * GROUP + (t + 1) * TLEN]
                    acc[2 * pair + h] += total
                dq = dot_nn(
                    jnp.concatenate([ds[:GROUP], ds[GROUP:]], 1),
                    jnp.concatenate([k * m0, k * m1], 0),
                )
                dk = dot_tn(ds, jnp.concatenate([q * m0, q * m1], 0))
                dv = dot_tn(pb, do_two)
                dqkv_ref[at, lo : lo + 128] = dq.astype(BF)
                dqkv_ref[at, width + lo : width + lo + 128] = dk.astype(BF)
                dqkv_ref[at, 2 * width + lo : 2 * width + lo + 128] = dv.astype(BF)
            return carry

        lax.fori_loop(0, groups, attend, 0)
        idv = ids_ref[...]
        lane = lax.broadcasted_iota(jnp.int32, (16, 128), 1)
        bias = jnp.zeros((16, 128), F32)
        accv = acc[...]
        pad = jnp.zeros((16 - heads, 1), F32)
        for b in used:
            part_sum = jnp.sum(jnp.where((idv == b)[None], accv, 0.0), axis=1)
            col = jnp.sum(part_sum, -1, keepdims=True)
            bias = jnp.where(lane == b, jnp.concatenate([col, pad], 0), bias)
        gbias_ref[...] = bias

    return call(
        "self_backward",
        body,
        (shape_of(BF, rows, 3 * width), shape_of(F32, 16, 128)),
        [VMEM] * 5,
        (VMEM,) * 2,
        (dh1, w_self_out, qkv, p1, jnp.asarray(small)),
        after,
        [pltpu.VMEM((rows, width), BF), pltpu.VMEM((heads, TLEN, GROUP), F32)],
        flops=6 * 10**9,
        nbytes=10 * 10**6,
    )


MISC_ROWS, MISC_LANES = 32, 512


def self_weights(
    place, dh1, o1, a1, dqkv, x, gain_self, w_qkv, gbias, gain_cross_grad, gain_ff_grad, columns, after
):
    rows, width = dh1.shape
    half = width // 2
    shapes = columns.shapes()
    n = len(shapes)

    def body(
        place_ref, dh1_ref, o1_ref, a1_ref, dqkv_ref, x_ref, gs_ref, wqkv_ref, gb_ref, ggc_ref, ggf_ref,
        out_ref, misc_ref, *refs,
    ):
        core = place_ref[0]
        for which, outs in ((1 - core, refs[n:]), (core, refs[:n])):
            at = pl.ds(pl.multiple_of(which * half, 128), half)
            columns.store(outs, "out", dot_tn(o1_ref[...], dh1_ref[:, at].astype(BF)), place_ref)
            at = pl.ds(pl.multiple_of(which * 3 * half, 128), 3 * half)
            columns.store(outs, "qkv", dot_tn(a1_ref[...], dqkv_ref[:, at]), place_ref)
        da1 = dot_nt(dqkv_ref[...], wqkv_ref[...])
        dv, dgain = rms_back(da1, x_ref[...].astype(F32), gs_ref[...])
        out_ref[...] = dh1_ref[...] + dv
        misc_ref[...] = jnp.zeros_like(misc_ref)
        misc_ref[0:16, 0:128] = gb_ref[...]
        for i, gain in enumerate((dgain, ggc_ref[...], ggf_ref[...])):
            misc_ref[16 + 2 * i : 17 + 2 * i, :] = gain[:, :MISC_LANES]
            misc_ref[17 + 2 * i : 18 + 2 * i, : width - MISC_LANES] = gain[:, MISC_LANES:]

    return call(
        "self_weights",
        body,
        (shape_of(F32, rows, width), shape_of(F32, MISC_ROWS, MISC_LANES), *shapes, *shapes),
        [SMEM] + [VMEM] * 10,
        (VMEM,) * (2 + 2 * n),
        (
            place, dh1, o1, a1, dqkv, x, gain_self.reshape(1, width), w_qkv, gbias,
            gain_cross_grad, gain_ff_grad,
        ),
        after,
        flops=57 * 10**8,
        nbytes=20 * 10**6,
    )


def swap(value, axis, bit):
    size = lax.axis_size(axis)
    return lax.ppermute(value, axis, [(i, i ^ bit) for i in range(size)])


def add_up(terms):
    total = terms[0].astype(F32)
    for term in terms[1:]:
        total = total + term.astype(F32)
    return total


class Bucket:
    def __init__(self, keep, send, y_parts, bits, y_bits, extra=None):
        cols = keep.shape[-1]
        self.rows, self.cols = math.prod(keep.shape[:-1]), cols
        self.terms = [keep.reshape(self.rows, cols)]
        self.send = None if send is None else send.reshape(self.rows, cols)
        self.extra = extra
        halves = [("blk", b) for b in bits]
        if send is None:
            last = []
        elif y_parts > 1:
            halves = [("dp", 2 * b) for b in y_bits] + halves
            last = [("gather", 2 * b) for b in reversed(y_bits)]
        else:
            last = [("full", 2 * b) for b in y_bits]
        self.steps = ([] if send is None else [("core", 1)]) + halves + last

    def next_sum(self):
        kind = self.steps[0][0]
        if kind in ("blk", "dp"):
            return 1, self.rows // 2
        return 0, self.rows


def sum_kernel(jobs, after):
    outs, specs, operands, plan = [], [], [], []
    for block, rows, terms, extra in jobs:
        cols = terms[0].shape[1]
        first = len(operands)
        for t in terms:
            operands.append(t)
            specs.append(pl.BlockSpec((rows, cols), functools.partial(lambda k, *_: (k, 0), block)))
        for t, row in extra:
            operands.append(t)
            specs.append(
                pl.BlockSpec((MISC_ROWS, cols), functools.partial(lambda k, *_: (k, 0), row // MISC_ROWS))
            )
        plan.append((first, len(terms), len(extra), rows))
        outs.append(shape_of(BF, rows + (MISC_ROWS if extra else 0), cols))
    count = len(operands)

    def body(*refs):
        for i, (first, n, m, rows) in enumerate(plan):
            total = refs[first][...].astype(F32)
            for r in refs[first + 1 : first + n]:
                total = total + r[...].astype(F32)
            refs[count + i][:rows, :] = total.astype(BF)
            if m:
                total = refs[first + n][...].astype(F32)
                for r in refs[first + n + 1 : first + n + m]:
                    total = total + r[...].astype(F32)
                refs[count + i][rows:, :] = total.astype(BF)

    got = call(
        "sum_kernel",
        body, tuple(outs), specs, tuple(whole(*o.shape) for o in outs), operands, after, grid=(1,),
        nbytes=sum(math.prod(o.shape) for o in outs) * 8,
    )
    return list(got)


def sum_plain(jobs):
    outs = []
    for block, rows, terms, extra in jobs:
        out = add_up([t[block * rows : (block + 1) * rows] for t in terms])
        if extra:
            out = jnp.concatenate([out, add_up([t[r : r + MISC_ROWS] for t, r in extra])], 0)
        outs.append(out.astype(BF))
    return outs


def send_round(buckets, after=()):
    jobs, which = [], []
    payloads = [None] * len(buckets)
    for i, b in enumerate(buckets):
        kind = b.steps[0][0]
        if kind == "core":
            payloads[i] = b.send
            if b.extra is not None:
                payloads[i] = jnp.concatenate([b.send, b.extra.astype(BF)], 0)
                b.extra = [(b.extra, 0)]
        elif b.rows == b.terms[0].shape[0] and len(b.terms) == 1 and kind == "gather":
            payloads[i] = b.terms[0]
        else:
            block, rows = b.next_sum()
            extra = [] if b.extra is None else b.extra
            if kind in ("blk", "dp") and len(b.terms) == 1:
                payloads[i] = b.terms[0][rows : 2 * rows]
            else:
                jobs.append((block, rows, b.terms, extra))
                which.append(i)
    if jobs:
        fits = all(rows % MISC_ROWS == 0 for _, rows, _, _ in jobs)
        outs = sum_kernel(jobs, list(after)) if fits else sum_plain(jobs)
        for i, out in zip(which, outs):
            payloads[i] = out
    gots = []
    for b, payload in zip(buckets, payloads):
        kind, bit = b.steps.pop(0)
        got = swap(payload, "blk" if kind == "blk" else "dp", bit)
        gots.append(got)
        rows = b.rows
        if kind == "core":
            b.terms.append(got)
            if b.extra is not None:
                b.extra = [(payload, rows), (got, rows)]
        elif kind in ("blk", "dp"):
            b.rows = rows // 2
            b.terms.append(got)
            if b.extra is not None:
                b.extra = [(payload, b.rows), (got, b.rows)]
        elif kind == "full":
            b.terms = [payload, got]
            if b.extra is not None:
                b.extra = [(payload, rows), (got, rows)]
        else:
            b.terms = [jnp.concatenate([payload, got], 0)]
            b.rows *= 2
    return payloads, gots


def side_by_side(buckets, part):
    cols = []
    for bucket in buckets:
        own = bucket.terms[0]
        if len(bucket.terms) > 1:
            own = add_up([t[: bucket.rows] for t in bucket.terms]).astype(BF)
        for i in range(bucket.rows // part):
            cols.append(own[i * part : (i + 1) * part])
    return jnp.concatenate(cols, 1)


def join_halves(place, own, other, groups, after):
    part = own.shape[0]
    outs = []
    for columns, arrays in groups:
        for name, stack in arrays:
            half = dict(columns.names)[name] // stack
            outs.append((columns, name, stack, half))

    def body(place_ref, own_ref, other_ref, *refs):
        core = place_ref[0]
        base = {}
        col = 0
        for columns, _ in groups:
            for i, (start, end, parts) in enumerate(columns.cuts):
                base[id(columns), i] = col
                col += end - start
        for ref, (columns, name, stack, half) in zip(refs, outs):
            for i, y, at, first, width in columns.pieces(name):
                parts = columns.cuts[i][2]
                size = (columns.cuts[i][1] - columns.cuts[i][0]) // parts
                yp = columns.y_place(y, place_ref, parts)
                done = 0
                while done < width:
                    j, off = divmod(first + done, half)
                    step = min(width - done, half - off)
                    src = pl.ds(
                        pl.multiple_of(base[id(columns), i] + yp * size + at + done, 128), step
                    )
                    for which, src_ref in ((core, own_ref), (1 - core, other_ref)):
                        dst = pl.ds(pl.multiple_of(which * half + off, 128), step)
                        ref[j * part : (j + 1) * part, dst] = src_ref[:, src].astype(F32)
                    done += step

    return call(
        "join_halves",
        body,
        tuple(shape_of(F32, stack * part, 2 * half) for _, _, stack, half in outs),
        [SMEM, VMEM, VMEM],
        (VMEM,) * len(outs),
        (place, own, other),
        after,
        nbytes=4 * 10**6,
    )


def gather_encodings(own, bits):
    if len(bits) == 3:
        x, z, far = bits
        r_far, r_x = swap(own, "blk", far), swap(own, "blk", x)

        def second():
            r_z, r_zf = swap(own, "blk", z), swap(r_far, "blk", z)
            r_xf = swap(r_far, "blk", x)

            def third():
                r_xz = swap(r_z, "blk", x)
                r_xzf = swap(r_xf, "blk", z)
                arrays = [own, r_far, r_x, r_z, r_zf, r_xf, r_xz, r_xzf]
                return arrays, [[0], [far], [x], [z], [z | far], [x | far], [x | z], [x | z | far]]

            return [r_z, r_zf, r_xf], third

        return [r_far, r_x], second
    got, rel = own, [0]
    for bit in reversed(bits):
        got = jnp.concatenate([got, swap(got, "blk", bit)], 0)
        rel = rel + [r ^ bit for r in rel]
    return [], lambda: ([], lambda: ([got], [rel]))


def local(
    dec_in,
    encodings,
    enc_question,
    enc_valid,
    tgt_question,
    gain_self,
    w_qkv,
    rel_bias,
    w_self_out,
    gain_cross,
    w_cross_q,
    w_cross_kv,
    w_cross_out,
    gain_ff,
    w_ff_in,
    w_ff_out,
    grad_out,
):
    x = dec_in[0]
    gy = grad_out[0]
    rows, width = x.shape
    bucket_count, heads = rel_bias.shape
    hidden = w_ff_in.shape[1]
    half = width // 2
    chunks = lax.axis_size("blk")
    part = width // chunks
    dp_size = lax.axis_size("dp")
    shard_rows = encodings.shape[1]
    bits = [1 << i for i in range(chunks.bit_length() - 1)]
    y_bits = [1 << i for i in range(dp_size.bit_length() - 2)]
    y_parts = dp_size // 2
    blk = lax.axis_index("blk")
    dp = lax.axis_index("dp")
    place = jnp.stack([lax.rem(dp, 2), blk, dp // 2]).astype(jnp.int32)

    layout = functools.partial(Columns, chunks=chunks, part=part, bits=bits, y_bits=y_bits)
    stack = hidden // width
    cols_out = layout([("out", stack * half)], [(0, stack * half, y_parts)])
    cols_in = layout([("in", hidden // 2)], [(0, hidden // 2, 1)])
    cols_x = layout([("out", half), ("q", half), ("kv", width)], [(0, 2 * width, 1)])
    cols_s = layout(
        [("out", half), ("qkv", 3 * half)], [(0, MISC_LANES, 1), (MISC_LANES, 2 * width, y_parts)]
    )

    tags = jnp.where(enc_valid[0] == 1, enc_question[0], -1).astype(BF)
    tag_rows = jnp.zeros((16, width), BF).at[0, :shard_rows].set(tags)
    enc_own = jnp.concatenate([encodings[0], tag_rows], 0)[None]
    got, second = gather_encodings(enc_own, bits)
    a1, qkv, p1, o1 = self_attention(x, gain_self, w_qkv, rel_bias, [enc_own])
    more, third = second()
    h1, a2, cq = self_project(x, o1, w_self_out, gain_cross, w_cross_q, got)
    pieces, rel = third()
    dhid = hidden_gradient(gy, w_ff_out, more)
    spots = [[int(chunk_spot(r, bits)) for r in group] for group in rel]
    enc, kv, e, inv, o2, h2, a3 = cross_forward(
        pieces, spots, shard_rows, tgt_question[0], cq, h1, w_cross_kv, w_cross_out, gain_ff, [dhid]
    )

    hid, dpre, keep, send = feed_hidden(place, a3, gy, dhid, w_ff_in, cols_out, [])
    b_out = Bucket(keep, send, y_parts, bits, y_bits)
    sent, _ = send_round([b_out])
    keep, send = feed_weights(place, a3, dpre, cols_in, sent)
    b_in = Bucket(keep, send, 1, bits, y_bits)
    sent, got_b = send_round([b_in, b_out])
    dh2, gain_ff_grad = feed_back(dpre, w_ff_in, h2, gain_ff, gy, sent)
    sent, got_c = send_round([b_in])
    pairs = heads // 2
    cut = pairs // 2
    parts_a = cross_backward(0, cut, dh2, o2, inv, cq, kv, e, w_cross_out, sent)
    parts_b = cross_backward(cut, pairs, dh2, o2, inv, cq, kv, e, w_cross_out, [parts_a[0]])
    dcq, dkt, dvt = zip(parts_a, parts_b)
    sent, got_d = send_round([b_out], [parts_b[0]])
    dh1, gain_cross_grad = cross_query_back(dcq, w_cross_q, h1, gain_cross, dh2, sent)
    sent, got_e = send_round([b_in], [dh1])
    genc, keep, send = cross_weights(
        place, dh2, o2, dcq, dkt, dvt, enc, a2, w_cross_kv, cols_x, [dh1, *sent]
    )
    b_x = Bucket(keep, send, 1, bits, y_bits)
    b_enc = Bucket(genc, None, 1, bits, y_bits)
    sent, got_f = send_round([b_x, b_out, b_in, b_enc])
    dqkv, gbias = self_backward(dh1, w_self_out, qkv, p1, bucket_count, heads, sent)
    sent, got_g = send_round([b_x, b_out, b_in, b_enc], [dqkv])
    grad_dec, misc, keep_a, keep_b, send_a, send_b = self_weights(
        place, dh1, o1, a1, dqkv, x, gain_self, w_qkv, gbias, gain_cross_grad, gain_ff_grad, cols_s,
        sent + got_f,
    )
    b_sa = Bucket(keep_a, send_a, 1, bits, y_bits, misc)
    b_sb = Bucket(keep_b, send_b, y_parts, bits, y_bits)
    sent, got_h = send_round([b_sa, b_sb])
    sent_h, got_i = send_round([b_out, b_enc], [keep_a])
    out = feed_out(hid, w_ff_out, h2, sent + sent_h + [got_g[1]])
    sent, got_j = send_round([b_sa, b_sb], [out])
    sent, got_k = send_round([b_x], got_g)
    everything = [b_out, b_in, b_x, b_sa, b_sb, b_enc]
    sent, got_l = send_round([b_sa])
    sent, got_m = send_round([b_x, b_sa], got_k)
    sent, got_n = send_round([b_sb], got_j)
    while any(b.steps for b in everything):
        send_round([b for b in everything if b.steps])
    grad_enc = add_up([t[: b_enc.rows] for t in b_enc.terms])
    own = side_by_side(everything[:5], part)
    other = swap(own, "dp", 1)
    misc = add_up([t[r : r + MISC_ROWS] for t, r in b_sa.extra]).astype(BF).astype(F32)
    (
        grad_ff_out, grad_ff_in, grad_cross_out, grad_cross_q, grad_cross_kv, grad_self_out, grad_qkv,
    ) = join_halves(
        place, own, other,
        [
            (cols_out, [("out", stack)]),
            (cols_in, [("in", 1)]),
            (cols_x, [("out", 1), ("q", 1), ("kv", 1)]),
            (cols_s, [("out", 1), ("qkv", 1)]),
        ],
        [],
    )
    gains = jnp.concatenate([misc[16:22:2], misc[17:22:2, : width - MISC_LANES]], 1)
    gains = lax.dynamic_slice(gains, (0, blk * part), (3, part))
    bias_part = bucket_count // chunks
    grad_bias = lax.dynamic_slice(misc, (0, blk * bias_part), (heads, bias_part)).T
    return (
        out[None],
        grad_dec[None],
        grad_enc[None],
        gains[0],
        grad_qkv,
        grad_bias,
        grad_self_out,
        gains[1],
        grad_cross_q,
        grad_cross_kv,
        grad_cross_out,
        gains[2],
        grad_ff_in,
        grad_ff_out,
    )


def solution(mesh):
    return jax.shard_map(
        local,
        mesh=mesh,
        in_specs=(
            P("dp", "blk", None),
            P("dp", "blk", None),
            P("dp", "blk"),
            P("dp", "blk"),
            P("dp", "blk"),
            P(),
            P(),
            P(),
            P(),
            P(),
            P(),
            P(),
            P(),
            P(),
            P(),
            P(),
            P("dp", "blk", None),
        ),
        out_specs=(
            P("dp", "blk", None),
            P("dp", "blk", None),
            P("dp", "blk", None),
            P("blk"),
            P("blk", None),
            P("blk", None),
            P("blk", None),
            P("blk"),
            P("blk", None),
            P("blk", None),
            P("blk", None),
            P("blk"),
            P("blk", None),
            P("blk", None),
        ),
        check_vma=False,
    )
```

```python
import functools
import math

import jax
import jax.numpy as jnp
import numpy as np
from jax import lax
from jax.experimental import pallas as pl
from jax.experimental.pallas import tpu as pltpu
from jax.sharding import PartitionSpec as P

TLEN = 32
EPSILON = 1e-06
NEG_LARGE = -1e30
GROUP = 128
LOG2E = 1.4426950408889634
BF = jnp.bfloat16
F32 = jnp.float32
VMEM = pl.BlockSpec(memory_space=pltpu.VMEM)
SMEM = pl.BlockSpec(memory_space=pltpu.SMEM)
ANY = pl.BlockSpec(memory_space=pl.ANY)
HBM, STREAM, DRAIN = "hbm", "stream", "drain"
MIB = 2**20
LIMITS = dict(
    self_attention=24, self_project=14, cross_forward=34, hidden_gradient=10, feed_hidden=32, feed_weights=20,
    feed_back=16, feed_out=14, cross_backward=20, cross_query_back=14, cross_weights=34, self_backward=18,
    self_weights=28, sum_kernel=16, finish=24, shadow=1,
)


def bucket_of(distance, bucket_count):
    exact_count = bucket_count // 2
    if distance < exact_count:
        return distance
    scaled = math.log(distance / exact_count) / math.log(128.0 / exact_count) * exact_count
    return min(bucket_count - 1, exact_count + int(scaled))


def bucket_firsts(bucket_count):
    firsts = {}
    for distance in range(TLEN):
        firsts.setdefault(bucket_of(distance, bucket_count), distance)
    return sorted(firsts.items())


def dot_nn(a, b):
    return jnp.dot(a, b, preferred_element_type=F32)


def dot_nt(a, b):
    return lax.dot_general(a, b, (((1,), (1,)), ((), ())), preferred_element_type=F32)


def dot_tn(a, b):
    return lax.dot_general(a, b, (((0,), (0,)), ((), ())), preferred_element_type=F32)


def inv_rms(v):
    return lax.rsqrt(jnp.mean(v * v, axis=-1, keepdims=True) + EPSILON)


def rms_back(dy, v, gain):
    r = inv_rms(v)
    vr = v * r
    dg = dy * gain
    dv = r * (dg - vr * jnp.mean(dg * vr, axis=-1, keepdims=True))
    return dv, jnp.sum(dy * vr, axis=0, keepdims=True)


def half_masks(rows):
    lane = lax.broadcasted_iota(jnp.int32, (rows, 128), 1)
    low = (lane < 64).astype(F32)
    return low.astype(BF), (1.0 - low).astype(BF)


def chunk_place(chunk, blk, bits):
    rel = jnp.bitwise_xor(chunk, blk)
    place = jnp.int32(0)
    for bit in bits:
        place = place * 2 + jnp.where(jnp.bitwise_and(rel, bit) != 0, 1, 0)
    return place


def chunk_spot(rel, bits):
    spot = 0
    for bit in bits:
        spot = spot * 2 + (1 if rel & bit else 0)
    return spot


def query_block(rows, tokens):
    return max(GROUP, min(rows, rows * 1024 // tokens))


def big(tokens):
    return 56 if tokens > 1024 else None


class Stream:
    def __init__(self, copy, ref):
        self.copy, self.ref, self.waited = copy, ref, False

    def ready(self):
        if not self.waited:
            self.copy.wait()
            self.waited = True
        return self.ref


class Drain:
    def __init__(self, copy, ref):
        self.copy, self.ref, self.started = copy, ref, False

    def flush(self):
        self.copy.start()
        self.started = True


ORDER = []


def in_hbm(x):
    return pltpu.with_memory_space_constraint(x, pltpu.HBM)


def call(
    name, body, out_shape, in_specs, out_specs, operands, scratch=(), grid=(), prefetch=0,
    limit=None, cost=0.001,
):
    operands, in_specs = list(operands), list(in_specs)
    after = list(ORDER)
    outs = isinstance(out_shape, (tuple, list))
    out_shape = list(out_shape) if outs else [out_shape]
    out_specs = list(out_specs) if outs else [out_specs]
    streams, drains = [], []
    extra_scratch = []
    for i, spec in enumerate(in_specs):
        at = prefetch + i
        if spec == STREAM:
            streams.append(at)
            in_specs[i] = ANY
            operands[at] = in_hbm(operands[at])
            extra_scratch += [pltpu.VMEM(operands[at].shape, operands[at].dtype), pltpu.SemaphoreType.DMA]
        elif isinstance(spec, tuple):
            in_specs[i] = spec[1]
            operands[at] = in_hbm(operands[at])
    real = prefetch + len(in_specs)
    for i, spec in enumerate(out_specs):
        shape = out_shape[i]
        if spec == DRAIN:
            drains.append(i)
            out_specs[i] = ANY
            out_shape[i] = pltpu.HBM(shape.shape, shape.dtype)
            extra_scratch += [pltpu.VMEM(shape.shape, shape.dtype), pltpu.SemaphoreType.DMA]
        elif isinstance(spec, tuple):
            out_specs[i] = spec[1]
            out_shape[i] = pltpu.HBM(shape.shape, shape.dtype)

    out_specs.append(ANY)
    out_shape.append(pltpu.HBM((8, 128), F32))

    def ordered(*refs):
        ins = list(refs[:real])
        results = list(refs[real + len(after) : real + len(after) + len(out_shape) - 1])
        rest = list(refs[real + len(after) + len(out_shape) :])
        own, extra = rest[: len(scratch)], rest[len(scratch) :]
        made = []
        for n, i in enumerate(streams):
            copy = pltpu.make_async_copy(ins[i], extra[2 * n], extra[2 * n + 1])
            copy.start()
            ins[i] = Stream(copy, extra[2 * n])
            made.append(ins[i])
        for n, i in enumerate(drains, len(streams)):
            copy = pltpu.make_async_copy(extra[2 * n], results[i], extra[2 * n + 1])
            results[i] = Drain(copy, extra[2 * n])
        body(*ins, *results, *own)
        for stream in made:
            stream.ready()
        for i in drains:
            if not results[i].started:
                results[i].flush()
            results[i].copy.wait()

    got = pl.pallas_call(
        ordered,
        out_shape=tuple(out_shape),
        grid_spec=pltpu.PrefetchScalarGridSpec(
            num_scalar_prefetch=prefetch,
            grid=grid,
            in_specs=in_specs + [ANY] * len(after),
            out_specs=tuple(out_specs),
            scratch_shapes=list(scratch) + extra_scratch,
        ),
        compiler_params=pltpu.CompilerParams(vmem_limit_bytes=(limit or LIMITS[name]) * MIB),
        name=name,
        cost_estimate=pl.CostEstimate(
            flops=int(cost * 1153 * 10**6), bytes_accessed=0, transcendentals=0
        ),
    )(*operands, *after)
    ORDER[:] = [in_hbm(got[-1])]
    return tuple(got[:-1]) if outs else got[0]


def shadow(cost):
    call("shadow", lambda: None, (), (), (), (), cost=cost)


def whole(*shape):
    return pl.BlockSpec(shape, lambda *_: (0,) * len(shape))


def shape_of(dtype, *shape):
    return jax.ShapeDtypeStruct(shape, dtype)


class Columns:
    def __init__(self, names, sections, y_parts, chunks, part):
        self.names, self.y_parts, self.chunks, self.part = names, y_parts, chunks, part
        self.sections = []
        first = unit = 0
        for blocks, order in sections:
            if blocks:
                self.sections.append((first, blocks, order, unit))
            first, unit = first + blocks, unit + chunks * blocks
        self.blocks, self.units = first, unit

    def shape(self, more=0):
        return shape_of(BF, self.units + more, self.part, 128)

    def first(self, name):
        done = 0
        for other, width in self.names:
            if other == name:
                return done
            done += width // 128

    def find(self, block):
        for i, (first, blocks, order, _) in enumerate(self.sections):
            if first <= block < first + blocks:
                if order != "y":
                    return i, None, block - first
                y, k = divmod(block - first, blocks // self.y_parts)
                return i, y, k

    def store(self, ref, name, value, place_ref, chunks=None, column=0):
        chunks = range(self.chunks) if chunks is None else chunks
        start = self.first(name) + column // 128
        for n, c in enumerate(chunks):
            spots = (place_ref[3 + c], place_ref[3 + self.chunks + c])
            for j in range(value.shape[1] // 128):
                i, y, k = self.find(start + j)
                _, blocks, order, unit = self.sections[i]
                if y is None:
                    unit = unit + spots[order] * blocks + k
                else:
                    y_spot = place_ref[3 + 2 * self.chunks + y]
                    unit = unit + (y_spot * self.chunks + spots[0]) * (blocks // self.y_parts) + k
                ref[unit] = value[n * self.part : (n + 1) * self.part, j * 128 : (j + 1) * 128].astype(BF)


def self_attention(x, gain_self, w_qkv, rel_bias):
    rows, width = x.shape
    bucket_count, heads = rel_bias.shape
    pairs = heads // 2
    groups = rows // GROUP
    firsts = bucket_firsts(bucket_count)

    def body(
        x, gs_ref, wqkv, rb_ref, a1_out, qkv_out, p1_out, o1_ref, o1_out, bias
    ):
        a1_ref, qkv_ref, p1_ref = a1_out.ref, qkv_out.ref, p1_out.ref
        xf = x.ready()[...].astype(F32)
        a1 = (xf * inv_rms(xf) * gs_ref[...]).astype(BF)
        a1_ref[...] = a1
        a1_out.flush()
        qkv_ref[...] = dot_nn(a1, wqkv.ready()[...]).astype(BF)
        qkv_out.flush()
        row = lax.broadcasted_iota(jnp.int32, (GROUP, GROUP), 0)
        col = lax.broadcasted_iota(jnp.int32, (GROUP, GROUP), 1)
        distance = row - col
        allowed = jnp.logical_and(distance >= 0, row // TLEN == col // TLEN)

        def make_bias(h, carry):
            val = jnp.full((GROUP, GROUP), NEG_LARGE, F32)
            for b, first in firsts:
                val = jnp.where(distance >= first, rb_ref[h, b], val)
            bias[h] = jnp.where(allowed, val, NEG_LARGE)
            return carry

        lax.fori_loop(0, heads, make_bias, 0)
        m0, m1 = half_masks(GROUP)

        def attend(g, carry):
            at = pl.ds(pl.multiple_of(g * GROUP, GROUP), GROUP)
            for pair in range(pairs):
                lo = pair * 128
                q = qkv_ref[at, lo : lo + 128]
                k = qkv_ref[at, width + lo : width + lo + 128]
                v = qkv_ref[at, 2 * width + lo : 2 * width + lo + 128]
                s = dot_nt(jnp.concatenate([q * m0, q * m1], 0), k)
                s = s + jnp.concatenate([bias[2 * pair], bias[2 * pair + 1]], 0)
                e = jnp.exp(s - jnp.max(s, -1, keepdims=True))
                p = (e / jnp.sum(e, -1, keepdims=True)).astype(BF)
                p1_ref[g, pair] = p
                o = dot_nn(
                    jnp.concatenate([p[:GROUP], p[GROUP:]], 1),
                    jnp.concatenate([v * m0, v * m1], 0),
                )
                o1_ref[at, lo : lo + 128] = o.astype(BF)
            return carry

        lax.fori_loop(0, groups, attend, 0)
        p1_out.flush()
        o1_out.ref[...] = o1_ref[...]
        o1_out.flush()

    return call(
        "self_attention",
        body,
        (
            shape_of(BF, rows, width),
            shape_of(BF, rows, 3 * width),
            shape_of(BF, groups, pairs, 2 * GROUP, GROUP),
            shape_of(BF, rows, width),
            shape_of(BF, rows, width),
        ),
        [STREAM, VMEM, STREAM, SMEM],
        (DRAIN, DRAIN, DRAIN, VMEM, DRAIN),
        (x, gain_self.reshape(1, width), w_qkv, rel_bias.T),
        [pltpu.VMEM((heads, GROUP, GROUP), F32)],
    )


def self_project(x, o1, w_self_out, gain_cross, w_cross_q):
    rows, width = x.shape

    def body(x, o1_ref, wso, gc_ref, wcq, h1_out, a2_out, cq_out):
        h1 = dot_nn(o1_ref[...], wso.ready()[...]) + x.ready()[...].astype(F32)
        h1_out.ref[...] = h1
        h1_out.flush()
        a2 = (h1 * inv_rms(h1) * gc_ref[...]).astype(BF)
        a2_out.ref[...] = a2
        a2_out.flush()
        cq_out.ref[...] = dot_nn(a2, wcq.ready()[...]).astype(BF)

    return call(
        "self_project",
        body,
        (shape_of(F32, rows, width), shape_of(BF, rows, width), shape_of(BF, rows, width)),
        [STREAM, VMEM, STREAM, VMEM, STREAM],
        (DRAIN,) * 3,
        (x, o1, w_self_out, gain_cross.reshape(1, width), w_cross_q),
    )


def cross_forward(
    pieces, order, shard_rows, tgt_question, cq, h1, w_cross_kv, w_cross_out, gain_ff
):
    rows, width = cq.shape
    pairs = width // 128
    tokens = sum(len(o) for o in order) * shard_rows
    targets = rows // TLEN
    block_rows = query_block(rows, tokens)
    blocks = rows // block_rows
    steps = pairs * blocks

    def body(*refs):
        piece_refs = refs[: len(pieces)]
        (
            tq_ref, cq, h1, wkv, wco, gf_ref,
            enc_out, kv_out, e_ref, inv_out, o2_out, h2_out, a3_ref,
            kfeat, qfeat, ebuf, sem,
        ) = refs[len(pieces) :]
        enc_ref, kv_ref, inv_ref, o2_ref = enc_out.ref, kv_out.ref, inv_out.ref, o2_out.ref
        lane = lax.rem(lax.broadcasted_iota(jnp.int32, (shard_rows, 128), 1), 64).astype(F32)
        for ref, places in zip(piece_refs, order):
            for j, spot in enumerate(places):
                at = slice(spot * shard_rows, (spot + 1) * shard_rows)
                enc_ref[at, :] = ref[j, :shard_rows, :]
                tag = ref[j, shard_rows : shard_rows + 1, :shard_rows].astype(F32)
                tag = jnp.transpose(jnp.broadcast_to(tag, (128, shard_rows)))
                kfeat[at, :] = jnp.where(tag == lane, 0.0, NEG_LARGE).astype(BF)
        lane_t = lax.rem(lax.broadcasted_iota(jnp.int32, (TLEN, 128), 1), 64)
        for t in range(targets):
            qfeat[t * TLEN : (t + 1) * TLEN, :] = jnp.where(lane_t == tq_ref[t], 1.0, 0.0).astype(BF)
        enc_out.flush()
        kv_ref[...] = dot_nn(enc_ref[...], wkv.ready()[...]).astype(BF)
        kv_out.flush()
        cq_ref = cq.ready()
        q0, q1 = half_masks(block_rows)
        k0, k1 = half_masks(tokens)
        qmask, kmask = (q0, q1), (k0, k1)
        low = lax.broadcasted_iota(jnp.int32, (block_rows, 128), 1) < 64

        def out_copy(slot, step):
            pair, block = step // blocks, lax.rem(step, blocks)
            return pltpu.make_async_copy(
                ebuf.at[slot],
                e_ref.at[pl.ds(2 * pair, 2), pl.ds(block * block_rows, block_rows)],
                sem.at[slot],
            )

        def attend(step, carry):
            slot = lax.rem(step, 2)
            pair, block = step // blocks, lax.rem(step, blocks)
            lo = pl.multiple_of(pair * 128, 128)
            at = pl.ds(pl.multiple_of(block * block_rows, block_rows), block_rows)

            @pl.when(step >= 2)
            def _():
                out_copy(slot, step - 2).wait()

            q = cq_ref[at, pl.ds(lo, 128)]
            k = kv_ref[:, pl.ds(lo, 128)]
            v = kv_ref[:, pl.ds(width + lo, 128)]
            outs = []
            for h in range(2):
                qa = q * qmask[h] + qfeat[at, :] * qmask[1 - h]
                ka = k * kmask[h] + kfeat[...] * kmask[1 - h]
                s = dot_nt(qa, ka)
                top = jnp.max(s, -1, keepdims=True)
                e = jnp.exp(s - top).astype(BF)
                ebuf[slot, h] = e
                outs.append(dot_nn(e, v * kmask[h] + kmask[1 - h]))
            out_copy(slot, step).start()
            total = jnp.where(low, pltpu.roll(outs[0], 64, 1), pltpu.roll(outs[1], 64, 1))
            inv = 1.0 / total
            inv_ref[at, pl.ds(lo, 128)] = inv
            o2_ref[at, pl.ds(lo, 128)] = (jnp.where(low, outs[0], outs[1]) * inv).astype(BF)
            return carry

        lax.fori_loop(0, steps, attend, 0)
        inv_out.flush()
        o2_out.flush()
        h2 = h1.ready()[...] + dot_nn(o2_ref[...], wco.ready()[...])
        h2_out.ref[...] = h2
        h2_out.flush()
        a3_ref[...] = (h2 * inv_rms(h2) * gf_ref[...]).astype(BF)
        for step in range(max(0, steps - 2), steps):
            out_copy(step % 2, jnp.int32(step)).wait()

    return call(
        "cross_forward",
        body,
        (
            shape_of(BF, tokens, width),
            shape_of(BF, tokens, 2 * width),
            shape_of(BF, 2 * pairs, rows, tokens),
            shape_of(F32, rows, width),
            shape_of(BF, rows, width),
            shape_of(F32, rows, width),
            shape_of(BF, rows, width),
        ),
        [VMEM] * len(pieces) + [SMEM] + [STREAM] * 4 + [VMEM],
        (DRAIN, DRAIN, (HBM, ANY), DRAIN, DRAIN, DRAIN, VMEM),
        (*pieces, tgt_question, cq, h1, w_cross_kv, w_cross_out, gain_ff.reshape(1, width)),
        [
            pltpu.VMEM((tokens, 128), BF),
            pltpu.VMEM((rows, 128), BF),
            pltpu.VMEM((2, 2, block_rows, tokens), BF),
            pltpu.SemaphoreType.DMA((2,)),
        ],
        limit=big(tokens),
    )


def hidden_gradient(gy, w_ff_out):
    rows, width = gy.shape
    hidden = w_ff_out.shape[0]

    def body(gy_ref, w2_ref, out_ref):
        out_ref[...] = dot_nt(gy_ref[...], w2_ref[...]).astype(BF)

    return call(
        "hidden_gradient",
        body,
        shape_of(BF, rows, hidden),
        [whole(rows, width), (HBM, pl.BlockSpec((width, width), lambda s: (s, 0)))],
        (HBM, pl.BlockSpec((rows, width), lambda s: (0, s))),
        (gy, w_ff_out),
        grid=(hidden // width,),
    )


def feed_hidden(place, a3, gy, dhid, w_ff_in, columns):
    rows, width = a3.shape
    hidden = w_ff_in.shape[1]
    tile = width
    steps = hidden // tile
    half = width // 2
    sub = hidden // width
    chunks, part = columns.chunks, columns.part
    per_tile = chunks * tile // hidden
    scale = math.sqrt(2.0 / math.pi)

    def body(place_ref, a3_ref, gy_ref, dhid_ref, w1_ref, hid_ref, dpre_ref, keep_ref, send_ref):
        core = place_ref[0]
        step = pl.program_id(0)
        gyv = gy_ref[...]
        pre = dot_nn(a3_ref[...], w1_ref[...])
        sq = pre * pre
        t = jnp.tanh(scale * pre * (1.0 + 0.044715 * sq))
        hid = (0.5 * pre * (1.0 + t)).astype(BF)
        slope = 0.5 * (1.0 + t) + 0.5 * pre * (1.0 - t * t) * (scale * (1.0 + 0.134145 * sq))
        hid_ref[...] = hid
        dpre_ref[...] = (dhid_ref[...].astype(F32) * slope).astype(BF)
        g = dot_tn(hid, gyv)
        swapped = core == 1
        keep = jnp.where(swapped, g[:, half:], g[:, :half])
        send = jnp.where(swapped, g[:, :half], g[:, half:])
        for value, ref in ((keep, keep_ref), (send, send_ref)):
            for i in range(per_tile):
                for j in range(sub):
                    first = (i * sub + j) * part
                    columns.store(
                        ref, "out", value[first : first + part], place_ref,
                        [step * per_tile + i], j * half,
                    )

    tiles = pl.BlockSpec((rows, tile), lambda s, *_: (0, s))
    return call(
        "feed_hidden",
        body,
        (shape_of(BF, rows, hidden), shape_of(BF, rows, hidden), columns.shape(), columns.shape()),
        [
            whole(rows, width),
            whole(rows, width),
            (HBM, tiles),
            (HBM, pl.BlockSpec((width, tile), lambda s, *_: (0, s))),
        ],
        ((HBM, tiles), tiles) + ((HBM, whole(*columns.shape().shape)),) * 2,
        (place, a3, gy, dhid, w_ff_in),
        grid=(steps,),
        prefetch=1,
    )


def feed_weights(place, a3, dpre, columns):
    rows, width = a3.shape
    hidden = dpre.shape[1]
    tile = width
    steps = hidden // tile
    half_steps = steps // 2

    def body(place_ref, a3_ref, dpre_ref, keep_ref, send_ref):
        core = place_ref[0]
        step = pl.program_id(0)
        g = dot_tn(a3_ref[...], dpre_ref[...])
        for s in range(steps):
            for c in range(2):

                @pl.when(jnp.logical_and(step == s, core == c))
                def _():
                    ref = keep_ref if s // half_steps == c else send_ref
                    columns.store(ref, "in", g, place_ref, None, (s % half_steps) * tile)

    return call(
        "feed_weights",
        body,
        (columns.shape(), columns.shape()),
        [whole(rows, width), pl.BlockSpec((rows, tile), lambda s, *_: (0, s))],
        ((HBM, whole(*columns.shape().shape)),) * 2,
        (place, a3, dpre),
        grid=(steps,),
        prefetch=1,
    )


def feed_back(dpre, w_ff_in, h2, gain_ff, gy):
    rows, width = h2.shape
    hidden = dpre.shape[1]
    tile = width
    steps = hidden // tile

    def body(dpre_ref, w1_ref, h2_ref, gf_ref, gy_ref, dh2_ref, gain_ref, acc):
        step = pl.program_id(0)
        term = dot_nt(dpre_ref[...], w1_ref[...])

        @pl.when(step == 0)
        def _():
            acc[...] = term

        @pl.when(step > 0)
        def _():
            acc[...] += term

        @pl.when(step == steps - 1)
        def _():
            dv, dgain = rms_back(acc[...], h2_ref[...], gf_ref[...])
            dh2_ref[...] = gy_ref[...].astype(F32) + dv
            gain_ref[...] = dgain

    return call(
        "feed_back",
        body,
        (shape_of(F32, rows, width), shape_of(F32, 1, width)),
        [
            pl.BlockSpec((rows, tile), lambda s: (0, s)),
            (HBM, pl.BlockSpec((width, tile), lambda s: (0, s))),
            (HBM, whole(rows, width)),
            whole(1, width),
            whole(rows, width),
        ],
        (whole(rows, width), whole(1, width)),
        (dpre, w_ff_in, h2, gain_ff.reshape(1, width), gy),
        [pltpu.VMEM((rows, width), F32)],
        grid=(steps,),
    )


def feed_out(hid, w_ff_out, h2):
    rows, width = h2.shape
    hidden = hid.shape[1]
    steps = hidden // width

    def body(hid_ref, w2_ref, h2_ref, out_ref, acc):
        step = pl.program_id(0)
        term = dot_nn(hid_ref[...], w2_ref[...])

        @pl.when(step == 0)
        def _():
            acc[...] = h2_ref[...] + term

        @pl.when(step > 0)
        def _():
            acc[...] += term

        @pl.when(step == steps - 1)
        def _():
            out_ref[...] = acc[...].astype(BF)

    return call(
        "feed_out",
        body,
        shape_of(BF, rows, width),
        [
            (HBM, pl.BlockSpec((rows, width), lambda s: (0, s))),
            (HBM, pl.BlockSpec((width, width), lambda s: (s, 0))),
            whole(rows, width),
        ],
        whole(rows, width),
        (hid, w_ff_out, h2),
        [pltpu.VMEM((rows, width), F32)],
        grid=(steps,),
    )


def cross_backward(first_pair, last_pair, dh2, o2, inv, cq, kv, e, w_cross_out):
    rows, width = cq.shape
    pairs = width // 128
    count = last_pair - first_pair
    tokens = kv.shape[0]
    block_rows = query_block(rows, tokens)
    blocks = rows // block_rows

    def body(
        dh2_ref, wco_ref, o2_ref, inv_ref, cq_ref, k_ref, v_ref, e_ref,
        dcq_ref, dkt_ref, dvt_ref,
        do2,
    ):
        pair = pl.program_id(0)

        @pl.when(pair == 0)
        def _():
            do2v = dot_nt(dh2_ref[...].astype(BF), wco_ref[...]).astype(BF)
            for i in range(count):
                do2[i] = do2v[:, i * 128 : (i + 1) * 128]

        q0, q1 = half_masks(block_rows)
        k0, k1 = half_masks(tokens)
        qmask, kmask = (q0, q1), (k0, k1)
        lane = lax.broadcasted_iota(jnp.int32, (block_rows, 128), 1)
        low = lane < 64
        first = lax.rem(lane, 64) == 0
        second = lax.rem(lane, 64) == 1
        k, v = k_ref[...], v_ref[...]
        sums = [0.0] * 4
        for block in range(blocks):
            at = slice(block * block_rows, (block + 1) * block_rows)
            q = cq_ref[at, :]
            dof = do2[pair, at, :].astype(F32) * inv_ref[at, :]
            dob = dof.astype(BF)
            prod = dof * o2_ref[at, :].astype(F32)
            qt = jnp.transpose(q)
            dot_t = jnp.transpose(dob)
            dqs = []
            for h in range(2):
                own = low if h == 0 else jnp.logical_not(low)
                delta = -jnp.sum(jnp.where(own, prod, 0.0), -1, keepdims=True)
                hi = delta.astype(BF).astype(F32)
                feat = jnp.where(first, hi, jnp.where(second, delta - hi, 0.0)).astype(BF)
                doa = dob * qmask[h] + feat * qmask[1 - h]
                dp = dot_nt(doa, v * kmask[h] + kmask[1 - h])
                ev = e_ref[h, at, :]
                ds = (ev.astype(F32) * dp).astype(BF)
                dqs.append(dot_nn(ds, k))
                sums[h] = sums[h] + dot_nn(qt[h * 64 : (h + 1) * 64, :], ds)
                sums[2 + h] = sums[2 + h] + dot_nn(dot_t[h * 64 : (h + 1) * 64, :], ev)
            dcq_ref[at, :] = jnp.where(low, dqs[0], dqs[1]).astype(BF)
        for h in range(2):
            dkt_ref[h * 64 : (h + 1) * 64, :] = sums[h].astype(BF)
            dvt_ref[h * 64 : (h + 1) * 64, :] = sums[2 + h].astype(BF)

    def column(n, first=first_pair):
        return pl.BlockSpec((n, 128), lambda p: (0, p + first))

    return call(
        "cross_backward",
        body,
        (
            shape_of(BF, rows, count * 128),
            shape_of(BF, count * 128, tokens),
            shape_of(BF, count * 128, tokens),
        ),
        [
            whole(rows, width),
            (HBM, pl.BlockSpec((count * 128, width), lambda p: (first_pair // count, 0))),
            (HBM, column(rows)),
            (HBM, column(rows)),
            (HBM, column(rows)),
            (HBM, column(tokens)),
            (HBM, column(tokens, first_pair + pairs)),
            (HBM, pl.BlockSpec((2, rows, tokens), lambda p: (p + first_pair, 0, 0))),
        ],
        (
            column(rows, 0),
            (HBM, pl.BlockSpec((128, tokens), lambda p: (p, 0))),
            (HBM, pl.BlockSpec((128, tokens), lambda p: (p, 0))),
        ),
        (dh2, w_cross_out, o2, inv, cq, kv, kv, e),
        [pltpu.VMEM((count, rows, 128), BF)],
        grid=(count,),
        limit=big(tokens),
    )


def cross_query_back(dcq, w_cross_q, h1, gain_cross, dh2):
    rows, width = h1.shape
    n = len(dcq)
    size = width // n

    def body(*refs):
        wcq, h1, gc_ref, dh2_ref, dh1_ref, gain_ref = refs[n:]
        wcq_ref = wcq.ready()
        da2 = 0.0
        for i in range(n):
            da2 = da2 + dot_nt(refs[i][...], wcq_ref[:, i * size : (i + 1) * size])
        dv, dgain = rms_back(da2, h1.ready()[...], gc_ref[...])
        dh1_ref[...] = dh2_ref[...] + dv
        gain_ref[...] = dgain

    return call(
        "cross_query_back",
        body,
        (shape_of(F32, rows, width), shape_of(F32, 1, width)),
        [VMEM] * n + [STREAM, STREAM, VMEM, VMEM],
        (VMEM,) * 2,
        (*dcq, w_cross_q, h1, gain_cross.reshape(1, width), dh2),
    )


def cross_weights(place, dh2, o2, dcq, dkt, dvt, enc, a2, w_cross_kv, dh1, o1, columns, enc_spots):
    rows, width = dh2.shape
    tokens = enc.shape[0]
    half = width // 2
    tile = min(tokens, 1024)
    n = len(dcq)
    blocks = width // 128
    shard_rows = tokens // columns.chunks

    def body(place_ref, dh2_ref, dh1_ref, a2, o2, o1, *refs):
        core = place_ref[0]
        dcq_refs, dkt, dvt = refs[:n], refs[n : 2 * n], refs[2 * n : 3 * n]
        wkv, enc_in, genc_out, keep, send = refs[3 * n :]
        swapped = core == 1

        def store(name, g):
            size = g.shape[1] // 2
            columns.store(keep, name, jnp.where(swapped, g[:, size:], g[:, :size]), place_ref)
            columns.store(send, name, jnp.where(swapped, g[:, :size], g[:, size:]), place_ref)

        store("q", dot_tn(a2.ready()[...], jnp.concatenate([r[...] for r in dcq_refs], 1)))
        store("out", dot_tn(o2.ready()[...], dh2_ref[...].astype(BF)))
        store("self", dot_tn(o1.ready()[...], dh1_ref[...].astype(BF)))
        parts = [r.ready() for r in dkt + dvt]
        wkt = jnp.transpose(wkv.ready()[...])
        for t in range(tokens // tile):
            at = slice(t * tile, (t + 1) * tile)
            dkvt = jnp.concatenate([r[:, at] for r in parts], 0)
            genc = dot_tn(dkvt, wkt).astype(BF)
            for i in range(tile // shard_rows):
                for j in range(blocks):
                    spot = enc_spots[t * tile // shard_rows + i]
                    genc_out.ref[spot * blocks + j] = genc[
                        i * shard_rows : (i + 1) * shard_rows, j * 128 : (j + 1) * 128
                    ]
        genc_out.flush()
        enc_ref = enc_in.ready()
        g = 0.0
        for t in range(tokens // tile):
            at = slice(t * tile, (t + 1) * tile)
            dkvt = jnp.concatenate([r[:, at] for r in parts], 0)
            g = g + dot_nt(jnp.transpose(enc_ref[at, :]), dkvt)
        store("kv", g)

    return call(
        "cross_weights",
        body,
        (shape_of(BF, columns.chunks * blocks, shard_rows, 128), columns.shape(), columns.shape()),
        [SMEM, VMEM, VMEM, STREAM, STREAM, STREAM] + [VMEM] * n + [STREAM] * (2 * n + 2),
        (DRAIN, (HBM, VMEM), (HBM, VMEM)),
        (place, dh2, dh1, a2, o2, o1, *dcq, *dkt, *dvt, w_cross_kv, enc),
        limit=big(tokens),
    )


def self_backward(dh1, w_self_out, qkv, p1, bucket_count, heads):
    rows, width = dh1.shape
    pairs = heads // 2
    groups = rows // GROUP
    firsts = bucket_firsts(bucket_count)
    ends = [first for _, first in firsts[1:]] + [TLEN]

    def body(dh1_ref, wso, qkv, p1, dqkv_ref, gbias_ref, do1, acc):
        do1[...] = dot_nt(dh1_ref[...].astype(BF), wso.ready()[...]).astype(BF)
        qkv_ref, p1_ref = qkv.ready(), p1.ready()
        m0, m1 = half_masks(GROUP)
        acc[...] = jnp.zeros_like(acc)

        def attend(g, carry):
            at = pl.ds(pl.multiple_of(g * GROUP, GROUP), GROUP)
            for pair in range(pairs):
                lo = pair * 128
                q = qkv_ref[at, lo : lo + 128]
                k = qkv_ref[at, width + lo : width + lo + 128]
                v = qkv_ref[at, 2 * width + lo : 2 * width + lo + 128]
                do = do1[at, lo : lo + 128]
                do_two = jnp.concatenate([do * m0, do * m1], 0)
                pb = p1_ref[g, pair]
                pf = pb.astype(F32)
                dp = dot_nt(do_two, v)
                ds = (pf * (dp - jnp.sum(pf * dp, -1, keepdims=True))).astype(BF)
                dsf = ds.astype(F32)
                for h in range(2):
                    total = dsf[h * GROUP : h * GROUP + TLEN]
                    for t in range(1, GROUP // TLEN):
                        total = total + dsf[h * GROUP + t * TLEN : h * GROUP + (t + 1) * TLEN]
                    acc[2 * pair + h] += total
                dq = dot_nn(
                    jnp.concatenate([ds[:GROUP], ds[GROUP:]], 1),
                    jnp.concatenate([k * m0, k * m1], 0),
                )
                dk = dot_tn(ds, jnp.concatenate([q * m0, q * m1], 0))
                dv = dot_tn(pb, do_two)
                dqkv_ref[at, lo : lo + 128] = dq.astype(BF)
                dqkv_ref[at, width + lo : width + lo + 128] = dk.astype(BF)
                dqkv_ref[at, 2 * width + lo : 2 * width + lo + 128] = dv.astype(BF)
            return carry

        lax.fori_loop(0, groups, attend, 0)
        row = lax.broadcasted_iota(jnp.int32, (TLEN, GROUP), 0)
        distance = row - lax.rem(lax.broadcasted_iota(jnp.int32, (TLEN, GROUP), 1), TLEN)
        lane = lax.broadcasted_iota(jnp.int32, (16, 128), 1)
        bias = jnp.zeros((16, 128), F32)
        accv = acc[...]
        pad = jnp.zeros((16 - heads, 1), F32)
        for (b, first), end in zip(firsts, ends):
            here = jnp.logical_and(distance >= first, distance < end)
            part_sum = jnp.sum(jnp.where(here[None], accv, 0.0), axis=1)
            col = jnp.sum(part_sum, -1, keepdims=True)
            bias = jnp.where(lane == b, jnp.concatenate([col, pad], 0), bias)
        gbias_ref[...] = bias

    return call(
        "self_backward",
        body,
        (shape_of(BF, rows, 3 * width), shape_of(F32, 16, 128)),
        [VMEM, STREAM, STREAM, STREAM],
        (VMEM,) * 2,
        (dh1, w_self_out, qkv, p1),
        [pltpu.VMEM((rows, width), BF), pltpu.VMEM((heads, TLEN, GROUP), F32)],
    )


def self_weights(
    place, dh1, a1, dqkv, x, gain_self, w_qkv, gbias, gain_cross_grad, gain_ff_grad, columns
):
    rows, width = dh1.shape
    half = width // 2
    part = columns.part
    misc_rows = 16 + width // 16
    more = -(-misc_rows // part)

    def body(
        place_ref, dh1_ref, wqkv, x, a1, dqkv_ref, gs_ref, gb_ref, ggc_ref, ggf_ref,
        out, keep_ref, send_ref,
    ):
        core = place_ref[0]
        da1 = dot_nt(dqkv_ref[...], wqkv.ready()[...])
        dv, dgain = rms_back(da1, x.ready()[...].astype(F32), gs_ref[...])
        out.ref[...] = dh1_ref[...] + dv
        out.flush()
        a1_ref = a1.ready()
        for which, ref in ((1 - core, send_ref), (core, keep_ref)):
            at = pl.ds(pl.multiple_of(which * 3 * half, 128), 3 * half)
            columns.store(ref, "qkv", dot_tn(a1_ref[...], dqkv_ref[:, at]), place_ref)
        gains = jnp.concatenate([dgain, ggc_ref[...], ggf_ref[...], jnp.zeros((5, width), F32)], 0)
        misc = [gb_ref[...]] + [gains[:, j * 128 : (j + 1) * 128] for j in range(width // 128)]
        misc.append(jnp.zeros((more * part - misc_rows, 128), F32))
        misc = jnp.concatenate(misc, 0).astype(BF)
        for i in range(more):
            keep_ref[columns.units + i] = misc[i * part : (i + 1) * part]
            send_ref[columns.units + i] = misc[i * part : (i + 1) * part]

    return call(
        "self_weights",
        body,
        (shape_of(F32, rows, width), columns.shape(more), columns.shape(more)),
        [SMEM, VMEM] + [STREAM] * 3 + [VMEM] * 5,
        (DRAIN, (HBM, VMEM), (HBM, VMEM)),
        (
            place, dh1, w_qkv, x, a1, dqkv, gain_self.reshape(1, width), gbias,
            gain_cross_grad, gain_ff_grad,
        ),
    )


def swap(value, axis, bit):
    size = lax.axis_size(axis)
    return lax.ppermute(value, axis, [(i, i ^ bit) for i in range(size)])


class Bucket:
    def __init__(self, rows, terms, steps, keep_all=False):
        self.rows, self.terms, self.steps, self.keep_all = rows, terms, list(steps), keep_all


def sum_kernel(groups, dtype=BF):
    operands, specs, plan = [], [], []
    for i, jobs in enumerate(groups):
        at = 0
        for rows, terms in jobs:
            plan.append((i, at, rows, len(operands), len(terms)))
            at += rows
            for array, off in terms:
                operands.append(array)
                spec = (pl.Element(rows), pl.Element(128))
                specs.append(pl.BlockSpec(spec, functools.partial(lambda off, *_: (off, 0), off)))
    sizes = [sum(rows for rows, _ in jobs) for jobs in groups]

    def body(*refs):
        outs = refs[len(operands) :]
        for i, at, rows, first, count in plan:
            total = refs[first][...].astype(F32)
            for r in refs[first + 1 : first + count]:
                total = total + r[...].astype(F32)
            outs[i][at : at + rows, :] = total.astype(dtype)

    return call(
        "sum_kernel",
        body,
        tuple(shape_of(dtype, size, 128) for size in sizes),
        specs,
        tuple(whole(size, 128) for size in sizes),
        operands,
        grid=(1,),
    )


def send_round(cost, *members, settle=()):
    groups = {}
    for m in members:
        step = m.steps[0]
        groups.setdefault((step, m) if isinstance(m, Total) else step, []).append(m)
    jobs = []
    for group in groups.values():
        jobs.append([])
        for m in group:
            if isinstance(m, Total):
                jobs[-1] += m.next_jobs()
            elif m.keep_all:
                jobs[-1].append((m.rows, m.terms))
            else:
                m.rows //= 2
                jobs[-1].append((m.rows, [(array, off + m.rows) for array, off in m.terms]))
    settle = [b for b in settle if not b.steps]
    if settle:
        jobs.append([(b.rows, b.terms) for b in settle])
    sent = sum_kernel(jobs)
    at = 0
    for b in settle:
        b.terms = [(sent[-1], at)]
        at += b.rows
    for group, payload in zip(groups.values(), sent):
        axis, bit = group[0].steps[0]
        got = swap(payload, axis, bit)
        at = 0
        for m in group:
            m.steps.pop(0)
            if isinstance(m, Total):
                m.moved(payload, got)
                continue
            if m.keep_all:
                m.terms = [(payload, at), (got, at)]
            else:
                m.terms = m.terms + [(got, at)]
            at += m.rows
    shadow(cost)


def rest_of(*buckets):
    while any(b.steps for b in buckets):
        send_round(3, *[b for b in buckets if b.steps])


def weight_buckets(columns, keep, send, orders, y_bits):
    rows = columns.units * columns.part
    keep, send = in_hbm(keep.reshape(-1, 128)), send.reshape(-1, 128)
    got = swap(send, "dp", 1)
    over = [[("blk", b) for b in order] for order in orders]
    along = [("dp", 2 * b) for b in y_bits]
    buckets = []
    for _, blocks, order, unit in columns.sections:
        steps = along + over[0] if order == "y" else over[order]
        at = unit * columns.part
        size = blocks * columns.chunks * columns.part
        buckets.append(Bucket(size, [(keep, at), (got, at)], steps))
    if keep.shape[0] > rows:
        buckets.append(Bucket(keep.shape[0] - rows, [(keep, rows), (got, rows)], over[0], keep_all=True))
    return buckets


class Total:
    def __init__(self, groups, small, dp_size):
        self.groups, self.small, self.dp_size = groups, small, dp_size
        self.jobs, self.bases = [], []
        at = 0
        for _, buckets in groups:
            base = []
            for bucket in buckets:
                self.jobs.append((bucket.rows, bucket.terms))
                base.append(at)
                at += bucket.rows
            self.bases.append(base)
        self.small_at = []
        for bucket in small:
            self.jobs.append((bucket.rows, bucket.terms))
            self.small_at.append((at, bucket.rows))
            at += bucket.rows
        self.rows = at
        self.steps = [("dp", 2 * m) for m in range(1, dp_size // 2)] + [("dp", 1)]
        self.parts = []

    def next_jobs(self):
        if len(self.steps) > 1 or not self.parts:
            return [(self.rows, [(self.parts[0], 0)])] if self.parts else self.jobs
        jobs, self.spots, at = [], [], 0
        for (columns, _), base in zip(self.groups, self.bases):
            spots = []
            for (_, blocks, order, _), first in zip(columns.sections, base):
                if order == "y":
                    rows = blocks // columns.y_parts * columns.part
                    spots.append([at + i * rows for i in range(len(self.parts))])
                    jobs += [(rows, [(p, first)]) for p in self.parts]
                    at += rows * len(self.parts)
                else:
                    rows = blocks * columns.part
                    spots.append(at)
                    jobs.append((rows, [(p, first) for p in self.parts]))
                    at += rows
            self.spots.append(spots)
        self.small_spots = []
        for first, rows in self.small_at:
            jobs.append((rows, [(p, first) for p in self.parts]))
            self.small_spots.append((at, rows))
            at += rows
        return jobs

    def moved(self, payload, got):
        if self.steps or not self.parts:
            self.parts = self.parts + [got] if self.parts else [payload, got]
        else:
            self.own, self.other = payload, got

    def finish(self, place, arrays):
        outs = []
        for (columns, _), spots, named in zip(self.groups, self.spots, arrays):
            for name, stack in named:
                outs.append((columns, spots, name, stack, dict(columns.names)[name] // stack))
        y_parts = self.dp_size // 2

        def body(place_ref, own_ref, other_ref, *refs):
            core, y = place_ref[0], place_ref[2]
            sides = ((core, own_ref), (1 - core, other_ref))

            def put(ref, columns, half, j, at):
                row, off = divmod(j * 128, half)
                for which, src in sides:
                    lane = pl.multiple_of(which * half + off, 128)
                    ref[row * columns.part : (row + 1) * columns.part, pl.ds(lane, 128)] = src[
                        at : at + columns.part, :
                    ].astype(F32)

            for ref, (columns, spots, name, stack, half) in zip(refs, outs):
                far = []
                for j in range(stack * half // 128):
                    i, y_of, k = columns.find(columns.first(name) + j)
                    if y_of is None:
                        put(ref, columns, half, j, spots[i] + k * columns.part)
                    else:
                        far.append((j, spots[i], y_of, k))
                for y_is in range(y_parts if far else 0):

                    @pl.when(y == y_is)
                    def _():
                        for j, at, y_of, k in far:
                            put(ref, columns, half, j, at[y_is ^ y_of] + k * columns.part)

            for ref, (at, rows) in zip(refs[len(outs) :], self.small_spots):
                ref[...] = own_ref[at : at + rows, :].astype(F32)

        shapes = [shape_of(F32, stack * columns.part, 2 * half) for columns, _, _, stack, half in outs]
        shapes += [shape_of(F32, rows, 128) for _, rows in self.small_spots]
        return call(
            "finish",
            body,
            tuple(shapes),
            [SMEM, VMEM, VMEM],
            (VMEM,) * len(shapes),
            (place, self.own, self.other),
        )


def gather_encodings(own, bits):
    if len(bits) == 3:
        x, z, far = bits
        r_far, r_x = swap(own, "blk", far), swap(own, "blk", x)

        def second():
            r_z, r_zf = swap(own, "blk", z), swap(r_far, "blk", z)
            r_xf = swap(r_far, "blk", x)

            def third():
                r_xz = swap(r_z, "blk", x)
                r_xzf = swap(r_xf, "blk", z)
                arrays = [own, r_far, r_x, r_z, r_zf, r_xf, r_xz, r_xzf]
                return arrays, [[0], [far], [x], [z], [z | far], [x | far], [x | z], [x | z | far]]

            return [r_z, r_zf, r_xf], third

        return [r_far, r_x], second
    got, rel = own, [0]
    for bit in reversed(bits):
        got = jnp.concatenate([got, swap(got, "blk", bit)], 0)
        rel = rel + [r ^ bit for r in rel]
    return [], lambda: ([], lambda: ([got], [rel]))


def local(
    dec_in,
    encodings,
    enc_question,
    enc_valid,
    tgt_question,
    gain_self,
    w_qkv,
    rel_bias,
    w_self_out,
    gain_cross,
    w_cross_q,
    w_cross_kv,
    w_cross_out,
    gain_ff,
    w_ff_in,
    w_ff_out,
    grad_out,
):
    x = dec_in[0]
    gy = grad_out[0]
    rows, width = x.shape
    bucket_count, heads = rel_bias.shape
    hidden = w_ff_in.shape[1]
    half = width // 2
    chunks = lax.axis_size("blk")
    part = width // chunks
    dp_size = lax.axis_size("dp")
    shard_rows = encodings.shape[1]
    bits = [1 << i for i in range(chunks.bit_length() - 1)]
    y_bits = [1 << i for i in range(dp_size.bit_length() - 2)]
    y_parts = dp_size // 2
    blk = lax.axis_index("blk")
    dp = lax.axis_index("dp")
    orders = [bits, bits[1::-1] + bits[2:]]
    places = [chunk_place(c, blk, order) for order in orders for c in range(chunks)]
    y_places = [chunk_place(y, dp // 2, y_bits) for y in range(y_parts)]
    place = jnp.stack([lax.rem(dp, 2), blk, dp // 2, *places, *y_places]).astype(jnp.int32)

    def layout(names, *sections):
        return Columns(names, sections, y_parts, chunks, part)

    def along_y(blocks):
        return blocks // (2 * y_parts) * y_parts

    stack = hidden // width
    blocks = half // 128
    cols_out = layout([("out", stack * half)], (stack * blocks, "y"))
    cols_in = layout([("in", hidden // 2)], (stack * blocks // 2, 0), (stack * blocks // 2, 1))
    far_x, far_s = along_y(5 * blocks), along_y(3 * blocks)
    cols_x = layout(
        [("out", half), ("q", half), ("self", half), ("kv", width)], (5 * blocks - far_x, 0), (far_x, "y")
    )
    cols_s = layout([("qkv", 3 * half)], (3 * blocks - far_s, 0), (far_s, "y"))

    ORDER.clear()
    tags = jnp.where(enc_valid[0] == 1, enc_question[0], -1).astype(BF)
    tag_rows = jnp.zeros((16, width), BF).at[0, :shard_rows].set(tags)
    enc_own = jnp.concatenate([encodings[0], tag_rows], 0)[None]
    got, second = gather_encodings(enc_own, bits)
    shadow(10)
    a1, qkv, p1, o1_near, o1 = self_attention(x, gain_self, w_qkv, rel_bias)
    more, third = second()
    shadow(10)
    h1, a2, cq = self_project(x, o1_near, w_self_out, gain_cross, w_cross_q)
    pieces, rel = third()
    shadow(10)
    dhid = hidden_gradient(gy, w_ff_out)
    enc_bits = bits[1:] + bits[:1]
    enc_spots = [0] * chunks
    for r in range(chunks):
        enc_spots[chunk_spot(r, bits)] = chunk_spot(r, enc_bits)
    spots = [[int(chunk_spot(r, bits)) for r in group] for group in rel]
    enc, kv, e, inv, o2, h2, a3 = cross_forward(
        pieces, spots, shard_rows, tgt_question[0], cq, h1, w_cross_kv, w_cross_out, gain_ff
    )

    hid, dpre, keep, send = feed_hidden(place, a3, gy, dhid, w_ff_in, cols_out)
    (b_out,) = weight_buckets(cols_out, keep, send, orders, y_bits)
    shadow(30)
    keep, send = feed_weights(place, a3, dpre, cols_in)
    b_in, b_jn = weight_buckets(cols_in, keep, send, orders, y_bits)
    send_round(30, b_out)
    dh2, gain_ff_grad = feed_back(dpre, w_ff_in, h2, gain_ff, gy)
    send_round(7, b_in, b_jn)
    pairs = heads // 2
    parts_a = cross_backward(0, pairs // 2, dh2, o2, inv, cq, kv, e, w_cross_out)
    parts_b = cross_backward(pairs // 2, pairs, dh2, o2, inv, cq, kv, e, w_cross_out)
    dcq, dkt, dvt = zip(parts_a, parts_b)
    dh1, gain_cross_grad = cross_query_back(dcq, w_cross_q, h1, gain_cross, dh2)
    send_round(12, b_jn, b_in, b_out)
    genc, keep, send = cross_weights(
        place, dh2, o2, dcq, dkt, dvt, enc, a2, w_cross_kv, dh1, o1, cols_x, enc_spots
    )
    enc_rows = chunks * shard_rows * width // 128
    b_enc = Bucket(enc_rows, [(in_hbm(genc.reshape(enc_rows, 128)), 0)], [("blk", b) for b in enc_bits])
    b_xa, b_xb = weight_buckets(cols_x, keep, send, orders, y_bits)
    send_round(40, b_in, b_jn, b_enc)
    dqkv, gbias = self_backward(dh1, w_self_out, qkv, p1, bucket_count, heads)
    send_round(12, b_xa, b_xb, b_out, b_enc, settle=[b_in, b_jn])
    out = feed_out(hid, w_ff_out, h2)
    grad_dec, keep, send = self_weights(
        place, dh1, a1, dqkv, x, gain_self, w_qkv, gbias, gain_cross_grad, gain_ff_grad, cols_s
    )
    b_sa, b_sb, b_misc = weight_buckets(cols_s, keep, send, orders, y_bits)
    send_round(25, b_out, b_xa, b_xb, b_enc)
    send_round(4, b_sa, b_misc, b_sb)
    rest_of(b_out, b_in, b_jn)
    total_ff = Total([(cols_out, [b_out]), (cols_in, [b_in, b_jn])], [], dp_size)
    send_round(4, b_xa, b_xb, total_ff)
    send_round(4, b_sa, b_misc, b_sb)
    send_round(4, b_xb, b_sa, b_misc, total_ff)
    send_round(4, b_sb)
    rest_of(total_ff)
    grad_ff_out, grad_ff_in = total_ff.finish(place, [[("out", stack)], [("in", 1)]])
    rest_of(b_xa, b_xb)
    total_x = Total([(cols_x, [b_xa, b_xb])], [], dp_size)
    send_round(4, total_x)
    send_round(4, b_sb)
    rest_of(b_sa, b_sb, b_misc, b_enc)
    total_s = Total([(cols_s, [b_sa, b_sb])], [b_misc], dp_size)
    send_round(4, total_s, total_x)
    rest_of(total_s, total_x)
    grad_cross_out, grad_cross_q, grad_self_out, grad_cross_kv = total_x.finish(
        place, [[("out", 1), ("q", 1), ("self", 1), ("kv", 1)]]
    )
    grad_qkv, misc = total_s.finish(place, [[("qkv", 1)]])
    (grad_enc,) = sum_kernel([[(b_enc.rows, b_enc.terms)]], F32)
    grad_enc = grad_enc.reshape(width // 128, shard_rows, 128).transpose(1, 0, 2).reshape(shard_rows, width)
    gains = misc[16 : 16 + width // 16].reshape(width // 128, 8, 128)[:, :3].transpose(1, 0, 2).reshape(3, width)
    gains = lax.dynamic_slice(gains, (0, blk * part), (3, part))
    bias_part = bucket_count // chunks
    grad_bias = lax.dynamic_slice(misc, (0, blk * bias_part), (heads, bias_part)).T
    return (
        out[None],
        grad_dec[None],
        grad_enc[None],
        gains[0],
        grad_qkv,
        grad_bias,
        grad_self_out,
        gains[1],
        grad_cross_q,
        grad_cross_kv,
        grad_cross_out,
        gains[2],
        grad_ff_in,
        grad_ff_out,
    )


def solution(mesh):
    return jax.shard_map(
        local,
        mesh=mesh,
        in_specs=(
            P("dp", "blk", None),
            P("dp", "blk", None),
            P("dp", "blk"),
            P("dp", "blk"),
            P("dp", "blk"),
            P(),
            P(),
            P(),
            P(),
            P(),
            P(),
            P(),
            P(),
            P(),
            P(),
            P(),
            P("dp", "blk", None),
        ),
        out_specs=(
            P("dp", "blk", None),
            P("dp", "blk", None),
            P("dp", "blk", None),
            P("blk"),
            P("blk", None),
            P("blk", None),
            P("blk", None),
            P("blk"),
            P("blk", None),
            P("blk", None),
            P("blk", None),
            P("blk"),
            P("blk", None),
            P("blk", None),
        ),
        check_vma=False,
    )
```

```python
import functools
import math

import jax
import jax.numpy as jnp
import numpy as np
from jax import lax
from jax.experimental import pallas as pl
from jax.experimental.pallas import tpu as pltpu
from jax.sharding import PartitionSpec as P

TLEN = 32
EPSILON = 1e-06
NEG_LARGE = -1e30
GROUP = 128
LOG2E = 1.4426950408889634
BF = jnp.bfloat16
F32 = jnp.float32
VMEM = pl.BlockSpec(memory_space=pltpu.VMEM)
SMEM = pl.BlockSpec(memory_space=pltpu.SMEM)
ANY = pl.BlockSpec(memory_space=pl.ANY)
HBM, STREAM, DRAIN, NEAR, PAIR = "hbm", "stream", "drain", "near", "pair"
MIB = 2**20
LIMITS = dict(
    self_attention=24, self_project=12, cross_forward=30, hidden_gradient=10, feed_hidden=26, feed_weights=18,
    feed_back=12, feed_out=12, cross_backward=20, cross_query_back=12, cross_weights=34, self_backward=14,
    self_weights=24, sum_kernel=16, finish=24, shadow=1, join_encodings=8,
)


def bucket_of(distance, bucket_count):
    exact_count = bucket_count // 2
    if distance < exact_count:
        return distance
    scaled = math.log(distance / exact_count) / math.log(128.0 / exact_count) * exact_count
    return min(bucket_count - 1, exact_count + int(scaled))


def bucket_firsts(bucket_count):
    firsts = {}
    for distance in range(TLEN):
        firsts.setdefault(bucket_of(distance, bucket_count), distance)
    return sorted(firsts.items())


def dot_nn(a, b):
    return jnp.dot(a, b, preferred_element_type=F32)


def dot_nt(a, b):
    return lax.dot_general(a, b, (((1,), (1,)), ((), ())), preferred_element_type=F32)


def dot_tn(a, b):
    return lax.dot_general(a, b, (((0,), (0,)), ((), ())), preferred_element_type=F32)


def inv_rms(v):
    return lax.rsqrt(jnp.mean(v * v, axis=-1, keepdims=True) + EPSILON)


def rms_back(dy, v, gain):
    r = inv_rms(v)
    vr = v * r
    dg = dy * gain
    dv = r * (dg - vr * jnp.mean(dg * vr, axis=-1, keepdims=True))
    return dv, jnp.sum(dy * vr, axis=0, keepdims=True)


def half_masks(rows):
    lane = lax.broadcasted_iota(jnp.int32, (rows, 128), 1)
    low = (lane < 64).astype(F32)
    return low.astype(BF), (1.0 - low).astype(BF)


def chunk_place(chunk, blk, bits):
    rel = jnp.bitwise_xor(chunk, blk)
    place = jnp.int32(0)
    for bit in bits:
        place = place * 2 + jnp.where(jnp.bitwise_and(rel, bit) != 0, 1, 0)
    return place


def chunk_spot(rel, bits):
    spot = 0
    for bit in bits:
        spot = spot * 2 + (1 if rel & bit else 0)
    return spot


def query_block(rows, tokens):
    return max(GROUP, min(rows, rows * 1024 // tokens))


def big(tokens):
    return 61 if tokens > 1024 else None


class Stream:
    def __init__(self, copy, ref):
        self.copy, self.ref, self.waited = copy, ref, False

    def ready(self):
        if not self.waited:
            self.copy.wait()
            self.waited = True
        return self.ref


class Drain:
    def __init__(self, copy, ref):
        self.copy, self.ref, self.started = copy, ref, False

    def flush(self):
        self.copy.start()
        self.started = True


ORDER = []
ROOMY = [True]


class Pair:
    def __init__(self, drains, ref):
        self.drains, self.ref = drains, ref


def in_hbm(x):
    return pltpu.with_memory_space_constraint(x, pltpu.HBM)


def call(
    name, body, out_shape, in_specs, out_specs, operands, scratch=(), grid=(), prefetch=0,
    limit=None, cost=0.001, ahead=(),
):
    operands, in_specs = list(operands), list(in_specs)
    after = list(ORDER)
    wanted = ahead
    ahead = wanted if ROOMY[0] else ()
    outs = isinstance(out_shape, (tuple, list))
    out_shape = list(out_shape) if outs else [out_shape]
    out_specs = list(out_specs) if outs else [out_specs]
    streams, drains, pairs = [], [], []
    extra_scratch = []
    for i, spec in enumerate(in_specs):
        at = prefetch + i
        if spec == STREAM:
            streams.append(at)
            in_specs[i] = ANY
            operands[at] = in_hbm(operands[at])
            extra_scratch += [pltpu.VMEM(operands[at].shape, operands[at].dtype), pltpu.SemaphoreType.DMA]
        elif isinstance(spec, tuple):
            in_specs[i] = spec[1]
            operands[at] = in_hbm(operands[at])
    real = prefetch + len(in_specs)
    for i, spec in enumerate(out_specs):
        shape = out_shape[i]
        if spec == PAIR:
            pairs.append(i)
            out_specs[i] = ANY
            out_shape[i] = pltpu.HBM(shape.shape, shape.dtype)
            if len(pairs) % 2:
                extra_scratch += [
                    pltpu.VMEM((2, *shape.shape), shape.dtype), pltpu.SemaphoreType.DMA((2,))
                ]
        elif spec == DRAIN:
            drains.append(i)
            out_specs[i] = ANY
            out_shape[i] = pltpu.HBM(shape.shape, shape.dtype)
            extra_scratch += [pltpu.VMEM(shape.shape, shape.dtype), pltpu.SemaphoreType.DMA]
        elif spec == NEAR or isinstance(spec, tuple):
            space = pltpu.VMEM if spec == NEAR or spec[0] == NEAR else pltpu.HBM
            out_specs[i] = VMEM if spec == NEAR else spec[1]
            if ROOMY[0] or space is pltpu.HBM:
                out_shape[i] = space(shape.shape, shape.dtype)
    count = len(out_shape)
    for array in ahead:
        out_specs.append(VMEM if not grid else ANY)
        out_shape.append(pltpu.VMEM(array.shape, array.dtype))
    if ahead:
        extra_scratch.append(pltpu.SemaphoreType.DMA((len(ahead),)))
    after = [in_hbm(array) for array in ahead] + after
    out_specs.append(ANY)
    out_shape.append(pltpu.HBM((8, 128), F32))

    def ordered(*refs):
        ins = list(refs[:real])
        results = list(refs[real + len(after) : real + len(after) + len(out_shape) - 1])
        rest = list(refs[real + len(after) + len(out_shape) :])
        early = [
            pltpu.make_async_copy(refs[real + i], results[count + i], rest[-1].at[i])
            for i in range(len(ahead))
        ]
        del results[count:]
        own, extra = rest[: len(scratch)], rest[len(scratch) :]
        made, ends = [], []
        for n, i in enumerate(streams):
            copy = pltpu.make_async_copy(ins[i], extra[2 * n], extra[2 * n + 1])
            copy.start()
            ins[i] = Stream(copy, extra[2 * n])
            made.append(ins[i])
        extra = extra[2 * len(streams) :]
        for i in sorted(drains + pairs[::2]):
            held, sem = extra[:2]
            extra = extra[2:]
            if i in drains:
                results[i] = Drain(pltpu.make_async_copy(held, results[i], sem), held)
                ends.append(results[i])
            else:
                copies = [
                    pltpu.make_async_copy(held.at[k], results[i + k], sem.at[k]) for k in range(2)
                ]
                results[i] = Pair([Drain(copy, held) for copy in copies], held)
                ends += results[i].drains
        for i in reversed(pairs[1::2]):
            del results[i]
        for n, copy in enumerate(early):
            if grid:
                pl.when(pl.program_id(0) == 0)(copy.start)
            else:
                copy.start()
        body(*ins, *results, *own)
        for copy in early:
            if grid:
                pl.when(pl.program_id(0) == grid[0] - 1)(copy.wait)
            else:
                copy.wait()
        for stream in made:
            stream.ready()
        for end in ends:
            if not end.started:
                end.flush()
        for end in ends:
            end.copy.wait()

    got = pl.pallas_call(
        ordered,
        out_shape=tuple(out_shape),
        grid_spec=pltpu.PrefetchScalarGridSpec(
            num_scalar_prefetch=prefetch,
            grid=grid,
            in_specs=in_specs + [ANY] * len(after),
            out_specs=tuple(out_specs),
            scratch_shapes=list(scratch) + extra_scratch,
        ),
        compiler_params=pltpu.CompilerParams(vmem_limit_bytes=(limit or LIMITS[name]) * MIB),
        name=name,
        cost_estimate=pl.CostEstimate(
            flops=int(cost * 1153 * 10**6), bytes_accessed=0, transcendentals=0
        ),
    )(*operands, *after)
    ORDER[:] = [in_hbm(got[-1])]
    got = (*got[:count], *(got[count:-1] if ahead else wanted))
    return got if outs or wanted else got[0]


def shadow(cost):
    call("shadow", lambda: None, (), (), (), (), cost=cost)


def whole(*shape):
    return pl.BlockSpec(shape, lambda *_: (0,) * len(shape))


def shape_of(dtype, *shape):
    return jax.ShapeDtypeStruct(shape, dtype)


class Columns:
    def __init__(self, names, sections, y_parts, chunks, part):
        self.names, self.y_parts, self.chunks, self.part = names, y_parts, chunks, part
        self.sections = []
        first = unit = 0
        for blocks, order in sections:
            if blocks:
                self.sections.append((first, blocks, order, unit))
            first, unit = first + blocks, unit + chunks * blocks
        self.blocks, self.units = first, unit

    def shape(self, more=0):
        return shape_of(BF, self.units + more, self.part, 128)

    def first(self, name):
        done = 0
        for other, width in self.names:
            if other == name:
                return done
            done += width // 128

    def find(self, block):
        for i, (first, blocks, order, _) in enumerate(self.sections):
            if first <= block < first + blocks:
                if order != "y":
                    return i, None, block - first
                y, k = divmod(block - first, blocks // self.y_parts)
                return i, y, k

    def table(self, spots, y_spots):
        units = []
        for c in range(self.chunks):
            for block in range(self.blocks):
                i, y, k = self.find(block)
                _, blocks, order, unit = self.sections[i]
                if y is None:
                    units.append(unit + spots[order][c] * blocks + k)
                else:
                    units.append(unit + (y_spots[y] * self.chunks + spots[0][c]) * (blocks // self.y_parts) + k)
        return units

    def store(self, ref, half, name, value, place_ref, chunks=None, block=0):
        chunks = range(self.chunks) if chunks is None else chunks
        start = self.first(name) + block
        slot = jnp.bitwise_xor(place_ref[0], half)
        for n, c in enumerate(chunks):
            for j in range(value.shape[1] // 128):
                unit = place_ref[self.at + c * self.blocks + start + j]
                ref[slot, unit] = value[n * self.part : (n + 1) * self.part, j * 128 : (j + 1) * 128].astype(BF)


def self_attention(x, gain_self, w_qkv, rel_bias, ahead):
    rows, width = x.shape
    bucket_count, heads = rel_bias.shape
    pairs = heads // 2
    groups = rows // GROUP
    firsts = bucket_firsts(bucket_count)

    def body(
        x, gs_ref, wqkv, rb_ref, a1_out, qkv_out, p1_out, o1_ref, o1_out, bias
    ):
        a1_ref, qkv_ref, p1_ref = a1_out.ref, qkv_out.ref, p1_out.ref
        xf = x.ready()[...].astype(F32)
        a1 = (xf * inv_rms(xf) * gs_ref[...]).astype(BF)
        a1_ref[...] = a1
        a1_out.flush()
        wqkv_ref = wqkv.ready()

        def project(t, carry):
            at = pl.ds(pl.multiple_of(t * width, 128), width)
            qkv_ref[:, at] = dot_nn(a1_ref[...], wqkv_ref[:, at]).astype(BF)
            return carry

        lax.fori_loop(0, 3, project, 0)
        qkv_out.flush()
        row = lax.broadcasted_iota(jnp.int32, (GROUP, GROUP), 0)
        col = lax.broadcasted_iota(jnp.int32, (GROUP, GROUP), 1)
        distance = row - col
        allowed = jnp.logical_and(distance >= 0, row // TLEN == col // TLEN)

        def make_bias(h, carry):
            val = jnp.full((GROUP, GROUP), NEG_LARGE, F32)
            for b, first in firsts:
                val = jnp.where(distance >= first, rb_ref[h, b], val)
            bias[h] = jnp.where(allowed, val, NEG_LARGE)
            return carry

        lax.fori_loop(0, heads, make_bias, 0)
        m0, m1 = half_masks(GROUP)

        def attend(g, carry):
            at = pl.ds(pl.multiple_of(g * GROUP, GROUP), GROUP)
            for pair in range(pairs):
                lo = pair * 128
                q = qkv_ref[at, lo : lo + 128]
                k = qkv_ref[at, width + lo : width + lo + 128]
                v = qkv_ref[at, 2 * width + lo : 2 * width + lo + 128]
                s = dot_nt(jnp.concatenate([q * m0, q * m1], 0), k)
                s = s + jnp.concatenate([bias[2 * pair], bias[2 * pair + 1]], 0)
                e = jnp.exp(s - jnp.max(s, -1, keepdims=True))
                p = (e / jnp.sum(e, -1, keepdims=True)).astype(BF)
                p1_ref[g, pair] = p
                o = dot_nn(
                    jnp.concatenate([p[:GROUP], p[GROUP:]], 1),
                    jnp.concatenate([v * m0, v * m1], 0),
                )
                o1_ref[at, lo : lo + 128] = o.astype(BF)
            return carry

        lax.fori_loop(0, groups, attend, 0)
        p1_out.flush()
        o1_out.ref[...] = o1_ref[...]
        o1_out.flush()

    return call(
        "self_attention",
        body,
        (
            shape_of(BF, rows, width),
            shape_of(BF, rows, 3 * width),
            shape_of(BF, groups, pairs, 2 * GROUP, GROUP),
            shape_of(BF, rows, width),
            shape_of(BF, rows, width),
        ),
        [STREAM, VMEM, STREAM, SMEM],
        (DRAIN, DRAIN, DRAIN, NEAR, DRAIN),
        (x, gain_self.reshape(1, width), w_qkv, rel_bias.T),
        ahead=ahead,
        scratch=[pltpu.VMEM((heads, GROUP, GROUP), F32)],
    )


def self_project(x, o1, w_self_out, gain_cross, w_cross_q, ahead):
    rows, width = x.shape

    def body(x_ref, o1_ref, wso_ref, gc_ref, wcq_ref, h1_ref, cq_ref, h1_out, a2_out, cq_out):
        h1 = dot_nn(o1_ref[...], wso_ref[...]) + x_ref[...].astype(F32)
        h1_ref[...] = h1
        h1_out.ref[...] = h1
        h1_out.flush()
        a2 = (h1 * inv_rms(h1) * gc_ref[...]).astype(BF)
        a2_out.ref[...] = a2
        a2_out.flush()
        cq = dot_nn(a2, wcq_ref[...]).astype(BF)
        cq_ref[...] = cq
        cq_out.ref[...] = cq

    low, full = shape_of(BF, rows, width), shape_of(F32, rows, width)
    return call(
        "self_project",
        body,
        (full, low, full, low, low),
        [VMEM] * 5,
        (NEAR, NEAR, DRAIN, DRAIN, DRAIN),
        (x, o1, w_self_out, gain_cross.reshape(1, width), w_cross_q),
        ahead=ahead,
    )


def cross_forward(
    pieces, order, shard_rows, tgt_question, cq, h1, w_cross_kv, w_cross_out, gain_ff, ahead
):
    rows, width = cq.shape
    pairs = width // 128
    tokens = sum(len(o) for o in order) * shard_rows
    targets = rows // TLEN
    block_rows = query_block(rows, tokens)
    blocks = rows // block_rows
    steps = pairs * blocks

    def body(*refs):
        piece_refs = refs[: len(pieces)]
        (
            tq_ref, cq_ref, h1_ref, wkv_ref, wco_ref, gf_ref,
            enc_out, kv_out, e_ref, inv_out, o2_out, h2_out, a3_ref,
            kfeat, qfeat, ebuf, sem,
        ) = refs[len(pieces) :]
        enc_ref, kv_ref, inv_ref, o2_ref = enc_out.ref, kv_out.ref, inv_out.ref, o2_out.ref
        lane = lax.rem(lax.broadcasted_iota(jnp.int32, (shard_rows, 128), 1), 64).astype(F32)
        for ref, places in zip(piece_refs, order):
            for j, spot in enumerate(places):
                at = slice(spot * shard_rows, (spot + 1) * shard_rows)
                enc_ref[at, :] = ref[j, :shard_rows, :]
                tag = ref[j, shard_rows : shard_rows + 1, :shard_rows].astype(F32)
                tag = jnp.transpose(jnp.broadcast_to(tag, (128, shard_rows)))
                kfeat[at, :] = jnp.where(tag == lane, 0.0, NEG_LARGE).astype(BF)
        lane_t = lax.rem(lax.broadcasted_iota(jnp.int32, (TLEN, 128), 1), 64)
        for t in range(targets):
            qfeat[t * TLEN : (t + 1) * TLEN, :] = jnp.where(lane_t == tq_ref[t], 1.0, 0.0).astype(BF)
        enc_out.flush()

        def project(t, carry):
            at = pl.ds(pl.multiple_of(t * 384, 128), 384)
            kv_ref[:, at] = dot_nn(enc_ref[...], wkv_ref[:, at]).astype(BF)
            return carry

        lax.fori_loop(0, 2 * width // 384, project, 0)
        kv_out.flush()
        q0, q1 = half_masks(block_rows)
        k0, k1 = half_masks(tokens)
        qmask, kmask = (q0, q1), (k0, k1)
        low = lax.broadcasted_iota(jnp.int32, (block_rows, 128), 1) < 64

        def out_copy(slot, step):
            pair, block = step // blocks, lax.rem(step, blocks)
            return pltpu.make_async_copy(
                ebuf.at[slot],
                e_ref.at[pl.ds(2 * pair, 2), pl.ds(block * block_rows, block_rows)],
                sem.at[slot],
            )

        def attend(step, carry):
            slot = lax.rem(step, 2)
            pair, block = step // blocks, lax.rem(step, blocks)
            lo = pl.multiple_of(pair * 128, 128)
            at = pl.ds(pl.multiple_of(block * block_rows, block_rows), block_rows)

            @pl.when(step >= 2)
            def _():
                out_copy(slot, step - 2).wait()

            q = cq_ref[at, pl.ds(lo, 128)]
            k = kv_ref[:, pl.ds(lo, 128)]
            v = kv_ref[:, pl.ds(width + lo, 128)]
            outs = []
            for h in range(2):
                qa = q * qmask[h] + qfeat[at, :] * qmask[1 - h]
                ka = k * kmask[h] + kfeat[...] * kmask[1 - h]
                s = dot_nt(qa, ka)
                top = jnp.max(s, -1, keepdims=True)
                e = jnp.exp(s - top).astype(BF)
                ebuf[slot, h] = e
                outs.append(dot_nn(e, v * kmask[h] + kmask[1 - h]))
            out_copy(slot, step).start()
            total = jnp.where(low, pltpu.roll(outs[0], 64, 1), pltpu.roll(outs[1], 64, 1))
            inv = 1.0 / total
            inv_ref[at, pl.ds(lo, 128)] = inv
            o2_ref[at, pl.ds(lo, 128)] = (jnp.where(low, outs[0], outs[1]) * inv).astype(BF)
            return carry

        lax.fori_loop(0, steps, attend, 0)
        inv_out.flush()
        o2_out.flush()
        h2 = h1_ref[...] + dot_nn(o2_ref[...], wco_ref[...])
        h2_out.ref[...] = h2
        h2_out.flush()
        a3_ref[...] = (h2 * inv_rms(h2) * gf_ref[...]).astype(BF)
        for step in range(max(0, steps - 2), steps):
            out_copy(step % 2, jnp.int32(step)).wait()

    return call(
        "cross_forward",
        body,
        (
            shape_of(BF, tokens, width),
            shape_of(BF, tokens, 2 * width),
            shape_of(BF, 2 * pairs, rows, tokens),
            shape_of(F32, rows, width),
            shape_of(BF, rows, width),
            shape_of(F32, rows, width),
            shape_of(BF, rows, width),
        ),
        [VMEM] * len(pieces) + [SMEM] + [VMEM] * 5,
        (DRAIN, DRAIN, (HBM, ANY), DRAIN, DRAIN, DRAIN, NEAR),
        (*pieces, tgt_question, cq, h1, w_cross_kv, w_cross_out, gain_ff.reshape(1, width)),
        scratch=[
            pltpu.VMEM((tokens, 128), BF),
            pltpu.VMEM((rows, 128), BF),
            pltpu.VMEM((2, 2, block_rows, tokens), BF),
            pltpu.SemaphoreType.DMA((2,)),
        ],
        limit=big(tokens),
        ahead=ahead,
    )


def hidden_gradient(gy, w_ff_out, ahead):
    rows, width = gy.shape
    hidden = w_ff_out.shape[0]

    def body(gy_ref, w2_ref, out_ref):
        def tile(t, carry):
            at = pl.ds(pl.multiple_of(t * width, 128), width)
            out_ref[:, at] = dot_nt(gy_ref[...], w2_ref[at, :]).astype(BF)
            return carry

        lax.fori_loop(0, hidden // width, tile, 0)

    return call(
        "hidden_gradient",
        body,
        shape_of(BF, rows, hidden),
        [VMEM, VMEM],
        NEAR,
        (gy, w_ff_out),
        ahead=ahead,
    )


def feed_hidden(place, a3, gy, dhid, w_ff_in, columns):
    rows, width = a3.shape
    hidden = w_ff_in.shape[1]
    tile = width
    half = width // 2
    sub = hidden // width
    part = columns.part
    per_tile = columns.chunks * tile // hidden
    scale = math.sqrt(2.0 / math.pi)

    def body(place_ref, a3_ref, gy_ref, dhid_ref, w1_ref, dpre_ref, hid_out, both):
        def one(step, carry):
            at = pl.ds(pl.multiple_of(step * tile, 128), tile)
            pre = dot_nn(a3_ref[...], w1_ref[:, at])
            sq = pre * pre
            t = jnp.tanh(pre * (scale + (scale * 0.044715) * sq))
            up = 0.5 + 0.5 * t
            hid = (pre * up).astype(BF)
            slope = up + pre * (up - up * up) * ((2.0 * scale) + (2.0 * scale * 0.134145) * sq)
            hid_out.ref[:, at] = hid
            dpre_ref[:, at] = (dhid_ref[:, at].astype(F32) * slope).astype(BF)
            g = dot_tn(hid, gy_ref[...])
            for h in range(2):
                for i in range(per_tile):
                    for j in range(sub):
                        first = (i * sub + j) * part
                        columns.store(
                            both.ref, h, "out", g[first : first + part, h * half : (h + 1) * half],
                            place_ref, [step * per_tile + i], j * half // 128,
                        )
            return carry

        lax.fori_loop(0, hidden // tile, one, 0)

    return call(
        "feed_hidden",
        body,
        (shape_of(BF, rows, hidden), shape_of(BF, rows, hidden), columns.shape(), columns.shape()),
        [SMEM, VMEM, VMEM, VMEM, VMEM],
        (NEAR, DRAIN, PAIR, PAIR),
        (place, a3, gy, dhid, w_ff_in),
    )


def feed_weights(place, a3, dpre, columns, ahead):
    width = a3.shape[1]
    hidden = dpre.shape[1]

    def body(place_ref, a3_ref, dpre_ref, both):
        tiles = hidden // width

        def one(t, carry):
            at = pl.ds(pl.multiple_of(t * width, 128), width)
            g = dot_tn(a3_ref[...], dpre_ref[:, at])
            block = lax.rem(t, tiles // 2) * (width // 128)
            columns.store(both.ref, t // (tiles // 2), "in", g, place_ref, None, block)
            return carry

        lax.fori_loop(0, tiles, one, 0)

    return call(
        "feed_weights",
        body,
        (columns.shape(), columns.shape()),
        [SMEM, VMEM, VMEM],
        (PAIR, PAIR),
        (place, a3, dpre),
        ahead=ahead,
    )


def feed_back(dpre, w_ff_in, h2, gain_ff, gy):
    rows, width = h2.shape

    def body(dpre_ref, w1_ref, h2_ref, gf_ref, gy_ref, dh2_ref, gain_ref, da3):
        da3[...] = jnp.zeros_like(da3)

        def one(t, carry):
            at = pl.ds(pl.multiple_of(t * width, 128), width)
            da3[...] += dot_nt(dpre_ref[:, at], w1_ref[:, at])
            return carry

        lax.fori_loop(0, dpre_ref.shape[1] // width, one, 0)
        dv, dgain = rms_back(da3[...], h2_ref[...], gf_ref[...])
        dh2_ref[...] = gy_ref[...].astype(F32) + dv
        gain_ref[...] = dgain

    return call(
        "feed_back",
        body,
        (shape_of(F32, rows, width), shape_of(F32, 1, width)),
        [VMEM] * 5,
        (NEAR, VMEM),
        (dpre, w_ff_in, h2, gain_ff.reshape(1, width), gy),
        scratch=[pltpu.VMEM((rows, width), F32)],
    )


def feed_out(hid, w_ff_out, h2, ahead):
    rows, width = h2.shape

    def body(hid_ref, w2_ref, h2_ref, out, total):
        total[...] = h2_ref[...]

        def one(t, carry):
            at = pl.ds(pl.multiple_of(t * width, 128), width)
            total[...] += dot_nn(hid_ref[:, at], w2_ref[at, :])
            return carry

        lax.fori_loop(0, hid_ref.shape[1] // width, one, 0)
        out.ref[...] = total[...].astype(BF)

    return call(
        "feed_out",
        body,
        (shape_of(BF, rows, width),),
        [VMEM] * 3,
        (DRAIN,),
        (hid, w_ff_out, h2),
        scratch=[pltpu.VMEM((rows, width), F32)],
        ahead=ahead,
    )


def cross_backward(first_pair, last_pair, dh2, o2, inv, cq, kv, e, w_cross_out, ahead):
    rows, width = cq.shape
    pairs = width // 128
    count = last_pair - first_pair
    tokens = kv.shape[0]
    block_rows = query_block(rows, tokens)
    blocks = rows // block_rows

    def body(
        dh2_ref, wco_ref, o2_ref, inv_ref, cq_ref, k_ref, v_ref, e_ref,
        dcq_ref, dkt_ref, dvt_ref,
        do2,
    ):
        pair = pl.program_id(0)

        @pl.when(pair == 0)
        def _():
            do2v = dot_nt(dh2_ref[...].astype(BF), wco_ref[...]).astype(BF)
            for i in range(count):
                do2[i] = do2v[:, i * 128 : (i + 1) * 128]

        q0, q1 = half_masks(block_rows)
        k0, k1 = half_masks(tokens)
        qmask, kmask = (q0, q1), (k0, k1)
        lane = lax.broadcasted_iota(jnp.int32, (block_rows, 128), 1)
        low = lane < 64
        first = lax.rem(lane, 64) == 0
        second = lax.rem(lane, 64) == 1
        k, v = k_ref[...], v_ref[...]
        sums = [0.0] * 4
        for block in range(blocks):
            at = slice(block * block_rows, (block + 1) * block_rows)
            q = cq_ref[at, :]
            dof = do2[pair, at, :].astype(F32) * inv_ref[at, :]
            dob = dof.astype(BF)
            prod = dof * o2_ref[at, :].astype(F32)
            qt = jnp.transpose(q)
            dot_t = jnp.transpose(dob)
            dqs = []
            for h in range(2):
                own = low if h == 0 else jnp.logical_not(low)
                delta = -jnp.sum(jnp.where(own, prod, 0.0), -1, keepdims=True)
                hi = delta.astype(BF).astype(F32)
                feat = jnp.where(first, hi, jnp.where(second, delta - hi, 0.0)).astype(BF)
                doa = dob * qmask[h] + feat * qmask[1 - h]
                dp = dot_nt(doa, v * kmask[h] + kmask[1 - h])
                ev = e_ref[h, at, :]
                ds = (ev.astype(F32) * dp).astype(BF)
                dqs.append(dot_nn(ds, k))
                sums[h] = sums[h] + dot_nn(qt[h * 64 : (h + 1) * 64, :], ds)
                sums[2 + h] = sums[2 + h] + dot_nn(dot_t[h * 64 : (h + 1) * 64, :], ev)
            dcq_ref[at, :] = jnp.where(low, dqs[0], dqs[1]).astype(BF)
        for h in range(2):
            dkt_ref[h * 64 : (h + 1) * 64, :] = sums[h].astype(BF)
            dvt_ref[h * 64 : (h + 1) * 64, :] = sums[2 + h].astype(BF)

    near = HBM if big(tokens) else NEAR

    def column(n, first=first_pair):
        return pl.BlockSpec((n, 128), lambda p: (0, p + first))

    return call(
        "cross_backward",
        body,
        (
            shape_of(BF, rows, count * 128),
            shape_of(BF, count * 128, tokens),
            shape_of(BF, count * 128, tokens),
        ),
        [
            whole(rows, width),
            pl.BlockSpec((count * 128, width), lambda p: (first_pair // count, 0)),
            (HBM, column(rows)),
            (HBM, column(rows)),
            (HBM, column(rows)),
            (HBM, column(tokens)),
            (HBM, column(tokens, first_pair + pairs)),
            (HBM, pl.BlockSpec((2, rows, tokens), lambda p: (p + first_pair, 0, 0))),
        ],
        (
            (NEAR, column(rows, 0)),
            (near, pl.BlockSpec((128, tokens), lambda p: (p, 0))),
            (near, pl.BlockSpec((128, tokens), lambda p: (p, 0))),
        ),
        (dh2, w_cross_out, o2, inv, cq, kv, kv, e),
        scratch=[pltpu.VMEM((count, rows, 128), BF)],
        grid=(count,),
        ahead=ahead,
        limit=big(tokens),
    )


def cross_query_back(dcq, w_cross_q, h1, gain_cross, dh2):
    rows, width = h1.shape
    n = len(dcq)
    size = width // n

    def body(*refs):
        wcq_ref, h1_ref, gc_ref, dh2_ref, dh1_ref, gain_ref = refs[n:]
        da2 = 0.0
        for i in range(n):
            da2 = da2 + dot_nt(refs[i][...], wcq_ref[:, i * size : (i + 1) * size])
        dv, dgain = rms_back(da2, h1_ref[...], gc_ref[...])
        dh1_ref[...] = dh2_ref[...] + dv
        gain_ref[...] = dgain

    return call(
        "cross_query_back",
        body,
        (shape_of(F32, rows, width), shape_of(F32, 1, width)),
        [VMEM] * (n + 4),
        (NEAR, VMEM),
        (*dcq, w_cross_q, h1, gain_cross.reshape(1, width), dh2),
    )


def shard_rows_of(tokens, chunks):
    return tokens // chunks


def cross_weights(place, dh2, o2, dcq, dkt, dvt, enc, a2, w_cross_kv, dh1, o1, columns, ahead):
    rows, width = dh2.shape
    tokens = enc.shape[0]
    half = width // 2
    tile = max(shard_rows_of(tokens, columns.chunks), 512)
    n = len(dcq)
    size = width // n
    blocks = width // 128
    shard_rows = tokens // columns.chunks

    def body(place_ref, dh2_ref, dh1_ref, a2_ref, o2_ref, o1_ref, *refs):
        dcq_refs, dkt, dvt = refs[:n], refs[n : 2 * n], refs[2 * n : 3 * n]
        wkv_ref, enc_ref, genc_out, both, lhs, rhs, dkvt = refs[3 * n :]
        for i, r in enumerate(dcq_refs):
            rhs[0, :, i * size : (i + 1) * size] = r[...]
        rhs[1] = dh2_ref[...].astype(BF)
        rhs[2] = dh1_ref[...].astype(BF)
        for i, r in enumerate((a2_ref, o2_ref, o1_ref)):
            lhs[i] = r[...]
        for i, r in enumerate(dkt + dvt):
            dkvt[i * size : (i + 1) * size, :] = r[...]

        def square(i, carry):
            g = dot_tn(lhs[i], rhs[i])
            for h in range(2):
                columns.store(both.ref, h, "q", g[:, h * half : (h + 1) * half], place_ref, None, i * (half // 128))
            return carry

        lax.fori_loop(0, 3, square, 0)

        def encodings(t, carry):
            at = pl.ds(pl.multiple_of(t * tile, 128), tile)
            genct = dot_nn(wkv_ref[...], dkvt[:, at]).astype(BF)
            for i in range(tile // shard_rows):
                spot = t * (tile // shard_rows) + i
                for j in range(blocks):
                    genc_out.ref[spot * blocks + j] = genct[
                        j * 128 : (j + 1) * 128, i * shard_rows : (i + 1) * shard_rows
                    ]
            return carry

        lax.fori_loop(0, tokens // tile, encodings, 0)
        genc_out.flush()

        def key_value(h, carry):
            g = 0.0
            rows_at = pl.ds(pl.multiple_of(h * width, 128), width)
            for t in range(0, tokens, 1024):
                end = min(tokens, t + 1024)
                g = g + dot_nt(jnp.transpose(enc_ref[t:end, :]), dkvt[rows_at, t:end])
            columns.store(both.ref, h, "kv", g, place_ref)
            return carry

        lax.fori_loop(0, 2, key_value, 0)

    return call(
        "cross_weights",
        body,
        (shape_of(BF, columns.chunks * blocks, 128, shard_rows), columns.shape(), columns.shape()),
        [SMEM] + [VMEM] * (3 * n + 7),
        (DRAIN, PAIR, PAIR),
        (place, dh2, dh1, a2, o2, o1, *dcq, *dkt, *dvt, w_cross_kv, enc),
        scratch=[
            pltpu.VMEM((3, rows, width), BF),
            pltpu.VMEM((3, rows, width), BF),
            pltpu.VMEM((2 * width, tokens), BF),
        ],
        ahead=ahead,
        limit=big(tokens),
    )


def self_backward(dh1, w_self_out, qkv, p1, bucket_count, heads, ahead):
    rows, width = dh1.shape
    pairs = heads // 2
    groups = rows // GROUP
    firsts = bucket_firsts(bucket_count)
    ends = [first for _, first in firsts[1:]] + [TLEN]

    def body(dh1_ref, wso_ref, qkv_ref, p1_ref, dqkv_ref, gbias_ref, do1, acc):
        do1[...] = dot_nt(dh1_ref[...].astype(BF), wso_ref[...]).astype(BF)
        m0, m1 = half_masks(GROUP)
        acc[...] = jnp.zeros_like(acc)

        def attend(g, carry):
            at = pl.ds(pl.multiple_of(g * GROUP, GROUP), GROUP)
            for pair in range(pairs):
                lo = pair * 128
                q = qkv_ref[at, lo : lo + 128]
                k = qkv_ref[at, width + lo : width + lo + 128]
                v = qkv_ref[at, 2 * width + lo : 2 * width + lo + 128]
                do = do1[at, lo : lo + 128]
                do_two = jnp.concatenate([do * m0, do * m1], 0)
                pb = p1_ref[g, pair]
                pf = pb.astype(F32)
                dp = dot_nt(do_two, v)
                ds = (pf * (dp - jnp.sum(pf * dp, -1, keepdims=True))).astype(BF)
                dsf = ds.astype(F32)
                for h in range(2):
                    total = dsf[h * GROUP : h * GROUP + TLEN]
                    for t in range(1, GROUP // TLEN):
                        total = total + dsf[h * GROUP + t * TLEN : h * GROUP + (t + 1) * TLEN]
                    acc[2 * pair + h] += total
                dq = dot_nn(
                    jnp.concatenate([ds[:GROUP], ds[GROUP:]], 1),
                    jnp.concatenate([k * m0, k * m1], 0),
                )
                dk = dot_tn(ds, jnp.concatenate([q * m0, q * m1], 0))
                dv = dot_tn(pb, do_two)
                dqkv_ref[at, lo : lo + 128] = dq.astype(BF)
                dqkv_ref[at, width + lo : width + lo + 128] = dk.astype(BF)
                dqkv_ref[at, 2 * width + lo : 2 * width + lo + 128] = dv.astype(BF)
            return carry

        lax.fori_loop(0, groups, attend, 0)
        row = lax.broadcasted_iota(jnp.int32, (TLEN, GROUP), 0)
        distance = row - lax.rem(lax.broadcasted_iota(jnp.int32, (TLEN, GROUP), 1), TLEN)
        lane = lax.broadcasted_iota(jnp.int32, (16, 128), 1)
        bias = jnp.zeros((16, 128), F32)
        accv = acc[...]
        pad = jnp.zeros((16 - heads, 1), F32)
        for (b, first), end in zip(firsts, ends):
            here = jnp.logical_and(distance >= first, distance < end)
            part_sum = jnp.sum(jnp.where(here[None], accv, 0.0), axis=1)
            col = jnp.sum(part_sum, -1, keepdims=True)
            bias = jnp.where(lane == b, jnp.concatenate([col, pad], 0), bias)
        gbias_ref[...] = bias

    return call(
        "self_backward",
        body,
        (shape_of(BF, rows, 3 * width), shape_of(F32, 16, 128)),
        [VMEM] * 4,
        (NEAR, VMEM),
        (dh1, w_self_out, qkv, p1),
        ahead=ahead,
        scratch=[pltpu.VMEM((rows, width), BF), pltpu.VMEM((heads, TLEN, GROUP), F32)],
    )


def self_weights(
    place, dh1, a1, dqkv, x, gain_self, w_qkv, gbias, gain_cross_grad, gain_ff_grad, columns
):
    rows, width = dh1.shape
    half = width // 2
    part = columns.part
    misc_rows = 16 + width // 16
    more = -(-misc_rows // part)

    def body(
        place_ref, dh1_ref, wqkv_ref, x_ref, a1_ref, dqkv_ref, gs_ref, gb_ref, ggc_ref, ggf_ref,
        out, both, da1,
    ):
        da1[...] = jnp.zeros_like(da1)

        def one(t, carry):
            at = pl.ds(pl.multiple_of(t * width, 128), width)
            da1[...] += dot_nt(dqkv_ref[:, at], wqkv_ref[:, at])
            return carry

        lax.fori_loop(0, 3, one, 0)
        dv, dgain = rms_back(da1[...], x_ref[...].astype(F32), gs_ref[...])
        out.ref[...] = dh1_ref[...] + dv
        out.flush()

        def weights(h, carry):
            at = pl.ds(pl.multiple_of(h * 3 * half, 128), 3 * half)
            columns.store(both.ref, h, "qkv", dot_tn(a1_ref[...], dqkv_ref[:, at]), place_ref)
            return carry

        lax.fori_loop(0, 2, weights, 0)
        gains = jnp.concatenate([dgain, ggc_ref[...], ggf_ref[...], jnp.zeros((5, width), F32)], 0)
        misc = [gb_ref[...]] + [gains[:, j * 128 : (j + 1) * 128] for j in range(width // 128)]
        misc.append(jnp.zeros((more * part - misc_rows, 128), F32))
        misc = jnp.concatenate(misc, 0).astype(BF)
        for i in range(more):
            for slot in range(2):
                both.ref[slot, columns.units + i] = misc[i * part : (i + 1) * part]

    return call(
        "self_weights",
        body,
        (shape_of(F32, rows, width), columns.shape(more), columns.shape(more)),
        [SMEM] + [VMEM] * 9,
        (DRAIN, PAIR, PAIR),
        (
            place, dh1, w_qkv, x, a1, dqkv, gain_self.reshape(1, width), gbias,
            gain_cross_grad, gain_ff_grad,
        ),
        scratch=[pltpu.VMEM((rows, width), F32)],
    )


def swap(value, axis, bit):
    size = lax.axis_size(axis)
    return lax.ppermute(value, axis, [(i, i ^ bit) for i in range(size)])


class Bucket:
    def __init__(self, rows, terms, steps, keep_all=False):
        self.rows, self.terms, self.steps, self.keep_all = rows, terms, list(steps), keep_all


def sum_kernel(groups, dtype=BF):
    operands, specs, plan = [], [], []
    for i, jobs in enumerate(groups):
        at = 0
        for rows, terms in jobs:
            plan.append((i, at, rows, len(operands), len(terms)))
            at += rows
            for array, off in terms:
                operands.append(array)
                spec = (pl.Element(rows), pl.Element(128))
                specs.append(pl.BlockSpec(spec, functools.partial(lambda off, *_: (off, 0), off)))
    sizes = [sum(rows for rows, _ in jobs) for jobs in groups]

    def body(*refs):
        outs = refs[len(operands) :]
        for i, at, rows, first, count in plan:
            total = refs[first][...].astype(F32)
            for r in refs[first + 1 : first + count]:
                total = total + r[...].astype(F32)
            outs[i][at : at + rows, :] = total.astype(dtype)

    return call(
        "sum_kernel",
        body,
        tuple(shape_of(dtype, size, 128) for size in sizes),
        specs,
        tuple(whole(size, 128) for size in sizes),
        operands,
        grid=(1,),
    )


def send_round(cost, *members, settle=()):
    groups = {}
    for m in members:
        step = m.steps[0]
        groups.setdefault((step, m) if isinstance(m, Total) else step, []).append(m)
    jobs = []
    for group in groups.values():
        jobs.append([])
        for m in group:
            if isinstance(m, Total):
                jobs[-1] += m.next_jobs()
            elif m.keep_all:
                jobs[-1].append((m.rows, m.terms))
            else:
                m.rows //= 2
                jobs[-1].append((m.rows, [(array, off + m.rows) for array, off in m.terms]))
    settle = [b for b in settle if not b.steps]
    if settle:
        jobs.append([(b.rows, b.terms) for b in settle])
    sent = sum_kernel(jobs)
    at = 0
    for b in settle:
        b.terms = [(sent[-1], at)]
        at += b.rows
    for group, payload in zip(groups.values(), sent):
        axis, bit = group[0].steps[0]
        got = swap(payload, axis, bit)
        at = 0
        for m in group:
            m.steps.pop(0)
            if isinstance(m, Total):
                m.moved(payload, got)
                continue
            if m.keep_all:
                m.terms = [(payload, at), (got, at)]
            else:
                m.terms = m.terms + [(got, at)]
            at += m.rows
    shadow(cost)


def rest_of(*buckets):
    while any(b.steps for b in buckets):
        send_round(3, *[b for b in buckets if b.steps])


def weight_buckets(columns, keep, send, orders, y_bits):
    rows = columns.units * columns.part
    keep, send = in_hbm(keep.reshape(-1, 128)), send.reshape(-1, 128)
    got = swap(send, "dp", 1)
    over = [[("blk", b) for b in order] for order in orders]
    along = [("dp", 2 * b) for b in y_bits]
    buckets = []
    for _, blocks, order, unit in columns.sections:
        steps = along + over[0] if order == "y" else over[order]
        at = unit * columns.part
        size = blocks * columns.chunks * columns.part
        buckets.append(Bucket(size, [(keep, at), (got, at)], steps))
    if keep.shape[0] > rows:
        buckets.append(Bucket(keep.shape[0] - rows, [(keep, rows), (got, rows)], over[0], keep_all=True))
    return buckets


def join_encodings(buckets, shard_rows, width):
    terms = [(bucket, array, off) for bucket in buckets for array, off in bucket.terms]

    def body(*refs):
        out = refs[-1]
        first = col = 0
        for bucket in buckets:
            mine = refs[first : first + len(bucket.terms)]
            first += len(bucket.terms)
            for at in range(0, bucket.rows, 128):
                total = mine[0][at : at + 128, :].astype(F32)
                for r in mine[1:]:
                    total = total + r[at : at + 128, :].astype(F32)
                out[:, col : col + 128] = jnp.transpose(total)
                col += 128

    return call(
        "join_encodings",
        body,
        shape_of(F32, shard_rows, width),
        [
            pl.BlockSpec(
                (pl.Element(bucket.rows), pl.Element(shard_rows)),
                functools.partial(lambda off, *_: (off, 0), off),
            )
            for bucket, _, off in terms
        ],
        whole(shard_rows, width),
        [array for _, array, _ in terms],
        grid=(1,),
    )


class Total:
    def __init__(self, groups, small, dp_size):
        self.groups, self.small, self.dp_size = groups, small, dp_size
        self.jobs, self.bases = [], []
        at = 0
        for _, buckets in groups:
            base = []
            for bucket in buckets:
                self.jobs.append((bucket.rows, bucket.terms))
                base.append(at)
                at += bucket.rows
            self.bases.append(base)
        self.small_at = []
        for bucket in small:
            self.jobs.append((bucket.rows, bucket.terms))
            self.small_at.append((at, bucket.rows))
            at += bucket.rows
        self.rows = at
        self.steps = [("dp", 2 * m) for m in range(1, dp_size // 2)] + [("dp", 1)]
        self.parts = []

    def next_jobs(self):
        if len(self.steps) > 1 or not self.parts:
            return [(self.rows, [(self.parts[0], 0)])] if self.parts else self.jobs
        jobs, self.spots, at = [], [], 0
        for (columns, _), base in zip(self.groups, self.bases):
            spots = []
            for (_, blocks, order, _), first in zip(columns.sections, base):
                if order == "y":
                    rows = blocks // columns.y_parts * columns.part
                    spots.append([at + i * rows for i in range(len(self.parts))])
                    jobs += [(rows, [(p, first)]) for p in self.parts]
                    at += rows * len(self.parts)
                else:
                    rows = blocks * columns.part
                    spots.append(at)
                    jobs.append((rows, [(p, first) for p in self.parts]))
                    at += rows
            self.spots.append(spots)
        self.small_spots = []
        for first, rows in self.small_at:
            jobs.append((rows, [(p, first) for p in self.parts]))
            self.small_spots.append((at, rows))
            at += rows
        return jobs

    def moved(self, payload, got):
        if self.steps or not self.parts:
            self.parts = self.parts + [got] if self.parts else [payload, got]
        else:
            self.own, self.other = payload, got

    def finish(self, place, arrays):
        outs = []
        for (columns, _), spots, named in zip(self.groups, self.spots, arrays):
            for name, stack in named:
                outs.append((columns, spots, name, stack, dict(columns.names)[name] // stack))
        y_parts = self.dp_size // 2

        def body(place_ref, own_ref, other_ref, *refs):
            core, y = place_ref[0], place_ref[2]
            sides = ((core, own_ref), (1 - core, other_ref))

            def put(ref, columns, half, j, at):
                row, off = divmod(j * 128, half)
                for which, src in sides:
                    lane = pl.multiple_of(which * half + off, 128)
                    ref[row * columns.part : (row + 1) * columns.part, pl.ds(lane, 128)] = src[
                        at : at + columns.part, :
                    ].astype(F32)

            for ref, (columns, spots, name, stack, half) in zip(refs, outs):
                far = []
                for j in range(stack * half // 128):
                    i, y_of, k = columns.find(columns.first(name) + j)
                    if y_of is None:
                        put(ref, columns, half, j, spots[i] + k * columns.part)
                    else:
                        far.append((j, spots[i], y_of, k))
                for y_is in range(y_parts if far else 0):

                    @pl.when(y == y_is)
                    def _():
                        for j, at, y_of, k in far:
                            put(ref, columns, half, j, at[y_is ^ y_of] + k * columns.part)

            for ref, (at, rows) in zip(refs[len(outs) :], self.small_spots):
                ref[...] = own_ref[at : at + rows, :].astype(F32)

        shapes = [shape_of(F32, stack * columns.part, 2 * half) for columns, _, _, stack, half in outs]
        shapes += [shape_of(F32, rows, 128) for _, rows in self.small_spots]
        return call(
            "finish",
            body,
            tuple(shapes),
            [SMEM, VMEM, VMEM],
            (VMEM,) * len(shapes),
            (place, self.own, self.other),
        )


def gather_encodings(own, bits):
    if len(bits) == 3:
        x, z, far = bits
        r_far, r_x = swap(own, "blk", far), swap(own, "blk", x)

        def second():
            r_z, r_zf = swap(own, "blk", z), swap(r_far, "blk", z)
            r_xf = swap(r_far, "blk", x)

            def third():
                r_xz = swap(r_z, "blk", x)
                r_xzf = swap(r_xf, "blk", z)
                arrays = [own, r_far, r_x, r_z, r_zf, r_xf, r_xz, r_xzf]
                return arrays, [[0], [far], [x], [z], [z | far], [x | far], [x | z], [x | z | far]]

            return [r_z, r_zf, r_xf], third

        return [r_far, r_x], second
    got, rel = own, [0]
    for bit in reversed(bits):
        got = jnp.concatenate([got, swap(got, "blk", bit)], 0)
        rel = rel + [r ^ bit for r in rel]
    return [], lambda: ([], lambda: ([got], [rel]))


def local(
    dec_in,
    encodings,
    enc_question,
    enc_valid,
    tgt_question,
    gain_self,
    w_qkv,
    rel_bias,
    w_self_out,
    gain_cross,
    w_cross_q,
    w_cross_kv,
    w_cross_out,
    gain_ff,
    w_ff_in,
    w_ff_out,
    grad_out,
):
    x = dec_in[0]
    gy = grad_out[0]
    rows, width = x.shape
    bucket_count, heads = rel_bias.shape
    hidden = w_ff_in.shape[1]
    half = width // 2
    chunks = lax.axis_size("blk")
    part = width // chunks
    dp_size = lax.axis_size("dp")
    shard_rows = encodings.shape[1]
    bits = [1 << i for i in range(chunks.bit_length() - 1)]
    y_bits = [1 << i for i in range(dp_size.bit_length() - 2)]
    y_parts = dp_size // 2
    blk = lax.axis_index("blk")
    dp = lax.axis_index("dp")
    orders = [bits, bits[1::-1] + bits[2:]]

    def layout(names, *sections):
        return Columns(names, sections, y_parts, chunks, part)

    def along_y(blocks):
        return blocks // (2 * y_parts) * y_parts

    stack = hidden // width
    blocks = half // 128
    cols_out = layout([("out", stack * half)], (stack * blocks, "y"))
    cols_in = layout([("in", hidden // 2)], (stack * blocks // 2, 0), (stack * blocks // 2, 1))
    far_x, far_s = along_y(16 * blocks // 3), along_y(3 * blocks)
    near_x, near_s = 5 * blocks - far_x, 3 * blocks - far_s
    cols_x = layout(
        [("q", half), ("out", half), ("self", half), ("kv", width)],
        (near_x, 0), (far_x, "y"),
    )
    cols_s = layout([("qkv", 3 * half)], (near_s, 0), (far_s, "y"))

    places = [[chunk_place(c, blk, order) for c in range(chunks)] for order in orders]
    y_places = [chunk_place(y, dp // 2, y_bits) for y in range(y_parts)]
    numbers = [lax.rem(dp, 2), blk, dp // 2]
    for columns in (cols_out, cols_in, cols_x, cols_s):
        columns.at = len(numbers)
        numbers += columns.table(places, y_places)
    place = jnp.stack(numbers).astype(jnp.int32)

    ORDER.clear()
    ROOMY[:] = [chunks * shard_rows <= 1024]
    tags = jnp.where(enc_valid[0] == 1, enc_question[0], -1).astype(BF)
    tag_rows = jnp.zeros((16, width), BF).at[0, :shard_rows].set(tags)
    enc_own = jnp.concatenate([encodings[0], tag_rows], 0)[None]
    got, second = gather_encodings(enc_own, bits)
    shadow(10)
    a1, qkv, p1, o1_near, o1, wso_near, wcq_near, x_near = self_attention(
        x, gain_self, w_qkv, rel_bias, [w_self_out, w_cross_q, x]
    )
    more, third = second()
    shadow(10)
    h1_near, cq_near, h1, a2, cq, w2_near, gy = self_project(
        x_near, o1_near, wso_near, gain_cross, wcq_near, [w_ff_out, gy]
    )
    pieces, rel = third()
    shadow(10)
    dhid, wkv_near, wco_near = hidden_gradient(gy, w2_near, [w_cross_kv, w_cross_out])
    spots = [[int(chunk_spot(r, bits)) for r in group] for group in rel]
    enc, kv, e, inv, o2, h2, a3, w1_near = cross_forward(
        pieces, spots, shard_rows, tgt_question[0], cq_near, h1_near, wkv_near, wco_near, gain_ff, [w_ff_in]
    )

    dpre, hid, keep, send = feed_hidden(place, a3, gy, dhid, w1_near, cols_out)
    (b_out,) = weight_buckets(cols_out, keep, send, orders, y_bits)
    shadow(30)
    keep, send, h2_near = feed_weights(place, a3, dpre, cols_in, [h2])
    b_in, b_jn = weight_buckets(cols_in, keep, send, orders, y_bits)
    send_round(30, b_out)
    dh2, gain_ff_grad = feed_back(dpre, w1_near, h2_near, gain_ff, gy)
    send_round(8, b_in, b_jn)
    pairs = heads // 2
    parts_a = cross_backward(0, pairs // 2, dh2, o2, inv, cq, kv, e, wco_near, [])
    parts_b = cross_backward(
        pairs // 2, pairs, dh2, o2, inv, cq, kv, e, wco_near, [w_cross_q, h1, a2, o2, o1, enc, w_cross_kv]
    )
    wcq_near, h1_near, a2, o2, o1, enc, wkv_near = parts_b[3:]
    dcq, dkt, dvt = zip(parts_a, parts_b[:3])
    dh1, gain_cross_grad = cross_query_back(dcq, wcq_near, h1_near, gain_cross, dh2)
    send_round(12, b_jn, b_out, b_in)
    genc, keep, send, hid, w2_near, h2_near = cross_weights(
        place, dh2, o2, dcq, dkt, dvt, enc, a2, wkv_near, dh1, o1, cols_x, [hid, w_ff_out, h2]
    )
    enc_rows = chunks * shard_rows * width // 128
    b_enc = Bucket(
        enc_rows, [(in_hbm(genc.reshape(enc_rows, shard_rows)), 0)], [("blk", b) for b in bits]
    )
    b_xa, b_xb = weight_buckets(cols_x, keep, send, orders, y_bits)
    out, wso_near, qkv, p1 = feed_out(hid, w2_near, h2_near, [w_self_out, qkv, p1])
    send_round(40, b_in, b_jn, b_enc, b_out)
    dqkv, gbias, wqkv_near, x_near, a1 = self_backward(
        dh1, wso_near, qkv, p1, bucket_count, heads, [w_qkv, x, a1]
    )
    send_round(8, b_xa, b_xb, b_enc, b_out, settle=[b_in, b_jn])
    grad_dec, keep, send = self_weights(
        place, dh1, a1, dqkv, x_near, gain_self, wqkv_near, gbias, gain_cross_grad, gain_ff_grad, cols_s
    )
    b_sa, b_sb, b_misc = weight_buckets(cols_s, keep, send, orders, y_bits)
    send_round(25, b_xa, b_xb, b_enc, settle=[b_out])
    send_round(4, b_sa, b_misc, b_sb)
    rest_of(b_out, b_in, b_jn)
    total_ff = Total([(cols_out, [b_out]), (cols_in, [b_in, b_jn])], [], dp_size)
    send_round(4, b_xa, b_xb, total_ff)
    rest_of(b_enc)
    send_round(4, b_sa, b_misc, b_sb)
    send_round(4, b_xb, b_sa, b_misc, total_ff)
    grad_enc = join_encodings([b_enc], shard_rows, width)
    send_round(4, b_sb)
    rest_of(total_ff)
    grad_ff_out, grad_ff_in = total_ff.finish(place, [[("out", stack)], [("in", 1)]])
    rest_of(b_xa, b_xb)
    total_x = Total([(cols_x, [b_xa, b_xb])], [], dp_size)
    send_round(4, total_x)
    send_round(4, b_sb)
    rest_of(b_sa, b_sb, b_misc)
    total_s = Total([(cols_s, [b_sa, b_sb])], [b_misc], dp_size)
    send_round(4, total_s, total_x)
    rest_of(total_s, total_x)
    grad_cross_out, grad_cross_q, grad_self_out, grad_cross_kv = total_x.finish(
        place, [[("out", 1), ("q", 1), ("self", 1), ("kv", 1)]]
    )
    grad_qkv, misc = total_s.finish(place, [[("qkv", 1)]])
    gains = misc[16 : 16 + width // 16].reshape(width // 128, 8, 128)[:, :3].transpose(1, 0, 2).reshape(3, width)
    gains = lax.dynamic_slice(gains, (0, blk * part), (3, part))
    bias_part = bucket_count // chunks
    grad_bias = lax.dynamic_slice(misc, (0, blk * bias_part), (heads, bias_part)).T
    return (
        out[None],
        grad_dec[None],
        grad_enc[None],
        gains[0],
        grad_qkv,
        grad_bias,
        grad_self_out,
        gains[1],
        grad_cross_q,
        grad_cross_kv,
        grad_cross_out,
        gains[2],
        grad_ff_in,
        grad_ff_out,
    )


def solution(mesh):
    return jax.shard_map(
        local,
        mesh=mesh,
        in_specs=(
            P("dp", "blk", None),
            P("dp", "blk", None),
            P("dp", "blk"),
            P("dp", "blk"),
            P("dp", "blk"),
            P(),
            P(),
            P(),
            P(),
            P(),
            P(),
            P(),
            P(),
            P(),
            P(),
            P(),
            P("dp", "blk", None),
        ),
        out_specs=(
            P("dp", "blk", None),
            P("dp", "blk", None),
            P("dp", "blk", None),
            P("blk"),
            P("blk", None),
            P("blk", None),
            P("blk", None),
            P("blk"),
            P("blk", None),
            P("blk", None),
            P("blk", None),
            P("blk"),
            P("blk", None),
            P("blk", None),
        ),
        check_vma=False,
    )
```

```python
import functools
import math

import jax
import jax.numpy as jnp
import numpy as np
from jax import lax
from jax.experimental import pallas as pl
from jax.experimental.pallas import tpu as pltpu
from jax.sharding import PartitionSpec as P

TLEN = 32
EPSILON = 1e-06
NEG_LARGE = -1e30
GROUP = 128
LOG2E = 1.4426950408889634
BF = jnp.bfloat16
F32 = jnp.float32
VMEM = pl.BlockSpec(memory_space=pltpu.VMEM)
SMEM = pl.BlockSpec(memory_space=pltpu.SMEM)
ANY = pl.BlockSpec(memory_space=pl.ANY)
HBM, STREAM, DRAIN, NEAR, PAIR = "hbm", "stream", "drain", "near", "pair"
MIB = 2**20
LIMITS = dict(
    self_attention=24, self_project=12, cross_forward=30, hidden_gradient=10, feed_hidden=26, feed_weights=18,
    feed_back=12, feed_out=12, cross_backward=20, cross_query_back=12, cross_weights=34, self_backward=14,
    self_weights=24, sum_kernel=16, finish=24, shadow=1, join_encodings=8,
)


def bucket_of(distance, bucket_count):
    exact_count = bucket_count // 2
    if distance < exact_count:
        return distance
    scaled = math.log(distance / exact_count) / math.log(128.0 / exact_count) * exact_count
    return min(bucket_count - 1, exact_count + int(scaled))


def bucket_firsts(bucket_count):
    firsts = {}
    for distance in range(TLEN):
        firsts.setdefault(bucket_of(distance, bucket_count), distance)
    return sorted(firsts.items())


def dot_nn(a, b):
    return jnp.dot(a, b, preferred_element_type=F32)


def dot_nt(a, b):
    return lax.dot_general(a, b, (((1,), (1,)), ((), ())), preferred_element_type=F32)


def dot_tn(a, b):
    return lax.dot_general(a, b, (((0,), (0,)), ((), ())), preferred_element_type=F32)


def inv_rms(v):
    return lax.rsqrt(jnp.mean(v * v, axis=-1, keepdims=True) + EPSILON)


def rms_back(dy, v, gain):
    r = inv_rms(v)
    vr = v * r
    dg = dy * gain
    dv = r * (dg - vr * jnp.mean(dg * vr, axis=-1, keepdims=True))
    return dv, jnp.sum(dy * vr, axis=0, keepdims=True)


def half_masks(rows):
    lane = lax.broadcasted_iota(jnp.int32, (rows, 128), 1)
    low = (lane < 64).astype(F32)
    return low.astype(BF), (1.0 - low).astype(BF)


def chunk_place(chunk, blk, bits):
    rel = jnp.bitwise_xor(chunk, blk)
    place = jnp.int32(0)
    for bit in bits:
        place = place * 2 + jnp.where(jnp.bitwise_and(rel, bit) != 0, 1, 0)
    return place


def chunk_spot(rel, bits):
    spot = 0
    for bit in bits:
        spot = spot * 2 + (1 if rel & bit else 0)
    return spot


def query_block(rows, tokens):
    return max(GROUP, min(rows, rows * 1024 // tokens))


def big(tokens):
    return 61 if tokens > 1024 else None


class Stream:
    def __init__(self, copy, ref):
        self.copy, self.ref, self.waited = copy, ref, False

    def ready(self):
        if not self.waited:
            self.copy.wait()
            self.waited = True
        return self.ref


class Drain:
    def __init__(self, copy, ref, out, sem):
        self.copy, self.ref, self.started = copy, ref, False
        self.out, self.sem = out, sem

    def flush(self):
        self.copy.start()
        self.started = True

    def flush_part(self, at):
        pltpu.make_async_copy(self.ref.at[at], self.out.at[at], self.sem).start()
        self.started = True


ORDER = []
ROOMY = [True]


class Pair:
    def __init__(self, drains, ref):
        self.drains, self.ref = drains, ref


def in_hbm(x):
    return pltpu.with_memory_space_constraint(x, pltpu.HBM)


def call(
    name, body, out_shape, in_specs, out_specs, operands, scratch=(), grid=(), prefetch=0,
    limit=None, cost=0.001, ahead=(),
):
    operands, in_specs = list(operands), list(in_specs)
    after = list(ORDER)
    wanted = ahead
    ahead = wanted if ROOMY[0] else ()
    outs = isinstance(out_shape, (tuple, list))
    out_shape = list(out_shape) if outs else [out_shape]
    out_specs = list(out_specs) if outs else [out_specs]
    streams, drains, pairs = [], [], []
    extra_scratch = []
    for i, spec in enumerate(in_specs):
        at = prefetch + i
        if spec == STREAM:
            streams.append(at)
            in_specs[i] = ANY
            operands[at] = in_hbm(operands[at])
            extra_scratch += [pltpu.VMEM(operands[at].shape, operands[at].dtype), pltpu.SemaphoreType.DMA]
        elif isinstance(spec, tuple):
            in_specs[i] = spec[1]
            operands[at] = in_hbm(operands[at])
    real = prefetch + len(in_specs)
    for i, spec in enumerate(out_specs):
        shape = out_shape[i]
        if spec == PAIR:
            pairs.append(i)
            out_specs[i] = ANY
            out_shape[i] = pltpu.HBM(shape.shape, shape.dtype)
            if len(pairs) % 2:
                extra_scratch += [
                    pltpu.VMEM((2, *shape.shape), shape.dtype), pltpu.SemaphoreType.DMA((2,))
                ]
        elif spec == DRAIN:
            drains.append(i)
            out_specs[i] = ANY
            out_shape[i] = pltpu.HBM(shape.shape, shape.dtype)
            extra_scratch += [pltpu.VMEM(shape.shape, shape.dtype), pltpu.SemaphoreType.DMA]
        elif spec == NEAR or isinstance(spec, tuple):
            space = pltpu.VMEM if spec == NEAR or spec[0] == NEAR else pltpu.HBM
            out_specs[i] = VMEM if spec == NEAR else spec[1]
            if ROOMY[0] or space is pltpu.HBM:
                out_shape[i] = space(shape.shape, shape.dtype)
    count = len(out_shape)
    for array in ahead:
        out_specs.append(VMEM if not grid else ANY)
        out_shape.append(pltpu.VMEM(array.shape, array.dtype))
    if ahead:
        extra_scratch.append(pltpu.SemaphoreType.DMA((len(ahead),)))
    after = [in_hbm(array) for array in ahead] + after
    out_specs.append(ANY)
    out_shape.append(pltpu.HBM((8, 128), F32))

    def ordered(*refs):
        ins = list(refs[:real])
        results = list(refs[real + len(after) : real + len(after) + len(out_shape) - 1])
        rest = list(refs[real + len(after) + len(out_shape) :])
        early = [
            pltpu.make_async_copy(refs[real + i], results[count + i], rest[-1].at[i])
            for i in range(len(ahead))
        ]
        del results[count:]
        own, extra = rest[: len(scratch)], rest[len(scratch) :]
        made, ends = [], []
        for n, i in enumerate(streams):
            copy = pltpu.make_async_copy(ins[i], extra[2 * n], extra[2 * n + 1])
            copy.start()
            ins[i] = Stream(copy, extra[2 * n])
            made.append(ins[i])
        extra = extra[2 * len(streams) :]
        for i in sorted(drains + pairs[::2]):
            held, sem = extra[:2]
            extra = extra[2:]
            if i in drains:
                copy = pltpu.make_async_copy(held, results[i], sem)
                results[i] = Drain(copy, held, results[i], sem)
                ends.append(results[i])
            else:
                halves = [
                    Drain(
                        pltpu.make_async_copy(held.at[k], results[i + k], sem.at[k]),
                        held.at[k], results[i + k], sem.at[k],
                    )
                    for k in range(2)
                ]
                results[i] = Pair(halves, held)
                ends += results[i].drains
        for i in reversed(pairs[1::2]):
            del results[i]
        for n, copy in enumerate(early):
            if grid:
                pl.when(pl.program_id(0) == 0)(copy.start)
            else:
                copy.start()
        body(*ins, *results, *own)
        for copy in early:
            if grid:
                pl.when(pl.program_id(0) == grid[0] - 1)(copy.wait)
            else:
                copy.wait()
        for stream in made:
            stream.ready()
        for end in ends:
            if not end.started:
                end.flush()
        for end in ends:
            end.copy.wait()

    got = pl.pallas_call(
        ordered,
        out_shape=tuple(out_shape),
        grid_spec=pltpu.PrefetchScalarGridSpec(
            num_scalar_prefetch=prefetch,
            grid=grid,
            in_specs=in_specs + [ANY] * len(after),
            out_specs=tuple(out_specs),
            scratch_shapes=list(scratch) + extra_scratch,
        ),
        compiler_params=pltpu.CompilerParams(vmem_limit_bytes=(limit or LIMITS[name]) * MIB),
        name=name,
        cost_estimate=pl.CostEstimate(
            flops=int(cost * 1153 * 10**6), bytes_accessed=0, transcendentals=0
        ),
    )(*operands, *after)
    ORDER[:] = [in_hbm(got[-1])]
    got = (*got[:count], *(got[count:-1] if ahead else wanted))
    return got if outs or wanted else got[0]


def shadow(cost):
    call("shadow", lambda: None, (), (), (), (), cost=cost)


def whole(*shape):
    return pl.BlockSpec(shape, lambda *_: (0,) * len(shape))


def shape_of(dtype, *shape):
    return jax.ShapeDtypeStruct(shape, dtype)


class Columns:
    def __init__(self, names, sections, y_parts, chunks, part):
        self.names, self.y_parts, self.chunks, self.part = names, y_parts, chunks, part
        self.sections = []
        first = unit = 0
        for blocks, order in sections:
            if blocks:
                self.sections.append((first, blocks, order, unit))
            first, unit = first + blocks, unit + chunks * blocks
        self.blocks, self.units = first, unit

    def shape(self, more=0):
        return shape_of(BF, self.units + more, self.part, 128)

    def first(self, name):
        done = 0
        for other, width in self.names:
            if other == name:
                return done
            done += width // 128

    def find(self, block):
        for i, (first, blocks, order, _) in enumerate(self.sections):
            if first <= block < first + blocks:
                if order != "y":
                    return i, None, block - first
                y, k = divmod(block - first, blocks // self.y_parts)
                return i, y, k

    def runs(self):
        found = []
        for first, blocks, order, _ in self.sections:
            size = blocks // self.y_parts if order == "y" else blocks
            found += [(at, size) for at in range(first, first + blocks, size)]
        return found

    def table(self, spots, y_spots):
        units = []
        for c in range(self.chunks):
            for block in range(self.blocks):
                i, y, k = self.find(block)
                _, blocks, order, unit = self.sections[i]
                if y is None:
                    units.append(unit + spots[order][c] * blocks + k)
                else:
                    units.append(unit + (y_spots[y] * self.chunks + spots[0][c]) * (blocks // self.y_parts) + k)
        return units

    def store(self, ref, half, name, value, place_ref, chunks=None, block=0):
        chunks = range(self.chunks) if chunks is None else chunks
        start = self.first(name) + block
        slot = jnp.bitwise_xor(place_ref[0], half)
        for n, c in enumerate(chunks):
            for j in range(value.shape[1] // 128):
                unit = place_ref[self.at + c * self.blocks + start + j]
                ref[slot, unit] = value[n * self.part : (n + 1) * self.part, j * 128 : (j + 1) * 128].astype(BF)


def self_attention(x, gains, w_qkv, rel_bias, ahead):
    rows, width = x.shape
    bucket_count, heads = rel_bias.shape
    pairs = heads // 2
    groups = rows // GROUP
    firsts = bucket_firsts(bucket_count)

    def body(
        x, gs_ref, wqkv, rb_ref, a1_out, qkv_out, p1_out, o1_ref, o1_out, bias
    ):
        a1_ref, qkv_ref, p1_ref = a1_out.ref, qkv_out.ref, p1_out.ref
        xf = x.ready()[...].astype(F32)
        a1 = (xf * inv_rms(xf) * gs_ref[0:1, :]).astype(BF)
        a1_ref[...] = a1
        a1_out.flush()
        row = lax.broadcasted_iota(jnp.int32, (TLEN, GROUP), 0)
        col = lax.broadcasted_iota(jnp.int32, (TLEN, GROUP), 1)
        distance = lax.rem(col, TLEN) - row

        def make_bias(h, carry):
            val = jnp.full((TLEN, GROUP), NEG_LARGE, F32)
            for b, first in firsts:
                val = jnp.where(distance >= first, rb_ref[h, b], val)
            lanes = pl.ds(pl.multiple_of(lax.rem(h, 2) * GROUP, GROUP), GROUP)
            for t in range(GROUP // TLEN):
                bias[h // 2, t * TLEN : (t + 1) * TLEN, lanes] = jnp.where(
                    col // TLEN == t, val, NEG_LARGE
                )
            return carry

        lax.fori_loop(0, heads, make_bias, 0)
        wqkv_ref = wqkv.ready()

        def project(t, carry):
            at = pl.ds(pl.multiple_of(t * width, 128), width)
            qkv_ref[:, at] = dot_nn(a1_ref[...], wqkv_ref[:, at]).astype(BF)
            return carry

        lax.fori_loop(0, 3, project, 0)
        qkv_out.flush()
        m0, m1 = half_masks(GROUP)

        def attend(g, carry):
            at = pl.ds(pl.multiple_of(g * GROUP, GROUP), GROUP)
            for pair in range(pairs):
                lo = pair * 128
                q = qkv_ref[at, lo : lo + 128]
                k = qkv_ref[at, width + lo : width + lo + 128]
                v = qkv_ref[at, 2 * width + lo : 2 * width + lo + 128]
                s = dot_nt(k, jnp.concatenate([q * m0, q * m1], 0)) + bias[pair]
                e = jnp.exp(s - jnp.max(s, 0, keepdims=True))
                p = (e / jnp.sum(e, 0, keepdims=True)).astype(BF)
                p1_ref[g, pair] = p
                o = dot_tn(
                    jnp.concatenate([p[:, :GROUP], p[:, GROUP:]], 0),
                    jnp.concatenate([v * m0, v * m1], 0),
                )
                o1_ref[at, lo : lo + 128] = o.astype(BF)
            p1_out.flush_part(pl.ds(g, 1))
            return carry

        lax.fori_loop(0, groups, attend, 0)
        o1_out.ref[...] = o1_ref[...]
        o1_out.flush()

    return call(
        "self_attention",
        body,
        (
            shape_of(BF, rows, width),
            shape_of(BF, rows, 3 * width),
            shape_of(BF, groups, pairs, GROUP, 2 * GROUP),
            shape_of(BF, rows, width),
            shape_of(BF, rows, width),
        ),
        [STREAM, VMEM, STREAM, SMEM],
        (DRAIN, DRAIN, DRAIN, NEAR, DRAIN),
        (x, gains, w_qkv, rel_bias.T),
        ahead=ahead,
        scratch=[pltpu.VMEM((pairs, GROUP, 2 * GROUP), F32)],
    )


def self_project(x, o1, w_self_out, gains, w_cross_q, ahead):
    rows, width = x.shape

    def body(x_ref, o1_ref, wso_ref, gc_ref, wcq_ref, h1_ref, cq_ref, h1_out, a2_out, cq_out):
        h1 = dot_nn(o1_ref[...], wso_ref[...]) + x_ref[...].astype(F32)
        h1_ref[...] = h1
        h1_out.ref[...] = h1
        h1_out.flush()
        a2 = (h1 * inv_rms(h1) * gc_ref[1:2, :]).astype(BF)
        a2_out.ref[...] = a2
        a2_out.flush()
        cq = dot_nn(a2, wcq_ref[...]).astype(BF)
        cq_ref[...] = cq
        cq_out.ref[...] = cq

    low, full = shape_of(BF, rows, width), shape_of(F32, rows, width)
    return call(
        "self_project",
        body,
        (full, low, full, low, low),
        [VMEM] * 5,
        (NEAR, NEAR, DRAIN, DRAIN, DRAIN),
        (x, o1, w_self_out, gains, w_cross_q),
        ahead=ahead,
    )


def cross_forward(
    pieces, order, shard_rows, tgt_question, cq, h1, w_cross_kv, w_cross_out, gains, ahead
):
    rows, width = cq.shape
    pairs = width // 128
    tokens = sum(len(o) for o in order) * shard_rows
    targets = rows // TLEN
    block_rows = query_block(rows, tokens)
    blocks = rows // block_rows
    steps = pairs * blocks

    def body(*refs):
        piece_refs = refs[: len(pieces)]
        (
            tq_ref, cq_ref, h1_ref, wkv_ref, wco_ref, gf_ref,
            enc_out, kv_out, e_ref, inv_out, o2_out, h2_out, a3_ref,
            kfeat, qfeat, ebuf, sem,
        ) = refs[len(pieces) :]
        enc_ref, kv_ref, inv_ref, o2_ref = enc_out.ref, kv_out.ref, inv_out.ref, o2_out.ref
        lane = lax.rem(lax.broadcasted_iota(jnp.int32, (shard_rows, 128), 1), 64).astype(F32)
        for ref, places in zip(piece_refs, order):
            for j, spot in enumerate(places):
                at = slice(spot * shard_rows, (spot + 1) * shard_rows)
                enc_ref[at, :] = ref[j, :shard_rows, :]
                tag = ref[j, shard_rows : shard_rows + 1, :shard_rows].astype(F32)
                tag = jnp.transpose(jnp.broadcast_to(tag, (128, shard_rows)))
                kfeat[at, :] = jnp.where(tag == lane, 0.0, NEG_LARGE).astype(BF)
        lane_t = lax.rem(lax.broadcasted_iota(jnp.int32, (TLEN, 128), 1), 64)
        for t in range(targets):
            qfeat[t * TLEN : (t + 1) * TLEN, :] = jnp.where(lane_t == tq_ref[t], 1.0, 0.0).astype(BF)
        enc_out.flush()

        def project(t, carry):
            at = pl.ds(pl.multiple_of(t * 384, 128), 384)
            kv_ref[:, at] = dot_nn(enc_ref[...], wkv_ref[:, at]).astype(BF)
            return carry

        lax.fori_loop(0, 2 * width // 384, project, 0)
        kv_out.flush()
        q0, q1 = half_masks(block_rows)
        k0, k1 = half_masks(tokens)
        qmask, kmask = (q0, q1), (k0, k1)
        low = lax.broadcasted_iota(jnp.int32, (block_rows, 128), 1) < 64

        def out_copy(slot, step):
            pair, block = step // blocks, lax.rem(step, blocks)
            return pltpu.make_async_copy(
                ebuf.at[slot],
                e_ref.at[pl.ds(2 * pair, 2), pl.ds(block * block_rows, block_rows)],
                sem.at[slot],
            )

        def attend(step, carry):
            slot = lax.rem(step, 2)
            pair, block = step // blocks, lax.rem(step, blocks)
            lo = pl.multiple_of(pair * 128, 128)
            at = pl.ds(pl.multiple_of(block * block_rows, block_rows), block_rows)

            @pl.when(step >= 2)
            def _():
                out_copy(slot, step - 2).wait()

            q = cq_ref[at, pl.ds(lo, 128)]
            k = kv_ref[:, pl.ds(lo, 128)]
            v = kv_ref[:, pl.ds(width + lo, 128)]
            keys = [k * kmask[h] + kfeat[...] * kmask[1 - h] for h in range(2)]
            values = [v * kmask[h] + kmask[1 - h] for h in range(2)]
            size = min(block_rows, 256)
            units = [(r, h) for r in range(0, block_rows, size) for h in range(2)]
            tagged = qfeat[at, :]

            def score(unit):
                r, h = unit
                qa = q[r : r + size] * qmask[h][:size] + tagged[r : r + size] * qmask[1 - h][:size]
                return dot_nt(qa, keys[h])

            outs, last = {}, None
            s = score(units[0])
            for i, unit in enumerate(units):
                later = score(units[i + 1]) if i + 1 < len(units) else None
                if last is not None:
                    outs[last[0]] = dot_nn(last[1], values[last[0][1]])
                e = jnp.exp(s - jnp.max(s, -1, keepdims=True)).astype(BF)
                ebuf[slot, unit[1], unit[0] : unit[0] + size, :] = e
                last, s = (unit, e), later
            outs[last[0]] = dot_nn(last[1], values[last[0][1]])
            outs = [
                jnp.concatenate([outs[r, h] for r in range(0, block_rows, size)], 0) for h in range(2)
            ]
            out_copy(slot, step).start()
            total = jnp.where(low, pltpu.roll(outs[0], 64, 1), pltpu.roll(outs[1], 64, 1))
            inv = 1.0 / total
            inv_ref[at, pl.ds(lo, 128)] = inv
            o2_ref[at, pl.ds(lo, 128)] = (jnp.where(low, outs[0], outs[1]) * inv).astype(BF)
            return carry

        lax.fori_loop(0, steps, attend, 0)
        inv_out.flush()
        o2_out.flush()
        h2 = h1_ref[...] + dot_nn(o2_ref[...], wco_ref[...])
        h2_out.ref[...] = h2
        h2_out.flush()
        a3_ref[...] = (h2 * inv_rms(h2) * gf_ref[2:3, :]).astype(BF)
        for step in range(max(0, steps - 2), steps):
            out_copy(step % 2, jnp.int32(step)).wait()

    return call(
        "cross_forward",
        body,
        (
            shape_of(BF, tokens, width),
            shape_of(BF, tokens, 2 * width),
            shape_of(BF, 2 * pairs, rows, tokens),
            shape_of(F32, rows, width),
            shape_of(BF, rows, width),
            shape_of(F32, rows, width),
            shape_of(BF, rows, width),
        ),
        [VMEM] * len(pieces) + [SMEM] + [VMEM] * 5,
        (DRAIN, DRAIN, (HBM, ANY), DRAIN, DRAIN, DRAIN, NEAR),
        (*pieces, tgt_question, cq, h1, w_cross_kv, w_cross_out, gains),
        scratch=[
            pltpu.VMEM((tokens, 128), BF),
            pltpu.VMEM((rows, 128), BF),
            pltpu.VMEM((2, 2, block_rows, tokens), BF),
            pltpu.SemaphoreType.DMA((2,)),
        ],
        limit=big(tokens),
        ahead=ahead,
    )


def hidden_gradient(gy, w_ff_out, ahead):
    rows, width = gy.shape
    hidden = w_ff_out.shape[0]

    tiles = hidden // width

    def body(gy_ref, w2_ref, out_ref, w2, sem):
        def copy(t):
            at = pl.ds(pl.multiple_of(t * width, 128), width)
            return pltpu.make_async_copy(w2_ref.at[at], w2.at[at], sem.at[t])

        for t in range(tiles):
            copy(t).start()

        def tile(t, carry):
            copy(t).wait()
            at = pl.ds(pl.multiple_of(t * width, 128), width)
            out_ref[:, at] = dot_nt(gy_ref[...], w2[at, :]).astype(BF)
            return carry

        lax.fori_loop(0, tiles, tile, 0)

    return call(
        "hidden_gradient",
        body,
        shape_of(BF, rows, hidden),
        [VMEM, (HBM, ANY)],
        NEAR,
        (gy, w_ff_out),
        scratch=[pltpu.VMEM((hidden, width), BF), pltpu.SemaphoreType.DMA((tiles,))],
        ahead=ahead,
    )


def feed_hidden(place, a3, gy, dhid, w_ff_in, columns):
    rows, width = a3.shape
    hidden = w_ff_in.shape[1]
    tile = width
    half = width // 2
    sub = hidden // width
    part = columns.part
    per_tile = columns.chunks * tile // hidden
    scale = math.sqrt(2.0 / math.pi)

    def body(place_ref, a3_ref, gy_ref, dhid_ref, w1_ref, dpre_ref, hid_out, both):
        def activate(pre, at):
            sq = pre * pre
            t = jnp.tanh(pre * (scale + (scale * 0.044715) * sq))
            up = 0.5 + 0.5 * t
            hid = (pre * up).astype(BF)
            slope = up + pre * (up - up * up) * ((2.0 * scale) + (2.0 * scale * 0.134145) * sq)
            hid_out.ref[:, at] = hid
            dpre_ref[:, at] = (dhid_ref[:, at].astype(F32) * slope).astype(BF)
            return hid

        def one(step, carry):
            parts = tile // 256
            ats = [pl.ds(pl.multiple_of(step * tile + i * 256, 128), 256) for i in range(parts)]
            a3, gyv = a3_ref[...], gy_ref[...]
            pre = dot_nn(a3, w1_ref[:, ats[0]])
            grads, hid = [], None
            for i in range(parts):
                later = dot_nn(a3, w1_ref[:, ats[i + 1]]) if i + 1 < parts else None
                if hid is not None:
                    grads.append(dot_tn(hid, gyv))
                hid = activate(pre, ats[i])
                pre = later
            grads.append(dot_tn(hid, gyv))
            hid_out.flush_part((slice(None), pl.ds(pl.multiple_of(step * tile, 128), tile)))
            g = jnp.concatenate(grads, 0)
            for i in range(per_tile):
                chunk = step * per_tile + i
                for h in range(2):
                    for j in range(sub):
                        first = (i * sub + j) * part
                        columns.store(
                            both.ref, h, "out", g[first : first + part, h * half : (h + 1) * half],
                            place_ref, [chunk], j * half // 128,
                        )
                for first, count in columns.runs():
                    unit = place_ref[columns.at + chunk * columns.blocks + first]
                    for drain in both.drains:
                        drain.flush_part(pl.ds(unit, count))
            return carry

        lax.fori_loop(0, hidden // tile, one, 0)

    return call(
        "feed_hidden",
        body,
        (shape_of(BF, rows, hidden), shape_of(BF, rows, hidden), columns.shape(), columns.shape()),
        [SMEM, VMEM, VMEM, VMEM, VMEM],
        (NEAR, DRAIN, PAIR, PAIR),
        (place, a3, gy, dhid, w_ff_in),
    )


def feed_weights(place, a3, dpre, columns, ahead):
    width = a3.shape[1]
    hidden = dpre.shape[1]

    def body(place_ref, a3_ref, dpre_ref, both):
        tiles = hidden // width

        def one(t, carry):
            at = pl.ds(pl.multiple_of(t * width, 128), width)
            g = dot_tn(a3_ref[...], dpre_ref[:, at])
            block = lax.rem(t, tiles // 2) * (width // 128)
            columns.store(both.ref, t // (tiles // 2), "in", g, place_ref, None, block)
            for slot in range(2):

                @pl.when(jnp.logical_and(t == tiles // 2 - 1, place_ref[0] == slot))
                def _():
                    both.drains[slot].flush_part(pl.ds(0, columns.units))

                @pl.when(jnp.logical_and(t == tiles - 1, place_ref[0] != slot))
                def _():
                    both.drains[slot].flush_part(pl.ds(0, columns.units))

            return carry

        lax.fori_loop(0, tiles, one, 0)

    return call(
        "feed_weights",
        body,
        (columns.shape(), columns.shape()),
        [SMEM, VMEM, VMEM],
        (PAIR, PAIR),
        (place, a3, dpre),
        ahead=ahead,
    )


def feed_back(dpre, w_ff_in, h2, gains, gy):
    rows, width = h2.shape

    def body(dpre_ref, w1_ref, h2_ref, gf_ref, gy_ref, dh2_ref, gain_ref, da3):
        da3[...] = jnp.zeros_like(da3)

        def one(t, carry):
            at = pl.ds(pl.multiple_of(t * width, 128), width)
            da3[...] += dot_nt(dpre_ref[:, at], w1_ref[:, at])
            return carry

        lax.fori_loop(0, dpre_ref.shape[1] // width, one, 0)
        dv, dgain = rms_back(da3[...], h2_ref[...], gf_ref[2:3, :])
        dh2_ref[...] = gy_ref[...].astype(F32) + dv
        gain_ref[...] = dgain

    return call(
        "feed_back",
        body,
        (shape_of(F32, rows, width), shape_of(F32, 1, width)),
        [VMEM] * 5,
        (NEAR, NEAR),
        (dpre, w_ff_in, h2, gains, gy),
        scratch=[pltpu.VMEM((rows, width), F32)],
    )


def feed_out(hid, w_ff_out, h2, ahead):
    rows, width = h2.shape

    def body(hid_ref, w2_ref, h2_ref, out, total):
        total[...] = h2_ref[...]

        def one(t, carry):
            at = pl.ds(pl.multiple_of(t * width, 128), width)
            total[...] += dot_nn(hid_ref[:, at], w2_ref[at, :])
            return carry

        lax.fori_loop(0, hid_ref.shape[1] // width, one, 0)
        out.ref[...] = total[...].astype(BF)

    return call(
        "feed_out",
        body,
        (shape_of(BF, rows, width),),
        [VMEM] * 3,
        (DRAIN,),
        (hid, w_ff_out, h2),
        scratch=[pltpu.VMEM((rows, width), F32)],
        ahead=ahead,
    )


def cross_backward(first_pair, last_pair, dh2, o2, inv, cq, kv, e, w_cross_out, ahead):
    rows, width = cq.shape
    pairs = width // 128
    count = last_pair - first_pair
    tokens = kv.shape[0]
    block_rows = query_block(rows, tokens)
    blocks = rows // block_rows

    def body(
        dh2_ref, wco_ref, o2_ref, inv_ref, cq_ref, k_ref, v_ref, e_ref,
        dcq_ref, dkt_ref, dvt_ref,
        do2,
    ):
        pair = pl.program_id(0)

        @pl.when(pair == 0)
        def _():
            do2v = dot_nt(dh2_ref[...].astype(BF), wco_ref[...]).astype(BF)
            for i in range(count):
                do2[i] = do2v[:, i * 128 : (i + 1) * 128]

        q0, q1 = half_masks(block_rows)
        k0, k1 = half_masks(tokens)
        qmask, kmask = (q0, q1), (k0, k1)
        lane = lax.broadcasted_iota(jnp.int32, (block_rows, 128), 1)
        low = lane < 64
        first = lax.rem(lane, 64) == 0
        second = lax.rem(lane, 64) == 1
        k, v = k_ref[...], v_ref[...]
        sums = [0.0] * 4
        for block in range(blocks):
            at = slice(block * block_rows, (block + 1) * block_rows)
            q = cq_ref[at, :]
            dof = do2[pair, at, :].astype(F32) * inv_ref[at, :]
            dob = dof.astype(BF)
            prod = dof * o2_ref[at, :].astype(F32)
            qt = jnp.transpose(q)
            dot_t = jnp.transpose(dob)
            dqs = []
            for h in range(2):
                own = low if h == 0 else jnp.logical_not(low)
                delta = -jnp.sum(jnp.where(own, prod, 0.0), -1, keepdims=True)
                hi = delta.astype(BF).astype(F32)
                feat = jnp.where(first, hi, jnp.where(second, delta - hi, 0.0)).astype(BF)
                doa = dob * qmask[h] + feat * qmask[1 - h]
                dp = dot_nt(doa, v * kmask[h] + kmask[1 - h])
                ev = e_ref[h, at, :]
                ds = (ev.astype(F32) * dp).astype(BF)
                dqs.append(dot_nn(ds, k))
                sums[h] = sums[h] + dot_nn(qt[h * 64 : (h + 1) * 64, :], ds)
                sums[2 + h] = sums[2 + h] + dot_nn(dot_t[h * 64 : (h + 1) * 64, :], ev)
            dcq_ref[at, :] = jnp.where(low, dqs[0], dqs[1]).astype(BF)
        for h in range(2):
            dkt_ref[h * 64 : (h + 1) * 64, :] = sums[h].astype(BF)
            dvt_ref[h * 64 : (h + 1) * 64, :] = sums[2 + h].astype(BF)

    near = HBM if big(tokens) else NEAR

    def column(n, first=first_pair):
        return pl.BlockSpec((n, 128), lambda p: (0, p + first))

    return call(
        "cross_backward",
        body,
        (
            shape_of(BF, rows, count * 128),
            shape_of(BF, count * 128, tokens),
            shape_of(BF, count * 128, tokens),
        ),
        [
            whole(rows, width),
            pl.BlockSpec((count * 128, width), lambda p: (first_pair // count, 0)),
            (HBM, column(rows)),
            (HBM, column(rows)),
            (HBM, column(rows)),
            (HBM, column(tokens)),
            (HBM, column(tokens, first_pair + pairs)),
            (HBM, pl.BlockSpec((2, rows, tokens), lambda p: (p + first_pair, 0, 0))),
        ],
        (
            (NEAR, column(rows, 0)),
            (near, pl.BlockSpec((128, tokens), lambda p: (p, 0))),
            (near, pl.BlockSpec((128, tokens), lambda p: (p, 0))),
        ),
        (dh2, w_cross_out, o2, inv, cq, kv, kv, e),
        scratch=[pltpu.VMEM((count, rows, 128), BF)],
        grid=(count,),
        ahead=ahead,
        limit=big(tokens),
    )


def cross_query_back(dcq, w_cross_q, h1, gains, dh2):
    rows, width = h1.shape
    n = len(dcq)
    size = width // n

    def body(*refs):
        wcq_ref, h1_ref, gc_ref, dh2_ref, dh1_ref, gain_ref = refs[n:]
        da2 = 0.0
        for i in range(n):
            da2 = da2 + dot_nt(refs[i][...], wcq_ref[:, i * size : (i + 1) * size])
        dv, dgain = rms_back(da2, h1_ref[...], gc_ref[1:2, :])
        dh1_ref[...] = dh2_ref[...] + dv
        gain_ref[...] = dgain

    return call(
        "cross_query_back",
        body,
        (shape_of(F32, rows, width), shape_of(F32, 1, width)),
        [VMEM] * (n + 4),
        (NEAR, NEAR),
        (*dcq, w_cross_q, h1, gains, dh2),
    )


def shard_rows_of(tokens, chunks):
    return tokens // chunks


def cross_weights(place, dh2, o2, dcq, dkt, dvt, enc, a2, w_cross_kv, dh1, o1, columns, ahead):
    rows, width = dh2.shape
    tokens = enc.shape[0]
    half = width // 2
    tile = max(shard_rows_of(tokens, columns.chunks), 512)
    n = len(dcq)
    size = width // n
    blocks = width // 128
    near = 2 * blocks // 3
    shard_rows = tokens // columns.chunks

    def body(place_ref, dh2_ref, dh1_ref, a2_ref, o2_ref, o1_ref, *refs):
        dcq_refs, dkt, dvt = refs[:n], refs[n : 2 * n], refs[2 * n : 3 * n]
        wkv_ref, enc_ref, genc_out, both, lhs, rhs, dkvt = refs[3 * n :]
        for i, r in enumerate(dcq_refs):
            rhs[0, :, i * size : (i + 1) * size] = r[...]
        rhs[1] = dh2_ref[...].astype(BF)
        rhs[2] = dh1_ref[...].astype(BF)
        for i, r in enumerate((a2_ref, o2_ref, o1_ref)):
            lhs[i] = r[...]
        for i, r in enumerate(dkt + dvt):
            dkvt[i * size : (i + 1) * size, :] = r[...]

        def square(i, carry):
            g = dot_tn(lhs[i], rhs[i])
            for h in range(2):
                columns.store(both.ref, h, "q", g[:, h * half : (h + 1) * half], place_ref, None, i * (half // 128))
            return carry

        lax.fori_loop(0, 3, square, 0)

        def encodings(t, carry):
            at = pl.ds(pl.multiple_of(t * tile, 128), tile)
            genct = dot_nn(wkv_ref[...], dkvt[:, at]).astype(BF)
            for i in range(tile // shard_rows):
                for j in range(blocks):
                    order = 0 if j < near else 1
                    size = blocks - near if order else near
                    spot = place_ref[3 + order * columns.chunks + t * (tile // shard_rows) + i]
                    genc_out.ref[order * columns.chunks * near + spot * size + j - order * near] = genct[
                        j * 128 : (j + 1) * 128, i * shard_rows : (i + 1) * shard_rows
                    ]
            return carry

        lax.fori_loop(0, tokens // tile, encodings, 0)
        genc_out.flush()

        def key_value(h, carry):
            g = 0.0
            rows_at = pl.ds(pl.multiple_of(h * width, 128), width)
            for t in range(0, tokens, 1024):
                end = min(tokens, t + 1024)
                g = g + dot_nt(jnp.transpose(enc_ref[t:end, :]), dkvt[rows_at, t:end])
            columns.store(both.ref, h, "kv", g, place_ref)
            return carry

        lax.fori_loop(0, 2, key_value, 0)

    return call(
        "cross_weights",
        body,
        (shape_of(BF, columns.chunks * blocks, 128, shard_rows), columns.shape(), columns.shape()),
        [SMEM] + [VMEM] * (3 * n + 7),
        (DRAIN, PAIR, PAIR),
        (place, dh2, dh1, a2, o2, o1, *dcq, *dkt, *dvt, w_cross_kv, enc),
        scratch=[
            pltpu.VMEM((3, rows, width), BF),
            pltpu.VMEM((3, rows, width), BF),
            pltpu.VMEM((2 * width, tokens), BF),
        ],
        ahead=ahead,
        limit=big(tokens),
    )


def self_backward(dh1, w_self_out, qkv, p1, bucket_count, heads, ahead):
    rows, width = dh1.shape
    pairs = heads // 2
    groups = rows // GROUP
    firsts = bucket_firsts(bucket_count)
    ends = [first for _, first in firsts[1:]] + [TLEN]

    def body(dh1_ref, wso_ref, qkv_ref, p1_ref, dqkv_ref, gbias_ref, do1, acc):
        do1[...] = dot_nt(dh1_ref[...].astype(BF), wso_ref[...]).astype(BF)
        m0, m1 = half_masks(GROUP)
        acc[...] = jnp.zeros_like(acc)

        def attend(g, carry):
            at = pl.ds(pl.multiple_of(g * GROUP, GROUP), GROUP)
            for pair in range(pairs):
                lo = pair * 128
                q = qkv_ref[at, lo : lo + 128]
                k = qkv_ref[at, width + lo : width + lo + 128]
                v = qkv_ref[at, 2 * width + lo : 2 * width + lo + 128]
                do = do1[at, lo : lo + 128]
                do_two = jnp.concatenate([do * m0, do * m1], 0)
                pb = p1_ref[g, pair]
                pf = pb.astype(F32)
                dp = dot_nt(v, do_two)
                ds = (pf * (dp - jnp.sum(pf * dp, 0, keepdims=True))).astype(BF)
                dsf = ds.astype(F32)
                total = dsf[:TLEN]
                for t in range(1, GROUP // TLEN):
                    total = total + dsf[t * TLEN : (t + 1) * TLEN]
                acc[2 * pair] += total[:, :GROUP]
                acc[2 * pair + 1] += total[:, GROUP:]
                dq = dot_tn(
                    jnp.concatenate([ds[:, :GROUP], ds[:, GROUP:]], 0),
                    jnp.concatenate([k * m0, k * m1], 0),
                )
                dk = dot_nn(ds, jnp.concatenate([q * m0, q * m1], 0))
                dv = dot_nn(pb, do_two)
                dqkv_ref[at, lo : lo + 128] = dq.astype(BF)
                dqkv_ref[at, width + lo : width + lo + 128] = dk.astype(BF)
                dqkv_ref[at, 2 * width + lo : 2 * width + lo + 128] = dv.astype(BF)
            return carry

        lax.fori_loop(0, groups, attend, 0)
        row = lax.broadcasted_iota(jnp.int32, (TLEN, GROUP), 0)
        distance = lax.rem(lax.broadcasted_iota(jnp.int32, (TLEN, GROUP), 1), TLEN) - row
        lane = lax.broadcasted_iota(jnp.int32, (16, 128), 1)
        bias = jnp.zeros((16, 128), F32)
        accv = acc[...]
        pad = jnp.zeros((16 - heads, 1), F32)
        for (b, first), end in zip(firsts, ends):
            here = jnp.logical_and(distance >= first, distance < end)
            part_sum = jnp.sum(jnp.where(here[None], accv, 0.0), axis=1)
            col = jnp.sum(part_sum, -1, keepdims=True)
            bias = jnp.where(lane == b, jnp.concatenate([col, pad], 0), bias)
        gbias_ref[...] = bias

    return call(
        "self_backward",
        body,
        (shape_of(BF, rows, 3 * width), shape_of(F32, 16, 128)),
        [VMEM] * 4,
        (NEAR, NEAR),
        (dh1, w_self_out, qkv, p1),
        ahead=ahead,
        scratch=[pltpu.VMEM((rows, width), BF), pltpu.VMEM((heads, TLEN, GROUP), F32)],
    )


def self_weights(
    place, dh1, a1, dqkv, x, gains, w_qkv, gbias, gain_cross_grad, gain_ff_grad, columns
):
    rows, width = dh1.shape
    half = width // 2
    part = columns.part
    misc_rows = 16 + width // 16
    more = -(-misc_rows // part)

    def body(
        place_ref, dh1_ref, wqkv_ref, x_ref, a1_ref, dqkv_ref, gs_ref, gb_ref, ggc_ref, ggf_ref,
        out, both, da1,
    ):
        da1[...] = jnp.zeros_like(da1)

        def one(t, carry):
            at = pl.ds(pl.multiple_of(t * width, 128), width)
            da1[...] += dot_nt(dqkv_ref[:, at], wqkv_ref[:, at])
            return carry

        lax.fori_loop(0, 3, one, 0)
        dv, dgain = rms_back(da1[...], x_ref[...].astype(F32), gs_ref[0:1, :])
        out.ref[...] = dh1_ref[...] + dv
        out.flush()

        def weights(h, carry):
            at = pl.ds(pl.multiple_of(h * 3 * half, 128), 3 * half)
            columns.store(both.ref, h, "qkv", dot_tn(a1_ref[...], dqkv_ref[:, at]), place_ref)
            return carry

        lax.fori_loop(0, 2, weights, 0)
        gains = jnp.concatenate([dgain, ggc_ref[...], ggf_ref[...], jnp.zeros((5, width), F32)], 0)
        misc = [gb_ref[...]] + [gains[:, j * 128 : (j + 1) * 128] for j in range(width // 128)]
        misc.append(jnp.zeros((more * part - misc_rows, 128), F32))
        misc = jnp.concatenate(misc, 0).astype(BF)
        for i in range(more):
            for slot in range(2):
                both.ref[slot, columns.units + i] = misc[i * part : (i + 1) * part]

    return call(
        "self_weights",
        body,
        (shape_of(F32, rows, width), columns.shape(more), columns.shape(more)),
        [SMEM] + [VMEM] * 9,
        (DRAIN, PAIR, PAIR),
        (
            place, dh1, w_qkv, x, a1, dqkv, gains, gbias,
            gain_cross_grad, gain_ff_grad,
        ),
        scratch=[pltpu.VMEM((rows, width), F32)],
    )


def swap(value, axis, bit):
    size = lax.axis_size(axis)
    return lax.ppermute(value, axis, [(i, i ^ bit) for i in range(size)])


class Bucket:
    def __init__(self, rows, terms, steps, keep_all=False):
        self.rows, self.terms, self.steps, self.keep_all = rows, terms, list(steps), keep_all


def sum_kernel(groups, dtype=BF):
    operands, specs, plan = [], [], []
    for i, jobs in enumerate(groups):
        at = 0
        for rows, terms in jobs:
            plan.append((i, at, rows, len(operands), len(terms)))
            at += rows
            for array, off in terms:
                operands.append(array)
                spec = (pl.Element(rows), pl.Element(128))
                specs.append(pl.BlockSpec(spec, functools.partial(lambda off, *_: (off, 0), off)))
    sizes = [sum(rows for rows, _ in jobs) for jobs in groups]

    def body(*refs):
        outs = refs[len(operands) :]
        for i, at, rows, first, count in plan:
            total = refs[first][...].astype(F32)
            for r in refs[first + 1 : first + count]:
                total = total + r[...].astype(F32)
            outs[i][at : at + rows, :] = total.astype(dtype)

    return call(
        "sum_kernel",
        body,
        tuple(shape_of(dtype, size, 128) for size in sizes),
        specs,
        tuple(whole(size, 128) for size in sizes),
        operands,
        grid=(1,),
    )


def send_round(cost, *members, settle=()):
    groups = {}
    for m in members:
        step = m.steps[0]
        groups.setdefault((step, m) if isinstance(m, Total) else step, []).append(m)
    jobs = []
    for group in groups.values():
        jobs.append([])
        for m in group:
            if isinstance(m, Total):
                jobs[-1] += m.next_jobs()
            elif m.keep_all:
                jobs[-1].append((m.rows, m.terms))
            else:
                m.rows //= 2
                jobs[-1].append((m.rows, [(array, off + m.rows) for array, off in m.terms]))
    settle = [b for b in settle if not b.steps]
    if settle:
        jobs.append([(b.rows, b.terms) for b in settle])
    sent = sum_kernel(jobs)
    at = 0
    for b in settle:
        b.terms = [(sent[-1], at)]
        at += b.rows
    for group, payload in zip(groups.values(), sent):
        axis, bit = group[0].steps[0]
        got = swap(payload, axis, bit)
        at = 0
        for m in group:
            m.steps.pop(0)
            if isinstance(m, Total):
                m.moved(payload, got)
                continue
            if m.keep_all:
                m.terms = [(payload, at), (got, at)]
            else:
                m.terms = m.terms + [(got, at)]
            at += m.rows
    shadow(cost)


def rest_of(*buckets):
    while any(b.steps for b in buckets):
        send_round(3, *[b for b in buckets if b.steps])


def weight_buckets(columns, keep, send, orders, y_bits):
    rows = columns.units * columns.part
    keep, send = in_hbm(keep.reshape(-1, 128)), send.reshape(-1, 128)
    got = swap(send, "dp", 1)
    over = [[("blk", b) for b in order] for order in orders]
    along = [("dp", 2 * b) for b in y_bits]
    buckets = []
    for _, blocks, order, unit in columns.sections:
        steps = along + over[0] if order == "y" else over[order]
        at = unit * columns.part
        size = blocks * columns.chunks * columns.part
        buckets.append(Bucket(size, [(keep, at), (got, at)], steps))
    if keep.shape[0] > rows:
        buckets.append(Bucket(keep.shape[0] - rows, [(keep, rows), (got, rows)], over[0], keep_all=True))
    return buckets


def join_encodings(buckets, shard_rows, width):
    terms = [(bucket, array, off) for bucket in buckets for array, off in bucket.terms]

    def body(*refs):
        out = refs[-1]
        first = col = 0
        for bucket in buckets:
            mine = refs[first : first + len(bucket.terms)]
            first += len(bucket.terms)
            for at in range(0, bucket.rows, 128):
                total = mine[0][at : at + 128, :].astype(F32)
                for r in mine[1:]:
                    total = total + r[at : at + 128, :].astype(F32)
                out[:, col : col + 128] = jnp.transpose(total)
                col += 128

    return call(
        "join_encodings",
        body,
        shape_of(F32, shard_rows, width),
        [
            pl.BlockSpec(
                (pl.Element(bucket.rows), pl.Element(shard_rows)),
                functools.partial(lambda off, *_: (off, 0), off),
            )
            for bucket, _, off in terms
        ],
        whole(shard_rows, width),
        [array for _, array, _ in terms],
        grid=(1,),
    )


class Total:
    def __init__(self, groups, small, dp_size):
        self.groups, self.small, self.dp_size = groups, small, dp_size
        self.jobs, self.bases = [], []
        at = 0
        for _, buckets in groups:
            base = []
            for bucket in buckets:
                self.jobs.append((bucket.rows, bucket.terms))
                base.append(at)
                at += bucket.rows
            self.bases.append(base)
        self.small_at = []
        for bucket in small:
            self.jobs.append((bucket.rows, bucket.terms))
            self.small_at.append((at, bucket.rows))
            at += bucket.rows
        self.rows = at
        self.steps = [("dp", 2 * m) for m in range(1, dp_size // 2)] + [("dp", 1)]
        self.parts = []

    def next_jobs(self):
        if len(self.steps) > 1 or not self.parts:
            return [(self.rows, [(self.parts[0], 0)])] if self.parts else self.jobs
        jobs, self.spots, at = [], [], 0
        for (columns, _), base in zip(self.groups, self.bases):
            spots = []
            for (_, blocks, order, _), first in zip(columns.sections, base):
                if order == "y":
                    rows = blocks // columns.y_parts * columns.part
                    spots.append([at + i * rows for i in range(len(self.parts))])
                    jobs += [(rows, [(p, first)]) for p in self.parts]
                    at += rows * len(self.parts)
                else:
                    rows = blocks * columns.part
                    spots.append(at)
                    jobs.append((rows, [(p, first) for p in self.parts]))
                    at += rows
            self.spots.append(spots)
        self.small_spots = []
        for first, rows in self.small_at:
            jobs.append((rows, [(p, first) for p in self.parts]))
            self.small_spots.append((at, rows))
            at += rows
        return jobs

    def moved(self, payload, got):
        if self.steps or not self.parts:
            self.parts = self.parts + [got] if self.parts else [payload, got]
        else:
            self.own, self.other = payload, got

    def finish(self, place, arrays):
        outs = []
        for (columns, _), spots, named in zip(self.groups, self.spots, arrays):
            for name, stack in named:
                outs.append((columns, spots, name, stack, dict(columns.names)[name] // stack))
        y_parts = self.dp_size // 2

        def body(place_ref, own_ref, other_ref, *refs):
            core, y = place_ref[0], place_ref[2]
            sides = ((core, own_ref), (1 - core, other_ref))

            def put(ref, columns, half, j, at):
                row, off = divmod(j * 128, half)
                for which, src in sides:
                    lane = pl.multiple_of(which * half + off, 128)
                    ref[row * columns.part : (row + 1) * columns.part, pl.ds(lane, 128)] = src[
                        at : at + columns.part, :
                    ].astype(F32)

            for ref, (columns, spots, name, stack, half) in zip(refs, outs):
                far = []
                for j in range(stack * half // 128):
                    i, y_of, k = columns.find(columns.first(name) + j)
                    if y_of is None:
                        put(ref, columns, half, j, spots[i] + k * columns.part)
                    else:
                        far.append((j, spots[i], y_of, k))
                for y_is in range(y_parts if far else 0):

                    @pl.when(y == y_is)
                    def _():
                        for j, at, y_of, k in far:
                            put(ref, columns, half, j, at[y_is ^ y_of] + k * columns.part)

            for ref, (at, rows) in zip(refs[len(outs) :], self.small_spots):
                ref[...] = own_ref[at : at + rows, :].astype(F32)

        shapes = [shape_of(F32, stack * columns.part, 2 * half) for columns, _, _, stack, half in outs]
        shapes += [shape_of(F32, rows, 128) for _, rows in self.small_spots]
        return call(
            "finish",
            body,
            tuple(shapes),
            [SMEM, VMEM, VMEM],
            (VMEM,) * len(shapes),
            (place, self.own, self.other),
        )


def gather_encodings(own, bits):
    if len(bits) == 3:
        x, z, far = bits
        r_far, r_x = swap(own, "blk", far), swap(own, "blk", x)

        def second():
            r_z, r_zf = swap(own, "blk", z), swap(r_far, "blk", z)
            r_xf = swap(r_far, "blk", x)

            def third():
                r_xz = swap(r_z, "blk", x)
                r_xzf = swap(r_xf, "blk", z)
                arrays = [own, r_far, r_x, r_z, r_zf, r_xf, r_xz, r_xzf]
                return arrays, [[0], [far], [x], [z], [z | far], [x | far], [x | z], [x | z | far]]

            return [r_z, r_zf, r_xf], third

        return [r_far, r_x], second
    got, rel = own, [0]
    for bit in reversed(bits):
        got = jnp.concatenate([got, swap(got, "blk", bit)], 0)
        rel = rel + [r ^ bit for r in rel]
    return [], lambda: ([], lambda: ([got], [rel]))


def local(
    dec_in,
    encodings,
    enc_question,
    enc_valid,
    tgt_question,
    gain_self,
    w_qkv,
    rel_bias,
    w_self_out,
    gain_cross,
    w_cross_q,
    w_cross_kv,
    w_cross_out,
    gain_ff,
    w_ff_in,
    w_ff_out,
    grad_out,
):
    x = dec_in[0]
    gy = grad_out[0]
    rows, width = x.shape
    bucket_count, heads = rel_bias.shape
    hidden = w_ff_in.shape[1]
    half = width // 2
    chunks = lax.axis_size("blk")
    part = width // chunks
    dp_size = lax.axis_size("dp")
    shard_rows = encodings.shape[1]
    bits = [1 << i for i in range(chunks.bit_length() - 1)]
    y_bits = [1 << i for i in range(dp_size.bit_length() - 2)]
    y_parts = dp_size // 2
    blk = lax.axis_index("blk")
    dp = lax.axis_index("dp")
    orders = [bits, bits[1::-1] + bits[2:]]

    def layout(names, *sections):
        return Columns(names, sections, y_parts, chunks, part)

    def along_y(blocks):
        return blocks // (2 * y_parts) * y_parts

    stack = hidden // width
    blocks = half // 128
    cols_out = layout([("out", stack * half)], (stack * blocks, "y"))
    cols_in = layout([("in", hidden // 2)], (stack * blocks // 2, 0), (stack * blocks // 2, 1))
    far_x, far_s = along_y(16 * blocks // 3), along_y(4 * blocks)
    near_x, near_s = 5 * blocks - far_x, 3 * blocks - far_s
    cols_x = layout(
        [("q", half), ("out", half), ("self", half), ("kv", width)],
        (near_x, 0), (far_x, "y"),
    )
    cols_s = layout([("qkv", 3 * half)], (near_s, 0), (far_s, "y"))

    places = [[chunk_place(c, blk, order) for c in range(chunks)] for order in orders]
    y_places = [chunk_place(y, dp // 2, y_bits) for y in range(y_parts)]
    numbers = [lax.rem(dp, 2), blk, dp // 2]
    for order in orders:
        spots = [0] * chunks
        for r in range(chunks):
            spots[chunk_spot(r, bits)] = chunk_spot(r, order)
        numbers += [jnp.int32(spot) for spot in spots]
    for columns in (cols_out, cols_in, cols_x, cols_s):
        columns.at = len(numbers)
        numbers += columns.table(places, y_places)
    place = jnp.stack(numbers).astype(jnp.int32)

    ORDER.clear()
    ROOMY[:] = [chunks * shard_rows <= 1024]
    tags = jnp.where(enc_valid[0] == 1, enc_question[0], -1).astype(BF)
    tag_rows = jnp.zeros((16, width), BF).at[0, :shard_rows].set(tags)
    enc_own = jnp.concatenate([encodings[0], tag_rows], 0)[None]
    gains = jnp.stack([gain_self, gain_cross, gain_ff])
    got, second = gather_encodings(enc_own, bits)
    shadow(10)
    a1, qkv, p1, o1_near, o1, wso_near, wcq_near, x_near = self_attention(
        x, gains, w_qkv, rel_bias, [w_self_out, w_cross_q, x]
    )
    more, third = second()
    shadow(10)
    h1_near, cq_near, h1, a2, cq, gy = self_project(
        x_near, o1_near, wso_near, gains, wcq_near, [gy]
    )
    pieces, rel = third()
    shadow(10)
    dhid, wkv_near, wco_near = hidden_gradient(gy, w_ff_out, [w_cross_kv, w_cross_out])
    spots = [[int(chunk_spot(r, bits)) for r in group] for group in rel]
    enc, kv, e, inv, o2, h2, a3, w1_near = cross_forward(
        pieces, spots, shard_rows, tgt_question[0], cq_near, h1_near, wkv_near, wco_near, gains, [w_ff_in]
    )

    dpre, hid, keep, send = feed_hidden(place, a3, gy, dhid, w1_near, cols_out)
    (b_out,) = weight_buckets(cols_out, keep, send, orders, y_bits)
    shadow(30)
    keep, send, h2_near = feed_weights(place, a3, dpre, cols_in, [h2])
    b_in, b_jn = weight_buckets(cols_in, keep, send, orders, y_bits)
    send_round(30, b_out)
    dh2, gain_ff_grad = feed_back(dpre, w1_near, h2_near, gains, gy)
    send_round(8, b_in, b_jn)
    pairs = heads // 2
    parts_a = cross_backward(0, pairs // 2, dh2, o2, inv, cq, kv, e, wco_near, [])
    parts_b = cross_backward(
        pairs // 2, pairs, dh2, o2, inv, cq, kv, e, wco_near, [w_cross_q, h1, a2, o2, o1, enc, w_cross_kv]
    )
    wcq_near, h1_near, a2, o2, o1, enc, wkv_near = parts_b[3:]
    dcq, dkt, dvt = zip(parts_a, parts_b[:3])
    dh1, gain_cross_grad = cross_query_back(dcq, wcq_near, h1_near, gains, dh2)
    send_round(12, b_jn, b_out, b_in)
    genc, keep, send, hid, w2_near, h2_near = cross_weights(
        place, dh2, o2, dcq, dkt, dvt, enc, a2, wkv_near, dh1, o1, cols_x, [hid, w_ff_out, h2]
    )
    enc_rows = chunks * shard_rows * width // 128
    genc = in_hbm(genc.reshape(enc_rows, shard_rows))
    cut = enc_rows // blocks * (2 * blocks // 3)
    b_ea = Bucket(cut, [(genc, 0)], [("blk", b) for b in orders[0]])
    b_eb = Bucket(enc_rows - cut, [(genc, cut)], [("blk", b) for b in orders[1]])
    b_xa, b_xb = weight_buckets(cols_x, keep, send, orders, y_bits)
    out, wso_near, qkv, p1 = feed_out(hid, w2_near, h2_near, [w_self_out, qkv, p1])
    send_round(40, b_ea, b_out, b_eb, b_jn)
    dqkv, gbias, wqkv_near, x_near, a1 = self_backward(
        dh1, wso_near, qkv, p1, bucket_count, heads, [w_qkv, x, a1]
    )
    send_round(8, b_xb, b_xa, b_eb, b_ea, b_in, b_out, settle=[b_jn])
    grad_dec, keep, send = self_weights(
        place, dh1, a1, dqkv, x_near, gains, wqkv_near, gbias, gain_cross_grad, gain_ff_grad, cols_s
    )
    b_sa, b_sb, b_misc = weight_buckets(cols_s, keep, send, orders, y_bits)
    send_round(25, b_xb, b_xa, b_ea, b_eb, settle=[b_in, b_out])
    send_round(4, b_sb, b_sa, b_misc)
    rest_of(b_out, b_in, b_jn)
    total_ff = Total([(cols_out, [b_out]), (cols_in, [b_in, b_jn])], [], dp_size)
    send_round(4, b_xa, b_xb, total_ff, settle=[b_ea, b_eb])
    rest_of(b_ea, b_eb)
    send_round(4, b_sa, b_misc, b_sb)
    send_round(4, b_xb, b_sa, b_misc, total_ff)
    grad_enc = join_encodings([b_ea, b_eb], shard_rows, width)
    send_round(4, b_sb)
    rest_of(total_ff)
    grad_ff_out, grad_ff_in = total_ff.finish(place, [[("out", stack)], [("in", 1)]])
    send_round(4, b_sb)
    rest_of(b_xa, b_xb)
    total_x = Total([(cols_x, [b_xa, b_xb])], [], dp_size)
    send_round(4, total_x)
    rest_of(b_sa, b_sb, b_misc)
    total_s = Total([(cols_s, [b_sa, b_sb])], [b_misc], dp_size)
    send_round(4, total_s, total_x)
    rest_of(total_s, total_x)
    grad_cross_out, grad_cross_q, grad_self_out, grad_cross_kv = total_x.finish(
        place, [[("out", 1), ("q", 1), ("self", 1), ("kv", 1)]]
    )
    grad_qkv, misc = total_s.finish(place, [[("qkv", 1)]])
    gains = misc[16 : 16 + width // 16].reshape(width // 128, 8, 128)[:, :3].transpose(1, 0, 2).reshape(3, width)
    gains = lax.dynamic_slice(gains, (0, blk * part), (3, part))
    bias_part = bucket_count // chunks
    grad_bias = lax.dynamic_slice(misc, (0, blk * bias_part), (heads, bias_part)).T
    return (
        out[None],
        grad_dec[None],
        grad_enc[None],
        gains[0],
        grad_qkv,
        grad_bias,
        grad_self_out,
        gains[1],
        grad_cross_q,
        grad_cross_kv,
        grad_cross_out,
        gains[2],
        grad_ff_in,
        grad_ff_out,
    )


def solution(mesh):
    return jax.shard_map(
        local,
        mesh=mesh,
        in_specs=(
            P("dp", "blk", None),
            P("dp", "blk", None),
            P("dp", "blk"),
            P("dp", "blk"),
            P("dp", "blk"),
            P(),
            P(),
            P(),
            P(),
            P(),
            P(),
            P(),
            P(),
            P(),
            P(),
            P(),
            P("dp", "blk", None),
        ),
        out_specs=(
            P("dp", "blk", None),
            P("dp", "blk", None),
            P("dp", "blk", None),
            P("blk"),
            P("blk", None),
            P("blk", None),
            P("blk", None),
            P("blk"),
            P("blk", None),
            P("blk", None),
            P("blk", None),
            P("blk"),
            P("blk", None),
            P("blk", None),
        ),
        check_vma=False,
    )
```

```python
import functools
import math

import jax
import jax.numpy as jnp
import numpy as np
from jax import lax
from jax.experimental import pallas as pl
from jax.experimental.pallas import tpu as pltpu
from jax.sharding import PartitionSpec as P

TLEN = 32
EPSILON = 1e-06
NEG_LARGE = -1e30
GROUP = 128
LOG2E = 1.4426950408889634
BF = jnp.bfloat16
F32 = jnp.float32
VMEM = pl.BlockSpec(memory_space=pltpu.VMEM)
SMEM = pl.BlockSpec(memory_space=pltpu.SMEM)
ANY = pl.BlockSpec(memory_space=pl.ANY)
HBM, STREAM, DRAIN, NEAR, PAIR = "hbm", "stream", "drain", "near", "pair"
MIB = 2**20
LIMITS = dict(
    self_attention=24, self_project=12, cross_forward=30, hidden_gradient=10, feed_hidden=26, feed_weights=18,
    feed_back=12, feed_out=12, cross_backward=20, cross_query_back=12, cross_weights=34, self_backward=14,
    self_weights=24, sum_kernel=16, finish=24, shadow=1, join_encodings=8,
)


def bucket_of(distance, bucket_count):
    exact_count = bucket_count // 2
    if distance < exact_count:
        return distance
    scaled = math.log(distance / exact_count) / math.log(128.0 / exact_count) * exact_count
    return min(bucket_count - 1, exact_count + int(scaled))


def bucket_firsts(bucket_count):
    firsts = {}
    for distance in range(TLEN):
        firsts.setdefault(bucket_of(distance, bucket_count), distance)
    return sorted(firsts.items())


def dot_nn(a, b):
    return jnp.dot(a, b, preferred_element_type=F32)


def dot_nt(a, b):
    return lax.dot_general(a, b, (((1,), (1,)), ((), ())), preferred_element_type=F32)


def dot_tn(a, b):
    return lax.dot_general(a, b, (((0,), (0,)), ((), ())), preferred_element_type=F32)


def inv_rms(v):
    return lax.rsqrt(jnp.mean(v * v, axis=-1, keepdims=True) + EPSILON)


def rms_back(dy, v, gain):
    r = inv_rms(v)
    vr = v * r
    dg = dy * gain
    dv = r * (dg - vr * jnp.mean(dg * vr, axis=-1, keepdims=True))
    return dv, jnp.sum(dy * vr, axis=0, keepdims=True)


def half_masks(rows):
    lane = lax.broadcasted_iota(jnp.int32, (rows, 128), 1)
    low = (lane < 64).astype(F32)
    return low.astype(BF), (1.0 - low).astype(BF)


def chunk_place(chunk, blk, bits):
    rel = jnp.bitwise_xor(chunk, blk)
    place = jnp.int32(0)
    for bit in bits:
        place = place * 2 + jnp.where(jnp.bitwise_and(rel, bit) != 0, 1, 0)
    return place


def chunk_spot(rel, bits):
    spot = 0
    for bit in bits:
        spot = spot * 2 + (1 if rel & bit else 0)
    return spot


def query_block(rows, tokens):
    return max(GROUP, min(rows, rows * 1024 // tokens))


def big(tokens):
    return 61 if tokens > 1024 else None


class Stream:
    def __init__(self, copy, ref):
        self.copy, self.ref, self.waited = copy, ref, False

    def ready(self):
        if not self.waited:
            self.copy.wait()
            self.waited = True
        return self.ref


class Drain:
    def __init__(self, copy, ref, out, sem):
        self.copy, self.ref, self.started = copy, ref, False
        self.out, self.sem = out, sem

    def flush(self):
        self.copy.start()
        self.started = True

    def flush_part(self, at):
        pltpu.make_async_copy(self.ref.at[at], self.out.at[at], self.sem).start()
        self.started = True


ORDER = []
ROOMY = [True]


class Pair:
    def __init__(self, drains, ref):
        self.drains, self.ref = drains, ref


def in_hbm(x):
    return pltpu.with_memory_space_constraint(x, pltpu.HBM)


def call(
    name, body, out_shape, in_specs, out_specs, operands, scratch=(), grid=(), prefetch=0,
    limit=None, cost=0.001, ahead=(),
):
    operands, in_specs = list(operands), list(in_specs)
    after = list(ORDER)
    wanted = ahead
    ahead = wanted if ROOMY[0] else ()
    outs = isinstance(out_shape, (tuple, list))
    out_shape = list(out_shape) if outs else [out_shape]
    out_specs = list(out_specs) if outs else [out_specs]
    streams, drains, pairs = [], [], []
    extra_scratch = []
    for i, spec in enumerate(in_specs):
        at = prefetch + i
        if spec == STREAM:
            streams.append(at)
            in_specs[i] = ANY
            operands[at] = in_hbm(operands[at])
            extra_scratch += [pltpu.VMEM(operands[at].shape, operands[at].dtype), pltpu.SemaphoreType.DMA]
        elif isinstance(spec, tuple):
            in_specs[i] = spec[1]
            operands[at] = in_hbm(operands[at])
    real = prefetch + len(in_specs)
    for i, spec in enumerate(out_specs):
        shape = out_shape[i]
        if spec == PAIR:
            pairs.append(i)
            out_specs[i] = ANY
            out_shape[i] = pltpu.HBM(shape.shape, shape.dtype)
            if len(pairs) % 2:
                extra_scratch += [
                    pltpu.VMEM((2, *shape.shape), shape.dtype), pltpu.SemaphoreType.DMA((2,))
                ]
        elif spec == DRAIN:
            drains.append(i)
            out_specs[i] = ANY
            out_shape[i] = pltpu.HBM(shape.shape, shape.dtype)
            extra_scratch += [pltpu.VMEM(shape.shape, shape.dtype), pltpu.SemaphoreType.DMA]
        elif spec == NEAR or isinstance(spec, tuple):
            space = pltpu.VMEM if spec == NEAR or spec[0] == NEAR else pltpu.HBM
            out_specs[i] = VMEM if spec == NEAR else spec[1]
            if ROOMY[0] or space is pltpu.HBM:
                out_shape[i] = space(shape.shape, shape.dtype)
    count = len(out_shape)
    for array in ahead:
        out_specs.append(VMEM if not grid else ANY)
        out_shape.append(pltpu.VMEM(array.shape, array.dtype))
    if ahead:
        extra_scratch.append(pltpu.SemaphoreType.DMA((len(ahead),)))
    after = [in_hbm(array) for array in ahead] + after
    out_specs.append(ANY)
    out_shape.append(pltpu.HBM((8, 128), F32))

    def ordered(*refs):
        ins = list(refs[:real])
        results = list(refs[real + len(after) : real + len(after) + len(out_shape) - 1])
        rest = list(refs[real + len(after) + len(out_shape) :])
        early = [
            pltpu.make_async_copy(refs[real + i], results[count + i], rest[-1].at[i])
            for i in range(len(ahead))
        ]
        del results[count:]
        own, extra = rest[: len(scratch)], rest[len(scratch) :]
        made, ends = [], []
        for n, i in enumerate(streams):
            copy = pltpu.make_async_copy(ins[i], extra[2 * n], extra[2 * n + 1])
            copy.start()
            ins[i] = Stream(copy, extra[2 * n])
            made.append(ins[i])
        extra = extra[2 * len(streams) :]
        for i in sorted(drains + pairs[::2]):
            held, sem = extra[:2]
            extra = extra[2:]
            if i in drains:
                copy = pltpu.make_async_copy(held, results[i], sem)
                results[i] = Drain(copy, held, results[i], sem)
                ends.append(results[i])
            else:
                halves = [
                    Drain(
                        pltpu.make_async_copy(held.at[k], results[i + k], sem.at[k]),
                        held.at[k], results[i + k], sem.at[k],
                    )
                    for k in range(2)
                ]
                results[i] = Pair(halves, held)
                ends += results[i].drains
        for i in reversed(pairs[1::2]):
            del results[i]
        for n, copy in enumerate(early):
            if grid:
                pl.when(pl.program_id(0) == 0)(copy.start)
            else:
                copy.start()
        body(*ins, *results, *own)
        for copy in early:
            if grid:
                pl.when(pl.program_id(0) == grid[0] - 1)(copy.wait)
            else:
                copy.wait()
        for stream in made:
            stream.ready()
        for end in ends:
            if not end.started:
                end.flush()
        for end in ends:
            end.copy.wait()

    got = pl.pallas_call(
        ordered,
        out_shape=tuple(out_shape),
        grid_spec=pltpu.PrefetchScalarGridSpec(
            num_scalar_prefetch=prefetch,
            grid=grid,
            in_specs=in_specs + [ANY] * len(after),
            out_specs=tuple(out_specs),
            scratch_shapes=list(scratch) + extra_scratch,
        ),
        compiler_params=pltpu.CompilerParams(vmem_limit_bytes=(limit or LIMITS[name]) * MIB),
        name=name,
        cost_estimate=pl.CostEstimate(
            flops=int(cost * 1153 * 10**6), bytes_accessed=0, transcendentals=0
        ),
    )(*operands, *after)
    ORDER[:] = [in_hbm(got[-1])]
    got = (*got[:count], *(got[count:-1] if ahead else wanted))
    return got if outs or wanted else got[0]


def shadow(cost, *arrays):
    call("shadow", lambda *_: None, (), [ANY] * len(arrays), (), arrays, cost=cost)


def whole(*shape):
    return pl.BlockSpec(shape, lambda *_: (0,) * len(shape))


def shape_of(dtype, *shape):
    return jax.ShapeDtypeStruct(shape, dtype)


class Columns:
    def __init__(self, names, sections, y_parts, chunks, part):
        self.names, self.y_parts, self.chunks, self.part = names, y_parts, chunks, part
        self.sections = []
        first = unit = 0
        for blocks, order in sections:
            if blocks:
                self.sections.append((first, blocks, order, unit))
            first, unit = first + blocks, unit + chunks * blocks
        self.blocks, self.units = first, unit

    def shape(self, more=0):
        return shape_of(BF, self.units + more, self.part, 128)

    def first(self, name):
        done = 0
        for other, width in self.names:
            if other == name:
                return done
            done += width // 128

    def find(self, block):
        for i, (first, blocks, order, _) in enumerate(self.sections):
            if first <= block < first + blocks:
                if order != "y":
                    return i, None, block - first
                y, k = divmod(block - first, blocks // self.y_parts)
                return i, y, k

    def runs(self):
        found = []
        for first, blocks, order, _ in self.sections:
            size = blocks // self.y_parts if order == "y" else blocks
            found += [(at, size) for at in range(first, first + blocks, size)]
        return found

    def table(self, spots, y_spots):
        units = []
        for c in range(self.chunks):
            for block in range(self.blocks):
                i, y, k = self.find(block)
                _, blocks, order, unit = self.sections[i]
                if y is None:
                    units.append(unit + spots[order][c] * blocks + k)
                else:
                    units.append(unit + (y_spots[y] * self.chunks + spots[0][c]) * (blocks // self.y_parts) + k)
        return units

    def store(self, ref, half, name, value, place_ref, chunks=None, block=0):
        chunks = range(self.chunks) if chunks is None else chunks
        start = self.first(name) + block
        slot = jnp.bitwise_xor(place_ref[0], half)
        for n, c in enumerate(chunks):
            for j in range(value.shape[1] // 128):
                unit = place_ref[self.at + c * self.blocks + start + j]
                ref[slot, unit] = value[n * self.part : (n + 1) * self.part, j * 128 : (j + 1) * 128].astype(BF)


def self_attention(x, gains, w_qkv, rel_bias, ahead):
    rows, width = x.shape
    bucket_count, heads = rel_bias.shape
    pairs = heads // 2
    groups = rows // GROUP
    firsts = bucket_firsts(bucket_count)

    def body(
        x, gs_ref, wqkv, rb_ref, a1_out, qkv_out, p1_out, o1_ref, o1_out, bias
    ):
        a1_ref, qkv_ref, p1_ref = a1_out.ref, qkv_out.ref, p1_out.ref
        xf = x.ready()[...].astype(F32)
        a1 = (xf * inv_rms(xf) * gs_ref[0:1, :]).astype(BF)
        a1_ref[...] = a1
        a1_out.flush()
        row = lax.broadcasted_iota(jnp.int32, (TLEN, GROUP), 0)
        col = lax.broadcasted_iota(jnp.int32, (TLEN, GROUP), 1)
        distance = lax.rem(col, TLEN) - row

        def make_bias(h, carry):
            val = jnp.full((TLEN, GROUP), NEG_LARGE, F32)
            for b, first in firsts:
                val = jnp.where(distance >= first, rb_ref[h, b], val)
            lanes = pl.ds(pl.multiple_of(lax.rem(h, 2) * GROUP, GROUP), GROUP)
            for t in range(GROUP // TLEN):
                bias[h // 2, t * TLEN : (t + 1) * TLEN, lanes] = jnp.where(
                    col // TLEN == t, val, NEG_LARGE
                )
            return carry

        lax.fori_loop(0, heads, make_bias, 0)
        wqkv_ref = wqkv.ready()

        def project(t, carry):
            at = pl.ds(pl.multiple_of(t * width, 128), width)
            qkv_ref[:, at] = dot_nn(a1_ref[...], wqkv_ref[:, at]).astype(BF)
            return carry

        lax.fori_loop(0, 3, project, 0)
        qkv_out.flush()
        m0, m1 = half_masks(GROUP)

        def attend(g, carry):
            at = pl.ds(pl.multiple_of(g * GROUP, GROUP), GROUP)
            for pair in range(pairs):
                lo = pair * 128
                q = qkv_ref[at, lo : lo + 128]
                k = qkv_ref[at, width + lo : width + lo + 128]
                v = qkv_ref[at, 2 * width + lo : 2 * width + lo + 128]
                s = dot_nt(k, jnp.concatenate([q * m0, q * m1], 0)) + bias[pair]
                e = jnp.exp(s - jnp.max(s, 0, keepdims=True))
                p = (e / jnp.sum(e, 0, keepdims=True)).astype(BF)
                p1_ref[g, pair] = p
                o = dot_tn(
                    jnp.concatenate([p[:, :GROUP], p[:, GROUP:]], 0),
                    jnp.concatenate([v * m0, v * m1], 0),
                )
                o1_ref[at, lo : lo + 128] = o.astype(BF)
            p1_out.flush_part(pl.ds(g, 1))
            return carry

        lax.fori_loop(0, groups, attend, 0)
        o1_out.ref[...] = o1_ref[...]
        o1_out.flush()

    return call(
        "self_attention",
        body,
        (
            shape_of(BF, rows, width),
            shape_of(BF, rows, 3 * width),
            shape_of(BF, groups, pairs, GROUP, 2 * GROUP),
            shape_of(BF, rows, width),
            shape_of(BF, rows, width),
        ),
        [STREAM, VMEM, STREAM, SMEM],
        (DRAIN, DRAIN, DRAIN, NEAR, DRAIN),
        (x, gains, w_qkv, rel_bias.T),
        ahead=ahead,
        scratch=[pltpu.VMEM((pairs, GROUP, 2 * GROUP), F32)],
    )


def self_project(x, o1, w_self_out, gains, w_cross_q, ahead):
    rows, width = x.shape

    def body(x_ref, o1_ref, wso_ref, gc_ref, wcq_ref, h1_ref, cq_ref, h1_out, a2_out, cq_out):
        h1 = dot_nn(o1_ref[...], wso_ref[...]) + x_ref[...].astype(F32)
        h1_ref[...] = h1
        h1_out.ref[...] = h1
        h1_out.flush()
        a2 = (h1 * inv_rms(h1) * gc_ref[1:2, :]).astype(BF)
        a2_out.ref[...] = a2
        a2_out.flush()
        cq = dot_nn(a2, wcq_ref[...]).astype(BF)
        cq_ref[...] = cq
        cq_out.ref[...] = cq

    low, full = shape_of(BF, rows, width), shape_of(F32, rows, width)
    return call(
        "self_project",
        body,
        (full, low, full, low, low),
        [VMEM] * 5,
        (NEAR, NEAR, DRAIN, DRAIN, DRAIN),
        (x, o1, w_self_out, gains, w_cross_q),
        ahead=ahead,
    )


def cross_forward(
    pieces, order, shard_rows, tgt_question, cq, h1, w_cross_kv, w_cross_out, gains, ahead
):
    rows, width = cq.shape
    pairs = width // 128
    tokens = sum(len(o) for o in order) * shard_rows
    targets = rows // TLEN
    block_rows = query_block(rows, tokens)
    blocks = rows // block_rows
    steps = pairs * blocks

    def body(*refs):
        piece_refs = refs[: len(pieces)]
        (
            tq_ref, cq_ref, h1_ref, wkv_ref, wco_ref, gf_ref,
            enc_out, kv_out, e_ref, inv_out, o2_out, h2_out, a3_ref,
            kfeat, qfeat, ebuf, sem,
        ) = refs[len(pieces) :]
        enc_ref, kv_ref, inv_ref, o2_ref = enc_out.ref, kv_out.ref, inv_out.ref, o2_out.ref
        lane = lax.rem(lax.broadcasted_iota(jnp.int32, (shard_rows, 128), 1), 64).astype(F32)
        for ref, places in zip(piece_refs, order):
            for j, spot in enumerate(places):
                at = slice(spot * shard_rows, (spot + 1) * shard_rows)
                enc_ref[at, :] = ref[j, :shard_rows, :]
                tag = ref[j, shard_rows : shard_rows + 1, :shard_rows].astype(F32)
                tag = jnp.transpose(jnp.broadcast_to(tag, (128, shard_rows)))
                kfeat[at, :] = jnp.where(tag == lane, 0.0, NEG_LARGE).astype(BF)
        lane_t = lax.rem(lax.broadcasted_iota(jnp.int32, (TLEN, 128), 1), 64)
        for t in range(targets):
            qfeat[t * TLEN : (t + 1) * TLEN, :] = jnp.where(lane_t == tq_ref[t], 1.0, 0.0).astype(BF)
        enc_out.flush()

        def project(t, carry):
            at = pl.ds(pl.multiple_of(t * 384, 128), 384)
            kv_ref[:, at] = dot_nn(enc_ref[...], wkv_ref[:, at]).astype(BF)
            return carry

        lax.fori_loop(0, 2 * width // 384, project, 0)
        kv_out.flush()
        q0, q1 = half_masks(block_rows)
        k0, k1 = half_masks(tokens)
        qmask, kmask = (q0, q1), (k0, k1)
        low = lax.broadcasted_iota(jnp.int32, (block_rows, 128), 1) < 64

        def out_copy(slot, step):
            pair, block = step // blocks, lax.rem(step, blocks)
            return pltpu.make_async_copy(
                ebuf.at[slot],
                e_ref.at[pl.ds(2 * pair, 2), pl.ds(block * block_rows, block_rows)],
                sem.at[slot],
            )

        def attend(step, carry):
            slot = lax.rem(step, 2)
            pair, block = step // blocks, lax.rem(step, blocks)
            lo = pl.multiple_of(pair * 128, 128)
            at = pl.ds(pl.multiple_of(block * block_rows, block_rows), block_rows)

            @pl.when(step >= 2)
            def _():
                out_copy(slot, step - 2).wait()

            q = cq_ref[at, pl.ds(lo, 128)]
            k = kv_ref[:, pl.ds(lo, 128)]
            v = kv_ref[:, pl.ds(width + lo, 128)]
            keys = [k * kmask[h] + kfeat[...] * kmask[1 - h] for h in range(2)]
            values = [v * kmask[h] + kmask[1 - h] for h in range(2)]
            size = min(block_rows, 256)
            units = [(r, h) for r in range(0, block_rows, size) for h in range(2)]
            tagged = qfeat[at, :]

            def score(unit):
                r, h = unit
                qa = q[r : r + size] * qmask[h][:size] + tagged[r : r + size] * qmask[1 - h][:size]
                return dot_nt(qa, keys[h])

            outs, last = {}, None
            s = score(units[0])
            for i, unit in enumerate(units):
                later = score(units[i + 1]) if i + 1 < len(units) else None
                if last is not None:
                    outs[last[0]] = dot_nn(last[1], values[last[0][1]])
                e = jnp.exp(s - jnp.max(s, -1, keepdims=True)).astype(BF)
                ebuf[slot, unit[1], unit[0] : unit[0] + size, :] = e
                last, s = (unit, e), later
            outs[last[0]] = dot_nn(last[1], values[last[0][1]])
            outs = [
                jnp.concatenate([outs[r, h] for r in range(0, block_rows, size)], 0) for h in range(2)
            ]
            out_copy(slot, step).start()
            total = jnp.where(low, pltpu.roll(outs[0], 64, 1), pltpu.roll(outs[1], 64, 1))
            inv = 1.0 / total
            inv_ref[at, pl.ds(lo, 128)] = inv
            o2_ref[at, pl.ds(lo, 128)] = (jnp.where(low, outs[0], outs[1]) * inv).astype(BF)
            return carry

        lax.fori_loop(0, steps, attend, 0)
        inv_out.flush()
        o2_out.flush()
        h2 = h1_ref[...] + dot_nn(o2_ref[...], wco_ref[...])
        h2_out.ref[...] = h2
        h2_out.flush()
        a3_ref[...] = (h2 * inv_rms(h2) * gf_ref[2:3, :]).astype(BF)
        for step in range(max(0, steps - 2), steps):
            out_copy(step % 2, jnp.int32(step)).wait()

    return call(
        "cross_forward",
        body,
        (
            shape_of(BF, tokens, width),
            shape_of(BF, tokens, 2 * width),
            shape_of(BF, 2 * pairs, rows, tokens),
            shape_of(F32, rows, width),
            shape_of(BF, rows, width),
            shape_of(F32, rows, width),
            shape_of(BF, rows, width),
        ),
        [VMEM] * len(pieces) + [SMEM] + [VMEM] * 5,
        (DRAIN, DRAIN, (HBM, ANY), DRAIN, DRAIN, DRAIN, NEAR),
        (*pieces, tgt_question, cq, h1, w_cross_kv, w_cross_out, gains),
        scratch=[
            pltpu.VMEM((tokens, 128), BF),
            pltpu.VMEM((rows, 128), BF),
            pltpu.VMEM((2, 2, block_rows, tokens), BF),
            pltpu.SemaphoreType.DMA((2,)),
        ],
        limit=big(tokens),
        ahead=ahead,
    )


def hidden_gradient(gy, w_ff_out, ahead):
    rows, width = gy.shape
    hidden = w_ff_out.shape[0]

    tiles = hidden // width

    def body(gy_ref, w2_ref, out_ref, w2, sem):
        def copy(t):
            at = pl.ds(pl.multiple_of(t * width, 128), width)
            return pltpu.make_async_copy(w2_ref.at[at], w2.at[at], sem.at[t])

        for t in range(tiles):
            copy(t).start()

        def tile(t, carry):
            copy(t).wait()
            at = pl.ds(pl.multiple_of(t * width, 128), width)
            out_ref[:, at] = dot_nt(gy_ref[...], w2[at, :]).astype(BF)
            return carry

        lax.fori_loop(0, tiles, tile, 0)

    return call(
        "hidden_gradient",
        body,
        shape_of(BF, rows, hidden),
        [VMEM, (HBM, ANY)],
        NEAR,
        (gy, w_ff_out),
        scratch=[pltpu.VMEM((hidden, width), BF), pltpu.SemaphoreType.DMA((tiles,))],
        ahead=ahead,
    )


def feed_hidden(place, a3, gy, dhid, w_ff_in, columns):
    rows, width = a3.shape
    hidden = w_ff_in.shape[1]
    tile = width
    half = width // 2
    sub = hidden // width
    part = columns.part
    per_tile = columns.chunks * tile // hidden
    scale = math.sqrt(2.0 / math.pi)

    def body(place_ref, a3_ref, gy_ref, dhid_ref, w1_ref, dpre_ref, hid_out, both):
        def activate(pre, at):
            sq = pre * pre
            t = jnp.tanh(pre * (scale + (scale * 0.044715) * sq))
            up = 0.5 + 0.5 * t
            hid = (pre * up).astype(BF)
            slope = up + pre * (up - up * up) * ((2.0 * scale) + (2.0 * scale * 0.134145) * sq)
            hid_out.ref[:, at] = hid
            dpre_ref[:, at] = (dhid_ref[:, at].astype(F32) * slope).astype(BF)
            return hid

        def one(step, carry):
            parts = tile // 256
            ats = [pl.ds(pl.multiple_of(step * tile + i * 256, 128), 256) for i in range(parts)]
            a3, gyv = a3_ref[...], gy_ref[...]
            pre = dot_nn(a3, w1_ref[:, ats[0]])
            grads, hid = [], None
            for i in range(parts):
                later = dot_nn(a3, w1_ref[:, ats[i + 1]]) if i + 1 < parts else None
                if hid is not None:
                    grads.append(dot_tn(hid, gyv))
                hid = activate(pre, ats[i])
                pre = later
            grads.append(dot_tn(hid, gyv))
            hid_out.flush_part((slice(None), pl.ds(pl.multiple_of(step * tile, 128), tile)))
            g = jnp.concatenate(grads, 0)
            for i in range(per_tile):
                chunk = step * per_tile + i
                for h in range(2):
                    for j in range(sub):
                        first = (i * sub + j) * part
                        columns.store(
                            both.ref, h, "out", g[first : first + part, h * half : (h + 1) * half],
                            place_ref, [chunk], j * half // 128,
                        )
                for first, count in columns.runs():
                    unit = place_ref[columns.at + chunk * columns.blocks + first]
                    for drain in both.drains:
                        drain.flush_part(pl.ds(unit, count))
            return carry

        lax.fori_loop(0, hidden // tile, one, 0)

    return call(
        "feed_hidden",
        body,
        (shape_of(BF, rows, hidden), shape_of(BF, rows, hidden), columns.shape(), columns.shape()),
        [SMEM, VMEM, VMEM, VMEM, VMEM],
        (NEAR, DRAIN, PAIR, PAIR),
        (place, a3, gy, dhid, w_ff_in),
    )


def feed_weights(place, a3, dpre, columns, ahead):
    width = a3.shape[1]
    hidden = dpre.shape[1]

    def body(place_ref, a3_ref, dpre_ref, both):
        tiles = hidden // width

        def one(t, carry):
            at = pl.ds(pl.multiple_of(t * width, 128), width)
            g = dot_tn(a3_ref[...], dpre_ref[:, at])
            block = lax.rem(t, tiles // 2) * (width // 128)
            columns.store(both.ref, t // (tiles // 2), "in", g, place_ref, None, block)
            for slot in range(2):

                @pl.when(jnp.logical_and(t == tiles // 2 - 1, place_ref[0] == slot))
                def _():
                    both.drains[slot].flush_part(pl.ds(0, columns.units))

                @pl.when(jnp.logical_and(t == tiles - 1, place_ref[0] != slot))
                def _():
                    both.drains[slot].flush_part(pl.ds(0, columns.units))

            return carry

        lax.fori_loop(0, tiles, one, 0)

    return call(
        "feed_weights",
        body,
        (columns.shape(), columns.shape()),
        [SMEM, VMEM, VMEM],
        (PAIR, PAIR),
        (place, a3, dpre),
        ahead=ahead,
    )


def feed_back(dpre, w_ff_in, h2, gains, gy):
    rows, width = h2.shape

    def body(dpre_ref, w1_ref, h2_ref, gf_ref, gy_ref, dh2_ref, gain_ref, da3):
        da3[...] = jnp.zeros_like(da3)

        def one(t, carry):
            at = pl.ds(pl.multiple_of(t * width, 128), width)
            da3[...] += dot_nt(dpre_ref[:, at], w1_ref[:, at])
            return carry

        lax.fori_loop(0, dpre_ref.shape[1] // width, one, 0)
        dv, dgain = rms_back(da3[...], h2_ref[...], gf_ref[2:3, :])
        dh2_ref[...] = gy_ref[...].astype(F32) + dv
        gain_ref[...] = dgain

    return call(
        "feed_back",
        body,
        (shape_of(F32, rows, width), shape_of(F32, 1, width)),
        [VMEM] * 5,
        (NEAR, NEAR),
        (dpre, w_ff_in, h2, gains, gy),
        scratch=[pltpu.VMEM((rows, width), F32)],
    )


def feed_out(hid, w_ff_out, h2, ahead):
    rows, width = h2.shape

    def body(hid_ref, w2_ref, h2_ref, out, total):
        total[...] = h2_ref[...]

        def one(t, carry):
            at = pl.ds(pl.multiple_of(t * width, 128), width)
            total[...] += dot_nn(hid_ref[:, at], w2_ref[at, :])
            return carry

        lax.fori_loop(0, hid_ref.shape[1] // width, one, 0)
        out.ref[...] = total[...].astype(BF)

    return call(
        "feed_out",
        body,
        (shape_of(BF, rows, width),),
        [VMEM] * 3,
        (DRAIN,),
        (hid, w_ff_out, h2),
        scratch=[pltpu.VMEM((rows, width), F32)],
        ahead=ahead,
    )


def cross_backward(first_pair, last_pair, dh2, o2, inv, cq, kv, e, w_cross_out, ahead):
    rows, width = cq.shape
    pairs = width // 128
    count = last_pair - first_pair
    tokens = kv.shape[0]
    block_rows = query_block(rows, tokens)
    blocks = rows // block_rows

    def body(
        dh2_ref, wco_ref, o2_ref, inv_ref, cq_ref, k_ref, v_ref, e_ref,
        dcq_ref, dkt_ref, dvt_ref,
        do2,
    ):
        pair = pl.program_id(0)

        @pl.when(pair == 0)
        def _():
            do2v = dot_nt(dh2_ref[...].astype(BF), wco_ref[...]).astype(BF)
            for i in range(count):
                do2[i] = do2v[:, i * 128 : (i + 1) * 128]

        q0, q1 = half_masks(block_rows)
        k0, k1 = half_masks(tokens)
        qmask, kmask = (q0, q1), (k0, k1)
        lane = lax.broadcasted_iota(jnp.int32, (block_rows, 128), 1)
        low = lane < 64
        first = lax.rem(lane, 64) == 0
        second = lax.rem(lane, 64) == 1
        k, v = k_ref[...], v_ref[...]
        sums = [0.0] * 4
        for block in range(blocks):
            at = slice(block * block_rows, (block + 1) * block_rows)
            q = cq_ref[at, :]
            dof = do2[pair, at, :].astype(F32) * inv_ref[at, :]
            dob = dof.astype(BF)
            prod = dof * o2_ref[at, :].astype(F32)
            qt = jnp.transpose(q)
            dot_t = jnp.transpose(dob)
            dqs = []
            for h in range(2):
                own = low if h == 0 else jnp.logical_not(low)
                delta = -jnp.sum(jnp.where(own, prod, 0.0), -1, keepdims=True)
                hi = delta.astype(BF).astype(F32)
                feat = jnp.where(first, hi, jnp.where(second, delta - hi, 0.0)).astype(BF)
                doa = dob * qmask[h] + feat * qmask[1 - h]
                dp = dot_nt(doa, v * kmask[h] + kmask[1 - h])
                ev = e_ref[h, at, :]
                ds = (ev.astype(F32) * dp).astype(BF)
                dqs.append(dot_nn(ds, k))
                sums[h] = sums[h] + dot_nn(qt[h * 64 : (h + 1) * 64, :], ds)
                sums[2 + h] = sums[2 + h] + dot_nn(dot_t[h * 64 : (h + 1) * 64, :], ev)
            dcq_ref[at, :] = jnp.where(low, dqs[0], dqs[1]).astype(BF)
        for h in range(2):
            dkt_ref[h * 64 : (h + 1) * 64, :] = sums[h].astype(BF)
            dvt_ref[h * 64 : (h + 1) * 64, :] = sums[2 + h].astype(BF)

    near = HBM if big(tokens) else NEAR

    def column(n, first=first_pair):
        return pl.BlockSpec((n, 128), lambda p: (0, p + first))

    return call(
        "cross_backward",
        body,
        (
            shape_of(BF, rows, count * 128),
            shape_of(BF, count * 128, tokens),
            shape_of(BF, count * 128, tokens),
        ),
        [
            whole(rows, width),
            pl.BlockSpec((count * 128, width), lambda p: (first_pair // count, 0)),
            (HBM, column(rows)),
            (HBM, column(rows)),
            (HBM, column(rows)),
            (HBM, column(tokens)),
            (HBM, column(tokens, first_pair + pairs)),
            (HBM, pl.BlockSpec((2, rows, tokens), lambda p: (p + first_pair, 0, 0))),
        ],
        (
            (NEAR, column(rows, 0)),
            (near, pl.BlockSpec((128, tokens), lambda p: (p, 0))),
            (near, pl.BlockSpec((128, tokens), lambda p: (p, 0))),
        ),
        (dh2, w_cross_out, o2, inv, cq, kv, kv, e),
        scratch=[pltpu.VMEM((count, rows, 128), BF)],
        grid=(count,),
        ahead=ahead,
        limit=big(tokens),
    )


def cross_query_back(dcq, w_cross_q, h1, gains, dh2):
    rows, width = h1.shape
    n = len(dcq)
    size = width // n

    def body(*refs):
        wcq_ref, h1_ref, gc_ref, dh2_ref, dh1_ref, gain_ref = refs[n:]
        da2 = 0.0
        for i in range(n):
            da2 = da2 + dot_nt(refs[i][...], wcq_ref[:, i * size : (i + 1) * size])
        dv, dgain = rms_back(da2, h1_ref[...], gc_ref[1:2, :])
        dh1_ref[...] = dh2_ref[...] + dv
        gain_ref[...] = dgain

    return call(
        "cross_query_back",
        body,
        (shape_of(F32, rows, width), shape_of(F32, 1, width)),
        [VMEM] * (n + 4),
        (NEAR, NEAR),
        (*dcq, w_cross_q, h1, gains, dh2),
    )


def shard_rows_of(tokens, chunks):
    return tokens // chunks


def cross_weights(place, dh2, o2, dcq, dkt, dvt, enc, a2, w_cross_kv, dh1, o1, columns, ahead):
    rows, width = dh2.shape
    tokens = enc.shape[0]
    half = width // 2
    tile = max(shard_rows_of(tokens, columns.chunks), 512)
    n = len(dcq)
    size = width // n
    blocks = width // 128
    near = 2 * blocks // 3
    shard_rows = tokens // columns.chunks

    def body(place_ref, dh2_ref, dh1_ref, a2_ref, o2_ref, o1_ref, *refs):
        dcq_refs, dkt, dvt = refs[:n], refs[n : 2 * n], refs[2 * n : 3 * n]
        wkv_ref, enc_ref, genc_out, both, lhs, rhs, dkvt = refs[3 * n :]
        for i, r in enumerate(dcq_refs):
            rhs[0, :, i * size : (i + 1) * size] = r[...]
        rhs[1] = dh2_ref[...].astype(BF)
        rhs[2] = dh1_ref[...].astype(BF)
        for i, r in enumerate((a2_ref, o2_ref, o1_ref)):
            lhs[i] = r[...]
        for i, r in enumerate(dkt + dvt):
            dkvt[i * size : (i + 1) * size, :] = r[...]

        def square(i, carry):
            g = dot_tn(lhs[i], rhs[i])
            for h in range(2):
                columns.store(both.ref, h, "q", g[:, h * half : (h + 1) * half], place_ref, None, i * (half // 128))
            return carry

        lax.fori_loop(0, 3, square, 0)

        def encodings(t, carry):
            at = pl.ds(pl.multiple_of(t * tile, 128), tile)
            genct = dot_nn(wkv_ref[...], dkvt[:, at]).astype(BF)
            for i in range(tile // shard_rows):
                for j in range(blocks):
                    order = 0 if j < near else 1
                    size = blocks - near if order else near
                    spot = place_ref[3 + order * columns.chunks + t * (tile // shard_rows) + i]
                    genc_out.ref[order * columns.chunks * near + spot * size + j - order * near] = genct[
                        j * 128 : (j + 1) * 128, i * shard_rows : (i + 1) * shard_rows
                    ]
            return carry

        lax.fori_loop(0, tokens // tile, encodings, 0)
        genc_out.flush()

        def key_value(h, carry):
            g = 0.0
            rows_at = pl.ds(pl.multiple_of(h * width, 128), width)
            for t in range(0, tokens, 1024):
                end = min(tokens, t + 1024)
                g = g + dot_nt(jnp.transpose(enc_ref[t:end, :]), dkvt[rows_at, t:end])
            columns.store(both.ref, h, "kv", g, place_ref)
            return carry

        lax.fori_loop(0, 2, key_value, 0)

    return call(
        "cross_weights",
        body,
        (shape_of(BF, columns.chunks * blocks, 128, shard_rows), columns.shape(), columns.shape()),
        [SMEM] + [VMEM] * (3 * n + 7),
        (DRAIN, PAIR, PAIR),
        (place, dh2, dh1, a2, o2, o1, *dcq, *dkt, *dvt, w_cross_kv, enc),
        scratch=[
            pltpu.VMEM((3, rows, width), BF),
            pltpu.VMEM((3, rows, width), BF),
            pltpu.VMEM((2 * width, tokens), BF),
        ],
        ahead=ahead,
        limit=big(tokens),
    )


def self_backward(dh1, w_self_out, qkv, p1, bucket_count, heads, ahead):
    rows, width = dh1.shape
    pairs = heads // 2
    groups = rows // GROUP
    firsts = bucket_firsts(bucket_count)
    ends = [first for _, first in firsts[1:]] + [TLEN]

    def body(dh1_ref, wso_ref, qkv_ref, p1_ref, dqkv_ref, gbias_ref, do1, acc):
        do1[...] = dot_nt(dh1_ref[...].astype(BF), wso_ref[...]).astype(BF)
        m0, m1 = half_masks(GROUP)
        acc[...] = jnp.zeros_like(acc)

        def attend(g, carry):
            at = pl.ds(pl.multiple_of(g * GROUP, GROUP), GROUP)
            for pair in range(pairs):
                lo = pair * 128
                q = qkv_ref[at, lo : lo + 128]
                k = qkv_ref[at, width + lo : width + lo + 128]
                v = qkv_ref[at, 2 * width + lo : 2 * width + lo + 128]
                do = do1[at, lo : lo + 128]
                do_two = jnp.concatenate([do * m0, do * m1], 0)
                pb = p1_ref[g, pair]
                pf = pb.astype(F32)
                dp = dot_nt(v, do_two)
                ds = (pf * (dp - jnp.sum(pf * dp, 0, keepdims=True))).astype(BF)
                dsf = ds.astype(F32)
                total = dsf[:TLEN]
                for t in range(1, GROUP // TLEN):
                    total = total + dsf[t * TLEN : (t + 1) * TLEN]
                acc[2 * pair] += total[:, :GROUP]
                acc[2 * pair + 1] += total[:, GROUP:]
                dq = dot_tn(
                    jnp.concatenate([ds[:, :GROUP], ds[:, GROUP:]], 0),
                    jnp.concatenate([k * m0, k * m1], 0),
                )
                dk = dot_nn(ds, jnp.concatenate([q * m0, q * m1], 0))
                dv = dot_nn(pb, do_two)
                dqkv_ref[at, lo : lo + 128] = dq.astype(BF)
                dqkv_ref[at, width + lo : width + lo + 128] = dk.astype(BF)
                dqkv_ref[at, 2 * width + lo : 2 * width + lo + 128] = dv.astype(BF)
            return carry

        lax.fori_loop(0, groups, attend, 0)
        row = lax.broadcasted_iota(jnp.int32, (TLEN, GROUP), 0)
        distance = lax.rem(lax.broadcasted_iota(jnp.int32, (TLEN, GROUP), 1), TLEN) - row
        lane = lax.broadcasted_iota(jnp.int32, (16, 128), 1)
        bias = jnp.zeros((16, 128), F32)
        accv = acc[...]
        pad = jnp.zeros((16 - heads, 1), F32)
        for (b, first), end in zip(firsts, ends):
            here = jnp.logical_and(distance >= first, distance < end)
            part_sum = jnp.sum(jnp.where(here[None], accv, 0.0), axis=1)
            col = jnp.sum(part_sum, -1, keepdims=True)
            bias = jnp.where(lane == b, jnp.concatenate([col, pad], 0), bias)
        gbias_ref[...] = bias

    return call(
        "self_backward",
        body,
        (shape_of(BF, rows, 3 * width), shape_of(F32, 16, 128)),
        [VMEM] * 4,
        (NEAR, NEAR),
        (dh1, w_self_out, qkv, p1),
        ahead=ahead,
        scratch=[pltpu.VMEM((rows, width), BF), pltpu.VMEM((heads, TLEN, GROUP), F32)],
    )


def self_weights(
    place, dh1, a1, dqkv, x, gains, w_qkv, gbias, gain_cross_grad, gain_ff_grad, columns
):
    rows, width = dh1.shape
    half = width // 2
    part = columns.part
    misc_rows = 16 + width // 16
    more = -(-misc_rows // part)

    def body(
        place_ref, dh1_ref, wqkv_ref, x_ref, a1_ref, dqkv_ref, gs_ref, gb_ref, ggc_ref, ggf_ref,
        out, both, da1,
    ):
        da1[...] = jnp.zeros_like(da1)

        def one(t, carry):
            at = pl.ds(pl.multiple_of(t * width, 128), width)
            da1[...] += dot_nt(dqkv_ref[:, at], wqkv_ref[:, at])
            return carry

        lax.fori_loop(0, 3, one, 0)
        dv, dgain = rms_back(da1[...], x_ref[...].astype(F32), gs_ref[0:1, :])
        out.ref[...] = dh1_ref[...] + dv
        out.flush()

        def weights(h, carry):
            at = pl.ds(pl.multiple_of(h * 3 * half, 128), 3 * half)
            columns.store(both.ref, h, "qkv", dot_tn(a1_ref[...], dqkv_ref[:, at]), place_ref)
            return carry

        lax.fori_loop(0, 2, weights, 0)
        gains = jnp.concatenate([dgain, ggc_ref[...], ggf_ref[...], jnp.zeros((5, width), F32)], 0)
        misc = [gb_ref[...]] + [gains[:, j * 128 : (j + 1) * 128] for j in range(width // 128)]
        misc.append(jnp.zeros((more * part - misc_rows, 128), F32))
        misc = jnp.concatenate(misc, 0).astype(BF)
        for i in range(more):
            for slot in range(2):
                both.ref[slot, columns.units + i] = misc[i * part : (i + 1) * part]

    return call(
        "self_weights",
        body,
        (shape_of(F32, rows, width), columns.shape(more), columns.shape(more)),
        [SMEM] + [VMEM] * 9,
        (DRAIN, PAIR, PAIR),
        (
            place, dh1, w_qkv, x, a1, dqkv, gains, gbias,
            gain_cross_grad, gain_ff_grad,
        ),
        scratch=[pltpu.VMEM((rows, width), F32)],
    )


def swap(value, axis, bit):
    size = lax.axis_size(axis)
    return lax.ppermute(value, axis, [(i, i ^ bit) for i in range(size)])


class Bucket:
    def __init__(self, rows, terms, steps, keep_all=False):
        self.rows, self.terms, self.steps, self.keep_all = rows, terms, list(steps), keep_all


def sum_kernel(groups, dtype=BF):
    operands, specs, plan = [], [], []
    for i, jobs in enumerate(groups):
        at = 0
        for rows, terms in jobs:
            plan.append((i, at, rows, len(operands), len(terms)))
            at += rows
            for array, off in terms:
                operands.append(array)
                spec = (pl.Element(rows), pl.Element(128))
                specs.append(pl.BlockSpec(spec, functools.partial(lambda off, *_: (off, 0), off)))
    sizes = [sum(rows for rows, _ in jobs) for jobs in groups]

    def body(*refs):
        outs = refs[len(operands) :]
        for i, at, rows, first, count in plan:
            total = refs[first][...].astype(F32)
            for r in refs[first + 1 : first + count]:
                total = total + r[...].astype(F32)
            outs[i][at : at + rows, :] = total.astype(dtype)

    return call(
        "sum_kernel",
        body,
        tuple(shape_of(dtype, size, 128) for size in sizes),
        specs,
        tuple(whole(size, 128) for size in sizes),
        operands,
        grid=(1,),
    )


def send_round(cost, *members, settle=()):
    groups = {}
    for m in members:
        step = m.steps[0]
        groups.setdefault((step, m) if isinstance(m, Total) else step, []).append(m)
    jobs = []
    for group in groups.values():
        jobs.append([])
        for m in group:
            if isinstance(m, Total):
                jobs[-1] += m.next_jobs()
            elif m.keep_all:
                jobs[-1].append((m.rows, m.terms))
            else:
                m.rows //= 2
                jobs[-1].append((m.rows, [(array, off + m.rows) for array, off in m.terms]))
    if settle:
        jobs.append([(b.rows, b.terms) for b in settle])
    sent = sum_kernel(jobs)
    at = 0
    for b in settle:
        b.terms = [(sent[-1], at)]
        at += b.rows
    for group, payload in zip(groups.values(), sent):
        axis, bit = group[0].steps[0]
        got = swap(payload, axis, bit)
        at = 0
        for m in group:
            m.steps.pop(0)
            if isinstance(m, Total):
                m.moved(payload, got)
                continue
            if m.keep_all:
                m.terms = [(payload, at), (got, at)]
            else:
                m.terms = m.terms + [(got, at)]
            at += m.rows
    shadow(cost)


def rest_of(*buckets):
    while any(b.steps for b in buckets):
        send_round(3, *[b for b in buckets if b.steps])


def weight_buckets(columns, keep, send, orders, y_bits):
    rows = columns.units * columns.part
    keep, send = in_hbm(keep.reshape(-1, 128)), send.reshape(-1, 128)
    got = swap(send, "dp", 1)
    over = [[("blk", b) for b in order] for order in orders]
    along = [("dp", 2 * b) for b in y_bits]
    buckets = []
    for _, blocks, order, unit in columns.sections:
        steps = along + over[0] if order == "y" else over[order]
        at = unit * columns.part
        size = blocks * columns.chunks * columns.part
        buckets.append(Bucket(size, [(keep, at), (got, at)], steps))
    if keep.shape[0] > rows:
        buckets.append(Bucket(keep.shape[0] - rows, [(keep, rows), (got, rows)], over[0], keep_all=True))
    return buckets


def join_encodings(buckets, shard_rows, width):
    terms = [(bucket, array, off) for bucket in buckets for array, off in bucket.terms]

    def body(*refs):
        out = refs[-1]
        first = col = 0
        for bucket in buckets:
            mine = refs[first : first + len(bucket.terms)]
            first += len(bucket.terms)
            for at in range(0, bucket.rows, 128):
                total = mine[0][at : at + 128, :].astype(F32)
                for r in mine[1:]:
                    total = total + r[at : at + 128, :].astype(F32)
                out[:, col : col + 128] = jnp.transpose(total)
                col += 128

    return call(
        "join_encodings",
        body,
        shape_of(F32, shard_rows, width),
        [
            pl.BlockSpec(
                (pl.Element(bucket.rows), pl.Element(shard_rows)),
                functools.partial(lambda off, *_: (off, 0), off),
            )
            for bucket, _, off in terms
        ],
        whole(shard_rows, width),
        [array for _, array, _ in terms],
        grid=(1,),
    )


class Total:
    def __init__(self, groups, small, dp_size):
        self.groups, self.small, self.dp_size = groups, small, dp_size
        self.jobs, self.bases = [], []
        at = 0
        for _, buckets in groups:
            base = []
            for bucket in buckets:
                self.jobs.append((bucket.rows, bucket.terms))
                base.append(at)
                at += bucket.rows
            self.bases.append(base)
        self.small_at = []
        for bucket in small:
            self.jobs.append((bucket.rows, bucket.terms))
            self.small_at.append((at, bucket.rows))
            at += bucket.rows
        self.rows = at
        self.steps = [("dp", 2 * m) for m in range(1, dp_size // 2)] + [("dp", 1)]
        self.parts = []

    def next_jobs(self):
        if len(self.steps) > 1 or not self.parts:
            return [(self.rows, [(self.parts[0], 0)])] if self.parts else self.jobs
        jobs, self.spots, at = [], [], 0
        for (columns, _), base in zip(self.groups, self.bases):
            spots = []
            for (_, blocks, order, _), first in zip(columns.sections, base):
                if order == "y":
                    rows = blocks // columns.y_parts * columns.part
                    spots.append([at + i * rows for i in range(len(self.parts))])
                    jobs += [(rows, [(p, first)]) for p in self.parts]
                    at += rows * len(self.parts)
                else:
                    rows = blocks * columns.part
                    spots.append(at)
                    jobs.append((rows, [(p, first) for p in self.parts]))
                    at += rows
            self.spots.append(spots)
        self.small_spots = []
        for first, rows in self.small_at:
            jobs.append((rows, [(p, first) for p in self.parts]))
            self.small_spots.append((at, rows))
            at += rows
        return jobs

    def moved(self, payload, got):
        if self.steps or not self.parts:
            self.parts = self.parts + [got] if self.parts else [payload, got]
        else:
            self.own, self.other = payload, got

    def finish(self, place, arrays):
        outs = []
        for (columns, _), spots, named in zip(self.groups, self.spots, arrays):
            for name, stack in named:
                outs.append((columns, spots, name, stack, dict(columns.names)[name] // stack))
        y_parts = self.dp_size // 2

        def body(place_ref, own_ref, other_ref, *refs):
            core, y = place_ref[0], place_ref[2]
            sides = ((core, own_ref), (1 - core, other_ref))

            def put(ref, columns, half, j, at):
                row, off = divmod(j * 128, half)
                for which, src in sides:
                    lane = pl.multiple_of(which * half + off, 128)
                    ref[row * columns.part : (row + 1) * columns.part, pl.ds(lane, 128)] = src[
                        at : at + columns.part, :
                    ].astype(F32)

            for ref, (columns, spots, name, stack, half) in zip(refs, outs):
                far = []
                for j in range(stack * half // 128):
                    i, y_of, k = columns.find(columns.first(name) + j)
                    if y_of is None:
                        put(ref, columns, half, j, spots[i] + k * columns.part)
                    else:
                        far.append((j, spots[i], y_of, k))
                for y_is in range(y_parts if far else 0):

                    @pl.when(y == y_is)
                    def _():
                        for j, at, y_of, k in far:
                            put(ref, columns, half, j, at[y_is ^ y_of] + k * columns.part)

            for ref, (at, rows) in zip(refs[len(outs) :], self.small_spots):
                ref[...] = own_ref[at : at + rows, :].astype(F32)

        shapes = [shape_of(F32, stack * columns.part, 2 * half) for columns, _, _, stack, half in outs]
        shapes += [shape_of(F32, rows, 128) for _, rows in self.small_spots]
        return call(
            "finish",
            body,
            tuple(shapes),
            [SMEM, VMEM, VMEM],
            (VMEM,) * len(shapes),
            (place, self.own, self.other),
        )


def gather_encodings(own, bits):
    if len(bits) == 3:
        x, z, far = bits
        r_far, r_x = swap(own, "blk", far), swap(own, "blk", x)

        def second():
            r_z, r_zf = swap(own, "blk", z), swap(r_far, "blk", z)
            r_xf = swap(r_far, "blk", x)

            def third():
                r_xz = swap(r_z, "blk", x)
                r_xzf = swap(r_xf, "blk", z)
                arrays = [own, r_far, r_x, r_z, r_zf, r_xf, r_xz, r_xzf]
                return arrays, [[0], [far], [x], [z], [z | far], [x | far], [x | z], [x | z | far]]

            return [r_z, r_zf, r_xf], third

        return [r_far, r_x], second
    got, rel = own, [0]
    for bit in reversed(bits):
        got = jnp.concatenate([got, swap(got, "blk", bit)], 0)
        rel = rel + [r ^ bit for r in rel]
    return [], lambda: ([], lambda: ([got], [rel]))


def local(
    dec_in,
    encodings,
    enc_question,
    enc_valid,
    tgt_question,
    gain_self,
    w_qkv,
    rel_bias,
    w_self_out,
    gain_cross,
    w_cross_q,
    w_cross_kv,
    w_cross_out,
    gain_ff,
    w_ff_in,
    w_ff_out,
    grad_out,
):
    x = dec_in[0]
    gy = grad_out[0]
    rows, width = x.shape
    bucket_count, heads = rel_bias.shape
    hidden = w_ff_in.shape[1]
    half = width // 2
    chunks = lax.axis_size("blk")
    part = width // chunks
    dp_size = lax.axis_size("dp")
    shard_rows = encodings.shape[1]
    bits = [1 << i for i in range(chunks.bit_length() - 1)]
    y_bits = [1 << i for i in range(dp_size.bit_length() - 2)]
    y_parts = dp_size // 2
    blk = lax.axis_index("blk")
    dp = lax.axis_index("dp")
    orders = [bits, bits[1::-1] + bits[2:]]

    def layout(names, *sections):
        return Columns(names, sections, y_parts, chunks, part)

    def along_y(blocks):
        return blocks // (2 * y_parts) * y_parts

    stack = hidden // width
    blocks = half // 128
    cols_out = layout([("out", stack * half)], (stack * blocks, "y"))
    cols_in = layout([("in", hidden // 2)], (2 * stack * blocks // 3, 0), (stack * blocks // 3, 1))
    far_x, far_s = along_y(16 * blocks // 3), along_y(4 * blocks)
    near_x, near_s = 5 * blocks - far_x, 3 * blocks - far_s
    cols_x = layout(
        [("q", half), ("out", half), ("self", half), ("kv", width)],
        (near_x, 0), (far_x, "y"),
    )
    cols_s = layout([("qkv", 3 * half)], (near_s, 0), (far_s, "y"))

    places = [[chunk_place(c, blk, order) for c in range(chunks)] for order in orders]
    y_places = [chunk_place(y, dp // 2, y_bits) for y in range(y_parts)]
    numbers = [lax.rem(dp, 2), blk, dp // 2]
    for order in orders:
        spots = [0] * chunks
        for r in range(chunks):
            spots[chunk_spot(r, bits)] = chunk_spot(r, order)
        numbers += [jnp.int32(spot) for spot in spots]
    for columns in (cols_out, cols_in, cols_x, cols_s):
        columns.at = len(numbers)
        numbers += columns.table(places, y_places)
    place = jnp.stack(numbers).astype(jnp.int32)

    ORDER.clear()
    ROOMY[:] = [chunks * shard_rows <= 1024]
    tags = jnp.where(enc_valid[0] == 1, enc_question[0], -1).astype(BF)
    tag_rows = jnp.zeros((16, width), BF).at[0, :shard_rows].set(tags)
    enc_own = jnp.concatenate([encodings[0], tag_rows], 0)[None]
    gains = jnp.stack([gain_self, gain_cross, gain_ff])
    got, second = gather_encodings(enc_own, bits)
    shadow(10)
    a1, qkv, p1, o1_near, o1, wso_near, wcq_near, x_near = self_attention(
        x, gains, w_qkv, rel_bias, [w_self_out, w_cross_q, x]
    )
    more, third = second()
    shadow(10)
    h1_near, cq_near, h1, a2, cq, gy = self_project(
        x_near, o1_near, wso_near, gains, wcq_near, [gy]
    )
    pieces, rel = third()
    shadow(10, *more[1:2])
    dhid, wkv_near, wco_near = hidden_gradient(gy, w_ff_out, [w_cross_kv, w_cross_out])
    spots = [[int(chunk_spot(r, bits)) for r in group] for group in rel]
    enc, kv, e, inv, o2, h2, a3, w1_near = cross_forward(
        pieces, spots, shard_rows, tgt_question[0], cq_near, h1_near, wkv_near, wco_near, gains, [w_ff_in]
    )

    dpre, hid, keep, send = feed_hidden(place, a3, gy, dhid, w1_near, cols_out)
    (b_out,) = weight_buckets(cols_out, keep, send, orders, y_bits)
    shadow(30)
    keep, send, h2_near = feed_weights(place, a3, dpre, cols_in, [h2])
    b_in, b_jn = weight_buckets(cols_in, keep, send, orders, y_bits)
    send_round(30, b_out)
    dh2, gain_ff_grad = feed_back(dpre, w1_near, h2_near, gains, gy)
    send_round(8, b_in, b_jn)
    pairs = heads // 2
    parts_a = cross_backward(0, pairs // 2, dh2, o2, inv, cq, kv, e, wco_near, [])
    parts_b = cross_backward(
        pairs // 2, pairs, dh2, o2, inv, cq, kv, e, wco_near, [w_cross_q, h1, a2, o2, o1, enc, w_cross_kv]
    )
    wcq_near, h1_near, a2, o2, o1, enc, wkv_near = parts_b[3:]
    dcq, dkt, dvt = zip(parts_a, parts_b[:3])
    dh1, gain_cross_grad = cross_query_back(dcq, wcq_near, h1_near, gains, dh2)
    send_round(12, b_jn, b_out, b_in)
    genc, keep, send, hid, w2_near, h2_near = cross_weights(
        place, dh2, o2, dcq, dkt, dvt, enc, a2, wkv_near, dh1, o1, cols_x, [hid, w_ff_out, h2]
    )
    enc_rows = chunks * shard_rows * width // 128
    genc = in_hbm(genc.reshape(enc_rows, shard_rows))
    cut = enc_rows // blocks * (2 * blocks // 3)
    b_ea = Bucket(cut, [(genc, 0)], [("blk", b) for b in orders[0]])
    b_eb = Bucket(enc_rows - cut, [(genc, cut)], [("blk", b) for b in orders[1]])
    b_xa, b_xb = weight_buckets(cols_x, keep, send, orders, y_bits)
    send_round(40, b_ea, b_out, b_eb, b_jn, settle=[b_in])
    out, wso_near, qkv, p1 = feed_out(hid, w2_near, h2_near, [w_self_out, qkv, p1])
    dqkv, gbias, wqkv_near, x_near, a1 = self_backward(
        dh1, wso_near, qkv, p1, bucket_count, heads, [w_qkv, x, a1]
    )
    send_round(8, b_xb, b_xa, b_eb, b_ea, b_in, b_out, settle=[b_jn])
    grad_dec, keep, send = self_weights(
        place, dh1, a1, dqkv, x_near, gains, wqkv_near, gbias, gain_cross_grad, gain_ff_grad, cols_s
    )
    b_sa, b_sb, b_misc = weight_buckets(cols_s, keep, send, orders, y_bits)
    send_round(25, b_xb, b_xa, b_ea, b_eb, settle=[b_in, b_out])
    send_round(4, b_sb, b_sa, b_misc)
    rest_of(b_out, b_in, b_jn)
    total_ff = Total([(cols_out, [b_out]), (cols_in, [b_in, b_jn])], [], dp_size)
    send_round(4, b_xa, b_xb, total_ff, settle=[b_ea, b_eb])
    rest_of(b_ea, b_eb)
    send_round(4, b_sa, b_misc, b_sb)
    send_round(4, b_xb, b_sa, b_misc, total_ff)
    grad_enc = join_encodings([b_ea, b_eb], shard_rows, width)
    send_round(4, b_sb)
    rest_of(total_ff)
    grad_ff_out, grad_ff_in = total_ff.finish(place, [[("out", stack)], [("in", 1)]])
    rest_of(b_xa, b_xb)
    total_x = Total([(cols_x, [b_xa, b_xb])], [], dp_size)
    send_round(4, b_sb, total_x)
    rest_of(b_sa, b_sb, b_misc)
    total_s = Total([(cols_s, [b_sa, b_sb])], [b_misc], dp_size)
    send_round(4, total_s, total_x)
    rest_of(total_s, total_x)
    grad_cross_out, grad_cross_q, grad_self_out, grad_cross_kv = total_x.finish(
        place, [[("out", 1), ("q", 1), ("self", 1), ("kv", 1)]]
    )
    grad_qkv, misc = total_s.finish(place, [[("qkv", 1)]])
    gains = misc[16 : 16 + width // 16].reshape(width // 128, 8, 128)[:, :3].transpose(1, 0, 2).reshape(3, width)
    gains = lax.dynamic_slice(gains, (0, blk * part), (3, part))
    bias_part = bucket_count // chunks
    grad_bias = lax.dynamic_slice(misc, (0, blk * bias_part), (heads, bias_part)).T
    return (
        out[None],
        grad_dec[None],
        grad_enc[None],
        gains[0],
        grad_qkv,
        grad_bias,
        grad_self_out,
        gains[1],
        grad_cross_q,
        grad_cross_kv,
        grad_cross_out,
        gains[2],
        grad_ff_in,
        grad_ff_out,
    )


def solution(mesh):
    return jax.shard_map(
        local,
        mesh=mesh,
        in_specs=(
            P("dp", "blk", None),
            P("dp", "blk", None),
            P("dp", "blk"),
            P("dp", "blk"),
            P("dp", "blk"),
            P(),
            P(),
            P(),
            P(),
            P(),
            P(),
            P(),
            P(),
            P(),
            P(),
            P(),
            P("dp", "blk", None),
        ),
        out_specs=(
            P("dp", "blk", None),
            P("dp", "blk", None),
            P("dp", "blk", None),
            P("blk"),
            P("blk", None),
            P("blk", None),
            P("blk", None),
            P("blk"),
            P("blk", None),
            P("blk", None),
            P("blk", None),
            P("blk"),
            P("blk", None),
            P("blk", None),
        ),
        check_vma=False,
    )
```

```python
import functools
import math

import jax
import jax.numpy as jnp
import numpy as np
from jax import lax
from jax.experimental import pallas as pl
from jax.experimental.pallas import tpu as pltpu
from jax.sharding import PartitionSpec as P

TLEN = 32
EPSILON = 1e-06
NEG_LARGE = -1e30
GROUP = 128
LOG2E = 1.4426950408889634
BF = jnp.bfloat16
F32 = jnp.float32
VMEM = pl.BlockSpec(memory_space=pltpu.VMEM)
SMEM = pl.BlockSpec(memory_space=pltpu.SMEM)
ANY = pl.BlockSpec(memory_space=pl.ANY)
HBM, STREAM, DRAIN, NEAR, PAIR = "hbm", "stream", "drain", "near", "pair"
MIB = 2**20
LIMITS = dict(
    self_attention=24, self_project=12, cross_forward=30, hidden_gradient=10, feed_hidden=26, feed_weights=18,
    feed_back=12, feed_out=12, cross_backward=20, cross_query_back=12, cross_weights=34, self_backward=14,
    self_weights=24, sum_kernel=16, finish=24, shadow=1, join_encodings=8,
)


def bucket_of(distance, bucket_count):
    exact_count = bucket_count // 2
    if distance < exact_count:
        return distance
    scaled = math.log(distance / exact_count) / math.log(128.0 / exact_count) * exact_count
    return min(bucket_count - 1, exact_count + int(scaled))


def bucket_firsts(bucket_count):
    firsts = {}
    for distance in range(TLEN):
        firsts.setdefault(bucket_of(distance, bucket_count), distance)
    return sorted(firsts.items())


def dot_nn(a, b):
    return jnp.dot(a, b, preferred_element_type=F32)


def dot_nt(a, b):
    return lax.dot_general(a, b, (((1,), (1,)), ((), ())), preferred_element_type=F32)


def dot_tn(a, b):
    return lax.dot_general(a, b, (((0,), (0,)), ((), ())), preferred_element_type=F32)


def inv_rms(v):
    return lax.rsqrt(jnp.mean(v * v, axis=-1, keepdims=True) + EPSILON)


def rms_back(dy, v, gain):
    r = inv_rms(v)
    vr = v * r
    dg = dy * gain
    dv = r * (dg - vr * jnp.mean(dg * vr, axis=-1, keepdims=True))
    return dv, jnp.sum(dy * vr, axis=0, keepdims=True)


def half_masks(rows):
    lane = lax.broadcasted_iota(jnp.int32, (rows, 128), 1)
    low = (lane < 64).astype(F32)
    return low.astype(BF), (1.0 - low).astype(BF)


def chunk_place(chunk, blk, bits):
    rel = jnp.bitwise_xor(chunk, blk)
    place = jnp.int32(0)
    for bit in bits:
        place = place * 2 + jnp.where(jnp.bitwise_and(rel, bit) != 0, 1, 0)
    return place


def chunk_spot(rel, bits):
    spot = 0
    for bit in bits:
        spot = spot * 2 + (1 if rel & bit else 0)
    return spot


def query_block(rows, tokens):
    return max(GROUP, min(rows, rows * 1024 // tokens))


def big(tokens):
    return 61 if tokens > 1024 else None


class Stream:
    def __init__(self, copy, ref):
        self.copy, self.ref, self.waited = copy, ref, False

    def ready(self):
        if not self.waited:
            self.copy.wait()
            self.waited = True
        return self.ref


class Drain:
    def __init__(self, copy, ref, out, sem):
        self.copy, self.ref, self.started = copy, ref, False
        self.out, self.sem = out, sem

    def flush(self):
        self.copy.start()
        self.started = True

    def flush_part(self, at):
        pltpu.make_async_copy(self.ref.at[at], self.out.at[at], self.sem).start()
        self.started = True


ORDER = []
ROOMY = [True]


class Pair:
    def __init__(self, drains, ref):
        self.drains, self.ref = drains, ref


def in_hbm(x):
    return pltpu.with_memory_space_constraint(x, pltpu.HBM)


def call(
    name, body, out_shape, in_specs, out_specs, operands, scratch=(), grid=(), prefetch=0,
    limit=None, cost=0.001, ahead=(),
):
    operands, in_specs = list(operands), list(in_specs)
    after = list(ORDER)
    wanted = ahead
    ahead = wanted if ROOMY[0] else ()
    outs = isinstance(out_shape, (tuple, list))
    out_shape = list(out_shape) if outs else [out_shape]
    out_specs = list(out_specs) if outs else [out_specs]
    streams, drains, pairs = [], [], []
    extra_scratch = []
    for i, spec in enumerate(in_specs):
        at = prefetch + i
        if spec == STREAM:
            streams.append(at)
            in_specs[i] = ANY
            operands[at] = in_hbm(operands[at])
            extra_scratch += [pltpu.VMEM(operands[at].shape, operands[at].dtype), pltpu.SemaphoreType.DMA]
        elif isinstance(spec, tuple):
            in_specs[i] = spec[1]
            operands[at] = in_hbm(operands[at])
    real = prefetch + len(in_specs)
    for i, spec in enumerate(out_specs):
        shape = out_shape[i]
        if spec == PAIR:
            pairs.append(i)
            out_specs[i] = ANY
            out_shape[i] = pltpu.HBM(shape.shape, shape.dtype)
            if len(pairs) % 2:
                extra_scratch += [
                    pltpu.VMEM((2, *shape.shape), shape.dtype), pltpu.SemaphoreType.DMA((2,))
                ]
        elif spec == DRAIN:
            drains.append(i)
            out_specs[i] = ANY
            out_shape[i] = pltpu.HBM(shape.shape, shape.dtype)
            extra_scratch += [pltpu.VMEM(shape.shape, shape.dtype), pltpu.SemaphoreType.DMA]
        elif spec == NEAR or isinstance(spec, tuple):
            space = pltpu.VMEM if spec == NEAR or spec[0] == NEAR else pltpu.HBM
            out_specs[i] = VMEM if spec == NEAR else spec[1]
            if ROOMY[0] or space is pltpu.HBM:
                out_shape[i] = space(shape.shape, shape.dtype)
    count = len(out_shape)
    for array in ahead:
        out_specs.append(VMEM if not grid else ANY)
        out_shape.append(pltpu.VMEM(array.shape, array.dtype))
    if ahead:
        extra_scratch.append(pltpu.SemaphoreType.DMA((len(ahead),)))
    after = [in_hbm(array) for array in ahead] + after
    out_specs.append(ANY)
    out_shape.append(pltpu.HBM((8, 128), F32))

    def ordered(*refs):
        ins = list(refs[:real])
        results = list(refs[real + len(after) : real + len(after) + len(out_shape) - 1])
        rest = list(refs[real + len(after) + len(out_shape) :])
        early = [
            pltpu.make_async_copy(refs[real + i], results[count + i], rest[-1].at[i])
            for i in range(len(ahead))
        ]
        del results[count:]
        own, extra = rest[: len(scratch)], rest[len(scratch) :]
        made, ends = [], []
        for n, i in enumerate(streams):
            copy = pltpu.make_async_copy(ins[i], extra[2 * n], extra[2 * n + 1])
            copy.start()
            ins[i] = Stream(copy, extra[2 * n])
            made.append(ins[i])
        extra = extra[2 * len(streams) :]
        for i in sorted(drains + pairs[::2]):
            held, sem = extra[:2]
            extra = extra[2:]
            if i in drains:
                copy = pltpu.make_async_copy(held, results[i], sem)
                results[i] = Drain(copy, held, results[i], sem)
                ends.append(results[i])
            else:
                halves = [
                    Drain(
                        pltpu.make_async_copy(held.at[k], results[i + k], sem.at[k]),
                        held.at[k], results[i + k], sem.at[k],
                    )
                    for k in range(2)
                ]
                results[i] = Pair(halves, held)
                ends += results[i].drains
        for i in reversed(pairs[1::2]):
            del results[i]
        for n, copy in enumerate(early):
            if grid:
                pl.when(pl.program_id(0) == 0)(copy.start)
            else:
                copy.start()
        body(*ins, *results, *own)
        for copy in early:
            if grid:
                pl.when(pl.program_id(0) == grid[0] - 1)(copy.wait)
            else:
                copy.wait()
        for stream in made:
            stream.ready()
        for end in ends:
            if not end.started:
                end.flush()
        for end in ends:
            end.copy.wait()

    got = pl.pallas_call(
        ordered,
        out_shape=tuple(out_shape),
        grid_spec=pltpu.PrefetchScalarGridSpec(
            num_scalar_prefetch=prefetch,
            grid=grid,
            in_specs=in_specs + [ANY] * len(after),
            out_specs=tuple(out_specs),
            scratch_shapes=list(scratch) + extra_scratch,
        ),
        compiler_params=pltpu.CompilerParams(vmem_limit_bytes=(limit or LIMITS[name]) * MIB),
        name=name,
        cost_estimate=pl.CostEstimate(
            flops=int(cost * 1153 * 10**6), bytes_accessed=0, transcendentals=0
        ),
    )(*operands, *after)
    ORDER[:] = [in_hbm(got[-1])]
    got = (*got[:count], *(got[count:-1] if ahead else wanted))
    return got if outs or wanted else got[0]


def shadow(cost, *arrays):
    call("shadow", lambda *_: None, (), [ANY] * len(arrays), (), arrays, cost=cost)


def whole(*shape):
    return pl.BlockSpec(shape, lambda *_: (0,) * len(shape))


def shape_of(dtype, *shape):
    return jax.ShapeDtypeStruct(shape, dtype)


class Columns:
    def __init__(self, names, sections, y_parts, chunks, part):
        self.names, self.y_parts, self.chunks, self.part = names, y_parts, chunks, part
        self.sections = []
        first = unit = 0
        for blocks, order in sections:
            if blocks:
                self.sections.append((first, blocks, order, unit))
            first, unit = first + blocks, unit + chunks * blocks
        self.blocks, self.units = first, unit

    def shape(self, more=0):
        return shape_of(BF, self.units + more, self.part, 128)

    def first(self, name):
        done = 0
        for other, width in self.names:
            if other == name:
                return done
            done += width // 128

    def find(self, block):
        for i, (first, blocks, order, _) in enumerate(self.sections):
            if first <= block < first + blocks:
                if order != "y":
                    return i, None, block - first
                y, k = divmod(block - first, blocks // self.y_parts)
                return i, y, k

    def runs(self):
        found = []
        for first, blocks, order, _ in self.sections:
            size = blocks // self.y_parts if order == "y" else blocks
            found += [(at, size) for at in range(first, first + blocks, size)]
        return found

    def table(self, spots, y_spots):
        units = []
        for c in range(self.chunks):
            for block in range(self.blocks):
                i, y, k = self.find(block)
                _, blocks, order, unit = self.sections[i]
                if y is None:
                    units.append(unit + spots[order][c] * blocks + k)
                else:
                    units.append(unit + (y_spots[y] * self.chunks + spots[0][c]) * (blocks // self.y_parts) + k)
        return units

    def store(self, ref, half, name, value, place_ref, chunks=None, block=0):
        chunks = range(self.chunks) if chunks is None else chunks
        start = self.first(name) + block
        slot = jnp.bitwise_xor(place_ref[0], half)
        for n, c in enumerate(chunks):
            for j in range(value.shape[1] // 128):
                unit = place_ref[self.at + c * self.blocks + start + j]
                ref[slot, unit] = value[n * self.part : (n + 1) * self.part, j * 128 : (j + 1) * 128].astype(BF)


def self_attention(x, gains, w_qkv, rel_bias, ahead):
    rows, width = x.shape
    bucket_count, heads = rel_bias.shape
    pairs = heads // 2
    groups = rows // GROUP
    firsts = bucket_firsts(bucket_count)

    def body(
        x, gs_ref, wqkv, rb_ref, a1_out, qkv_out, p1_out, o1_ref, o1_out, bias
    ):
        a1_ref, qkv_ref, p1_ref = a1_out.ref, qkv_out.ref, p1_out.ref
        xf = x.ready()[...].astype(F32)
        a1 = (xf * inv_rms(xf) * gs_ref[0:1, :]).astype(BF)
        a1_ref[...] = a1
        a1_out.flush()
        row = lax.broadcasted_iota(jnp.int32, (TLEN, GROUP), 0)
        col = lax.broadcasted_iota(jnp.int32, (TLEN, GROUP), 1)
        distance = lax.rem(col, TLEN) - row

        def make_bias(h, carry):
            val = jnp.full((TLEN, GROUP), NEG_LARGE, F32)
            for b, first in firsts:
                val = jnp.where(distance >= first, rb_ref[h, b], val)
            lanes = pl.ds(pl.multiple_of(lax.rem(h, 2) * GROUP, GROUP), GROUP)
            for t in range(GROUP // TLEN):
                bias[h // 2, t * TLEN : (t + 1) * TLEN, lanes] = jnp.where(
                    col // TLEN == t, val, NEG_LARGE
                )
            return carry

        lax.fori_loop(0, heads, make_bias, 0)
        wqkv_ref = wqkv.ready()

        def project(t, carry):
            at = pl.ds(pl.multiple_of(t * width, 128), width)
            qkv_ref[:, at] = dot_nn(a1_ref[...], wqkv_ref[:, at]).astype(BF)
            return carry

        lax.fori_loop(0, 3, project, 0)
        qkv_out.flush()
        m0, m1 = half_masks(GROUP)

        def attend(g, carry):
            at = pl.ds(pl.multiple_of(g * GROUP, GROUP), GROUP)
            for pair in range(pairs):
                lo = pair * 128
                q = qkv_ref[at, lo : lo + 128]
                k = qkv_ref[at, width + lo : width + lo + 128]
                v = qkv_ref[at, 2 * width + lo : 2 * width + lo + 128]
                s = dot_nt(k, jnp.concatenate([q * m0, q * m1], 0)) + bias[pair]
                e = jnp.exp(s - jnp.max(s, 0, keepdims=True))
                p = (e / jnp.sum(e, 0, keepdims=True)).astype(BF)
                p1_ref[g, pair] = p
                o = dot_tn(
                    jnp.concatenate([p[:, :GROUP], p[:, GROUP:]], 0),
                    jnp.concatenate([v * m0, v * m1], 0),
                )
                o1_ref[at, lo : lo + 128] = o.astype(BF)
            p1_out.flush_part(pl.ds(g, 1))
            return carry

        lax.fori_loop(0, groups, attend, 0)
        o1_out.ref[...] = o1_ref[...]
        o1_out.flush()

    return call(
        "self_attention",
        body,
        (
            shape_of(BF, rows, width),
            shape_of(BF, rows, 3 * width),
            shape_of(BF, groups, pairs, GROUP, 2 * GROUP),
            shape_of(BF, rows, width),
            shape_of(BF, rows, width),
        ),
        [STREAM, VMEM, STREAM, SMEM],
        (DRAIN, DRAIN, DRAIN, NEAR, DRAIN),
        (x, gains, w_qkv, rel_bias.T),
        ahead=ahead,
        scratch=[pltpu.VMEM((pairs, GROUP, 2 * GROUP), F32)],
    )


def self_project(x, o1, w_self_out, gains, w_cross_q, ahead):
    rows, width = x.shape

    def body(x_ref, o1_ref, wso_ref, gc_ref, wcq_ref, h1_ref, cq_ref, h1_out, a2_out, cq_out):
        h1 = dot_nn(o1_ref[...], wso_ref[...]) + x_ref[...].astype(F32)
        h1_ref[...] = h1
        h1_out.ref[...] = h1
        h1_out.flush()
        a2 = (h1 * inv_rms(h1) * gc_ref[1:2, :]).astype(BF)
        a2_out.ref[...] = a2
        a2_out.flush()
        cq = dot_nn(a2, wcq_ref[...]).astype(BF)
        cq_ref[...] = cq
        cq_out.ref[...] = cq

    low, full = shape_of(BF, rows, width), shape_of(F32, rows, width)
    return call(
        "self_project",
        body,
        (full, low, full, low, low),
        [VMEM] * 5,
        (NEAR, NEAR, DRAIN, DRAIN, DRAIN),
        (x, o1, w_self_out, gains, w_cross_q),
        ahead=ahead,
    )


def cross_forward(
    pieces, order, shard_rows, tgt_question, cq, h1, w_cross_kv, w_cross_out, gains, ahead
):
    rows, width = cq.shape
    pairs = width // 128
    tokens = sum(len(o) for o in order) * shard_rows
    targets = rows // TLEN
    block_rows = query_block(rows, tokens)
    blocks = rows // block_rows
    steps = pairs * blocks

    def body(*refs):
        piece_refs = refs[: len(pieces)]
        (
            tq_ref, cq_ref, h1_ref, wkv_ref, wco_ref, gf_ref,
            enc_out, kv_out, e_ref, inv_out, o2_out, h2_out, a3_ref,
            kfeat, qfeat, ebuf, sem,
        ) = refs[len(pieces) :]
        enc_ref, kv_ref, inv_ref, o2_ref = enc_out.ref, kv_out.ref, inv_out.ref, o2_out.ref
        lane = lax.rem(lax.broadcasted_iota(jnp.int32, (shard_rows, 128), 1), 64).astype(F32)
        for ref, places in zip(piece_refs, order):
            for j, spot in enumerate(places):
                at = slice(spot * shard_rows, (spot + 1) * shard_rows)
                enc_ref[at, :] = ref[j, :shard_rows, :]
                tag = ref[j, shard_rows : shard_rows + 1, :shard_rows].astype(F32)
                tag = jnp.transpose(jnp.broadcast_to(tag, (128, shard_rows)))
                kfeat[at, :] = jnp.where(tag == lane, 0.0, NEG_LARGE).astype(BF)
        lane_t = lax.rem(lax.broadcasted_iota(jnp.int32, (TLEN, 128), 1), 64)
        for t in range(targets):
            qfeat[t * TLEN : (t + 1) * TLEN, :] = jnp.where(lane_t == tq_ref[t], 1.0, 0.0).astype(BF)
        enc_out.flush()

        def project(t, carry):
            at = pl.ds(pl.multiple_of(t * width, 128), width)
            kv_ref[:, at] = dot_nn(enc_ref[...], wkv_ref[:, at]).astype(BF)
            return carry

        lax.fori_loop(0, 2, project, 0)
        kv_out.flush()
        q0, q1 = half_masks(block_rows)
        k0, k1 = half_masks(tokens)
        qmask, kmask = (q0, q1), (k0, k1)
        low = lax.broadcasted_iota(jnp.int32, (block_rows, 128), 1) < 64

        def out_copy(slot, step):
            pair, block = step // blocks, lax.rem(step, blocks)
            return pltpu.make_async_copy(
                ebuf.at[slot],
                e_ref.at[pl.ds(2 * pair, 2), pl.ds(block * block_rows, block_rows)],
                sem.at[slot],
            )

        def attend(step, carry):
            slot = lax.rem(step, 2)
            pair, block = step // blocks, lax.rem(step, blocks)
            lo = pl.multiple_of(pair * 128, 128)
            at = pl.ds(pl.multiple_of(block * block_rows, block_rows), block_rows)

            @pl.when(step >= 2)
            def _():
                out_copy(slot, step - 2).wait()

            q = cq_ref[at, pl.ds(lo, 128)]
            k = kv_ref[:, pl.ds(lo, 128)]
            v = kv_ref[:, pl.ds(width + lo, 128)]
            keys = [k * kmask[h] + kfeat[...] * kmask[1 - h] for h in range(2)]
            values = [v * kmask[h] + kmask[1 - h] for h in range(2)]
            size = min(block_rows, 256)
            units = [(r, h) for r in range(0, block_rows, size) for h in range(2)]
            tagged = qfeat[at, :]

            def score(unit):
                r, h = unit
                qa = q[r : r + size] * qmask[h][:size] + tagged[r : r + size] * qmask[1 - h][:size]
                return dot_nt(qa, keys[h])

            outs, last = {}, None
            s = score(units[0])
            for i, unit in enumerate(units):
                later = score(units[i + 1]) if i + 1 < len(units) else None
                if last is not None:
                    outs[last[0]] = dot_nn(last[1], values[last[0][1]])
                e = jnp.exp(s - jnp.max(s, -1, keepdims=True)).astype(BF)
                ebuf[slot, unit[1], unit[0] : unit[0] + size, :] = e
                last, s = (unit, e), later
            outs[last[0]] = dot_nn(last[1], values[last[0][1]])
            outs = [
                jnp.concatenate([outs[r, h] for r in range(0, block_rows, size)], 0) for h in range(2)
            ]
            out_copy(slot, step).start()
            total = jnp.where(low, pltpu.roll(outs[0], 64, 1), pltpu.roll(outs[1], 64, 1))
            inv = 1.0 / total
            inv_ref[at, pl.ds(lo, 128)] = inv
            o2_ref[at, pl.ds(lo, 128)] = (jnp.where(low, outs[0], outs[1]) * inv).astype(BF)
            if blocks == 1:
                inv_out.flush_part((slice(None), pl.ds(lo, 128)))
                o2_out.flush_part((slice(None), pl.ds(lo, 128)))
            return carry

        lax.fori_loop(0, steps, attend, 0)
        if blocks > 1:
            inv_out.flush()
            o2_out.flush()
        h2 = h1_ref[...] + dot_nn(o2_ref[...], wco_ref[...])
        h2_out.ref[...] = h2
        h2_out.flush()
        a3_ref[...] = (h2 * inv_rms(h2) * gf_ref[2:3, :]).astype(BF)
        for step in range(max(0, steps - 2), steps):
            out_copy(step % 2, jnp.int32(step)).wait()

    return call(
        "cross_forward",
        body,
        (
            shape_of(BF, tokens, width),
            shape_of(BF, tokens, 2 * width),
            shape_of(BF, 2 * pairs, rows, tokens),
            shape_of(F32, rows, width),
            shape_of(BF, rows, width),
            shape_of(F32, rows, width),
            shape_of(BF, rows, width),
        ),
        [VMEM] * len(pieces) + [SMEM] + [VMEM] * 5,
        (DRAIN, DRAIN, (HBM, ANY), DRAIN, DRAIN, DRAIN, NEAR),
        (*pieces, tgt_question, cq, h1, w_cross_kv, w_cross_out, gains),
        scratch=[
            pltpu.VMEM((tokens, 128), BF),
            pltpu.VMEM((rows, 128), BF),
            pltpu.VMEM((2, 2, block_rows, tokens), BF),
            pltpu.SemaphoreType.DMA((2,)),
        ],
        limit=big(tokens),
        ahead=ahead,
    )


def hidden_gradient(gy, w_ff_out, ahead):
    rows, width = gy.shape
    hidden = w_ff_out.shape[0]

    tiles = hidden // width

    def body(gy_ref, w2_ref, out_ref, w2, sem):
        def copy(t):
            at = pl.ds(pl.multiple_of(t * width, 128), width)
            return pltpu.make_async_copy(w2_ref.at[at], w2.at[at], sem.at[t])

        for t in range(tiles):
            copy(t).start()

        def tile(t, carry):
            copy(t).wait()
            at = pl.ds(pl.multiple_of(t * width, 128), width)
            out_ref[:, at] = dot_nt(gy_ref[...], w2[at, :]).astype(BF)
            return carry

        lax.fori_loop(0, tiles, tile, 0)

    return call(
        "hidden_gradient",
        body,
        shape_of(BF, rows, hidden),
        [VMEM, (HBM, ANY)],
        NEAR,
        (gy, w_ff_out),
        scratch=[pltpu.VMEM((hidden, width), BF), pltpu.SemaphoreType.DMA((tiles,))],
        ahead=ahead,
    )


def feed_hidden(place, a3, gy, dhid, w_ff_in, columns):
    rows, width = a3.shape
    hidden = w_ff_in.shape[1]
    tile = width
    half = width // 2
    sub = hidden // width
    part = columns.part
    per_tile = columns.chunks * tile // hidden
    scale = math.sqrt(2.0 / math.pi)

    def body(place_ref, a3_ref, gy_ref, dhid_ref, w1_ref, dpre_ref, hid_out, both):
        def activate(pre, at):
            sq = pre * pre
            t = jnp.tanh(pre * (scale + (scale * 0.044715) * sq))
            up = 0.5 + 0.5 * t
            hid = (pre * up).astype(BF)
            slope = up + pre * (up - up * up) * ((2.0 * scale) + (2.0 * scale * 0.134145) * sq)
            hid_out.ref[:, at] = hid
            dpre_ref[:, at] = (dhid_ref[:, at].astype(F32) * slope).astype(BF)
            return hid

        def one(step, carry):
            parts = tile // 256
            ats = [pl.ds(pl.multiple_of(step * tile + i * 256, 128), 256) for i in range(parts)]
            a3, gyv = a3_ref[...], gy_ref[...]
            pre = dot_nn(a3, w1_ref[:, ats[0]])
            grads, hid = [], None
            for i in range(parts):
                later = dot_nn(a3, w1_ref[:, ats[i + 1]]) if i + 1 < parts else None
                if hid is not None:
                    grads.append(dot_tn(hid, gyv))
                hid = activate(pre, ats[i])
                pre = later
            grads.append(dot_tn(hid, gyv))
            hid_out.flush_part((slice(None), pl.ds(pl.multiple_of(step * tile, 128), tile)))
            g = jnp.concatenate(grads, 0)
            for i in range(per_tile):
                chunk = step * per_tile + i
                for h in range(2):
                    for j in range(sub):
                        first = (i * sub + j) * part
                        columns.store(
                            both.ref, h, "out", g[first : first + part, h * half : (h + 1) * half],
                            place_ref, [chunk], j * half // 128,
                        )
                for first, count in columns.runs():
                    unit = place_ref[columns.at + chunk * columns.blocks + first]
                    for drain in both.drains:
                        drain.flush_part(pl.ds(unit, count))
            return carry

        lax.fori_loop(0, hidden // tile, one, 0)

    return call(
        "feed_hidden",
        body,
        (shape_of(BF, rows, hidden), shape_of(BF, rows, hidden), columns.shape(), columns.shape()),
        [SMEM, VMEM, VMEM, VMEM, VMEM],
        (NEAR, DRAIN, PAIR, PAIR),
        (place, a3, gy, dhid, w_ff_in),
    )


def feed_weights(place, a3, dpre, columns, ahead):
    width = a3.shape[1]
    hidden = dpre.shape[1]

    def body(place_ref, a3_ref, dpre_ref, both):
        tiles = hidden // width

        def one(t, carry):
            at = pl.ds(pl.multiple_of(t * width, 128), width)
            g = dot_tn(a3_ref[...], dpre_ref[:, at])
            block = lax.rem(t, tiles // 2) * (width // 128)
            columns.store(both.ref, t // (tiles // 2), "in", g, place_ref, None, block)
            for slot in range(2):

                @pl.when(jnp.logical_and(t == tiles // 2 - 1, place_ref[0] == slot))
                def _():
                    both.drains[slot].flush_part(pl.ds(0, columns.units))

                @pl.when(jnp.logical_and(t == tiles - 1, place_ref[0] != slot))
                def _():
                    both.drains[slot].flush_part(pl.ds(0, columns.units))

            return carry

        lax.fori_loop(0, tiles, one, 0)

    return call(
        "feed_weights",
        body,
        (columns.shape(), columns.shape()),
        [SMEM, VMEM, VMEM],
        (PAIR, PAIR),
        (place, a3, dpre),
        ahead=ahead,
    )


def feed_back(dpre, w_ff_in, h2, gains, gy):
    rows, width = h2.shape

    def body(dpre_ref, w1_ref, h2_ref, gf_ref, gy_ref, dh2_ref, gain_ref, da3):
        da3[...] = jnp.zeros_like(da3)

        def one(t, carry):
            at = pl.ds(pl.multiple_of(t * width, 128), width)
            da3[...] += dot_nt(dpre_ref[:, at], w1_ref[:, at])
            return carry

        lax.fori_loop(0, dpre_ref.shape[1] // width, one, 0)
        dv, dgain = rms_back(da3[...], h2_ref[...], gf_ref[2:3, :])
        dh2_ref[...] = gy_ref[...].astype(F32) + dv
        gain_ref[...] = dgain

    return call(
        "feed_back",
        body,
        (shape_of(F32, rows, width), shape_of(F32, 1, width)),
        [VMEM] * 5,
        (NEAR, NEAR),
        (dpre, w_ff_in, h2, gains, gy),
        scratch=[pltpu.VMEM((rows, width), F32)],
    )


def feed_out(hid, w_ff_out, h2, ahead):
    rows, width = h2.shape

    def body(hid_ref, w2_ref, h2_ref, out, total):
        total[...] = h2_ref[...]

        def one(t, carry):
            at = pl.ds(pl.multiple_of(t * width, 128), width)
            total[...] += dot_nn(hid_ref[:, at], w2_ref[at, :])
            return carry

        lax.fori_loop(0, hid_ref.shape[1] // width, one, 0)
        out.ref[...] = total[...].astype(BF)

    return call(
        "feed_out",
        body,
        (shape_of(BF, rows, width),),
        [VMEM] * 3,
        (DRAIN,),
        (hid, w_ff_out, h2),
        scratch=[pltpu.VMEM((rows, width), F32)],
        ahead=ahead,
    )


def cross_backward(first_pair, last_pair, dh2, o2, inv, cq, kv, e, w_cross_out, ahead):
    rows, width = cq.shape
    pairs = width // 128
    count = last_pair - first_pair
    tokens = kv.shape[0]
    block_rows = query_block(rows, tokens)
    blocks = rows // block_rows

    def body(
        dh2_ref, wco_ref, o2_ref, inv_ref, cq_ref, k_ref, v_ref, e_ref,
        dcq_ref, dkt_ref, dvt_ref,
        do2,
    ):
        pair = pl.program_id(0)

        @pl.when(pair == 0)
        def _():
            do2v = dot_nt(dh2_ref[...].astype(BF), wco_ref[...]).astype(BF)
            for i in range(count):
                do2[i] = do2v[:, i * 128 : (i + 1) * 128]

        q0, q1 = half_masks(block_rows)
        k0, k1 = half_masks(tokens)
        qmask, kmask = (q0, q1), (k0, k1)
        lane = lax.broadcasted_iota(jnp.int32, (block_rows, 128), 1)
        low = lane < 64
        first = lax.rem(lane, 64) == 0
        second = lax.rem(lane, 64) == 1
        k, v = k_ref[...], v_ref[...]
        sums = [0.0] * 4
        for block in range(blocks):
            at = slice(block * block_rows, (block + 1) * block_rows)
            q = cq_ref[at, :]
            dof = do2[pair, at, :].astype(F32) * inv_ref[at, :]
            dob = dof.astype(BF)
            prod = dof * o2_ref[at, :].astype(F32)
            qt = jnp.transpose(q)
            dot_t = jnp.transpose(dob)
            dqs = []
            for h in range(2):
                own = low if h == 0 else jnp.logical_not(low)
                delta = -jnp.sum(jnp.where(own, prod, 0.0), -1, keepdims=True)
                hi = delta.astype(BF).astype(F32)
                feat = jnp.where(first, hi, jnp.where(second, delta - hi, 0.0)).astype(BF)
                doa = dob * qmask[h] + feat * qmask[1 - h]
                dp = dot_nt(doa, v * kmask[h] + kmask[1 - h])
                ev = e_ref[h, at, :]
                ds = (ev.astype(F32) * dp).astype(BF)
                dqs.append(dot_nn(ds, k))
                sums[h] = sums[h] + dot_nn(qt[h * 64 : (h + 1) * 64, :], ds)
                sums[2 + h] = sums[2 + h] + dot_nn(dot_t[h * 64 : (h + 1) * 64, :], ev)
            dcq_ref[at, :] = jnp.where(low, dqs[0], dqs[1]).astype(BF)
        for h in range(2):
            dkt_ref[h * 64 : (h + 1) * 64, :] = sums[h].astype(BF)
            dvt_ref[h * 64 : (h + 1) * 64, :] = sums[2 + h].astype(BF)

    near = HBM if big(tokens) else NEAR

    def column(n, first=first_pair):
        return pl.BlockSpec((n, 128), lambda p: (0, p + first))

    return call(
        "cross_backward",
        body,
        (
            shape_of(BF, rows, count * 128),
            shape_of(BF, count * 128, tokens),
            shape_of(BF, count * 128, tokens),
        ),
        [
            whole(rows, width),
            pl.BlockSpec((count * 128, width), lambda p: (first_pair // count, 0)),
            (HBM, column(rows)),
            (HBM, column(rows)),
            (HBM, column(rows)),
            (HBM, column(tokens)),
            (HBM, column(tokens, first_pair + pairs)),
            (HBM, pl.BlockSpec((2, rows, tokens), lambda p: (p + first_pair, 0, 0))),
        ],
        (
            (NEAR, column(rows, 0)),
            (near, pl.BlockSpec((128, tokens), lambda p: (p, 0))),
            (near, pl.BlockSpec((128, tokens), lambda p: (p, 0))),
        ),
        (dh2, w_cross_out, o2, inv, cq, kv, kv, e),
        scratch=[pltpu.VMEM((count, rows, 128), BF)],
        grid=(count,),
        ahead=ahead,
        limit=big(tokens),
    )


def cross_query_back(dcq, w_cross_q, h1, gains, dh2):
    rows, width = h1.shape
    n = len(dcq)
    size = width // n

    def body(*refs):
        wcq_ref, h1_ref, gc_ref, dh2_ref, dh1_ref, gain_ref = refs[n:]
        da2 = 0.0
        for i in range(n):
            da2 = da2 + dot_nt(refs[i][...], wcq_ref[:, i * size : (i + 1) * size])
        dv, dgain = rms_back(da2, h1_ref[...], gc_ref[1:2, :])
        dh1_ref[...] = dh2_ref[...] + dv
        gain_ref[...] = dgain

    return call(
        "cross_query_back",
        body,
        (shape_of(F32, rows, width), shape_of(F32, 1, width)),
        [VMEM] * (n + 4),
        (NEAR, NEAR),
        (*dcq, w_cross_q, h1, gains, dh2),
    )


def shard_rows_of(tokens, chunks):
    return tokens // chunks


def cross_weights(place, dh2, o2, dcq, dkt, dvt, enc, a2, w_cross_kv, dh1, o1, columns, ahead):
    rows, width = dh2.shape
    tokens = enc.shape[0]
    half = width // 2
    tile = max(shard_rows_of(tokens, columns.chunks), 512)
    n = len(dcq)
    size = width // n
    blocks = width // 128
    near = 2 * blocks // 3
    shard_rows = tokens // columns.chunks

    def body(place_ref, dh2_ref, dh1_ref, a2_ref, o2_ref, o1_ref, *refs):
        dcq_refs, dkt, dvt = refs[:n], refs[n : 2 * n], refs[2 * n : 3 * n]
        wkv_ref, enc_ref, genc_out, both, lhs, rhs, dkvt = refs[3 * n :]
        for i, r in enumerate(dcq_refs):
            rhs[0, :, i * size : (i + 1) * size] = r[...]
        rhs[1] = dh2_ref[...].astype(BF)
        rhs[2] = dh1_ref[...].astype(BF)
        for i, r in enumerate((a2_ref, o2_ref, o1_ref)):
            lhs[i] = r[...]
        for i, r in enumerate(dkt + dvt):
            dkvt[i * size : (i + 1) * size, :] = r[...]

        def square(i, carry):
            g = dot_tn(lhs[i], rhs[i])
            for h in range(2):
                columns.store(both.ref, h, "q", g[:, h * half : (h + 1) * half], place_ref, None, i * (half // 128))
            return carry

        lax.fori_loop(0, 3, square, 0)

        def encodings(t, carry):
            at = pl.ds(pl.multiple_of(t * tile, 128), tile)
            genct = dot_nn(wkv_ref[...], dkvt[:, at]).astype(BF)
            for i in range(tile // shard_rows):
                for j in range(blocks):
                    order = 0 if j < near else 1
                    size = blocks - near if order else near
                    spot = place_ref[3 + order * columns.chunks + t * (tile // shard_rows) + i]
                    genc_out.ref[order * columns.chunks * near + spot * size + j - order * near] = genct[
                        j * 128 : (j + 1) * 128, i * shard_rows : (i + 1) * shard_rows
                    ]
            return carry

        lax.fori_loop(0, tokens // tile, encodings, 0)
        genc_out.flush()

        def key_value(h, carry):
            g = 0.0
            rows_at = pl.ds(pl.multiple_of(h * width, 128), width)
            for t in range(0, tokens, 1024):
                end = min(tokens, t + 1024)
                g = g + dot_nt(jnp.transpose(enc_ref[t:end, :]), dkvt[rows_at, t:end])
            columns.store(both.ref, h, "kv", g, place_ref)
            return carry

        lax.fori_loop(0, 2, key_value, 0)

    return call(
        "cross_weights",
        body,
        (shape_of(BF, columns.chunks * blocks, 128, shard_rows), columns.shape(), columns.shape()),
        [SMEM] + [VMEM] * (3 * n + 7),
        (DRAIN, PAIR, PAIR),
        (place, dh2, dh1, a2, o2, o1, *dcq, *dkt, *dvt, w_cross_kv, enc),
        scratch=[
            pltpu.VMEM((3, rows, width), BF),
            pltpu.VMEM((3, rows, width), BF),
            pltpu.VMEM((2 * width, tokens), BF),
        ],
        ahead=ahead,
        limit=big(tokens),
    )


def self_backward(dh1, w_self_out, qkv, p1, bucket_count, heads, ahead):
    rows, width = dh1.shape
    pairs = heads // 2
    groups = rows // GROUP
    firsts = bucket_firsts(bucket_count)
    ends = [first for _, first in firsts[1:]] + [TLEN]

    def body(dh1_ref, wso_ref, qkv_ref, p1_ref, dqkv_ref, gbias_ref, do1, acc):
        do1[...] = dot_nt(dh1_ref[...].astype(BF), wso_ref[...]).astype(BF)
        m0, m1 = half_masks(GROUP)
        acc[...] = jnp.zeros_like(acc)

        def attend(g, carry):
            at = pl.ds(pl.multiple_of(g * GROUP, GROUP), GROUP)
            for pair in range(pairs):
                lo = pair * 128
                q = qkv_ref[at, lo : lo + 128]
                k = qkv_ref[at, width + lo : width + lo + 128]
                v = qkv_ref[at, 2 * width + lo : 2 * width + lo + 128]
                do = do1[at, lo : lo + 128]
                do_two = jnp.concatenate([do * m0, do * m1], 0)
                pb = p1_ref[g, pair]
                pf = pb.astype(F32)
                dp = dot_nt(v, do_two)
                ds = (pf * (dp - jnp.sum(pf * dp, 0, keepdims=True))).astype(BF)
                dsf = ds.astype(F32)
                total = dsf[:TLEN]
                for t in range(1, GROUP // TLEN):
                    total = total + dsf[t * TLEN : (t + 1) * TLEN]
                acc[2 * pair] += total[:, :GROUP]
                acc[2 * pair + 1] += total[:, GROUP:]
                dq = dot_tn(
                    jnp.concatenate([ds[:, :GROUP], ds[:, GROUP:]], 0),
                    jnp.concatenate([k * m0, k * m1], 0),
                )
                dk = dot_nn(ds, jnp.concatenate([q * m0, q * m1], 0))
                dv = dot_nn(pb, do_two)
                dqkv_ref[at, lo : lo + 128] = dq.astype(BF)
                dqkv_ref[at, width + lo : width + lo + 128] = dk.astype(BF)
                dqkv_ref[at, 2 * width + lo : 2 * width + lo + 128] = dv.astype(BF)
            return carry

        lax.fori_loop(0, groups, attend, 0)
        row = lax.broadcasted_iota(jnp.int32, (TLEN, GROUP), 0)
        distance = lax.rem(lax.broadcasted_iota(jnp.int32, (TLEN, GROUP), 1), TLEN) - row
        lane = lax.broadcasted_iota(jnp.int32, (16, 128), 1)
        bias = jnp.zeros((16, 128), F32)
        accv = acc[...]
        pad = jnp.zeros((16 - heads, 1), F32)
        for (b, first), end in zip(firsts, ends):
            here = jnp.logical_and(distance >= first, distance < end)
            part_sum = jnp.sum(jnp.where(here[None], accv, 0.0), axis=1)
            col = jnp.sum(part_sum, -1, keepdims=True)
            bias = jnp.where(lane == b, jnp.concatenate([col, pad], 0), bias)
        gbias_ref[...] = bias

    return call(
        "self_backward",
        body,
        (shape_of(BF, rows, 3 * width), shape_of(F32, 16, 128)),
        [VMEM] * 4,
        (NEAR, NEAR),
        (dh1, w_self_out, qkv, p1),
        ahead=ahead,
        scratch=[pltpu.VMEM((rows, width), BF), pltpu.VMEM((heads, TLEN, GROUP), F32)],
    )


def self_weights(
    place, dh1, a1, dqkv, x, gains, w_qkv, gbias, gain_cross_grad, gain_ff_grad, columns
):
    rows, width = dh1.shape
    half = width // 2
    part = columns.part
    misc_rows = 16 + width // 16
    more = -(-misc_rows // part)

    def body(
        place_ref, dh1_ref, wqkv_ref, x_ref, a1_ref, dqkv_ref, gs_ref, gb_ref, ggc_ref, ggf_ref,
        out, both, da1,
    ):
        da1[...] = jnp.zeros_like(da1)

        def one(t, carry):
            at = pl.ds(pl.multiple_of(t * width, 128), width)
            da1[...] += dot_nt(dqkv_ref[:, at], wqkv_ref[:, at])
            return carry

        lax.fori_loop(0, 3, one, 0)
        dv, dgain = rms_back(da1[...], x_ref[...].astype(F32), gs_ref[0:1, :])
        out.ref[...] = dh1_ref[...] + dv
        out.flush()

        def weights(h, carry):
            at = pl.ds(pl.multiple_of(h * 3 * half, 128), 3 * half)
            columns.store(both.ref, h, "qkv", dot_tn(a1_ref[...], dqkv_ref[:, at]), place_ref)
            return carry

        lax.fori_loop(0, 2, weights, 0)
        gains = jnp.concatenate([dgain, ggc_ref[...], ggf_ref[...], jnp.zeros((5, width), F32)], 0)
        misc = [gb_ref[...]] + [gains[:, j * 128 : (j + 1) * 128] for j in range(width // 128)]
        misc.append(jnp.zeros((more * part - misc_rows, 128), F32))
        misc = jnp.concatenate(misc, 0).astype(BF)
        for i in range(more):
            for slot in range(2):
                both.ref[slot, columns.units + i] = misc[i * part : (i + 1) * part]

    return call(
        "self_weights",
        body,
        (shape_of(F32, rows, width), columns.shape(more), columns.shape(more)),
        [SMEM] + [VMEM] * 9,
        (DRAIN, PAIR, PAIR),
        (
            place, dh1, w_qkv, x, a1, dqkv, gains, gbias,
            gain_cross_grad, gain_ff_grad,
        ),
        scratch=[pltpu.VMEM((rows, width), F32)],
    )


def swap(value, axis, bit):
    size = lax.axis_size(axis)
    return lax.ppermute(value, axis, [(i, i ^ bit) for i in range(size)])


class Bucket:
    def __init__(self, rows, terms, steps, keep_all=False):
        self.rows, self.terms, self.steps, self.keep_all = rows, terms, list(steps), keep_all


def sum_kernel(groups, dtype=BF):
    operands, specs, plan = [], [], []
    for i, jobs in enumerate(groups):
        at = 0
        for rows, terms in jobs:
            plan.append((i, at, rows, len(operands), len(terms)))
            at += rows
            for array, off in terms:
                operands.append(array)
                spec = (pl.Element(rows), pl.Element(128))
                specs.append(pl.BlockSpec(spec, functools.partial(lambda off, *_: (off, 0), off)))
    sizes = [sum(rows for rows, _ in jobs) for jobs in groups]

    def body(*refs):
        outs = refs[len(operands) :]
        for i, at, rows, first, count in plan:
            total = refs[first][...].astype(F32)
            for r in refs[first + 1 : first + count]:
                total = total + r[...].astype(F32)
            outs[i][at : at + rows, :] = total.astype(dtype)

    return call(
        "sum_kernel",
        body,
        tuple(shape_of(dtype, size, 128) for size in sizes),
        specs,
        tuple(whole(size, 128) for size in sizes),
        operands,
        grid=(1,),
    )


def send_round(cost, *members, settle=()):
    groups = {}
    for m in members:
        step = m.steps[0]
        groups.setdefault((step, m) if isinstance(m, Total) else step, []).append(m)
    jobs = []
    for group in groups.values():
        jobs.append([])
        for m in group:
            if isinstance(m, Total):
                jobs[-1] += m.next_jobs()
            elif m.keep_all:
                jobs[-1].append((m.rows, m.terms))
            else:
                m.rows //= 2
                jobs[-1].append((m.rows, [(array, off + m.rows) for array, off in m.terms]))
    if settle:
        jobs.append([(b.rows, b.terms) for b in settle])
    sent = sum_kernel(jobs)
    at = 0
    for b in settle:
        b.terms = [(sent[-1], at)]
        at += b.rows
    for group, payload in zip(groups.values(), sent):
        axis, bit = group[0].steps[0]
        got = swap(payload, axis, bit)
        at = 0
        for m in group:
            m.steps.pop(0)
            if isinstance(m, Total):
                m.moved(payload, got)
                continue
            if m.keep_all:
                m.terms = [(payload, at), (got, at)]
            else:
                m.terms = m.terms + [(got, at)]
            at += m.rows
    shadow(cost)


def rest_of(*buckets):
    while any(b.steps for b in buckets):
        send_round(3, *[b for b in buckets if b.steps])


def weight_buckets(columns, keep, send, orders, y_bits):
    rows = columns.units * columns.part
    keep, send = in_hbm(keep.reshape(-1, 128)), send.reshape(-1, 128)
    got = swap(send, "dp", 1)
    over = [[("blk", b) for b in order] for order in orders]
    along = [("dp", 2 * b) for b in y_bits]
    buckets = []
    for _, blocks, order, unit in columns.sections:
        steps = along + over[0] if order == "y" else over[order]
        at = unit * columns.part
        size = blocks * columns.chunks * columns.part
        buckets.append(Bucket(size, [(keep, at), (got, at)], steps))
    if keep.shape[0] > rows:
        buckets.append(Bucket(keep.shape[0] - rows, [(keep, rows), (got, rows)], over[0], keep_all=True))
    return buckets


def join_encodings(buckets, shard_rows, width):
    terms = [(bucket, array, off) for bucket in buckets for array, off in bucket.terms]

    def body(*refs):
        out = refs[-1]
        first = col = 0
        for bucket in buckets:
            mine = refs[first : first + len(bucket.terms)]
            first += len(bucket.terms)
            for at in range(0, bucket.rows, 128):
                total = mine[0][at : at + 128, :].astype(F32)
                for r in mine[1:]:
                    total = total + r[at : at + 128, :].astype(F32)
                out[:, col : col + 128] = jnp.transpose(total)
                col += 128

    return call(
        "join_encodings",
        body,
        shape_of(F32, shard_rows, width),
        [
            pl.BlockSpec(
                (pl.Element(bucket.rows), pl.Element(shard_rows)),
                functools.partial(lambda off, *_: (off, 0), off),
            )
            for bucket, _, off in terms
        ],
        whole(shard_rows, width),
        [array for _, array, _ in terms],
        grid=(1,),
    )


class Total:
    def __init__(self, groups, small, dp_size):
        self.groups, self.small, self.dp_size = groups, small, dp_size
        self.jobs, self.bases = [], []
        at = 0
        for _, buckets in groups:
            base = []
            for bucket in buckets:
                self.jobs.append((bucket.rows, bucket.terms))
                base.append(at)
                at += bucket.rows
            self.bases.append(base)
        self.small_at = []
        for bucket in small:
            self.jobs.append((bucket.rows, bucket.terms))
            self.small_at.append((at, bucket.rows))
            at += bucket.rows
        self.rows = at
        self.steps = [("dp", 2 * m) for m in range(1, dp_size // 2)] + [("dp", 1)]
        self.parts = []

    def next_jobs(self):
        if len(self.steps) > 1 or not self.parts:
            return [(self.rows, [(self.parts[0], 0)])] if self.parts else self.jobs
        jobs, self.spots, at = [], [], 0
        for (columns, _), base in zip(self.groups, self.bases):
            spots = []
            for (_, blocks, order, _), first in zip(columns.sections, base):
                if order == "y":
                    rows = blocks // columns.y_parts * columns.part
                    spots.append([at + i * rows for i in range(len(self.parts))])
                    jobs += [(rows, [(p, first)]) for p in self.parts]
                    at += rows * len(self.parts)
                else:
                    rows = blocks * columns.part
                    spots.append(at)
                    jobs.append((rows, [(p, first) for p in self.parts]))
                    at += rows
            self.spots.append(spots)
        self.small_spots = []
        for first, rows in self.small_at:
            jobs.append((rows, [(p, first) for p in self.parts]))
            self.small_spots.append((at, rows))
            at += rows
        return jobs

    def moved(self, payload, got):
        if self.steps or not self.parts:
            self.parts = self.parts + [got] if self.parts else [payload, got]
        else:
            self.own, self.other = payload, got

    def finish(self, place, arrays, small=None):
        outs = []
        for (columns, _), spots, named in zip(self.groups, self.spots, arrays):
            for name, stack in named:
                outs.append((columns, spots, name, stack, dict(columns.names)[name] // stack))
        y_parts = self.dp_size // 2

        def body(place_ref, own_ref, other_ref, *refs):
            core, y = place_ref[0], place_ref[2]
            sides = ((core, own_ref), (1 - core, other_ref))

            def put(ref, columns, half, j, at):
                row, off = divmod(j * 128, half)
                for which, src in sides:
                    lane = pl.multiple_of(which * half + off, 128)
                    ref[row * columns.part : (row + 1) * columns.part, pl.ds(lane, 128)] = src[
                        at : at + columns.part, :
                    ].astype(F32)

            for ref, (columns, spots, name, stack, half) in zip(refs, outs):
                far = []
                for j in range(stack * half // 128):
                    i, y_of, k = columns.find(columns.first(name) + j)
                    if y_of is None:
                        put(ref, columns, half, j, spots[i] + k * columns.part)
                    else:
                        far.append((j, spots[i], y_of, k))
                for y_is in range(y_parts if far else 0):

                    @pl.when(y == y_is)
                    def _():
                        for j, at, y_of, k in far:
                            put(ref, columns, half, j, at[y_is ^ y_of] + k * columns.part)

            if small:
                bias_ref, *gain_refs = refs[len(outs) :]
                blk = place_ref[1]
                at, rows = self.small_spots[0]
                misc = own_ref[at : at + rows, :].astype(F32)
                bias = jnp.concatenate([misc[:16], jnp.zeros((112, 128), F32)], 0)
                bias = pltpu.roll(bias, lax.rem(128 - blk * bias_part, 128), 1)
                bias_ref[...] = jnp.transpose(bias)[:bias_part, :heads]
                gains = jnp.concatenate(
                    [misc[16 + 8 * j : 24 + 8 * j] for j in range(width // 128)], 1
                )
                gains = pltpu.roll(gains, lax.rem(width - blk * part, width), 1)
                for i, ref in enumerate(gain_refs):
                    ref[...] = gains[i : i + 1, :part]

        shapes = [shape_of(F32, stack * columns.part, 2 * half) for columns, _, _, stack, half in outs]
        if small:
            heads, buckets, chunks = small
            bias_part = buckets // chunks
            part = self.groups[0][0].part
            width = part * chunks
            shapes += [shape_of(F32, bias_part, heads)] + [shape_of(F32, 1, part)] * 3
        return call(
            "finish",
            body,
            tuple(shapes),
            [SMEM, VMEM, VMEM],
            (VMEM,) * len(shapes),
            (place, self.own, self.other),
        )


def gather_encodings(own, bits):
    if len(bits) == 3:
        x, z, far = bits
        r_far, r_x = swap(own, "blk", far), swap(own, "blk", x)

        def second():
            r_z, r_zf = swap(own, "blk", z), swap(r_far, "blk", z)
            r_xf = swap(r_far, "blk", x)

            def third():
                r_xz = swap(r_z, "blk", x)
                r_xzf = swap(r_xf, "blk", z)
                arrays = [own, r_far, r_x, r_z, r_zf, r_xf, r_xz, r_xzf]
                return arrays, [[0], [far], [x], [z], [z | far], [x | far], [x | z], [x | z | far]]

            return [r_z, r_zf, r_xf], third

        return [r_far, r_x], second
    got, rel = own, [0]
    for bit in reversed(bits):
        got = jnp.concatenate([got, swap(got, "blk", bit)], 0)
        rel = rel + [r ^ bit for r in rel]
    return [], lambda: ([], lambda: ([got], [rel]))


def local(
    dec_in,
    encodings,
    enc_question,
    enc_valid,
    tgt_question,
    gain_self,
    w_qkv,
    rel_bias,
    w_self_out,
    gain_cross,
    w_cross_q,
    w_cross_kv,
    w_cross_out,
    gain_ff,
    w_ff_in,
    w_ff_out,
    grad_out,
):
    x = dec_in[0]
    gy = grad_out[0]
    rows, width = x.shape
    bucket_count, heads = rel_bias.shape
    hidden = w_ff_in.shape[1]
    half = width // 2
    chunks = lax.axis_size("blk")
    part = width // chunks
    dp_size = lax.axis_size("dp")
    shard_rows = encodings.shape[1]
    bits = [1 << i for i in range(chunks.bit_length() - 1)]
    y_bits = [1 << i for i in range(dp_size.bit_length() - 2)]
    y_parts = dp_size // 2
    blk = lax.axis_index("blk")
    dp = lax.axis_index("dp")
    orders = [bits, bits[1::-1] + bits[2:]]

    def layout(names, *sections):
        return Columns(names, sections, y_parts, chunks, part)

    def along_y(blocks):
        return blocks // (2 * y_parts) * y_parts

    stack = hidden // width
    blocks = half // 128
    cols_out = layout([("out", stack * half)], (stack * blocks, "y"))
    cols_in = layout([("in", hidden // 2)], (2 * stack * blocks // 3, 0), (stack * blocks // 3, 1))
    far_x, far_s = along_y(16 * blocks // 3), along_y(4 * blocks)
    near_x, near_s = 5 * blocks - far_x, 3 * blocks - far_s
    cols_x = layout(
        [("q", half), ("out", half), ("self", half), ("kv", width)],
        (near_x, 0), (far_x, "y"),
    )
    cols_s = layout([("qkv", 3 * half)], (near_s, 0), (far_s, "y"))

    places = [[chunk_place(c, blk, order) for c in range(chunks)] for order in orders]
    y_places = [chunk_place(y, dp // 2, y_bits) for y in range(y_parts)]
    numbers = [lax.rem(dp, 2), blk, dp // 2]
    for order in orders:
        spots = [0] * chunks
        for r in range(chunks):
            spots[chunk_spot(r, bits)] = chunk_spot(r, order)
        numbers += [jnp.int32(spot) for spot in spots]
    for columns in (cols_out, cols_in, cols_x, cols_s):
        columns.at = len(numbers)
        numbers += columns.table(places, y_places)
    place = jnp.stack(numbers).astype(jnp.int32)

    ORDER.clear()
    ROOMY[:] = [chunks * shard_rows <= 1024]
    tags = jnp.where(enc_valid[0] == 1, enc_question[0], -1).astype(BF)
    tag_rows = jnp.zeros((16, width), BF).at[0, :shard_rows].set(tags)
    enc_own = jnp.concatenate([encodings[0], tag_rows], 0)[None]
    gains = jnp.stack([gain_self, gain_cross, gain_ff])
    got, second = gather_encodings(enc_own, bits)
    shadow(10)
    a1, qkv, p1, o1_near, o1, wso_near, wcq_near, x_near = self_attention(
        x, gains, w_qkv, rel_bias, [w_self_out, w_cross_q, x]
    )
    more, third = second()
    shadow(10)
    h1_near, cq_near, h1, a2, cq, gy = self_project(
        x_near, o1_near, wso_near, gains, wcq_near, [gy]
    )
    pieces, rel = third()
    shadow(10, *more[1:2])
    dhid, wkv_near, wco_near = hidden_gradient(gy, w_ff_out, [w_cross_kv, w_cross_out])
    spots = [[int(chunk_spot(r, bits)) for r in group] for group in rel]
    enc, kv, e, inv, o2, h2, a3, w1_near = cross_forward(
        pieces, spots, shard_rows, tgt_question[0], cq_near, h1_near, wkv_near, wco_near, gains, [w_ff_in]
    )

    dpre, hid, keep, send = feed_hidden(place, a3, gy, dhid, w1_near, cols_out)
    (b_out,) = weight_buckets(cols_out, keep, send, orders, y_bits)
    shadow(30)
    keep, send, h2_near = feed_weights(place, a3, dpre, cols_in, [h2])
    b_in, b_jn = weight_buckets(cols_in, keep, send, orders, y_bits)
    send_round(30, b_out)
    dh2, gain_ff_grad = feed_back(dpre, w1_near, h2_near, gains, gy)
    send_round(8, b_in, b_jn)
    pairs = heads // 2
    parts_a = cross_backward(0, pairs // 2, dh2, o2, inv, cq, kv, e, wco_near, [])
    parts_b = cross_backward(
        pairs // 2, pairs, dh2, o2, inv, cq, kv, e, wco_near, [w_cross_q, h1, a2, o2, o1, enc, w_cross_kv]
    )
    wcq_near, h1_near, a2, o2, o1, enc, wkv_near = parts_b[3:]
    dcq, dkt, dvt = zip(parts_a, parts_b[:3])
    dh1, gain_cross_grad = cross_query_back(dcq, wcq_near, h1_near, gains, dh2)
    send_round(12, b_jn, b_out, b_in)
    genc, keep, send, hid, w2_near, h2_near = cross_weights(
        place, dh2, o2, dcq, dkt, dvt, enc, a2, wkv_near, dh1, o1, cols_x, [hid, w_ff_out, h2]
    )
    enc_rows = chunks * shard_rows * width // 128
    genc = in_hbm(genc.reshape(enc_rows, shard_rows))
    cut = enc_rows // blocks * (2 * blocks // 3)
    b_ea = Bucket(cut, [(genc, 0)], [("blk", b) for b in orders[0]])
    b_eb = Bucket(enc_rows - cut, [(genc, cut)], [("blk", b) for b in orders[1]])
    b_xa, b_xb = weight_buckets(cols_x, keep, send, orders, y_bits)
    send_round(40, b_ea, b_out, b_eb, b_jn, settle=[b_in])
    out, wso_near, qkv, p1 = feed_out(hid, w2_near, h2_near, [w_self_out, qkv, p1])
    dqkv, gbias, wqkv_near, x_near, a1 = self_backward(
        dh1, wso_near, qkv, p1, bucket_count, heads, [w_qkv, x, a1]
    )
    send_round(8, b_xb, b_xa, b_eb, b_ea, b_in, b_out, settle=[b_jn])
    grad_dec, keep, send = self_weights(
        place, dh1, a1, dqkv, x_near, gains, wqkv_near, gbias, gain_cross_grad, gain_ff_grad, cols_s
    )
    b_sa, b_sb, b_misc = weight_buckets(cols_s, keep, send, orders, y_bits)
    send_round(25, b_xa, b_ea, b_eb, settle=[b_in, b_out, b_xb])
    send_round(4, b_sb, b_sa, b_misc)
    send_round(4, b_xb)
    send_round(4, b_sa, b_misc, b_sb)
    rest_of(b_out, b_in, b_jn)
    total_ff = Total([(cols_out, [b_out]), (cols_in, [b_in, b_jn])], [], dp_size)
    send_round(4, b_xa, b_xb, total_ff, settle=[b_ea, b_eb])
    rest_of(b_ea, b_eb)
    send_round(4, b_sb, b_sa, b_misc)
    send_round(4, b_xb, total_ff)
    grad_enc = join_encodings([b_ea, b_eb], shard_rows, width)
    send_round(4, b_sb)
    rest_of(total_ff)
    grad_ff_out, grad_ff_in = total_ff.finish(place, [[("out", stack)], [("in", 1)]])
    rest_of(b_xa, b_xb)
    total_x = Total([(cols_x, [b_xa, b_xb])], [], dp_size)
    send_round(4, total_x)
    rest_of(b_sa, b_sb, b_misc)
    total_s = Total([(cols_s, [b_sa, b_sb])], [b_misc], dp_size)
    send_round(0.5, total_s)
    rest_of(total_x)
    rest_of(total_s)
    grad_cross_out, grad_cross_q, grad_self_out, grad_cross_kv = total_x.finish(
        place, [[("out", 1), ("q", 1), ("self", 1), ("kv", 1)]]
    )
    grad_qkv, grad_bias, *gains = total_s.finish(
        place, [[("qkv", 1)]], (heads, bucket_count, chunks)
    )
    gains = [gain.reshape(part) for gain in gains]
    return (
        out[None],
        grad_dec[None],
        grad_enc[None],
        gains[0],
        grad_qkv,
        grad_bias,
        grad_self_out,
        gains[1],
        grad_cross_q,
        grad_cross_kv,
        grad_cross_out,
        gains[2],
        grad_ff_in,
        grad_ff_out,
    )


def solution(mesh):
    return jax.shard_map(
        local,
        mesh=mesh,
        in_specs=(
            P("dp", "blk", None),
            P("dp", "blk", None),
            P("dp", "blk"),
            P("dp", "blk"),
            P("dp", "blk"),
            P(),
            P(),
            P(),
            P(),
            P(),
            P(),
            P(),
            P(),
            P(),
            P(),
            P(),
            P("dp", "blk", None),
        ),
        out_specs=(
            P("dp", "blk", None),
            P("dp", "blk", None),
            P("dp", "blk", None),
            P("blk"),
            P("blk", None),
            P("blk", None),
            P("blk", None),
            P("blk"),
            P("blk", None),
            P("blk", None),
            P("blk", None),
            P("blk"),
            P("blk", None),
            P("blk", None),
        ),
        check_vma=False,
    )
```

```python
import functools
import math

import jax
import jax.numpy as jnp
import numpy as np
from jax import lax
from jax.experimental import pallas as pl
from jax.experimental.pallas import tpu as pltpu
from jax.sharding import PartitionSpec as P

TLEN = 32
EPSILON = 1e-06
NEG_LARGE = -1e30
GROUP = 128
LOG2E = 1.4426950408889634
BF = jnp.bfloat16
F32 = jnp.float32
VMEM = pl.BlockSpec(memory_space=pltpu.VMEM)
SMEM = pl.BlockSpec(memory_space=pltpu.SMEM)
ANY = pl.BlockSpec(memory_space=pl.ANY)
HBM, STREAM, DRAIN, NEAR, PAIR = "hbm", "stream", "drain", "near", "pair"
MIB = 2**20
LIMITS = dict(
    self_attention=24, self_project=12, cross_forward=30, hidden_gradient=10, feed_hidden=26, feed_weights=18,
    feed_back=12, feed_out=12, cross_backward=20, cross_query_back=12, cross_weights=34, self_backward=14,
    self_weights=24, sum_kernel=16, finish=24, shadow=1, join_encodings=8,
)


def bucket_of(distance, bucket_count):
    exact_count = bucket_count // 2
    if distance < exact_count:
        return distance
    scaled = math.log(distance / exact_count) / math.log(128.0 / exact_count) * exact_count
    return min(bucket_count - 1, exact_count + int(scaled))


def bucket_firsts(bucket_count):
    firsts = {}
    for distance in range(TLEN):
        firsts.setdefault(bucket_of(distance, bucket_count), distance)
    return sorted(firsts.items())


def dot_nn(a, b):
    return jnp.dot(a, b, preferred_element_type=F32)


def dot_nt(a, b):
    return lax.dot_general(a, b, (((1,), (1,)), ((), ())), preferred_element_type=F32)


def dot_tn(a, b):
    return lax.dot_general(a, b, (((0,), (0,)), ((), ())), preferred_element_type=F32)


def inv_rms(v):
    return lax.rsqrt(jnp.mean(v * v, axis=-1, keepdims=True) + EPSILON)


def rms_back(dy, v, gain):
    r = inv_rms(v)
    vr = v * r
    dg = dy * gain
    dv = r * (dg - vr * jnp.mean(dg * vr, axis=-1, keepdims=True))
    return dv, jnp.sum(dy * vr, axis=0, keepdims=True)


def half_masks(rows):
    lane = lax.broadcasted_iota(jnp.int32, (rows, 128), 1)
    low = (lane < 64).astype(F32)
    return low.astype(BF), (1.0 - low).astype(BF)


def chunk_place(chunk, blk, bits):
    rel = jnp.bitwise_xor(chunk, blk)
    place = jnp.int32(0)
    for bit in bits:
        place = place * 2 + jnp.where(jnp.bitwise_and(rel, bit) != 0, 1, 0)
    return place


def chunk_spot(rel, bits):
    spot = 0
    for bit in bits:
        spot = spot * 2 + (1 if rel & bit else 0)
    return spot


def query_block(rows, tokens):
    return max(GROUP, min(rows, rows * 1024 // tokens))


def big(tokens):
    return 61 if tokens > 1024 else None


class Stream:
    def __init__(self, copy, ref):
        self.copy, self.ref, self.waited = copy, ref, False

    def ready(self):
        if not self.waited:
            self.copy.wait()
            self.waited = True
        return self.ref


class Drain:
    def __init__(self, copy, ref, out, sem):
        self.copy, self.ref, self.started = copy, ref, False
        self.out, self.sem = out, sem

    def flush(self):
        self.copy.start()
        self.started = True

    def flush_part(self, at):
        pltpu.make_async_copy(self.ref.at[at], self.out.at[at], self.sem).start()
        self.started = True


ORDER = []
ROOMY = [True]


class Pair:
    def __init__(self, drains, ref):
        self.drains, self.ref = drains, ref


def in_hbm(x):
    return pltpu.with_memory_space_constraint(x, pltpu.HBM)


def call(
    name, body, out_shape, in_specs, out_specs, operands, scratch=(), grid=(), prefetch=0,
    limit=None, cost=0.001, ahead=(),
):
    operands, in_specs = list(operands), list(in_specs)
    after = list(ORDER)
    wanted = ahead
    ahead = wanted if ROOMY[0] else ()
    outs = isinstance(out_shape, (tuple, list))
    out_shape = list(out_shape) if outs else [out_shape]
    out_specs = list(out_specs) if outs else [out_specs]
    streams, drains, pairs = [], [], []
    extra_scratch = []
    for i, spec in enumerate(in_specs):
        at = prefetch + i
        if spec == STREAM:
            streams.append(at)
            in_specs[i] = ANY
            operands[at] = in_hbm(operands[at])
            extra_scratch += [pltpu.VMEM(operands[at].shape, operands[at].dtype), pltpu.SemaphoreType.DMA]
        elif isinstance(spec, tuple):
            in_specs[i] = spec[1]
            operands[at] = in_hbm(operands[at])
    real = prefetch + len(in_specs)
    for i, spec in enumerate(out_specs):
        shape = out_shape[i]
        if spec == PAIR:
            pairs.append(i)
            out_specs[i] = ANY
            out_shape[i] = pltpu.HBM(shape.shape, shape.dtype)
            if len(pairs) % 2:
                extra_scratch += [
                    pltpu.VMEM((2, *shape.shape), shape.dtype), pltpu.SemaphoreType.DMA((2,))
                ]
        elif spec == DRAIN:
            drains.append(i)
            out_specs[i] = ANY
            out_shape[i] = pltpu.HBM(shape.shape, shape.dtype)
            extra_scratch += [pltpu.VMEM(shape.shape, shape.dtype), pltpu.SemaphoreType.DMA]
        elif spec == NEAR or isinstance(spec, tuple):
            space = pltpu.VMEM if spec == NEAR or spec[0] == NEAR else pltpu.HBM
            out_specs[i] = VMEM if spec == NEAR else spec[1]
            if ROOMY[0] or space is pltpu.HBM:
                out_shape[i] = space(shape.shape, shape.dtype)
    count = len(out_shape)
    for array in ahead:
        out_specs.append(VMEM if not grid else ANY)
        out_shape.append(pltpu.VMEM(array.shape, array.dtype))
    if ahead:
        extra_scratch.append(pltpu.SemaphoreType.DMA((len(ahead),)))
    after = [in_hbm(array) for array in ahead] + after
    out_specs.append(ANY)
    out_shape.append(pltpu.HBM((8, 128), F32))

    def ordered(*refs):
        ins = list(refs[:real])
        results = list(refs[real + len(after) : real + len(after) + len(out_shape) - 1])
        rest = list(refs[real + len(after) + len(out_shape) :])
        early = [
            pltpu.make_async_copy(refs[real + i], results[count + i], rest[-1].at[i])
            for i in range(len(ahead))
        ]
        del results[count:]
        own, extra = rest[: len(scratch)], rest[len(scratch) :]
        made, ends = [], []
        for n, i in enumerate(streams):
            copy = pltpu.make_async_copy(ins[i], extra[2 * n], extra[2 * n + 1])
            copy.start()
            ins[i] = Stream(copy, extra[2 * n])
            made.append(ins[i])
        extra = extra[2 * len(streams) :]
        for i in sorted(drains + pairs[::2]):
            held, sem = extra[:2]
            extra = extra[2:]
            if i in drains:
                copy = pltpu.make_async_copy(held, results[i], sem)
                results[i] = Drain(copy, held, results[i], sem)
                ends.append(results[i])
            else:
                halves = [
                    Drain(
                        pltpu.make_async_copy(held.at[k], results[i + k], sem.at[k]),
                        held.at[k], results[i + k], sem.at[k],
                    )
                    for k in range(2)
                ]
                results[i] = Pair(halves, held)
                ends += results[i].drains
        for i in reversed(pairs[1::2]):
            del results[i]
        for n, copy in enumerate(early):
            if grid:
                pl.when(pl.program_id(0) == 0)(copy.start)
            else:
                copy.start()
        body(*ins, *results, *own)
        for copy in early:
            if grid:
                pl.when(pl.program_id(0) == grid[0] - 1)(copy.wait)
            else:
                copy.wait()
        for stream in made:
            stream.ready()
        for end in ends:
            if not end.started:
                end.flush()
        for end in ends:
            end.copy.wait()

    got = pl.pallas_call(
        ordered,
        out_shape=tuple(out_shape),
        grid_spec=pltpu.PrefetchScalarGridSpec(
            num_scalar_prefetch=prefetch,
            grid=grid,
            in_specs=in_specs + [ANY] * len(after),
            out_specs=tuple(out_specs),
            scratch_shapes=list(scratch) + extra_scratch,
        ),
        compiler_params=pltpu.CompilerParams(vmem_limit_bytes=(limit or LIMITS[name]) * MIB),
        name=name,
        cost_estimate=pl.CostEstimate(
            flops=int(cost * 1153 * 10**6), bytes_accessed=0, transcendentals=0
        ),
    )(*operands, *after)
    ORDER[:] = [in_hbm(got[-1])]
    got = (*got[:count], *(got[count:-1] if ahead else wanted))
    return got if outs or wanted else got[0]


def shadow(cost, *arrays):
    call("shadow", lambda *_: None, (), [ANY] * len(arrays), (), arrays, cost=cost)


def whole(*shape):
    return pl.BlockSpec(shape, lambda *_: (0,) * len(shape))


def shape_of(dtype, *shape):
    return jax.ShapeDtypeStruct(shape, dtype)


class Columns:
    def __init__(self, names, sections, y_parts, chunks, part):
        self.names, self.y_parts, self.chunks, self.part = names, y_parts, chunks, part
        self.sections = []
        first = unit = 0
        for blocks, order in sections:
            if blocks:
                self.sections.append((first, blocks, order, unit))
            first, unit = first + blocks, unit + chunks * blocks
        self.blocks, self.units = first, unit

    def shape(self, more=0):
        return shape_of(BF, self.units + more, self.part, 128)

    def first(self, name):
        done = 0
        for other, width in self.names:
            if other == name:
                return done
            done += width // 128

    def find(self, block):
        for i, (first, blocks, order, _) in enumerate(self.sections):
            if first <= block < first + blocks:
                if order != "y":
                    return i, None, block - first
                y, k = divmod(block - first, blocks // self.y_parts)
                return i, y, k

    def runs(self):
        found = []
        for first, blocks, order, _ in self.sections:
            size = blocks // self.y_parts if order == "y" else blocks
            found += [(at, size) for at in range(first, first + blocks, size)]
        return found

    def table(self, spots, y_spots):
        units = []
        for c in range(self.chunks):
            for block in range(self.blocks):
                i, y, k = self.find(block)
                _, blocks, order, unit = self.sections[i]
                if y is None:
                    units.append(unit + spots[order][c] * blocks + k)
                else:
                    units.append(unit + (y_spots[y] * self.chunks + spots[0][c]) * (blocks // self.y_parts) + k)
        return units

    def store(self, ref, half, name, value, place_ref, chunks=None, block=0):
        chunks = range(self.chunks) if chunks is None else chunks
        start = self.first(name) + block
        slot = jnp.bitwise_xor(place_ref[0], half)
        for n, c in enumerate(chunks):
            for j in range(value.shape[1] // 128):
                unit = place_ref[self.at + c * self.blocks + start + j]
                ref[slot, unit] = value[n * self.part : (n + 1) * self.part, j * 128 : (j + 1) * 128].astype(BF)


def self_attention(x, gains, w_qkv, rel_bias, ahead):
    rows, width = x.shape
    bucket_count, heads = rel_bias.shape
    pairs = heads // 2
    groups = rows // GROUP
    firsts = bucket_firsts(bucket_count)

    def body(
        x, gs_ref, wqkv, rb_ref, a1_out, qkv_out, p1_out, o1_ref, o1_out, bias
    ):
        a1_ref, qkv_ref, p1_ref = a1_out.ref, qkv_out.ref, p1_out.ref
        xf = x.ready()[...].astype(F32)
        a1 = (xf * inv_rms(xf) * gs_ref[0:1, :]).astype(BF)
        a1_ref[...] = a1
        a1_out.flush()
        row = lax.broadcasted_iota(jnp.int32, (TLEN, GROUP), 0)
        col = lax.broadcasted_iota(jnp.int32, (TLEN, GROUP), 1)
        distance = lax.rem(col, TLEN) - row

        def make_bias(h, carry):
            val = jnp.full((TLEN, GROUP), NEG_LARGE, F32)
            for b, first in firsts:
                val = jnp.where(distance >= first, rb_ref[h, b], val)
            lanes = pl.ds(pl.multiple_of(lax.rem(h, 2) * GROUP, GROUP), GROUP)
            for t in range(GROUP // TLEN):
                bias[h // 2, t * TLEN : (t + 1) * TLEN, lanes] = jnp.where(
                    col // TLEN == t, val, NEG_LARGE
                )
            return carry

        lax.fori_loop(0, heads, make_bias, 0)
        wqkv_ref = wqkv.ready()

        def project(t, carry):
            at = pl.ds(pl.multiple_of(t * width, 128), width)
            qkv_ref[:, at] = dot_nn(a1_ref[...], wqkv_ref[:, at]).astype(BF)
            return carry

        lax.fori_loop(0, 3, project, 0)
        qkv_out.flush()
        m0, m1 = half_masks(GROUP)

        def attend(g, carry):
            at = pl.ds(pl.multiple_of(g * GROUP, GROUP), GROUP)
            for pair in range(pairs):
                lo = pair * 128
                q = qkv_ref[at, lo : lo + 128]
                k = qkv_ref[at, width + lo : width + lo + 128]
                v = qkv_ref[at, 2 * width + lo : 2 * width + lo + 128]
                s = dot_nt(k, jnp.concatenate([q * m0, q * m1], 0)) + bias[pair]
                e = jnp.exp(s - jnp.max(s, 0, keepdims=True))
                p = (e / jnp.sum(e, 0, keepdims=True)).astype(BF)
                p1_ref[g, pair] = p
                o = dot_tn(
                    jnp.concatenate([p[:, :GROUP], p[:, GROUP:]], 0),
                    jnp.concatenate([v * m0, v * m1], 0),
                )
                o1_ref[at, lo : lo + 128] = o.astype(BF)
            p1_out.flush_part(pl.ds(g, 1))
            return carry

        lax.fori_loop(0, groups, attend, 0)
        o1_out.ref[...] = o1_ref[...]
        o1_out.flush()

    return call(
        "self_attention",
        body,
        (
            shape_of(BF, rows, width),
            shape_of(BF, rows, 3 * width),
            shape_of(BF, groups, pairs, GROUP, 2 * GROUP),
            shape_of(BF, rows, width),
            shape_of(BF, rows, width),
        ),
        [STREAM, VMEM, STREAM, SMEM],
        (DRAIN, DRAIN, DRAIN, NEAR, DRAIN),
        (x, gains, w_qkv, rel_bias.T),
        ahead=ahead,
        scratch=[pltpu.VMEM((pairs, GROUP, 2 * GROUP), F32)],
    )


def self_project(x, o1, w_self_out, gains, w_cross_q, ahead):
    rows, width = x.shape

    def body(x_ref, o1_ref, wso_ref, gc_ref, wcq_ref, h1_ref, cq_ref, h1_out, a2_out, cq_out):
        h1 = dot_nn(o1_ref[...], wso_ref[...]) + x_ref[...].astype(F32)
        h1_ref[...] = h1
        h1_out.ref[...] = h1
        h1_out.flush()
        a2 = (h1 * inv_rms(h1) * gc_ref[1:2, :]).astype(BF)
        a2_out.ref[...] = a2
        a2_out.flush()
        cq = dot_nn(a2, wcq_ref[...]).astype(BF)
        cq_ref[...] = cq
        cq_out.ref[...] = cq

    low, full = shape_of(BF, rows, width), shape_of(F32, rows, width)
    return call(
        "self_project",
        body,
        (full, low, full, low, low),
        [VMEM] * 5,
        (NEAR, NEAR, DRAIN, DRAIN, DRAIN),
        (x, o1, w_self_out, gains, w_cross_q),
        ahead=ahead,
    )


def cross_forward(
    pieces, order, shard_rows, tgt_question, cq, h1, w_cross_kv, w_cross_out, gains, ahead
):
    rows, width = cq.shape
    pairs = width // 128
    tokens = sum(len(o) for o in order) * shard_rows
    targets = rows // TLEN
    block_rows = query_block(rows, tokens)
    blocks = rows // block_rows
    steps = pairs * blocks

    def body(*refs):
        piece_refs = refs[: len(pieces)]
        (
            tq_ref, cq_ref, h1_ref, wkv_ref, wco_ref, gf_ref,
            enc_out, kv_out, e_ref, inv_out, o2_out, h2_out, a3_ref,
            kfeat, qfeat, ebuf, sem,
        ) = refs[len(pieces) :]
        enc_ref, kv_ref, inv_ref, o2_ref = enc_out.ref, kv_out.ref, inv_out.ref, o2_out.ref
        lane = lax.rem(lax.broadcasted_iota(jnp.int32, (shard_rows, 128), 1), 64).astype(F32)
        for ref, places in zip(piece_refs, order):
            for j, spot in enumerate(places):
                at = slice(spot * shard_rows, (spot + 1) * shard_rows)
                enc_ref[at, :] = ref[j, :shard_rows, :]
                tag = ref[j, shard_rows : shard_rows + 1, :shard_rows].astype(F32)
                tag = jnp.transpose(jnp.broadcast_to(tag, (128, shard_rows)))
                kfeat[at, :] = jnp.where(tag == lane, 0.0, NEG_LARGE).astype(BF)
        lane_t = lax.rem(lax.broadcasted_iota(jnp.int32, (TLEN, 128), 1), 64)
        for t in range(targets):
            qfeat[t * TLEN : (t + 1) * TLEN, :] = jnp.where(lane_t == tq_ref[t], 1.0, 0.0).astype(BF)
        enc_out.flush()

        def project(t, carry):
            at = pl.ds(pl.multiple_of(t * width, 128), width)
            kv_ref[:, at] = dot_nn(enc_ref[...], wkv_ref[:, at]).astype(BF)
            return carry

        lax.fori_loop(0, 2, project, 0)
        kv_out.flush()
        q0, q1 = half_masks(block_rows)
        k0, k1 = half_masks(tokens)
        qmask, kmask = (q0, q1), (k0, k1)
        low = lax.broadcasted_iota(jnp.int32, (block_rows, 128), 1) < 64

        def out_copy(slot, step):
            pair, block = step // blocks, lax.rem(step, blocks)
            return pltpu.make_async_copy(
                ebuf.at[slot],
                e_ref.at[pl.ds(2 * pair, 2), pl.ds(block * block_rows, block_rows)],
                sem.at[slot],
            )

        def attend(step, carry):
            slot = lax.rem(step, 2)
            pair, block = step // blocks, lax.rem(step, blocks)
            lo = pl.multiple_of(pair * 128, 128)
            at = pl.ds(pl.multiple_of(block * block_rows, block_rows), block_rows)

            @pl.when(step >= 2)
            def _():
                out_copy(slot, step - 2).wait()

            q = cq_ref[at, pl.ds(lo, 128)]
            k = kv_ref[:, pl.ds(lo, 128)]
            v = kv_ref[:, pl.ds(width + lo, 128)]
            keys = [k * kmask[h] + kfeat[...] * kmask[1 - h] for h in range(2)]
            values = [v * kmask[h] + kmask[1 - h] for h in range(2)]
            size = min(block_rows, 256)
            units = [(r, h) for r in range(0, block_rows, size) for h in range(2)]
            tagged = qfeat[at, :]

            def score(unit):
                r, h = unit
                qa = q[r : r + size] * qmask[h][:size] + tagged[r : r + size] * qmask[1 - h][:size]
                return dot_nt(qa, keys[h])

            outs, last = {}, None
            s = score(units[0])
            for i, unit in enumerate(units):
                later = score(units[i + 1]) if i + 1 < len(units) else None
                if last is not None:
                    outs[last[0]] = dot_nn(last[1], values[last[0][1]])
                e = jnp.exp(s - jnp.max(s, -1, keepdims=True)).astype(BF)
                ebuf[slot, unit[1], unit[0] : unit[0] + size, :] = e
                last, s = (unit, e), later
            outs[last[0]] = dot_nn(last[1], values[last[0][1]])
            outs = [
                jnp.concatenate([outs[r, h] for r in range(0, block_rows, size)], 0) for h in range(2)
            ]
            out_copy(slot, step).start()
            total = jnp.where(low, pltpu.roll(outs[0], 64, 1), pltpu.roll(outs[1], 64, 1))
            inv = 1.0 / total
            inv_ref[at, pl.ds(lo, 128)] = inv
            o2_ref[at, pl.ds(lo, 128)] = (jnp.where(low, outs[0], outs[1]) * inv).astype(BF)
            if blocks == 1:
                inv_out.flush_part((slice(None), pl.ds(lo, 128)))
                o2_out.flush_part((slice(None), pl.ds(lo, 128)))
            return carry

        lax.fori_loop(0, steps, attend, 0)
        if blocks > 1:
            inv_out.flush()
            o2_out.flush()
        h2 = h1_ref[...] + dot_nn(o2_ref[...], wco_ref[...])
        h2_out.ref[...] = h2
        h2_out.flush()
        a3_ref[...] = (h2 * inv_rms(h2) * gf_ref[2:3, :]).astype(BF)
        for step in range(max(0, steps - 2), steps):
            out_copy(step % 2, jnp.int32(step)).wait()

    return call(
        "cross_forward",
        body,
        (
            shape_of(BF, tokens, width),
            shape_of(BF, tokens, 2 * width),
            shape_of(BF, 2 * pairs, rows, tokens),
            shape_of(F32, rows, width),
            shape_of(BF, rows, width),
            shape_of(F32, rows, width),
            shape_of(BF, rows, width),
        ),
        [VMEM] * len(pieces) + [SMEM] + [VMEM] * 5,
        (DRAIN, DRAIN, (HBM, ANY), DRAIN, DRAIN, DRAIN, NEAR),
        (*pieces, tgt_question, cq, h1, w_cross_kv, w_cross_out, gains),
        scratch=[
            pltpu.VMEM((tokens, 128), BF),
            pltpu.VMEM((rows, 128), BF),
            pltpu.VMEM((2, 2, block_rows, tokens), BF),
            pltpu.SemaphoreType.DMA((2,)),
        ],
        limit=big(tokens),
        ahead=ahead,
    )


def hidden_gradient(gy, w_ff_out, ahead):
    rows, width = gy.shape
    hidden = w_ff_out.shape[0]

    tiles = hidden // width

    def body(gy_ref, w2_ref, out_ref, w2, sem):
        def copy(t):
            at = pl.ds(pl.multiple_of(t * width, 128), width)
            return pltpu.make_async_copy(w2_ref.at[at], w2.at[at], sem.at[t])

        for t in range(tiles):
            copy(t).start()

        def tile(t, carry):
            copy(t).wait()
            at = pl.ds(pl.multiple_of(t * width, 128), width)
            out_ref[:, at] = dot_nt(gy_ref[...], w2[at, :]).astype(BF)
            return carry

        lax.fori_loop(0, tiles, tile, 0)

    return call(
        "hidden_gradient",
        body,
        shape_of(BF, rows, hidden),
        [VMEM, (HBM, ANY)],
        NEAR,
        (gy, w_ff_out),
        scratch=[pltpu.VMEM((hidden, width), BF), pltpu.SemaphoreType.DMA((tiles,))],
        ahead=ahead,
    )


def feed_hidden(place, a3, gy, dhid, w_ff_in, columns):
    rows, width = a3.shape
    hidden = w_ff_in.shape[1]
    tile = width
    half = width // 2
    sub = hidden // width
    part = columns.part
    per_tile = columns.chunks * tile // hidden
    scale = math.sqrt(2.0 / math.pi)

    def body(place_ref, a3_ref, gy_ref, dhid_ref, w1_ref, dpre_ref, hid_out, both):
        def activate(pre, at):
            sq = pre * pre
            t = jnp.tanh(pre * (scale + (scale * 0.044715) * sq))
            up = 0.5 + 0.5 * t
            hid = (pre * up).astype(BF)
            slope = up + pre * (up - up * up) * ((2.0 * scale) + (2.0 * scale * 0.134145) * sq)
            hid_out.ref[:, at] = hid
            dpre_ref[:, at] = (dhid_ref[:, at].astype(F32) * slope).astype(BF)
            return hid

        def one(step, carry):
            parts = tile // 256
            ats = [pl.ds(pl.multiple_of(step * tile + i * 256, 128), 256) for i in range(parts)]
            a3, gyv = a3_ref[...], gy_ref[...]
            pre = dot_nn(a3, w1_ref[:, ats[0]])
            grads, hid = [], None
            for i in range(parts):
                later = dot_nn(a3, w1_ref[:, ats[i + 1]]) if i + 1 < parts else None
                if hid is not None:
                    grads.append(dot_tn(hid, gyv))
                hid = activate(pre, ats[i])
                pre = later
            grads.append(dot_tn(hid, gyv))
            hid_out.flush_part((slice(None), pl.ds(pl.multiple_of(step * tile, 128), tile)))
            g = jnp.concatenate(grads, 0)
            for i in range(per_tile):
                chunk = step * per_tile + i
                for h in range(2):
                    for j in range(sub):
                        first = (i * sub + j) * part
                        columns.store(
                            both.ref, h, "out", g[first : first + part, h * half : (h + 1) * half],
                            place_ref, [chunk], j * half // 128,
                        )
                for first, count in columns.runs():
                    unit = place_ref[columns.at + chunk * columns.blocks + first]
                    for drain in both.drains:
                        drain.flush_part(pl.ds(unit, count))
            return carry

        lax.fori_loop(0, hidden // tile, one, 0)

    return call(
        "feed_hidden",
        body,
        (shape_of(BF, rows, hidden), shape_of(BF, rows, hidden), columns.shape(), columns.shape()),
        [SMEM, VMEM, VMEM, VMEM, VMEM],
        (NEAR, DRAIN, PAIR, PAIR),
        (place, a3, gy, dhid, w_ff_in),
    )


def feed_weights(place, a3, dpre, columns, ahead):
    width = a3.shape[1]
    hidden = dpre.shape[1]

    def body(place_ref, a3_ref, dpre_ref, both):
        tiles = hidden // width

        def one(t, carry):
            at = pl.ds(pl.multiple_of(t * width, 128), width)
            g = dot_tn(a3_ref[...], dpre_ref[:, at])
            block = lax.rem(t, tiles // 2) * (width // 128)
            columns.store(both.ref, t // (tiles // 2), "in", g, place_ref, None, block)
            for slot in range(2):

                @pl.when(jnp.logical_and(t == tiles // 2 - 1, place_ref[0] == slot))
                def _():
                    both.drains[slot].flush_part(pl.ds(0, columns.units))

                @pl.when(jnp.logical_and(t == tiles - 1, place_ref[0] != slot))
                def _():
                    both.drains[slot].flush_part(pl.ds(0, columns.units))

            return carry

        lax.fori_loop(0, tiles, one, 0)

    return call(
        "feed_weights",
        body,
        (columns.shape(), columns.shape()),
        [SMEM, VMEM, VMEM],
        (PAIR, PAIR),
        (place, a3, dpre),
        ahead=ahead,
    )


def feed_back(dpre, w_ff_in, h2, gains, gy):
    rows, width = h2.shape

    def body(dpre_ref, w1_ref, h2_ref, gf_ref, gy_ref, dh2_ref, gain_ref, da3):
        da3[...] = jnp.zeros_like(da3)

        def one(t, carry):
            at = pl.ds(pl.multiple_of(t * width, 128), width)
            da3[...] += dot_nt(dpre_ref[:, at], w1_ref[:, at])
            return carry

        lax.fori_loop(0, dpre_ref.shape[1] // width, one, 0)
        dv, dgain = rms_back(da3[...], h2_ref[...], gf_ref[2:3, :])
        dh2_ref[...] = gy_ref[...].astype(F32) + dv
        gain_ref[...] = dgain

    return call(
        "feed_back",
        body,
        (shape_of(F32, rows, width), shape_of(F32, 1, width)),
        [VMEM] * 5,
        (NEAR, NEAR),
        (dpre, w_ff_in, h2, gains, gy),
        scratch=[pltpu.VMEM((rows, width), F32)],
    )


def feed_out(hid, w_ff_out, h2, ahead):
    rows, width = h2.shape

    def body(hid_ref, w2_ref, h2_ref, out, total):
        total[...] = h2_ref[...]

        def one(t, carry):
            at = pl.ds(pl.multiple_of(t * width, 128), width)
            total[...] += dot_nn(hid_ref[:, at], w2_ref[at, :])
            return carry

        lax.fori_loop(0, hid_ref.shape[1] // width, one, 0)
        out.ref[...] = total[...].astype(BF)

    return call(
        "feed_out",
        body,
        (shape_of(BF, rows, width),),
        [VMEM] * 3,
        (DRAIN,),
        (hid, w_ff_out, h2),
        scratch=[pltpu.VMEM((rows, width), F32)],
        ahead=ahead,
    )


def cross_backward(first_pair, last_pair, dh2, o2, inv, cq, kv, e, w_cross_out, ahead):
    rows, width = cq.shape
    pairs = width // 128
    count = last_pair - first_pair
    tokens = kv.shape[0]
    block_rows = query_block(rows, tokens)
    blocks = rows // block_rows

    def body(
        dh2_ref, wco_ref, o2_ref, inv_ref, cq_ref, k_ref, v_ref, e_ref,
        dcq_ref, dkt_ref, dvt_ref,
        do2,
    ):
        pair = pl.program_id(0)

        @pl.when(pair == 0)
        def _():
            do2v = dot_nt(dh2_ref[...].astype(BF), wco_ref[...]).astype(BF)
            for i in range(count):
                do2[i] = do2v[:, i * 128 : (i + 1) * 128]

        q0, q1 = half_masks(block_rows)
        k0, k1 = half_masks(tokens)
        qmask, kmask = (q0, q1), (k0, k1)
        lane = lax.broadcasted_iota(jnp.int32, (block_rows, 128), 1)
        low = lane < 64
        first = lax.rem(lane, 64) == 0
        second = lax.rem(lane, 64) == 1
        k, v = k_ref[...], v_ref[...]
        sums = [0.0] * 4
        for block in range(blocks):
            at = slice(block * block_rows, (block + 1) * block_rows)
            q = cq_ref[at, :]
            dof = do2[pair, at, :].astype(F32) * inv_ref[at, :]
            dob = dof.astype(BF)
            prod = dof * o2_ref[at, :].astype(F32)
            qt = jnp.transpose(q)
            dot_t = jnp.transpose(dob)
            dqs = []
            for h in range(2):
                own = low if h == 0 else jnp.logical_not(low)
                delta = -jnp.sum(jnp.where(own, prod, 0.0), -1, keepdims=True)
                hi = delta.astype(BF).astype(F32)
                feat = jnp.where(first, hi, jnp.where(second, delta - hi, 0.0)).astype(BF)
                doa = dob * qmask[h] + feat * qmask[1 - h]
                dp = dot_nt(doa, v * kmask[h] + kmask[1 - h])
                ev = e_ref[h, at, :]
                ds = (ev.astype(F32) * dp).astype(BF)
                dqs.append(dot_nn(ds, k))
                sums[h] = sums[h] + dot_nn(qt[h * 64 : (h + 1) * 64, :], ds)
                sums[2 + h] = sums[2 + h] + dot_nn(dot_t[h * 64 : (h + 1) * 64, :], ev)
            dcq_ref[at, :] = jnp.where(low, dqs[0], dqs[1]).astype(BF)
        for h in range(2):
            dkt_ref[h * 64 : (h + 1) * 64, :] = sums[h].astype(BF)
            dvt_ref[h * 64 : (h + 1) * 64, :] = sums[2 + h].astype(BF)

    near = HBM if big(tokens) else NEAR

    def column(n, first=first_pair):
        return pl.BlockSpec((n, 128), lambda p: (0, p + first))

    return call(
        "cross_backward",
        body,
        (
            shape_of(BF, rows, count * 128),
            shape_of(BF, count * 128, tokens),
            shape_of(BF, count * 128, tokens),
        ),
        [
            whole(rows, width),
            pl.BlockSpec((count * 128, width), lambda p: (first_pair // count, 0)),
            (HBM, column(rows)),
            (HBM, column(rows)),
            (HBM, column(rows)),
            (HBM, column(tokens)),
            (HBM, column(tokens, first_pair + pairs)),
            (HBM, pl.BlockSpec((2, rows, tokens), lambda p: (p + first_pair, 0, 0))),
        ],
        (
            (NEAR, column(rows, 0)),
            (near, pl.BlockSpec((128, tokens), lambda p: (p, 0))),
            (near, pl.BlockSpec((128, tokens), lambda p: (p, 0))),
        ),
        (dh2, w_cross_out, o2, inv, cq, kv, kv, e),
        scratch=[pltpu.VMEM((count, rows, 128), BF)],
        grid=(count,),
        ahead=ahead,
        limit=big(tokens),
    )


def cross_query_back(dcq, w_cross_q, h1, gains, dh2):
    rows, width = h1.shape
    n = len(dcq)
    size = width // n

    def body(*refs):
        wcq_ref, h1_ref, gc_ref, dh2_ref, dh1_ref, gain_ref = refs[n:]
        da2 = 0.0
        for i in range(n):
            da2 = da2 + dot_nt(refs[i][...], wcq_ref[:, i * size : (i + 1) * size])
        dv, dgain = rms_back(da2, h1_ref[...], gc_ref[1:2, :])
        dh1_ref[...] = dh2_ref[...] + dv
        gain_ref[...] = dgain

    return call(
        "cross_query_back",
        body,
        (shape_of(F32, rows, width), shape_of(F32, 1, width)),
        [VMEM] * (n + 4),
        (NEAR, NEAR),
        (*dcq, w_cross_q, h1, gains, dh2),
    )


def shard_rows_of(tokens, chunks):
    return tokens // chunks


def cross_weights(place, dh2, o2, dcq, dkt, dvt, enc, a2, w_cross_kv, dh1, o1, columns, ahead):
    rows, width = dh2.shape
    tokens = enc.shape[0]
    half = width // 2
    tile = max(shard_rows_of(tokens, columns.chunks), 512)
    n = len(dcq)
    size = width // n
    blocks = width // 128
    near = 2 * blocks // 3
    shard_rows = tokens // columns.chunks

    def body(place_ref, dh2_ref, dh1_ref, a2_ref, o2_ref, o1_ref, *refs):
        dcq_refs, dkt, dvt = refs[:n], refs[n : 2 * n], refs[2 * n : 3 * n]
        wkv_ref, enc_ref, genc_out, both, lhs, rhs, dkvt = refs[3 * n :]
        for i, r in enumerate(dcq_refs):
            rhs[0, :, i * size : (i + 1) * size] = r[...]
        rhs[1] = dh2_ref[...].astype(BF)
        rhs[2] = dh1_ref[...].astype(BF)
        for i, r in enumerate((a2_ref, o2_ref, o1_ref)):
            lhs[i] = r[...]
        for i, r in enumerate(dkt + dvt):
            dkvt[i * size : (i + 1) * size, :] = r[...]

        def square(i, carry):
            g = dot_tn(lhs[i], rhs[i])
            for h in range(2):
                columns.store(both.ref, h, "q", g[:, h * half : (h + 1) * half], place_ref, None, i * (half // 128))
            return carry

        lax.fori_loop(0, 3, square, 0)

        def encodings(t, carry):
            at = pl.ds(pl.multiple_of(t * tile, 128), tile)
            genct = dot_nn(wkv_ref[...], dkvt[:, at]).astype(BF)
            for i in range(tile // shard_rows):
                for j in range(blocks):
                    order = 0 if j < near else 1
                    size = blocks - near if order else near
                    spot = place_ref[3 + order * columns.chunks + t * (tile // shard_rows) + i]
                    genc_out.ref[order * columns.chunks * near + spot * size + j - order * near] = genct[
                        j * 128 : (j + 1) * 128, i * shard_rows : (i + 1) * shard_rows
                    ]
            return carry

        lax.fori_loop(0, tokens // tile, encodings, 0)
        genc_out.flush()

        def key_value(h, carry):
            g = 0.0
            rows_at = pl.ds(pl.multiple_of(h * width, 128), width)
            for t in range(0, tokens, 1024):
                end = min(tokens, t + 1024)
                g = g + dot_nt(jnp.transpose(enc_ref[t:end, :]), dkvt[rows_at, t:end])
            columns.store(both.ref, h, "kv", g, place_ref)
            return carry

        lax.fori_loop(0, 2, key_value, 0)

    return call(
        "cross_weights",
        body,
        (shape_of(BF, columns.chunks * blocks, 128, shard_rows), columns.shape(), columns.shape()),
        [SMEM] + [VMEM] * (3 * n + 7),
        (DRAIN, PAIR, PAIR),
        (place, dh2, dh1, a2, o2, o1, *dcq, *dkt, *dvt, w_cross_kv, enc),
        scratch=[
            pltpu.VMEM((3, rows, width), BF),
            pltpu.VMEM((3, rows, width), BF),
            pltpu.VMEM((2 * width, tokens), BF),
        ],
        ahead=ahead,
        limit=big(tokens),
    )


def self_backward(dh1, w_self_out, qkv, p1, bucket_count, heads, ahead):
    rows, width = dh1.shape
    pairs = heads // 2
    groups = rows // GROUP
    firsts = bucket_firsts(bucket_count)
    ends = [first for _, first in firsts[1:]] + [TLEN]

    def body(dh1_ref, wso_ref, qkv_ref, p1_ref, dqkv_ref, gbias_ref, do1, acc):
        do1[...] = dot_nt(dh1_ref[...].astype(BF), wso_ref[...]).astype(BF)
        m0, m1 = half_masks(GROUP)
        acc[...] = jnp.zeros_like(acc)

        def attend(g, carry):
            at = pl.ds(pl.multiple_of(g * GROUP, GROUP), GROUP)
            for pair in range(pairs):
                lo = pair * 128
                q = qkv_ref[at, lo : lo + 128]
                k = qkv_ref[at, width + lo : width + lo + 128]
                v = qkv_ref[at, 2 * width + lo : 2 * width + lo + 128]
                do = do1[at, lo : lo + 128]
                do_two = jnp.concatenate([do * m0, do * m1], 0)
                pb = p1_ref[g, pair]
                pf = pb.astype(F32)
                dp = dot_nt(v, do_two)
                ds = (pf * (dp - jnp.sum(pf * dp, 0, keepdims=True))).astype(BF)
                dsf = ds.astype(F32)
                total = dsf[:TLEN]
                for t in range(1, GROUP // TLEN):
                    total = total + dsf[t * TLEN : (t + 1) * TLEN]
                acc[2 * pair] += total[:, :GROUP]
                acc[2 * pair + 1] += total[:, GROUP:]
                dq = dot_tn(
                    jnp.concatenate([ds[:, :GROUP], ds[:, GROUP:]], 0),
                    jnp.concatenate([k * m0, k * m1], 0),
                )
                dk = dot_nn(ds, jnp.concatenate([q * m0, q * m1], 0))
                dv = dot_nn(pb, do_two)
                dqkv_ref[at, lo : lo + 128] = dq.astype(BF)
                dqkv_ref[at, width + lo : width + lo + 128] = dk.astype(BF)
                dqkv_ref[at, 2 * width + lo : 2 * width + lo + 128] = dv.astype(BF)
            return carry

        lax.fori_loop(0, groups, attend, 0)
        row = lax.broadcasted_iota(jnp.int32, (TLEN, GROUP), 0)
        distance = lax.rem(lax.broadcasted_iota(jnp.int32, (TLEN, GROUP), 1), TLEN) - row
        lane = lax.broadcasted_iota(jnp.int32, (16, 128), 1)
        bias = jnp.zeros((16, 128), F32)
        accv = acc[...]
        pad = jnp.zeros((16 - heads, 1), F32)
        for (b, first), end in zip(firsts, ends):
            here = jnp.logical_and(distance >= first, distance < end)
            part_sum = jnp.sum(jnp.where(here[None], accv, 0.0), axis=1)
            col = jnp.sum(part_sum, -1, keepdims=True)
            bias = jnp.where(lane == b, jnp.concatenate([col, pad], 0), bias)
        gbias_ref[...] = bias

    return call(
        "self_backward",
        body,
        (shape_of(BF, rows, 3 * width), shape_of(F32, 16, 128)),
        [VMEM] * 4,
        (NEAR, NEAR),
        (dh1, w_self_out, qkv, p1),
        ahead=ahead,
        scratch=[pltpu.VMEM((rows, width), BF), pltpu.VMEM((heads, TLEN, GROUP), F32)],
    )


def self_weights(
    place, dh1, a1, dqkv, x, gains, w_qkv, gbias, gain_cross_grad, gain_ff_grad, columns
):
    rows, width = dh1.shape
    half = width // 2
    part = columns.part
    misc_rows = 16 + width // 16
    more = -(-misc_rows // part)

    def body(
        place_ref, dh1_ref, wqkv_ref, x_ref, a1_ref, dqkv_ref, gs_ref, gb_ref, ggc_ref, ggf_ref,
        out, both, da1,
    ):
        da1[...] = jnp.zeros_like(da1)

        def one(t, carry):
            at = pl.ds(pl.multiple_of(t * width, 128), width)
            da1[...] += dot_nt(dqkv_ref[:, at], wqkv_ref[:, at])
            return carry

        lax.fori_loop(0, 3, one, 0)
        dv, dgain = rms_back(da1[...], x_ref[...].astype(F32), gs_ref[0:1, :])
        out.ref[...] = dh1_ref[...] + dv
        out.flush()

        def weights(h, carry):
            at = pl.ds(pl.multiple_of(h * 3 * half, 128), 3 * half)
            columns.store(both.ref, h, "qkv", dot_tn(a1_ref[...], dqkv_ref[:, at]), place_ref)
            return carry

        lax.fori_loop(0, 2, weights, 0)
        gains = jnp.concatenate([dgain, ggc_ref[...], ggf_ref[...], jnp.zeros((5, width), F32)], 0)
        misc = [gb_ref[...]] + [gains[:, j * 128 : (j + 1) * 128] for j in range(width // 128)]
        misc.append(jnp.zeros((more * part - misc_rows, 128), F32))
        misc = jnp.concatenate(misc, 0).astype(BF)
        for i in range(more):
            for slot in range(2):
                both.ref[slot, columns.units + i] = misc[i * part : (i + 1) * part]

    return call(
        "self_weights",
        body,
        (shape_of(F32, rows, width), columns.shape(more), columns.shape(more)),
        [SMEM] + [VMEM] * 9,
        (DRAIN, PAIR, PAIR),
        (
            place, dh1, w_qkv, x, a1, dqkv, gains, gbias,
            gain_cross_grad, gain_ff_grad,
        ),
        scratch=[pltpu.VMEM((rows, width), F32)],
    )


def swap(value, axis, bit):
    size = lax.axis_size(axis)
    return lax.ppermute(value, axis, [(i, i ^ bit) for i in range(size)])


class Bucket:
    def __init__(self, rows, terms, steps, keep_all=False):
        self.rows, self.terms, self.steps, self.keep_all = rows, terms, list(steps), keep_all


def sum_kernel(groups, dtype=BF):
    operands, specs, plan = [], [], []
    for i, jobs in enumerate(groups):
        at = 0
        for rows, terms in jobs:
            plan.append((i, at, rows, len(operands), len(terms)))
            at += rows
            for array, off in terms:
                operands.append(array)
                spec = (pl.Element(rows), pl.Element(128))
                specs.append(pl.BlockSpec(spec, functools.partial(lambda off, *_: (off, 0), off)))
    sizes = [sum(rows for rows, _ in jobs) for jobs in groups]

    def body(*refs):
        outs = refs[len(operands) :]
        for i, at, rows, first, count in plan:
            total = refs[first][...].astype(F32)
            for r in refs[first + 1 : first + count]:
                total = total + r[...].astype(F32)
            outs[i][at : at + rows, :] = total.astype(dtype)

    return call(
        "sum_kernel",
        body,
        tuple(shape_of(dtype, size, 128) for size in sizes),
        specs,
        tuple(whole(size, 128) for size in sizes),
        operands,
        grid=(1,),
    )


def send_round(cost, *members, settle=()):
    groups = {}
    for m in members:
        step = m.steps[0]
        groups.setdefault((step, m) if isinstance(m, Total) else step, []).append(m)
    jobs = []
    for group in groups.values():
        jobs.append([])
        for m in group:
            if isinstance(m, Total):
                jobs[-1] += m.next_jobs()
            elif m.keep_all:
                jobs[-1].append((m.rows, m.terms))
            else:
                m.rows //= 2
                jobs[-1].append((m.rows, [(array, off + m.rows) for array, off in m.terms]))
    if settle:
        jobs.append([(b.rows, b.terms) for b in settle])
    sent = sum_kernel(jobs)
    at = 0
    for b in settle:
        b.terms = [(sent[-1], at)]
        at += b.rows
    for group, payload in zip(groups.values(), sent):
        axis, bit = group[0].steps[0]
        got = swap(payload, axis, bit)
        at = 0
        for m in group:
            m.steps.pop(0)
            if isinstance(m, Total):
                m.moved(payload, got)
                continue
            if m.keep_all:
                m.terms = [(payload, at), (got, at)]
            else:
                m.terms = m.terms + [(got, at)]
            at += m.rows
    shadow(cost)


def rest_of(*buckets):
    while any(b.steps for b in buckets):
        send_round(3, *[b for b in buckets if b.steps])


def weight_buckets(columns, keep, send, orders, y_bits):
    rows = columns.units * columns.part
    keep, send = in_hbm(keep.reshape(-1, 128)), send.reshape(-1, 128)
    got = swap(send, "dp", 1)
    over = [[("blk", b) for b in order] for order in orders]
    along = [("dp", 2 * b) for b in y_bits]
    buckets = []
    for _, blocks, order, unit in columns.sections:
        steps = along + over[0] if order == "y" else over[order]
        at = unit * columns.part
        size = blocks * columns.chunks * columns.part
        buckets.append(Bucket(size, [(keep, at), (got, at)], steps))
    if keep.shape[0] > rows:
        buckets.append(Bucket(keep.shape[0] - rows, [(keep, rows), (got, rows)], over[0], keep_all=True))
    return buckets


def join_encodings(buckets, shard_rows, width):
    terms = [(bucket, array, off) for bucket in buckets for array, off in bucket.terms]

    def body(*refs):
        out = refs[-1]
        first = col = 0
        for bucket in buckets:
            mine = refs[first : first + len(bucket.terms)]
            first += len(bucket.terms)
            for at in range(0, bucket.rows, 128):
                total = mine[0][at : at + 128, :].astype(F32)
                for r in mine[1:]:
                    total = total + r[at : at + 128, :].astype(F32)
                out[:, col : col + 128] = jnp.transpose(total)
                col += 128

    return call(
        "join_encodings",
        body,
        shape_of(F32, shard_rows, width),
        [
            pl.BlockSpec(
                (pl.Element(bucket.rows), pl.Element(shard_rows)),
                functools.partial(lambda off, *_: (off, 0), off),
            )
            for bucket, _, off in terms
        ],
        whole(shard_rows, width),
        [array for _, array, _ in terms],
        grid=(1,),
    )


class Total:
    def __init__(self, groups, small, dp_size):
        self.groups, self.small, self.dp_size = groups, small, dp_size
        self.jobs, self.bases = [], []
        at = 0
        for _, buckets in groups:
            base = []
            for bucket in buckets:
                self.jobs.append((bucket.rows, bucket.terms))
                base.append(at)
                at += bucket.rows
            self.bases.append(base)
        self.small_at = []
        for bucket in small:
            self.jobs.append((bucket.rows, bucket.terms))
            self.small_at.append((at, bucket.rows))
            at += bucket.rows
        self.rows = at
        self.steps = [("dp", 2 * m) for m in range(1, dp_size // 2)] + [("dp", 1)]
        self.parts = []

    def next_jobs(self):
        if len(self.steps) > 1 or not self.parts:
            return [(self.rows, [(self.parts[0], 0)])] if self.parts else self.jobs
        jobs, self.spots, at = [], [], 0
        for (columns, _), base in zip(self.groups, self.bases):
            spots = []
            for (_, blocks, order, _), first in zip(columns.sections, base):
                if order == "y":
                    rows = blocks // columns.y_parts * columns.part
                    spots.append([at + i * rows for i in range(len(self.parts))])
                    jobs += [(rows, [(p, first)]) for p in self.parts]
                    at += rows * len(self.parts)
                else:
                    rows = blocks * columns.part
                    spots.append(at)
                    jobs.append((rows, [(p, first) for p in self.parts]))
                    at += rows
            self.spots.append(spots)
        self.small_spots = []
        for first, rows in self.small_at:
            jobs.append((rows, [(p, first) for p in self.parts]))
            self.small_spots.append((at, rows))
            at += rows
        return jobs

    def moved(self, payload, got):
        if self.steps or not self.parts:
            self.parts = self.parts + [got] if self.parts else [payload, got]
        else:
            self.own, self.other = payload, got

    def finish(self, place, arrays, small=None):
        outs = []
        for (columns, _), spots, named in zip(self.groups, self.spots, arrays):
            for name, stack in named:
                outs.append((columns, spots, name, stack, dict(columns.names)[name] // stack))
        y_parts = self.dp_size // 2

        def body(place_ref, own_ref, other_ref, *refs):
            core, y = place_ref[0], place_ref[2]
            sides = ((core, own_ref), (1 - core, other_ref))

            def put(ref, columns, half, j, at):
                row, off = divmod(j * 128, half)
                for which, src in sides:
                    lane = pl.multiple_of(which * half + off, 128)
                    ref[row * columns.part : (row + 1) * columns.part, pl.ds(lane, 128)] = src[
                        at : at + columns.part, :
                    ].astype(F32)

            for ref, (columns, spots, name, stack, half) in zip(refs, outs):
                far = []
                for j in range(stack * half // 128):
                    i, y_of, k = columns.find(columns.first(name) + j)
                    if y_of is None:
                        put(ref, columns, half, j, spots[i] + k * columns.part)
                    else:
                        far.append((j, spots[i], y_of, k))
                for y_is in range(y_parts if far else 0):

                    @pl.when(y == y_is)
                    def _():
                        for j, at, y_of, k in far:
                            put(ref, columns, half, j, at[y_is ^ y_of] + k * columns.part)

            if small:
                bias_ref, *gain_refs = refs[len(outs) :]
                blk = place_ref[1]
                at, rows = self.small_spots[0]
                misc = own_ref[at : at + rows, :].astype(F32)
                bias = jnp.concatenate([misc[:16], jnp.zeros((112, 128), F32)], 0)
                bias = pltpu.roll(bias, lax.rem(128 - blk * bias_part, 128), 1)
                bias_ref[...] = jnp.transpose(bias)[:bias_part, :heads]
                gains = jnp.concatenate(
                    [misc[16 + 8 * j : 24 + 8 * j] for j in range(width // 128)], 1
                )
                gains = pltpu.roll(gains, lax.rem(width - blk * part, width), 1)
                for i, ref in enumerate(gain_refs):
                    ref[...] = gains[i : i + 1, :part]

        shapes = [shape_of(F32, stack * columns.part, 2 * half) for columns, _, _, stack, half in outs]
        if small:
            heads, buckets, chunks = small
            bias_part = buckets // chunks
            part = self.groups[0][0].part
            width = part * chunks
            shapes += [shape_of(F32, bias_part, heads)] + [shape_of(F32, 1, part)] * 3
        return call(
            "finish",
            body,
            tuple(shapes),
            [SMEM, VMEM, VMEM],
            (VMEM,) * len(shapes),
            (place, self.own, self.other),
        )


def gather_encodings(own, bits):
    if len(bits) == 3:
        x, z, far = bits
        r_far, r_x = swap(own, "blk", far), swap(own, "blk", x)

        def second():
            r_z, r_zf = swap(own, "blk", z), swap(r_far, "blk", z)
            r_xf = swap(r_far, "blk", x)

            def third():
                r_xz = swap(r_z, "blk", x)
                r_xzf = swap(r_xf, "blk", z)
                arrays = [own, r_far, r_x, r_z, r_zf, r_xf, r_xz, r_xzf]
                return arrays, [[0], [far], [x], [z], [z | far], [x | far], [x | z], [x | z | far]]

            return [r_z, r_zf, r_xf], third

        return [r_far, r_x], second
    got, rel = own, [0]
    for bit in reversed(bits):
        got = jnp.concatenate([got, swap(got, "blk", bit)], 0)
        rel = rel + [r ^ bit for r in rel]
    return [], lambda: ([], lambda: ([got], [rel]))


def local(
    dec_in,
    encodings,
    enc_question,
    enc_valid,
    tgt_question,
    gain_self,
    w_qkv,
    rel_bias,
    w_self_out,
    gain_cross,
    w_cross_q,
    w_cross_kv,
    w_cross_out,
    gain_ff,
    w_ff_in,
    w_ff_out,
    grad_out,
):
    x = dec_in[0]
    gy = grad_out[0]
    rows, width = x.shape
    bucket_count, heads = rel_bias.shape
    hidden = w_ff_in.shape[1]
    half = width // 2
    chunks = lax.axis_size("blk")
    part = width // chunks
    dp_size = lax.axis_size("dp")
    shard_rows = encodings.shape[1]
    bits = [1 << i for i in range(chunks.bit_length() - 1)]
    y_bits = [1 << i for i in range(dp_size.bit_length() - 2)]
    y_parts = dp_size // 2
    blk = lax.axis_index("blk")
    dp = lax.axis_index("dp")
    orders = [bits, bits[1::-1] + bits[2:]]

    def layout(names, *sections):
        return Columns(names, sections, y_parts, chunks, part)

    def along_y(blocks):
        return blocks // (2 * y_parts) * y_parts

    stack = hidden // width
    blocks = half // 128
    cols_out = layout([("out", stack * half)], (stack * blocks, "y"))
    cols_in = layout([("in", hidden // 2)], (2 * stack * blocks // 3, 0), (stack * blocks // 3, 1))
    far_x, far_s = along_y(16 * blocks // 3), along_y(4 * blocks)
    near_x, near_s = 5 * blocks - far_x, 3 * blocks - far_s
    cols_x = layout(
        [("q", half), ("out", half), ("self", half), ("kv", width)],
        (near_x, 0), (far_x, "y"),
    )
    cols_s = layout([("qkv", 3 * half)], (near_s, 0), (far_s, "y"))

    places = [[chunk_place(c, blk, order) for c in range(chunks)] for order in orders]
    y_places = [chunk_place(y, dp // 2, y_bits) for y in range(y_parts)]
    numbers = [lax.rem(dp, 2), blk, dp // 2]
    for order in orders:
        spots = [0] * chunks
        for r in range(chunks):
            spots[chunk_spot(r, bits)] = chunk_spot(r, order)
        numbers += [jnp.int32(spot) for spot in spots]
    for columns in (cols_out, cols_in, cols_x, cols_s):
        columns.at = len(numbers)
        numbers += columns.table(places, y_places)
    place = jnp.stack(numbers).astype(jnp.int32)

    ORDER.clear()
    ROOMY[:] = [chunks * shard_rows <= 1024]
    tags = jnp.where(enc_valid[0] == 1, enc_question[0], -1).astype(BF)
    tag_rows = jnp.zeros((16, width), BF).at[0, :shard_rows].set(tags)
    enc_own = jnp.concatenate([encodings[0], tag_rows], 0)[None]
    gains = jnp.stack([gain_self, gain_cross, gain_ff])
    got, second = gather_encodings(enc_own, bits)
    shadow(10)
    a1, qkv, p1, o1_near, o1, wso_near, wcq_near, x_near = self_attention(
        x, gains, w_qkv, rel_bias, [w_self_out, w_cross_q, x]
    )
    more, third = second()
    shadow(10)
    h1_near, cq_near, h1, a2, cq, gy = self_project(
        x_near, o1_near, wso_near, gains, wcq_near, [gy]
    )
    pieces, rel = third()
    shadow(10, *more[1:2])
    dhid, wkv_near, wco_near = hidden_gradient(gy, w_ff_out, [w_cross_kv, w_cross_out])
    spots = [[int(chunk_spot(r, bits)) for r in group] for group in rel]
    enc, kv, e, inv, o2, h2, a3, w1_near = cross_forward(
        pieces, spots, shard_rows, tgt_question[0], cq_near, h1_near, wkv_near, wco_near, gains, [w_ff_in]
    )

    dpre, hid, keep, send = feed_hidden(place, a3, gy, dhid, w1_near, cols_out)
    (b_out,) = weight_buckets(cols_out, keep, send, orders, y_bits)
    shadow(30)
    keep, send, h2_near = feed_weights(place, a3, dpre, cols_in, [h2])
    b_in, b_jn = weight_buckets(cols_in, keep, send, orders, y_bits)
    send_round(30, b_out)
    dh2, gain_ff_grad = feed_back(dpre, w1_near, h2_near, gains, gy)
    send_round(5.5, b_in, b_jn)
    pairs = heads // 2
    dcq, dkt, dvt, wcq_near, h1_near, a2, o2, o1, enc, wkv_near = cross_backward(
        0, pairs, dh2, o2, inv, cq, kv, e, wco_near, [w_cross_q, h1, a2, o2, o1, enc, w_cross_kv]
    )
    dcq, dkt, dvt = [dcq], [dkt], [dvt]
    dh1, gain_cross_grad = cross_query_back(dcq, wcq_near, h1_near, gains, dh2)
    send_round(5.5, b_jn, b_out, b_in)
    genc, keep, send, hid, w2_near, h2_near = cross_weights(
        place, dh2, o2, dcq, dkt, dvt, enc, a2, wkv_near, dh1, o1, cols_x, [hid, w_ff_out, h2]
    )
    enc_rows = chunks * shard_rows * width // 128
    genc = in_hbm(genc.reshape(enc_rows, shard_rows))
    cut = enc_rows // blocks * (2 * blocks // 3)
    b_ea = Bucket(cut, [(genc, 0)], [("blk", b) for b in orders[0]])
    b_eb = Bucket(enc_rows - cut, [(genc, cut)], [("blk", b) for b in orders[1]])
    b_xa, b_xb = weight_buckets(cols_x, keep, send, orders, y_bits)
    send_round(40, b_ea, b_out, b_eb, b_jn, settle=[b_in])
    out, wso_near, qkv, p1 = feed_out(hid, w2_near, h2_near, [w_self_out, qkv, p1])
    dqkv, gbias, wqkv_near, x_near, a1 = self_backward(
        dh1, wso_near, qkv, p1, bucket_count, heads, [w_qkv, x, a1]
    )
    send_round(5, b_xb, b_xa, b_eb, b_ea, b_in, b_out, settle=[b_jn])
    grad_dec, keep, send = self_weights(
        place, dh1, a1, dqkv, x_near, gains, wqkv_near, gbias, gain_cross_grad, gain_ff_grad, cols_s
    )
    b_sa, b_sb, b_misc = weight_buckets(cols_s, keep, send, orders, y_bits)
    send_round(25, b_xa, b_ea, b_eb, settle=[b_in, b_out, b_xb])
    send_round(4, b_sb, b_sa, b_misc)
    send_round(4, b_xb)
    send_round(4, b_sa, b_misc, b_sb)
    rest_of(b_out, b_in, b_jn)
    total_ff = Total([(cols_out, [b_out]), (cols_in, [b_in, b_jn])], [], dp_size)
    send_round(4, b_xa, b_xb, total_ff, settle=[b_ea, b_eb])
    rest_of(b_ea, b_eb)
    send_round(4, b_sb, b_sa, b_misc)
    send_round(4, b_xb, total_ff)
    grad_enc = join_encodings([b_ea, b_eb], shard_rows, width)
    send_round(4, b_sb)
    rest_of(total_ff)
    grad_ff_out, grad_ff_in = total_ff.finish(place, [[("out", stack)], [("in", 1)]])
    rest_of(b_xa, b_xb)
    total_x = Total([(cols_x, [b_xa, b_xb])], [], dp_size)
    send_round(4, total_x)
    rest_of(b_sa, b_sb, b_misc)
    total_s = Total([(cols_s, [b_sa, b_sb])], [b_misc], dp_size)
    send_round(0.5, total_s)
    rest_of(total_x)
    rest_of(total_s)
    grad_cross_out, grad_cross_q, grad_self_out, grad_cross_kv = total_x.finish(
        place, [[("out", 1), ("q", 1), ("self", 1), ("kv", 1)]]
    )
    grad_qkv, grad_bias, *gains = total_s.finish(
        place, [[("qkv", 1)]], (heads, bucket_count, chunks)
    )
    gains = [gain.reshape(part) for gain in gains]
    return (
        out[None],
        grad_dec[None],
        grad_enc[None],
        gains[0],
        grad_qkv,
        grad_bias,
        grad_self_out,
        gains[1],
        grad_cross_q,
        grad_cross_kv,
        grad_cross_out,
        gains[2],
        grad_ff_in,
        grad_ff_out,
    )


def solution(mesh):
    return jax.shard_map(
        local,
        mesh=mesh,
        in_specs=(
            P("dp", "blk", None),
            P("dp", "blk", None),
            P("dp", "blk"),
            P("dp", "blk"),
            P("dp", "blk"),
            P(),
            P(),
            P(),
            P(),
            P(),
            P(),
            P(),
            P(),
            P(),
            P(),
            P(),
            P("dp", "blk", None),
        ),
        out_specs=(
            P("dp", "blk", None),
            P("dp", "blk", None),
            P("dp", "blk", None),
            P("blk"),
            P("blk", None),
            P("blk", None),
            P("blk", None),
            P("blk"),
            P("blk", None),
            P("blk", None),
            P("blk", None),
            P("blk"),
            P("blk", None),
            P("blk", None),
        ),
        check_vma=False,
    )
```
